32 devices in a mesh: seq: 16 (over z, y, core), fsdp: 2 (over x).
Axes of the slice: x: 2, y: 2, z: 4, core: 2. Of those that a mesh axis runs over, the one named last changes fastest.
Arguments:
- tokens: bfloat16 [4096, 1536], P(('seq', 'fsdp')), may hold values from -6 to 6
- cotangent: bfloat16 [4096, 1536], P(('seq', 'fsdp')), may hold values from -6 to 6
- lengths: int32 [2, 5], replicated, may hold values from 1 to 1920, as said below
- mix_weight: float32 [1, 1536, 3072], P(None, ('seq', 'fsdp')), may hold values from -0.078125 to 0.078125
- out_weight: float32 [1, 1536, 1536], P(None, ('seq', 'fsdp')), may hold values from -0.875 to 0.875
- in_weight: float32 [1, 1536, 8192], P(None, ('seq', 'fsdp')), may hold values from -0.078125 to 0.078125
- down_weight: float32 [1, 4096, 1536], P(None, ('seq', 'fsdp')), may hold values from -0.09375 to 0.09375
- norm_gains: float32 [1, 2, 1536], P(None, None, ('seq', 'fsdp')), may hold values from 0.5 to 6
- mix_first: float32 [1, 1536, 3072], P(None, ('seq', 'fsdp')), may hold values from -0.00012207031 to 0.00012207031
- out_first: float32 [1, 1536, 1536], P(None, ('seq', 'fsdp')), may hold values from -1.9073486e-05 to 1.9073486e-05
- in_first: float32 [1, 1536, 8192], P(None, ('seq', 'fsdp')), may hold values from -9.1552734e-05 to 9.1552734e-05
- down_first: float32 [1, 4096, 1536], P(None, ('seq', 'fsdp')), may hold values from -9.1552734e-05 to 9.1552734e-05
- norm_first: float32 [1, 2, 1536], P(None, None, ('seq', 'fsdp')), may hold values from -7.6293945e-05 to 7.6293945e-05
- mix_second: float32 [1, 1536, 3072], P(None, ('seq', 'fsdp')), may hold values from 3.8913012e-10 to 1.5565205e-09
- out_second: float32 [1, 1536, 1536], P(None, ('seq', 'fsdp')), may hold values from 4.8912163e-12 to 1.9564865e-11
- in_second: float32 [1, 1536, 8192], P(None, ('seq', 'fsdp')), may hold values from 9.6319334e-11 to 3.8527734e-10
- down_second: float32 [1, 4096, 1536], P(None, ('seq', 'fsdp')), may hold values from 9.6319334e-11 to 3.8527734e-10
- norm_second: float32 [1, 2, 1536], P(None, None, ('seq', 'fsdp')), may hold values from 7.705547e-11 to 3.082219e-10
Outputs:
- hidden_out: bfloat16 [4096, 1536], P(('seq', 'fsdp'))
- grad_tokens: float32 [4096, 1536], P(('seq', 'fsdp'))
- grad_norm: float32 [], replicated
- mix_grad: float32 [1, 1536, 3072], P(None, ('seq', 'fsdp'))
- mix_new: float32 [1, 1536, 3072], P(None, ('seq', 'fsdp'))
- mix_moment: float32 [1, 1536, 3072], P(None, ('seq', 'fsdp'))
- mix_square: float32 [1, 1536, 3072], P(None, ('seq', 'fsdp'))
- mix_copy: bfloat16 [1, 1536, 3072], P(None, ('seq', 'fsdp'))
- out_grad: float32 [1, 1536, 1536], P(None, ('seq', 'fsdp'))
- out_new: float32 [1, 1536, 1536], P(None, ('seq', 'fsdp'))
- out_moment: float32 [1, 1536, 1536], P(None, ('seq', 'fsdp'))
- out_square: float32 [1, 1536, 1536], P(None, ('seq', 'fsdp'))
- out_copy: bfloat16 [1, 1536, 1536], P(None, ('seq', 'fsdp'))
- in_grad: float32 [1, 1536, 8192], P(None, ('seq', 'fsdp'))
- in_new: float32 [1, 1536, 8192], P(None, ('seq', 'fsdp'))
- in_moment: float32 [1, 1536, 8192], P(None, ('seq', 'fsdp'))
- in_square: float32 [1, 1536, 8192], P(None, ('seq', 'fsdp'))
- in_copy: bfloat16 [1, 1536, 8192], P(None, ('seq', 'fsdp'))
- down_grad: float32 [1, 4096, 1536], P(None, ('seq', 'fsdp'))
- down_new: float32 [1, 4096, 1536], P(None, ('seq', 'fsdp'))
- down_moment: float32 [1, 4096, 1536], P(None, ('seq', 'fsdp'))
- down_square: float32 [1, 4096, 1536], P(None, ('seq', 'fsdp'))
- down_copy: bfloat16 [1, 4096, 1536], P(None, ('seq', 'fsdp'))
- norm_grad: float32 [1, 2, 1536], P(None, None, ('seq', 'fsdp'))
- norm_new: float32 [1, 2, 1536], P(None, None, ('seq', 'fsdp'))
- norm_moment: float32 [1, 2, 1536], P(None, None, ('seq', 'fsdp'))
- norm_square: float32 [1, 2, 1536], P(None, None, ('seq', 'fsdp'))
- norm_copy: bfloat16 [1, 2, 1536], P(None, None, ('seq', 'fsdp'))
The draws below stay inside these ranges and needn't reach their ends.
Inputs may be any that keep to these rules, and one draw needn't show every extreme that they name: `lengths`: in each group one document, which one drawn from the seed, is 128 * (15) tokens long and begins within the group's first 64 tokens; every other document is at most 21 tokens long; the group's tokens after its documents are padding.
All inputs are finite; a program needn't handle non-finite values.
Results may differ from the reference program's by a relative error of at most 0.025.
The reference program's roundings to bfloat16 on the way count: a program that leaves them out, or rounds other values in their place, can miss the bound.
Values may be sent and summed in bfloat16 or wider, within the bound.
A program may use at most 448 MiB of HBM per device.

```python
import math
import jax
import jax.numpy as jnp
from jax import lax

D = 1536
HEADS = 16
KV_HEADS = 8
HEAD_DIM = 96
FF = 4096
LAYERS = 1
TOK_DEV = 128
DOCS = 5
STEP_NUMBER = 10
GROUP = 2048
TOKENS = 4096
PARAMS = 25955328
N_SEQ = 16
N_FSDP = 2


def draw_lengths(key, part):
    key = jax.random.fold_in(key, 7)
    count_key, head_key, tail_key = jax.random.split(key, 3)
    short_most = TOK_DEV // 6
    head_count = jax.random.randint(count_key, (N_FSDP, 1), 1, DOCS - 1).astype(jnp.int32)
    head_lens = jax.random.randint(head_key, (N_FSDP, DOCS), 1, short_most + 1).astype(jnp.int32)
    tail_lens = jax.random.randint(tail_key, (N_FSDP, DOCS), 1, short_most + 1).astype(jnp.int32)
    slot_index = jnp.arange(DOCS, dtype=jnp.int32)[None, :]
    longest = jnp.full((N_FSDP, DOCS), TOK_DEV * N_SEQ - TOK_DEV, jnp.int32)
    chosen = jnp.where(slot_index < head_count, head_lens, jnp.where(slot_index == head_count, longest, tail_lens))
    return chosen.astype(jnp.int32)


def draw_norm_gains(key, part):
    key = jax.random.fold_in(key, 11)
    slope_ramp = jnp.arange(D, dtype=jnp.float32) / (D - 1)
    rough = 1.0 + 0.15 * jnp.clip(jax.random.normal(key, (LAYERS, 2, D), jnp.float32), -3.0, 3.0)
    return (1.0 + 2.0 * slope_ramp) * rough


def block_levels(stream_key, extent, pieces, smallest, top_value):
    factor_of = 1.0
    for axis_at, shards_of in pieces:
        draws = jax.random.uniform(jax.random.fold_in(jax.random.fold_in(stream_key, 6), axis_at), (shards_of,), jnp.float32, smallest / len(pieces), top_value / len(pieces))
        factor_of = factor_of * jnp.repeat(jnp.exp(draws), extent[axis_at] // shards_of).reshape((-1,) + (1,) * (len(extent) - 1 - axis_at))
    return factor_of


def bell_draw(own_key, shape, width, most, cuts=(), kind=jnp.bfloat16):
    level = block_levels(own_key, shape, cuts, -0.22, 0.18) if cuts else 1.0
    values = jax.random.normal(own_key, shape, jnp.float32) * width * level
    return jnp.minimum(jnp.maximum(values, -most), most).astype(kind)


def setup_inputs(seed: int = 0) -> dict:
    arg_keys = jax.random.split(jax.random.key(seed), 19)
    tokens = bell_draw(arg_keys[0], (TOKENS, D), 1.0, 6.0, ((0, 32),))
    cotangent = bell_draw(arg_keys[1], (TOKENS, D), 1.0, 6.0, ((0, 32),))
    lengths = draw_lengths(jax.random.fold_in(arg_keys[18], 71), 0)
    mix_weight = bell_draw(arg_keys[3], (LAYERS, D, D + 2 * KV_HEADS * HEAD_DIM), (4 * D) ** -0.5, 0.078125, ((1, 32),), jnp.float32)
    out_weight = bell_draw(arg_keys[4], (LAYERS, D, D), (max(1, 64 * D // (TOK_DEV * N_SEQ))) ** -0.5, 0.875, ((1, 32),), jnp.float32)
    in_weight = bell_draw(arg_keys[5], (LAYERS, D, 2 * FF), (4 * D) ** -0.5, 0.078125, ((1, 32),), jnp.float32)
    down_weight = bell_draw(arg_keys[6], (LAYERS, FF, D), FF ** -0.5, 0.09375, ((1, 32),), jnp.float32)
    norm_gains = draw_norm_gains(jax.random.fold_in(arg_keys[18], 71), 0)
    mix_first = bell_draw(arg_keys[8], (LAYERS, D, D + 2 * KV_HEADS * HEAD_DIM), (0.11 / PARAMS ** 0.5), 0.00012207031, ((1, 32),), jnp.float32)
    out_first = bell_draw(arg_keys[9], (LAYERS, D, D), (0.8 / (GROUP * PARAMS) ** 0.5), 1.9073486328125e-05, ((1, 32),), jnp.float32)
    in_first = bell_draw(arg_keys[10], (LAYERS, D, 2 * FF), (0.08 / PARAMS ** 0.5), 9.1552734375e-05, ((1, 32),), jnp.float32)
    down_first = bell_draw(arg_keys[11], (LAYERS, FF, D), (0.08 / PARAMS ** 0.5), 9.1552734375e-05, ((1, 32),), jnp.float32)
    norm_first = bell_draw(arg_keys[12], (LAYERS, 2, D), (0.07 / PARAMS ** 0.5), 7.62939453125e-05, ((2, 32),), jnp.float32)
    mix_second = jnp.clip(jnp.exp(math.log(1.5565204680711986e-09) - 1.3862944 * jax.random.uniform(arg_keys[13], (LAYERS, D, D + 2 * KV_HEADS * HEAD_DIM), jnp.float32) ** block_levels(arg_keys[13], (LAYERS, D, D + 2 * KV_HEADS * HEAD_DIM), ((1, 32),), -0.2, 0.2)), 3.8913011701779965e-10, 1.5565204680711986e-09)
    out_second = jnp.clip(jnp.exp(math.log(1.9564865352816874e-11) - 1.3862944 * jax.random.uniform(arg_keys[14], (LAYERS, D, D), jnp.float32) ** block_levels(arg_keys[14], (LAYERS, D, D), ((1, 32),), -0.2, 0.2)), 4.8912163382042184e-12, 1.9564865352816874e-11)
    in_second = jnp.clip(jnp.exp(math.log(3.852773378110186e-10) - 1.3862944 * jax.random.uniform(arg_keys[15], (LAYERS, D, 2 * FF), jnp.float32) ** block_levels(arg_keys[15], (LAYERS, D, 2 * FF), ((1, 32),), -0.2, 0.2)), 9.631933445275465e-11, 3.852773378110186e-10)
    down_second = jnp.clip(jnp.exp(math.log(3.852773378110186e-10) - 1.3862944 * jax.random.uniform(arg_keys[16], (LAYERS, FF, D), jnp.float32) ** block_levels(arg_keys[16], (LAYERS, FF, D), ((1, 32),), -0.2, 0.2)), 9.631933445275465e-11, 3.852773378110186e-10)
    norm_second = jnp.clip(jnp.exp(math.log(3.0822189245327536e-10) - 1.3862944 * jax.random.uniform(arg_keys[17], (LAYERS, 2, D), jnp.float32) ** block_levels(arg_keys[17], (LAYERS, 2, D), ((2, 32),), -0.2, 0.2)), 7.705547311331884e-11, 3.0822189245327536e-10)
    return {"tokens": tokens, "cotangent": cotangent, "lengths": lengths, "mix_weight": mix_weight, "out_weight": out_weight, "in_weight": in_weight, "down_weight": down_weight, "norm_gains": norm_gains, "mix_first": mix_first, "out_first": out_first, "in_first": in_first, "down_first": down_first, "norm_first": norm_first, "mix_second": mix_second, "out_second": out_second, "in_second": in_second, "down_second": down_second, "norm_second": norm_second}


@jax.custom_vjp
def low(v):
    return lax.optimization_barrier(v.astype(jnp.bfloat16)).astype(jnp.float32)

@jax.custom_vjp
def low_back(v):
    return v

def low_keep(v):
    return (low(v), None)

def low_pass(kept, grad):
    return (grad,)

def back_keep(v):
    return (v, None)

def back_low(kept, grad):
    return (low(grad),)
low.defvjp(low_keep, low_pass)
low_back.defvjp(back_keep, back_low)
EPS_NORM = 1e-05
ROPE_BASE = 100000.0
FLOOR_SCORE = -1e+30
LEARN_RATE = 0.05
OUT_RATE = 0.2
GAIN_RATE = 2.0
BETA_ONE = 0.9
BETA_TWO = 0.99
EPS_ADAM = 1e-08
WEIGHT_DECAY = 0.1
CLIP_NORM = 1.0

def product(left, right):
    return jnp.dot(left, right, precision=lax.Precision.HIGHEST, preferred_element_type=jnp.float32)

def doc_layout(places, doc_lens):
    doc_ends = jnp.cumsum(doc_lens).astype(jnp.int32)
    passed = (places[:, None] >= doc_ends[None, :]).astype(jnp.int32)
    segment = lax.optimization_barrier(jnp.sum(passed, axis=1)).astype(jnp.int32)
    offset = lax.optimization_barrier(jnp.sum(passed * doc_lens[None, :], axis=1)).astype(jnp.int32)
    return (segment, (places - offset).astype(jnp.int32))

def group_layout(lengths):
    token_index = jnp.arange(TOK_DEV * N_SEQ, dtype=jnp.int32)
    layout_pairs = [doc_layout(token_index, lengths[group_index]) for group_index in range(N_FSDP)]
    segment = jnp.stack([layout_pair[0] for layout_pair in layout_pairs])
    places = jnp.stack([layout_pair[1] for layout_pair in layout_pairs])
    keep_rows = (segment < DOCS).astype(jnp.float32)
    return (segment, places, keep_rows)

def arrange(values):
    width_last = values.shape[-1]
    return values.reshape(N_SEQ, N_FSDP, TOK_DEV, width_last).transpose(1, 0, 2, 3).reshape(N_FSDP * N_SEQ * TOK_DEV, width_last)

def disarrange(values):
    width_last = values.shape[-1]
    return values.reshape(N_FSDP, N_SEQ, TOK_DEV, width_last).transpose(1, 0, 2, 3).reshape(N_FSDP * N_SEQ * TOK_DEV, width_last)

def rotate(vectors, places, direction):
    half_dim = vectors.shape[-1] // 2
    inverse = ROPE_BASE ** (-jnp.arange(half_dim, dtype=jnp.float32) * 2.0 / vectors.shape[-1])
    angles = places.astype(jnp.float32)[:, None] * inverse[None, :]
    cosine = jnp.cos(angles)[:, None, :]
    sine_term = direction * jnp.sin(angles)[:, None, :]
    former = vectors[..., :half_dim]
    latter = vectors[..., half_dim:]
    return jnp.concatenate([former * cosine - latter * sine_term, latter * cosine + former * sine_term], axis=-1)

def rms_norm(values, gain):
    return values * lax.rsqrt(lax.optimization_barrier(jnp.mean(values * values, axis=-1, keepdims=True)) + EPS_NORM) * gain

def attend_group(queries, keys, values, segment):
    row_total = queries.shape[0]
    block_rows = min(512, row_total)
    token_index = jnp.arange(row_total, dtype=jnp.int32)
    count = row_total // block_rows
    block_args = (queries.reshape(count, block_rows, KV_HEADS, HEADS // KV_HEADS, HEAD_DIM), segment.reshape(count, block_rows), token_index.reshape(count, block_rows))

    @jax.checkpoint
    def one_block(block_arg):
        block_queries, block_segment, block_index = block_arg
        raw_scores = jnp.einsum('qkgd,skd->qkgs', block_queries, keys, precision=lax.Precision.HIGHEST) * HEAD_DIM ** (-0.5)
        allowed = (block_segment[:, None] == segment[None, :]) & (token_index[None, :] <= block_index[:, None])
        scores = jnp.where(allowed[:, None, None, :], low_back(raw_scores), FLOOR_SCORE)
        weights = low(jax.nn.softmax(scores, axis=-1))
        return jnp.einsum('qkgs,skd->qkgd', weights, values, precision=lax.Precision.HIGHEST)
    return lax.map(one_block, block_args).reshape(row_total, HEADS * HEAD_DIM)

def block_forward(stream, mix_full, out_full, in_full, down_full, gain_full, segment, places, keep_rows):
    row_total = stream.shape[0]
    group_rows = row_total // N_FSDP
    key_width = KV_HEADS * HEAD_DIM
    normed = low(rms_norm(stream, gain_full[0]))
    projected = low_back(product(normed, mix_full))
    queries = low(rotate(projected[:, :D].reshape(row_total, HEADS, HEAD_DIM), places, 1.0))
    keys = low(rotate(projected[:, D:D + key_width].reshape(row_total, KV_HEADS, HEAD_DIM), places, 1.0))
    values = low(projected[:, D + key_width:].reshape(row_total, KV_HEADS, HEAD_DIM))
    queries = queries.reshape(N_FSDP, group_rows, KV_HEADS, HEADS // KV_HEADS, HEAD_DIM)
    keys = keys.reshape(N_FSDP, group_rows, KV_HEADS, HEAD_DIM)
    values = values.reshape(N_FSDP, group_rows, KV_HEADS, HEAD_DIM)
    attended = jnp.concatenate([attend_group(queries[group_index], keys[group_index], values[group_index], segment[group_index]) for group_index in range(N_FSDP)], axis=0)
    attended = low(low_back(attended * keep_rows[:, None]))
    middle = stream + low_back(product(attended, out_full))
    normed_two = low(rms_norm(middle, gain_full[1]))
    gate_up = low_back(product(normed_two, in_full))
    hidden = low(jax.nn.silu(gate_up[:, :FF]) * gate_up[:, FF:])
    return middle + low_back(product(hidden, down_full))

def forward_pass(stream, mix_all, out_all, in_all, down_all, gain_all, segment, places, keep_rows):
    for layer_index in range(LAYERS):
        stream = block_forward(stream, low(mix_all[layer_index]), low(out_all[layer_index]), low(in_all[layer_index]), low(down_all[layer_index]), low(gain_all[layer_index]), segment, places, keep_rows)
    return stream

def adam_update(weight, first, second, grad, clip_scale, rate):
    clipped = grad * clip_scale
    first_new = BETA_ONE * first + (1.0 - BETA_ONE) * clipped
    second_new = BETA_TWO * second + (1.0 - BETA_TWO) * clipped * clipped
    first_hat = first_new / (1.0 - BETA_ONE ** STEP_NUMBER)
    second_hat = second_new / (1.0 - BETA_TWO ** STEP_NUMBER)
    updated = weight - rate * (first_hat / (jnp.sqrt(second_hat) + EPS_ADAM) + WEIGHT_DECAY * weight)
    return (updated, first_new, second_new)

def reference(tokens, cotangent, lengths, mix_weight, out_weight, in_weight, down_weight, norm_gains, mix_first, out_first, in_first, down_first, norm_first, mix_second, out_second, in_second, down_second, norm_second):
    segment, places, keep_rows = group_layout(lengths)
    flat_places = places.reshape(-1)
    flat_keep = keep_rows.reshape(-1)
    stream = arrange(tokens.astype(jnp.float32))
    seed_grad = arrange(cotangent.astype(jnp.float32))

    def run(stream_in, mix_all, out_all, in_all, down_all, gain_all):
        return forward_pass(stream_in, mix_all, out_all, in_all, down_all, gain_all, segment, flat_places, flat_keep)
    result, pullback = jax.vjp(run, stream, mix_weight, out_weight, in_weight, down_weight, norm_gains)
    grad_stream, mix_grad, out_grad, in_grad, down_grad, norm_grad = pullback(seed_grad)
    hidden_out = disarrange(result).astype(jnp.bfloat16)
    grad_tokens = disarrange(grad_stream)
    squares = jnp.sum(mix_grad * mix_grad) + jnp.sum(out_grad * out_grad) + jnp.sum(in_grad * in_grad) + jnp.sum(down_grad * down_grad) + jnp.sum(norm_grad * norm_grad)
    grad_norm = jnp.sqrt(squares)
    clip_scale = CLIP_NORM / jnp.maximum(grad_norm, CLIP_NORM)
    mix_new, mix_moment, mix_square = adam_update(mix_weight, mix_first, mix_second, mix_grad, clip_scale, LEARN_RATE)
    out_new, out_moment, out_square = adam_update(out_weight, out_first, out_second, out_grad, clip_scale, OUT_RATE)
    in_new, in_moment, in_square = adam_update(in_weight, in_first, in_second, in_grad, clip_scale, LEARN_RATE)
    down_new, down_moment, down_square = adam_update(down_weight, down_first, down_second, down_grad, clip_scale, LEARN_RATE)
    norm_new, norm_moment, norm_square = adam_update(norm_gains, norm_first, norm_second, norm_grad, clip_scale, GAIN_RATE)
    return (hidden_out, grad_tokens, grad_norm, mix_grad, mix_new, mix_moment, mix_square, mix_new.astype(jnp.bfloat16), out_grad, out_new, out_moment, out_square, out_new.astype(jnp.bfloat16), in_grad, in_new, in_moment, in_square, in_new.astype(jnp.bfloat16), down_grad, down_new, down_moment, down_square, down_new.astype(jnp.bfloat16), norm_grad, norm_new, norm_moment, norm_square, norm_new.astype(jnp.bfloat16))
```

```python
import jax
import jax.numpy as jnp
from jax import lax
from jax.experimental import pallas as pl
from jax.experimental.pallas import tpu as pltpu
from jax.sharding import PartitionSpec as P

D = 1536
HEADS = 16
KV_HEADS = 8
HEAD_DIM = 96
FF = 4096
LAYERS = 1
STEP_NUMBER = 10


EPS_NORM = 1e-05
ROPE_BASE = 100000.0
FLOOR_SCORE = -1e30
LEARN_RATE = 0.05
OUT_RATE = 0.2
GAIN_RATE = 2.0
BETA_ONE = 0.9
BETA_TWO = 0.99
EPS_ADAM = 1e-08
WEIGHT_DECAY = 0.1
CLIP_NORM = 1.0


def doc_layout(places, doc_lens):
    doc_ends = jnp.cumsum(doc_lens)
    passed = (places[:, None] >= doc_ends[None, :]).astype(jnp.int32)
    segment = jnp.sum(passed, axis=1)
    offset = jnp.sum(passed * doc_lens[None, :], axis=1)
    return (segment, places - offset)


def rotate(vectors, places, direction):
    half_dim = vectors.shape[-1] // 2
    inverse = ROPE_BASE ** (-jnp.arange(half_dim, dtype=jnp.float32) * 2.0 / vectors.shape[-1])
    angles = places.astype(jnp.float32)[:, None] * inverse[None, :]
    cosine = jnp.cos(angles)[:, None, :]
    sine_term = direction * jnp.sin(angles)[:, None, :]
    former = vectors[..., :half_dim]
    latter = vectors[..., half_dim:]
    return jnp.concatenate(
        [former * cosine - latter * sine_term, latter * cosine + former * sine_term], axis=-1
    )


def normalize(values, gain):
    scale_rows = lax.rsqrt(jnp.mean(values * values, axis=-1, keepdims=True) + EPS_NORM)
    unit_rows = values * scale_rows
    return (unit_rows * gain, unit_rows, scale_rows)


def norm_backward(grad_normed, unit_rows, scale_rows, gain):
    grad_gain = jnp.sum(grad_normed * unit_rows, axis=0)
    grad_unit = grad_normed * gain
    grad_values = scale_rows * (
        grad_unit - unit_rows * jnp.mean(grad_unit * unit_rows, axis=-1, keepdims=True)
    )
    return (grad_gain, grad_values)


def masked_scores(queries, key_block, first_key, query_places, query_segment, doc_lens):
    block_rows = key_block.shape[0]
    key_places = first_key + jnp.arange(block_rows, dtype=jnp.int32)
    key_segment, unused_places = doc_layout(key_places, doc_lens)
    allowed = (query_segment[:, None] == key_segment[None, :]) & (
        key_places[None, :] <= query_places[:, None]
    )
    key_heads = key_block.reshape(block_rows, KV_HEADS, HEAD_DIM)
    raw_scores = jnp.einsum(
        "qkgd,skd->qkgs", queries, key_heads, preferred_element_type=jnp.float32
    ) * HEAD_DIM ** (-0.5)
    return (jnp.where(allowed[:, None, None, :], raw_scores, FLOOR_SCORE), allowed)


def fold_block(carry, key_block, value_block, first_key, setting):
    queries, query_places, query_segment, doc_lens = setting
    running, totals, accumulated = carry
    block_rows = key_block.shape[0]
    scores, allowed = masked_scores(
        queries, key_block, first_key, query_places, query_segment, doc_lens
    )
    newest = jnp.maximum(running, jnp.max(scores, axis=-1))
    factor = jnp.exp(running - newest)
    weights = jnp.where(allowed[:, None, None, :], jnp.exp(scores - newest[..., None]), 0.0)
    totals = totals * factor + jnp.sum(weights, axis=-1)
    value_heads = value_block.reshape(block_rows, KV_HEADS, HEAD_DIM)
    accumulated = accumulated * factor[..., None] + jnp.einsum(
        "qkgs,skd->qkgd",
        weights.astype(jnp.bfloat16),
        value_heads,
        preferred_element_type=jnp.float32,
    )
    return (newest, totals, accumulated)


def fold_piece(carry, key_rows, value_rows, start, setting):
    total_rows = key_rows.shape[0]
    block_rows = 512

    def step(inner_state, number):
        first_key = start + number * block_rows
        key_block = lax.dynamic_slice_in_dim(key_rows, number * block_rows, block_rows, 0)
        value_block = lax.dynamic_slice_in_dim(value_rows, number * block_rows, block_rows, 0)
        state_out = fold_block(inner_state, key_block, value_block, first_key, setting)
        return (state_out, None)

    carry, unused_out = lax.scan(step, carry, jnp.arange(total_rows // block_rows, dtype=jnp.int32))
    return carry


def fetch_layer(mix_weight, out_weight, norm_gains, in_weight, down_weight, layer_index):
    mix_full, out_full, gain_full, in_full, down_full = (
        lax.all_gather(
            mix_weight[layer_index].astype(jnp.bfloat16), ("seq", "fsdp"), axis=0, tiled=True
        ),
        lax.all_gather(
            out_weight[layer_index].astype(jnp.bfloat16), ("seq", "fsdp"), axis=0, tiled=True
        ),
        lax.all_gather(
            norm_gains[layer_index].astype(jnp.bfloat16), ("seq", "fsdp"), axis=1, tiled=True
        ),
        lax.all_gather(
            in_weight[layer_index].astype(jnp.bfloat16), ("seq", "fsdp"), axis=0, tiled=True
        ),
        lax.all_gather(
            down_weight[layer_index].astype(jnp.bfloat16), ("seq", "fsdp"), axis=0, tiled=True
        ),
    )
    return ((mix_full, out_full, gain_full), (in_full, down_full))


def layer_forward(stream, attn_set, mlp_set, context):
    query_places, query_segment, positions, keep_rows, doc_lens = context
    mix_full, out_full, gain_full = attn_set
    in_full, down_full = mlp_set
    row_count = stream.shape[0]
    key_width = KV_HEADS * HEAD_DIM
    groups_per = HEADS // KV_HEADS
    gain_attn = gain_full[0].astype(jnp.float32)
    gain_mlp = gain_full[1].astype(jnp.float32)
    normed, unit_attn, scale_attn = normalize(stream, gain_attn)
    normed_low = normed.astype(jnp.bfloat16)
    projected = jnp.dot(normed_low, mix_full, preferred_element_type=jnp.float32)
    queries = (
        rotate(projected[:, :D].reshape(row_count, HEADS, HEAD_DIM), positions, 1.0)
        .astype(jnp.bfloat16)
        .reshape(row_count, KV_HEADS, groups_per, HEAD_DIM)
    )
    keys_low = (
        rotate(
            projected[:, D : D + key_width].reshape(row_count, KV_HEADS, HEAD_DIM), positions, 1.0
        )
        .astype(jnp.bfloat16)
        .reshape(row_count, key_width)
    )
    values_low = projected[:, D + key_width :].astype(jnp.bfloat16)
    setting = (queries, query_places, query_segment, doc_lens)
    key_all, value_all = (
        lax.all_gather(keys_low, "seq", axis=0, tiled=True),
        lax.all_gather(values_low, "seq", axis=0, tiled=True),
    )
    start_carry = (
        jnp.full((row_count, KV_HEADS, groups_per), FLOOR_SCORE, jnp.float32),
        jnp.zeros((row_count, KV_HEADS, groups_per), jnp.float32),
        jnp.zeros((row_count, KV_HEADS, groups_per, HEAD_DIM), jnp.float32),
    )
    running, totals, accumulated = fold_piece(start_carry, key_all, value_all, 0, setting)
    log_total = running + jnp.log(totals)
    attended = (accumulated / totals[..., None]).reshape(row_count, D) * keep_rows
    attended_low = attended.astype(jnp.bfloat16)
    middle = stream + jnp.dot(attended_low, out_full, preferred_element_type=jnp.float32)
    normed_two, unit_mlp, scale_mlp = normalize(middle, gain_mlp)
    normed_two_low = normed_two.astype(jnp.bfloat16)
    gate_up = jnp.dot(normed_two_low, in_full, preferred_element_type=jnp.float32)
    hidden_low = (jax.nn.silu(gate_up[:, :FF]) * gate_up[:, FF:]).astype(jnp.bfloat16)
    result = middle + jnp.dot(hidden_low, down_full, preferred_element_type=jnp.float32)
    kv_saved = (key_all, value_all)
    saved = (
        normed_low,
        unit_attn,
        scale_attn,
        queries,
        keys_low,
        values_low,
        log_total,
        attended,
        attended_low,
        unit_mlp,
        scale_mlp,
        normed_two_low,
        gate_up,
        hidden_low,
        kv_saved,
    )
    return (result, saved)


def layer_backward(grad_stream, saved, attn_set, mlp_set, context):
    query_places, query_segment, positions, keep_rows, doc_lens = context
    mix_full, out_full, gain_full = attn_set
    in_full, down_full = mlp_set
    (
        normed_low,
        unit_attn,
        scale_attn,
        queries,
        keys_low,
        values_low,
        log_total,
        attended,
        attended_low,
        unit_mlp,
        scale_mlp,
        normed_two_low,
        gate_up,
        hidden_low,
        kv_saved,
    ) = saved
    row_count = grad_stream.shape[0]
    key_width = KV_HEADS * HEAD_DIM
    groups_per = HEADS // KV_HEADS
    score_scale = HEAD_DIM ** (-0.5)
    gain_attn = gain_full[0].astype(jnp.float32)
    gain_mlp = gain_full[1].astype(jnp.float32)
    grad_branch = grad_stream.astype(jnp.bfloat16)
    grad_down = jnp.einsum("nf,nd->fd", hidden_low, grad_branch, preferred_element_type=jnp.float32)
    grad_hidden = jnp.einsum(
        "nd,fd->nf", grad_branch, down_full, preferred_element_type=jnp.float32
    )
    gate_part = gate_up[:, :FF]
    up_part = gate_up[:, FF:]
    sigmoid_gate = jax.nn.sigmoid(gate_part)
    grad_gate = grad_hidden * up_part * sigmoid_gate * (1.0 + gate_part * (1.0 - sigmoid_gate))
    grad_up = grad_hidden * gate_part * sigmoid_gate
    grad_gate_up = jnp.concatenate([grad_gate, grad_up], axis=1).astype(jnp.bfloat16)
    grad_in = jnp.einsum(
        "nd,nf->df", normed_two_low, grad_gate_up, preferred_element_type=jnp.float32
    )
    grad_normed_two = jnp.einsum(
        "nf,df->nd", grad_gate_up, in_full, preferred_element_type=jnp.float32
    )
    mlp_part = (
        lax.psum_scatter(grad_in, ("seq", "fsdp"), scatter_dimension=0, tiled=True),
        lax.psum_scatter(grad_down, ("seq", "fsdp"), scatter_dimension=0, tiled=True),
    )
    grad_gain_mlp, grad_middle_norm = norm_backward(grad_normed_two, unit_mlp, scale_mlp, gain_mlp)
    grad_middle = grad_stream + grad_middle_norm
    attn_branch = grad_middle.astype(jnp.bfloat16)
    grad_out = jnp.einsum(
        "nd,ne->de", attended_low, attn_branch, preferred_element_type=jnp.float32
    )
    grad_attended = (
        jnp.einsum("ne,de->nd", attn_branch, out_full, preferred_element_type=jnp.float32)
        * keep_rows
    )
    grad_heads = grad_attended.astype(jnp.bfloat16).reshape(
        row_count, KV_HEADS, groups_per, HEAD_DIM
    )
    row_delta = jnp.sum(
        grad_heads.astype(jnp.float32)
        * attended.reshape(row_count, KV_HEADS, groups_per, HEAD_DIM),
        axis=-1,
    )
    key_all, value_all = kv_saved
    total_keys = key_all.shape[0]
    block_rows = 512

    def back_step(grad_queries, number):
        first_key = number * block_rows
        key_block = lax.dynamic_slice_in_dim(key_all, first_key, block_rows, 0)
        value_block = lax.dynamic_slice_in_dim(value_all, first_key, block_rows, 0)
        scores, allowed = masked_scores(
            queries, key_block, first_key, query_places, query_segment, doc_lens
        )
        soft_weight = jnp.where(
            allowed[:, None, None, :], jnp.exp(scores - log_total[..., None]), 0.0
        )
        value_heads = value_block.reshape(block_rows, KV_HEADS, HEAD_DIM)
        key_heads = key_block.reshape(block_rows, KV_HEADS, HEAD_DIM)
        grad_weight = jnp.einsum(
            "qkgd,skd->qkgs", grad_heads, value_heads, preferred_element_type=jnp.float32
        )
        grad_score = (soft_weight * (grad_weight - row_delta[..., None])).astype(jnp.bfloat16)
        state_out = grad_queries + jnp.einsum(
            "qkgs,skd->qkgd", grad_score, key_heads, preferred_element_type=jnp.float32
        )
        grad_key = (
            jnp.einsum("qkgs,qkgd->skd", grad_score, queries, preferred_element_type=jnp.float32)
            * score_scale
        )
        grad_value = jnp.einsum(
            "qkgs,qkgd->skd",
            soft_weight.astype(jnp.bfloat16),
            grad_heads,
            preferred_element_type=jnp.float32,
        )
        return (
            state_out,
            jnp.concatenate(
                [
                    grad_key.reshape(block_rows, key_width),
                    grad_value.reshape(block_rows, key_width),
                ],
                axis=1,
            ),
        )

    start_grad = jnp.zeros((row_count, KV_HEADS, groups_per, HEAD_DIM), jnp.float32)
    grad_queries, pair_blocks = lax.scan(
        back_step, start_grad, jnp.arange(total_keys // block_rows, dtype=jnp.int32)
    )
    pair_terms = pair_blocks.reshape(total_keys, 2 * key_width)
    pair_sums = lax.psum_scatter(pair_terms, "seq", scatter_dimension=0, tiled=True)
    grad_rot_queries = rotate(
        (grad_queries * score_scale).reshape(row_count, HEADS, HEAD_DIM), positions, -1.0
    ).reshape(row_count, D)
    grad_rot_keys = rotate(
        pair_sums[:, :key_width].reshape(row_count, KV_HEADS, HEAD_DIM), positions, -1.0
    ).reshape(row_count, key_width)
    grad_projected = jnp.concatenate(
        [grad_rot_queries, grad_rot_keys, pair_sums[:, key_width:]], axis=1
    ).astype(jnp.bfloat16)
    grad_mix = jnp.einsum(
        "nd,nf->df", normed_low, grad_projected, preferred_element_type=jnp.float32
    )
    grad_normed = jnp.einsum(
        "nf,df->nd", grad_projected, mix_full, preferred_element_type=jnp.float32
    )
    grad_gain_attn, grad_input_norm = norm_backward(grad_normed, unit_attn, scale_attn, gain_attn)
    grad_gains = jnp.stack([grad_gain_attn, grad_gain_mlp])
    attn_part = (
        lax.psum_scatter(grad_mix, ("seq", "fsdp"), scatter_dimension=0, tiled=True),
        lax.psum_scatter(grad_out, ("seq", "fsdp"), scatter_dimension=0, tiled=True),
        lax.psum_scatter(grad_gains, ("seq", "fsdp"), scatter_dimension=1, tiled=True),
    )
    return (grad_middle + grad_input_norm, attn_part, mlp_part)


def adam_update(weight, first, second, grad, clip_scale, rate):
    clipped = grad * clip_scale
    first_new = BETA_ONE * first + (1.0 - BETA_ONE) * clipped
    second_new = BETA_TWO * second + (1.0 - BETA_TWO) * clipped * clipped
    first_hat = first_new / (1.0 - BETA_ONE**STEP_NUMBER)
    second_hat = second_new / (1.0 - BETA_TWO**STEP_NUMBER)
    updated = weight - rate * (
        first_hat / (jnp.sqrt(second_hat) + EPS_ADAM) + WEIGHT_DECAY * weight
    )
    return (updated, first_new, second_new)


def local(
    tokens,
    cotangent,
    lengths,
    mix_weight,
    out_weight,
    in_weight,
    down_weight,
    norm_gains,
    mix_first,
    out_first,
    in_first,
    down_first,
    norm_first,
    mix_second,
    out_second,
    in_second,
    down_second,
    norm_second,
):
    row_count = tokens.shape[0]
    group_index = lax.axis_index("fsdp")
    cycle_index = lax.axis_index("seq")
    doc_lens = lax.dynamic_index_in_dim(lengths, group_index, 0, keepdims=False)
    query_places = cycle_index * row_count + jnp.arange(row_count, dtype=jnp.int32)
    query_segment, positions = doc_layout(query_places, doc_lens)
    keep_rows = (query_segment < doc_lens.shape[0]).astype(jnp.float32)[:, None]
    context = (query_places, query_segment, positions, keep_rows, doc_lens)
    stream = tokens.astype(jnp.float32)
    layer_index = 0
    attn_set, mlp_set = fetch_layer(
        mix_weight, out_weight, norm_gains, in_weight, down_weight, layer_index
    )
    stream, saved = layer_forward(stream, attn_set, mlp_set, context)
    saved_list = [saved]
    weight_list = [(attn_set, mlp_set)]
    hidden_out = stream.astype(jnp.bfloat16)
    grad_stream = cotangent.astype(jnp.float32)
    attn_sums = [None] * LAYERS
    mlp_sums = [None] * LAYERS
    for layer_index in reversed(range(LAYERS)):
        attn_set, mlp_set = weight_list[layer_index]
        grad_stream, attn_part, mlp_part = layer_backward(
            grad_stream, saved_list[layer_index], attn_set, mlp_set, context
        )
        attn_sums[layer_index] = attn_part
        mlp_sums[layer_index] = mlp_part
    mix_grad = jnp.stack([attn_sums[0][0]])
    out_grad = jnp.stack([attn_sums[0][1]])
    norm_grad = jnp.stack([attn_sums[0][2]])
    in_grad = jnp.stack([mlp_sums[0][0]])
    down_grad = jnp.stack([mlp_sums[0][1]])
    squares = (
        jnp.sum(mix_grad * mix_grad)
        + jnp.sum(out_grad * out_grad)
        + jnp.sum(in_grad * in_grad)
        + jnp.sum(down_grad * down_grad)
        + jnp.sum(norm_grad * norm_grad)
    )
    total_squares = lax.psum(squares, ("seq", "fsdp"))
    grad_norm = jnp.sqrt(total_squares)
    clip_scale = CLIP_NORM / jnp.maximum(grad_norm, CLIP_NORM)
    mix_new, mix_moment, mix_square = adam_update(
        mix_weight, mix_first, mix_second, mix_grad, clip_scale, LEARN_RATE
    )
    out_new, out_moment, out_square = adam_update(
        out_weight, out_first, out_second, out_grad, clip_scale, OUT_RATE
    )
    in_new, in_moment, in_square = adam_update(
        in_weight, in_first, in_second, in_grad, clip_scale, LEARN_RATE
    )
    down_new, down_moment, down_square = adam_update(
        down_weight, down_first, down_second, down_grad, clip_scale, LEARN_RATE
    )
    norm_new, norm_moment, norm_square = adam_update(
        norm_gains, norm_first, norm_second, norm_grad, clip_scale, GAIN_RATE
    )
    return (
        hidden_out,
        grad_stream,
        grad_norm,
        mix_grad,
        mix_new,
        mix_moment,
        mix_square,
        mix_new.astype(jnp.bfloat16),
        out_grad,
        out_new,
        out_moment,
        out_square,
        out_new.astype(jnp.bfloat16),
        in_grad,
        in_new,
        in_moment,
        in_square,
        in_new.astype(jnp.bfloat16),
        down_grad,
        down_new,
        down_moment,
        down_square,
        down_new.astype(jnp.bfloat16),
        norm_grad,
        norm_new,
        norm_moment,
        norm_square,
        norm_new.astype(jnp.bfloat16),
    )


MESH = pl.DeviceIdType.MESH
ANY = pl.BlockSpec(memory_space=pl.ANY)
VMEM = pl.BlockSpec(memory_space=pltpu.VMEM)
LOW = jnp.bfloat16
SQUARE = 8
SEQ = 16
FLEET = 32
ROWS = 128
HALF_ROWS = 64
KEYS = 1024
BLOCK = 256
CORE, NEAR_Y, NEAR_Z = 1, 2, 4
LOG2E = 1.4426950408889634
SCALE2 = HEAD_DIM ** (-0.5) * LOG2E
WALL = 2.0**100


def flip(value, bits):
    for bit in (1, 2, 4, 8):
        if bits & bit:
            value = value + bit - 2 * bit * (lax.rem(lax.div(value, bit), 2))
    return value


class Place:
    def __init__(self):
        self.seq = lax.axis_index("seq")
        self.fsdp = lax.axis_index("fsdp")
        self.member = lax.rem(self.seq, SQUARE)
        self.half = lax.div(self.seq, SQUARE)
        self.rank = self.seq * 2 + self.fsdp

    def peer(self, bits):
        return (flip(self.seq, bits), self.fsdp)

    def slot(self, bits):
        return flip(self.member, bits)

    def after(self, step):
        rank = lax.rem(self.rank + step, FLEET)
        return rank, (lax.div(rank, 2), lax.rem(rank, 2))

    def before(self, step):
        return lax.rem(self.rank + FLEET - step, FLEET)


def send(src, dst, sems, index, device):
    return pltpu.make_async_remote_copy(
        src_ref=src,
        dst_ref=dst,
        send_sem=sems[0].at[index],
        recv_sem=sems[1].at[index],
        device_id=device,
        device_id_type=MESH,
    )


def greet(devices):
    barrier = pltpu.get_barrier_semaphore()
    for device in devices:
        pl.semaphore_signal(barrier, inc=1, device_id=device, device_id_type=MESH)
    pl.semaphore_wait(barrier, len(devices))


def pair_sems(count):
    return [pltpu.SemaphoreType.DMA((count,)), pltpu.SemaphoreType.DMA((count,))]


class SquareGather:
    COPIES = 10

    def __init__(self, place, src, out, sems, local_sem):
        p, h = place, HALF_ROWS
        own, ys, zs = p.slot(0), p.slot(NEAR_Y), p.slot(NEAR_Z)
        ds = p.slot(NEAR_Y | NEAR_Z)
        to_y, to_z, to_c = p.peer(NEAR_Y), p.peer(NEAR_Z), p.peer(CORE)
        top, low = pl.ds(0, h), pl.ds(h, h)
        self.local = pltpu.make_async_copy(src, out.at[own], local_sem)
        self.y0 = send(src.at[top], out.at[own, top], sems, 0, to_y)
        self.y1 = send(src.at[low], out.at[own, low], sems, 1, to_y)
        self.z1 = send(src.at[low], out.at[own, low], sems, 2, to_z)
        self.z0 = send(src.at[top], out.at[own, top], sems, 3, to_z)
        self.fz = send(out.at[ys, top], out.at[ys, top], sems, 4, to_z)
        self.fy = send(out.at[zs, low], out.at[zs, low], sems, 5, to_y)
        self.c = [
            send(src, out.at[own], sems, 6, to_c),
            send(out.at[ys], out.at[ys], sems, 7, to_c),
            send(out.at[zs], out.at[zs], sems, 8, to_c),
            send(out.at[ds], out.at[ds], sems, 9, to_c),
        ]

    def start(self):
        for copy in (self.y0, self.z1, self.y1, self.z0, self.c[0], self.local):
            copy.start()

    def relay(self):
        self.y0.wait_recv()
        self.fz.start()
        self.z1.wait_recv()
        self.fy.start()

    def share(self):
        self.y1.wait_recv()
        self.c[1].start()
        self.z0.wait_recv()
        self.c[2].start()

    def finish(self):
        self.fz.wait_recv()
        self.fy.wait_recv()
        self.c[3].start()
        for copy in self.c:
            copy.wait_recv()
        for copy in [self.y0, self.y1, self.z0, self.z1, self.fz, self.fy] + self.c:
            copy.wait_send()
        self.local.wait()


def first_kernel(tok, cot, gain, mix, inn, out, tok_o, cot_o, gain_o, mix_o, inn_o, out_o, *sems):
    place = Place()
    tok_s, cot_s, gain_s, mix_s, inn_s, out_s = (sems[2 * i : 2 * i + 2] for i in range(6))
    local_sem = sems[12]
    greet([place.after(step)[1] for step in range(1, FLEET)])
    gather_tok = SquareGather(place, tok, tok_o, tok_s, local_sem.at[0])
    gather_cot = SquareGather(place, cot, cot_o, cot_s, local_sem.at[1])
    gather_tok.start()
    copies = []
    for step in range(1, FLEET):
        rank, device = place.after(step)
        column = lax.rem(device[0], SQUARE)
        copies.append(send(gain, gain_o.at[place.rank], gain_s, step, device))
        copies.append(send(mix.at[column], mix_o.at[place.rank], mix_s, step, device))
    locals_ = [
        pltpu.make_async_copy(gain, gain_o.at[place.rank], local_sem.at[2]),
        pltpu.make_async_copy(mix.at[place.member], mix_o.at[place.rank], local_sem.at[3]),
        pltpu.make_async_copy(inn.at[place.member], inn_o.at[place.member], local_sem.at[4]),
    ]
    for bits in range(1, SQUARE):
        copies.append(
            send(inn.at[place.slot(bits)], inn_o.at[place.member], inn_s, bits, place.peer(bits))
        )
    for copy in copies + locals_:
        copy.start()
    keeper = lax.div(place.seq, 2)
    spot = lax.rem(place.seq, 2) * 2 + place.fsdp

    def out_copy(number):
        device = ((number // 2) * SQUARE + keeper, number % 2)
        remote = pltpu.make_async_remote_copy(
            src_ref=out,
            dst_ref=out_o.at[spot],
            send_sem=out_s[0].at[number],
            recv_sem=out_s[1].at[spot],
            device_id=device,
            device_id_type=MESH,
        )
        local = pltpu.make_async_copy(out, out_o.at[spot], local_sem.at[5])
        mine = (device[0] == place.seq) & (device[1] == place.fsdp)
        return remote, local, mine

    for number in range(4):
        remote, local, mine = out_copy(number)
        pl.when(mine)(local.start)
        pl.when(jnp.logical_not(mine))(remote.start)
    gather_tok.relay()
    gather_tok.share()
    gather_cot.start()
    gather_cot.relay()
    gather_cot.share()
    gather_tok.finish()
    gather_cot.finish()
    for copy in copies + locals_:
        copy.wait()
    for number in range(4):
        remote, local, mine = out_copy(number)
        pl.when(mine)(local.wait)
        pl.when(jnp.logical_not(mine))(remote.wait_send)
    for number in range(4):
        source_seq = place.member * 2 + number // 2
        mine = (source_seq == place.seq) & (number % 2 == place.fsdp)
        arrival = pltpu.make_async_remote_copy(
            src_ref=out,
            dst_ref=out_o.at[number],
            send_sem=out_s[0].at[number],
            recv_sem=out_s[1].at[number],
            device_id=(source_seq, number % 2),
            device_id_type=MESH,
        )
        pl.when(jnp.logical_not(mine))(arrival.wait_recv)


def first_exchange(tok, cot, gain, mix, inn, out):
    shape = jax.ShapeDtypeStruct
    return pl.pallas_call(
        first_kernel,
        out_shape=(
            shape((SQUARE,) + tok.shape, LOW),
            shape((SQUARE,) + cot.shape, LOW),
            shape((FLEET,) + gain.shape, gain.dtype),
            shape((FLEET,) + mix.shape[1:], LOW),
            shape(inn.shape, LOW),
            shape((4,) + out.shape, LOW),
        ),
        in_specs=[ANY] * 6,
        out_specs=(ANY,) * 6,
        scratch_shapes=pair_sems(SquareGather.COPIES)
        + pair_sems(SquareGather.COPIES)
        + pair_sems(FLEET)
        + pair_sems(FLEET)
        + pair_sems(SQUARE)
        + pair_sems(4)
        + [pltpu.SemaphoreType.DMA((6,))],
        compiler_params=pltpu.CompilerParams(collective_id=0, has_side_effects=True),
        name="first_exchange",
    )(tok, cot, gain, mix, inn, out)


def gather_kernel(src, out, send_sems, recv_sems, local_sem):
    place = Place()
    greet([place.peer(bits) for bits in (CORE, NEAR_Y, NEAR_Z)])
    gather = SquareGather(place, src, out, (send_sems, recv_sems), local_sem.at[0])
    gather.start()
    gather.relay()
    gather.share()
    gather.finish()


def square_gather(block):
    return pl.pallas_call(
        gather_kernel,
        out_shape=jax.ShapeDtypeStruct((SQUARE,) + block.shape, block.dtype),
        in_specs=[ANY],
        out_specs=ANY,
        scratch_shapes=pair_sems(SquareGather.COPIES) + [pltpu.SemaphoreType.DMA((1,))],
        compiler_params=pltpu.CompilerParams(collective_id=1, has_side_effects=True),
        name="square_gather",
    )(block).reshape(SQUARE * block.shape[0], block.shape[1])


def add_rows(target, left, right, start, count):
    step = 16

    def body(number, _):
        rows = pl.ds(pl.multiple_of(start + number * step, step), step)
        target[rows] = (left[rows].astype(jnp.float32) + right[rows].astype(jnp.float32)).astype(
            target.dtype
        )
        return 0

    lax.fori_loop(0, count // step, body, 0)


def scatter_kernel(part, total, sib, away, passed, landed, send_sems, recv_sems):
    place = Place()
    sems = (send_sems, recv_sems)
    greet([place.peer(bits) for bits in (CORE, NEAR_Y, NEAR_Z)])
    h = HALF_ROWS
    top, low = pl.ds(0, h), pl.ds(h, h)
    far = NEAR_Y | NEAR_Z
    to_y, to_z, to_c = place.peer(NEAR_Y), place.peer(NEAR_Z), place.peer(CORE)
    cores = [
        send(part.at[place.slot(bits | CORE)], sib.at[number], sems, number, to_c)
        for number, bits in enumerate((far, NEAR_Y, NEAR_Z, 0))
    ]
    for copy in cores:
        copy.start()
    d0 = send(away.at[0, top], passed.at[top], sems, 4, to_y)
    d1 = send(away.at[0, low], passed.at[low], sems, 5, to_z)
    y0 = send(away.at[1, top], landed.at[0, top], sems, 6, to_y)
    y1 = send(away.at[1, low], landed.at[0, low], sems, 7, to_y)
    z0 = send(away.at[2, top], landed.at[1, top], sems, 8, to_z)
    z1 = send(away.at[2, low], landed.at[1, low], sems, 9, to_z)
    cores[0].wait_recv()
    add_rows(away.at[0], part.at[place.slot(far)], sib.at[0], 0, ROWS)
    d0.start()
    d1.start()
    cores[1].wait_recv()
    add_rows(away.at[1], part.at[place.slot(NEAR_Y)], sib.at[1], 0, ROWS)
    y0.start()
    cores[2].wait_recv()
    add_rows(away.at[2], part.at[place.slot(NEAR_Z)], sib.at[2], 0, ROWS)
    z1.start()
    cores[3].wait_recv()
    add_rows(total, part.at[place.slot(0)], sib.at[3], 0, ROWS)
    d0.wait_recv()
    add_rows(away.at[2], away.at[2], passed, 0, h)
    z0.start()
    d1.wait_recv()
    add_rows(away.at[1], away.at[1], passed, h, h)
    y1.start()
    y0.wait_recv()
    z1.wait_recv()
    add_rows(total, total, landed.at[0], 0, h)
    add_rows(total, total, landed.at[1], h, h)
    z0.wait_recv()
    add_rows(total, total, landed.at[1], 0, h)
    y1.wait_recv()
    add_rows(total, total, landed.at[0], h, h)
    for copy in cores + [d0, d1, y0, y1, z0, z1]:
        copy.wait_send()


def square_scatter(part):
    width = part.shape[-1]
    return pl.pallas_call(
        scatter_kernel,
        out_shape=jax.ShapeDtypeStruct((ROWS, width), jnp.float32),
        in_specs=[VMEM],
        out_specs=VMEM,
        scratch_shapes=[
            pltpu.VMEM((4, ROWS, width), LOW),
            pltpu.VMEM((3, ROWS, width), LOW),
            pltpu.VMEM((ROWS, width), LOW),
            pltpu.VMEM((2, ROWS, width), LOW),
        ]
        + pair_sems(10),
        compiler_params=pltpu.CompilerParams(
            collective_id=2, has_side_effects=True, vmem_limit_bytes=32 << 20
        ),
        name="square_scatter",
    )(part.reshape(SQUARE, ROWS, width))


def last_kernel(inn, mix, out, gain, inn_o, mix_o, out_o, gain_o, *sems):
    place = Place()
    inn_s, mix_s, out_s, gain_s = (sems[2 * i : 2 * i + 2] for i in range(4))
    local_sem = sems[8]
    greet([place.after(step)[1] for step in range(1, FLEET)])
    copies = []
    for bits in range(1, SQUARE):
        peer, slot = place.peer(bits), place.slot(bits)
        copies.append(send(mix.at[slot], mix_o.at[place.member], mix_s, bits, peer))
        copies.append(send(inn.at[slot], inn_o.at[place.member], inn_s, bits, peer))
    for step in range(1, FLEET):
        rank, device = place.after(step)
        copies.append(send(gain.at[rank], gain_o.at[place.rank], gain_s, step, device))
    copies += [
        pltpu.make_async_copy(inn.at[place.member], inn_o.at[place.member], local_sem.at[0]),
        pltpu.make_async_copy(mix.at[place.member], mix_o.at[place.member], local_sem.at[1]),
        pltpu.make_async_copy(gain.at[place.rank], gain_o.at[place.rank], local_sem.at[2]),
    ]
    for copy in copies:
        copy.start()

    def out_copy(number):
        owner = place.member * 2 + number
        remote = pltpu.make_async_remote_copy(
            src_ref=out.at[number],
            dst_ref=out_o.at[place.half],
            send_sem=out_s[0].at[number],
            recv_sem=out_s[1].at[place.half],
            device_id=(owner, place.fsdp),
            device_id_type=MESH,
        )
        local = pltpu.make_async_copy(out.at[number], out_o.at[place.half], local_sem.at[3])
        return remote, local, owner == place.seq

    for number in range(2):
        remote, local, mine = out_copy(number)
        pl.when(mine)(local.start)
        pl.when(jnp.logical_not(mine))(remote.start)
    for copy in copies:
        copy.wait()
    for number in range(2):
        remote, local, mine = out_copy(number)
        pl.when(mine)(local.wait)
        pl.when(jnp.logical_not(mine))(remote.wait_send)
    for half in range(2):
        source_seq = half * SQUARE + lax.div(place.seq, 2)
        arrival = pltpu.make_async_remote_copy(
            src_ref=out.at[0],
            dst_ref=out_o.at[half],
            send_sem=out_s[0].at[half],
            recv_sem=out_s[1].at[half],
            device_id=(source_seq, place.fsdp),
            device_id_type=MESH,
        )
        pl.when(source_seq != place.seq)(arrival.wait_recv)


def last_exchange(inn, mix, out, gain):
    shape = jax.ShapeDtypeStruct
    return pl.pallas_call(
        last_kernel,
        out_shape=tuple(shape(v.shape, v.dtype) for v in (inn, mix, out, gain)),
        in_specs=[ANY] * 4,
        out_specs=(ANY,) * 4,
        scratch_shapes=pair_sems(SQUARE)
        + pair_sems(SQUARE)
        + pair_sems(2)
        + pair_sems(FLEET)
        + [pltpu.SemaphoreType.DMA((4,))],
        compiler_params=pltpu.CompilerParams(collective_id=3, has_side_effects=True),
        name="last_exchange",
    )(inn, mix, out, gain)


def share_kernel(value, out, send_sems, recv_sems):
    place = Place()
    greet([place.after(step)[1] for step in range(1, FLEET)])
    out[place.rank] = value[...]
    copies = []
    for step in range(1, FLEET):
        rank, device = place.after(step)
        copies.append(send(value, out.at[place.rank], (send_sems, recv_sems), step, device))
    for copy in copies:
        copy.start()
    for copy in copies:
        copy.wait()


def share_all(value):
    return pl.pallas_call(
        share_kernel,
        out_shape=jax.ShapeDtypeStruct((FLEET,) + value.shape, value.dtype),
        in_specs=[VMEM],
        out_specs=VMEM,
        scratch_shapes=pair_sems(FLEET),
        compiler_params=pltpu.CompilerParams(collective_id=4, has_side_effects=True),
        name="share_all",
    )(value)


def dot32(left, right, dims=((1,), (0,))):
    return lax.dot_general(left, right, (dims, ((), ())), preferred_element_type=jnp.float32)


def block_of(number):
    return pl.ds(pl.multiple_of(number * BLOCK, BLOCK), BLOCK)


def later(number_of_columns):
    key_at = lax.broadcasted_iota(jnp.int32, (BLOCK, number_of_columns), 0)
    query_at = lax.rem(lax.broadcasted_iota(jnp.int32, (BLOCK, number_of_columns), 1), BLOCK)
    return key_at > query_at


def attend_kernel(half, query_t, keys, values_t, out_t, log_sum):
    first = jnp.where(half[0] == 1, 0, KEYS // BLOCK)
    for number in range(KEYS // BLOCK):
        columns = pl.ds(number * BLOCK, BLOCK)
        queries = jnp.concatenate([query_t[0, :, columns], query_t[1, :, columns]], axis=1)

        def fold(place, carry, diagonal=False):
            score = dot32(keys[block_of(place), :], queries)
            if diagonal:
                score = jnp.where(later(2 * BLOCK), -WALL, score)
            top = jnp.max(score, axis=0, keepdims=True)
            if carry is not None:
                top = jnp.maximum(carry[0], top)
            weight = jnp.exp2((score - top) * SCALE2)
            total = jnp.sum(weight, axis=0, keepdims=True)
            mixed = dot32(values_t[:, block_of(place)], weight.astype(LOW))
            if carry is not None:
                fade = jnp.exp2((carry[0] - top) * SCALE2)
                total = total + carry[1] * fade
                mixed = mixed + carry[2] * fade
            return (top, total, mixed)

        last = KEYS // BLOCK + number
        carry = fold(last, None, diagonal=True)
        top, total, mixed = lax.fori_loop(first, last, fold, carry)
        mixed = mixed * (1.0 / total)
        level = top * SCALE2 + jnp.log2(total)
        for head in range(2):
            side = slice(head * BLOCK, (head + 1) * BLOCK)
            out_t[head, :, columns] = mixed[:, side]
            log_sum[pl.ds(head, 1), columns] = level[:, side]


def attend(half, query_t, keys, values_t):
    return pl.pallas_call(
        attend_kernel,
        out_shape=(
            jax.ShapeDtypeStruct((2, HEAD_DIM, KEYS), jnp.float32),
            jax.ShapeDtypeStruct((2, KEYS), jnp.float32),
        ),
        in_specs=[pl.BlockSpec(memory_space=pltpu.SMEM)] + [VMEM] * 3,
        out_specs=(VMEM, VMEM),
        compiler_params=pltpu.CompilerParams(vmem_limit_bytes=40 << 20),
        name="attend",
    )(half, query_t, keys, values_t)


def attend_back_kernel(
    half, query_t, queries_r, keys, keys_t, values, grad_t, grad_r, log_sum, delta, dq_t, dk, dv
):
    first = jnp.where(half[0] == 1, 0, KEYS // BLOCK)
    dk[...] = jnp.zeros_like(dk)
    dv[...] = jnp.zeros_like(dv)
    for number in range(KEYS // BLOCK):
        columns = pl.ds(number * BLOCK, BLOCK)

        def both(ref, axis):
            if axis == 1:
                return jnp.concatenate([ref[0, :, columns], ref[1, :, columns]], axis=1)
            return jnp.concatenate([ref[0, columns, :], ref[1, columns, :]], axis=0)

        query_c, grad_c = both(query_t, 1), both(grad_t, 1)
        query_b, grad_b = both(queries_r, 0), both(grad_r, 0)
        level = jnp.concatenate([log_sum[0:1, columns], log_sum[1:2, columns]], axis=1)
        shift = jnp.concatenate([delta[0:1, columns], delta[1:2, columns]], axis=1)

        def fold(place, total, diagonal=False):
            rows = block_of(place)
            score = dot32(keys[rows, :], query_c)
            if diagonal:
                score = jnp.where(later(2 * BLOCK), -WALL, score)
            weight = jnp.exp2(score * SCALE2 - level)
            grad_weight = dot32(values[rows, :], grad_c)
            grad_score = (weight * (grad_weight - shift)).astype(LOW)
            dk[rows, :] += dot32(grad_score, query_b)
            dv[rows, :] += dot32(weight.astype(LOW), grad_b)
            return total + dot32(keys_t[:, rows], grad_score)

        last = KEYS // BLOCK + number
        total = fold(last, jnp.zeros((HEAD_DIM, 2 * BLOCK), jnp.float32), diagonal=True)
        total = lax.fori_loop(first, last, fold, total)
        for head in range(2):
            dq_t[head, :, columns] = total[:, head * BLOCK : (head + 1) * BLOCK]


def attend_back(half, *arrays):
    shape = jax.ShapeDtypeStruct
    return pl.pallas_call(
        attend_back_kernel,
        out_shape=(
            shape((2, HEAD_DIM, KEYS), jnp.float32),
            shape((2 * KEYS, HEAD_DIM), jnp.float32),
            shape((2 * KEYS, HEAD_DIM), jnp.float32),
        ),
        in_specs=[pl.BlockSpec(memory_space=pltpu.SMEM)] + [VMEM] * 9,
        out_specs=(VMEM,) * 3,
        compiler_params=pltpu.CompilerParams(vmem_limit_bytes=48 << 20),
        name="attend_back",
    )(half, *arrays)


def swap_fsdp(value):
    return lax.ppermute(value, "fsdp", [(0, 1), (1, 0)])


def swap_half(value):
    return lax.ppermute(value, "seq", [(i, i ^ SQUARE) for i in range(SEQ)])


def in_order(flag, mine, other, axis):
    return jnp.where(
        flag == 0, jnp.stack([mine, other], axis=axis), jnp.stack([other, mine], axis=axis)
    )


def four_parts(half, fsdp, block, axis):
    across = swap_half(block)
    near = in_order(fsdp, block, swap_fsdp(block), axis)
    far = in_order(fsdp, across, swap_fsdp(across), axis)
    return in_order(half, near, far, 0)


def keep_part(value, index, axis):
    mine = lax.dynamic_index_in_dim(value, index, axis, keepdims=False)
    other = lax.dynamic_index_in_dim(value, 1 - index, axis, keepdims=False)
    return mine, other


def sum_fsdp(value, fsdp, axis):
    mine, other = keep_part(value, fsdp, axis)
    return mine + swap_fsdp(other.astype(LOW)).astype(jnp.float32)


def sum_half(value, half):
    mine, other = keep_part(value, half, 0)
    return mine + swap_half(other.astype(LOW)).astype(jnp.float32)


def turn(values_t, cosine, sine):
    former, latter = values_t[:, : HEAD_DIM // 2], values_t[:, HEAD_DIM // 2 :]
    return jnp.concatenate(
        [former * cosine - latter * sine, latter * cosine + former * sine], axis=1
    )


def local_squares(
    tokens,
    cotangent,
    lengths,
    mix_weight,
    out_weight,
    in_weight,
    down_weight,
    norm_gains,
    mix_first,
    out_first,
    in_first,
    down_first,
    norm_first,
    mix_second,
    out_second,
    in_second,
    down_second,
    norm_second,
):
    f32 = jnp.float32
    fsdp = lax.axis_index("fsdp")
    seq = lax.axis_index("seq")
    half, member = seq // SQUARE, seq % SQUARE
    doc_lens = lax.dynamic_index_in_dim(lengths, fsdp, 0, keepdims=False)
    places = half * KEYS + jnp.arange(KEYS, dtype=jnp.int32)
    segment, positions = doc_layout(places, doc_lens)
    other_segment, _ = doc_layout(jnp.arange(KEYS, dtype=jnp.int32), doc_lens)
    keep_t = (segment < doc_lens.shape[0]).astype(f32)[None, :]
    inverse = ROPE_BASE ** (-jnp.arange(HEAD_DIM // 2, dtype=f32) * 2.0 / HEAD_DIM)
    angles = inverse[:, None] * positions.astype(f32)[None, :]
    cosine, sine = jnp.cos(angles), jnp.sin(angles)

    wide = 2 * HEAD_DIM
    key_width = KV_HEADS * HEAD_DIM
    mix_low = mix_weight[0].astype(LOW)
    share = mix_low.shape[0]
    mix_blocks = jnp.concatenate(
        [
            mix_low[:, :D].reshape(share, SQUARE, wide),
            mix_low[:, D : D + key_width].reshape(share, SQUARE, HEAD_DIM),
            mix_low[:, D + key_width :].reshape(share, SQUARE, HEAD_DIM),
        ],
        axis=2,
    ).transpose(1, 0, 2)
    unit = FF // FLEET
    in_blocks = (
        in_weight[0]
        .astype(LOW)
        .reshape(share, 2, 2, SQUARE, 2 * unit)
        .transpose(3, 0, 1, 2, 4)
        .reshape(SQUARE, share, 8 * unit)
    )
    out_low = out_weight[0].astype(LOW)
    down_low = down_weight[0].astype(LOW)
    gain_block = jnp.pad(norm_gains[0].astype(LOW), ((0, 14), (0, 128 - share)))
    tok_all, cot_all, gain_all, mix_full, in_square, out_mine = first_exchange(
        tokens, cotangent, gain_block, mix_blocks, in_blocks, out_low
    )
    rows = SQUARE * ROWS
    tok_all = tok_all.reshape(rows, D)
    cot_all = cot_all.reshape(rows, D)
    gains = gain_all[:, :2, :share].transpose(1, 0, 2).reshape(2, D).astype(f32)
    gain_attn, gain_mlp = gains[0], gains[1]
    mix_full = mix_full.reshape(D, 4 * HEAD_DIM)
    out_mine = out_mine.reshape(wide, D)
    in_mine = four_parts(half, fsdp, in_square, 1).reshape(D, 8 * unit)
    down_mine = four_parts(half, fsdp, down_low, 0).reshape(4 * unit, D)

    normed_low = normalize(tok_all.astype(f32), gain_attn)[0].astype(LOW)
    projected_t = dot32(mix_full, normed_low, ((0,), (1,)))
    heads_t = turn(projected_t[: 3 * HEAD_DIM].reshape(3, HEAD_DIM, rows), cosine, sine).astype(LOW)
    value_t = projected_t[3 * HEAD_DIM :].astype(LOW)
    kinds = jnp.arange(6, dtype=jnp.int32)
    query_t = jnp.concatenate(
        [
            heads_t[:2],
            jnp.broadcast_to(
                (segment[None, :] == kinds[:, None]).astype(LOW)[None], (2, 6, rows)
            ),
            jnp.zeros((2, 26, rows), LOW),
        ],
        axis=1,
    )
    key_value_t = jnp.concatenate([heads_t[2], value_t], axis=0)
    arrived_t = lax.ppermute(key_value_t, "seq", [(i, i + SQUARE) for i in range(SQUARE)])
    both_t = jnp.concatenate([arrived_t, key_value_t], axis=1)
    keys_t, values_t = both_t[:HEAD_DIM], both_t[HEAD_DIM:]
    all_segment = jnp.concatenate([other_segment, segment])
    keys_r = jnp.concatenate(
        [
            keys_t.T,
            jnp.where(all_segment[:, None] == kinds[None, :], 0.0, -WALL).astype(LOW),
            jnp.zeros((2 * rows, 26), LOW),
        ],
        axis=1,
    )
    half_flag = half.astype(jnp.int32).reshape(1)
    mixed_t, log_sum = attend(half_flag, query_t, keys_r, values_t)
    attended_t = mixed_t.reshape(wide, rows) * keep_t
    attended_low = attended_t.astype(LOW)
    out_part = dot32(attended_low, out_mine, ((0,), (0,))).astype(LOW)
    stream = tokens.astype(f32)
    middle = stream + square_scatter(out_part)

    normed_two, unit_mlp, scale_mlp = normalize(middle, gain_mlp)
    two_all = square_gather(normed_two.astype(LOW))
    gate_up = dot32(two_all, in_mine)
    gate, up = gate_up[:, : 4 * unit], gate_up[:, 4 * unit :]
    sigmoid_gate = jax.nn.sigmoid(gate)
    hidden_low = (gate * sigmoid_gate * up).astype(LOW)
    y_part = dot32(hidden_low, down_mine).astype(LOW)
    grad_hidden = dot32(cot_all, down_mine, ((1,), (1,)))
    grad_gate = grad_hidden * up * sigmoid_gate * (1.0 + gate * (1.0 - sigmoid_gate))
    grad_up = grad_hidden * gate * sigmoid_gate
    grad_gate_up = jnp.concatenate([grad_gate, grad_up], axis=1).astype(LOW)
    two_part = dot32(grad_gate_up, in_mine, ((1,), (1,))).astype(LOW)
    grad_normed_two = square_scatter(two_part)
    grad_down = dot32(hidden_low, cot_all, ((0,), (0,)))
    grad_in = dot32(two_all, grad_gate_up, ((0,), (0,)))
    grad_stream = cotangent.astype(f32)
    grad_gain_mlp, grad_middle_norm = norm_backward(grad_normed_two, unit_mlp, scale_mlp, gain_mlp)
    grad_middle = grad_stream + grad_middle_norm
    hidden_out = (middle + square_scatter(y_part)).astype(LOW)
    in_sum = sum_half(sum_fsdp(grad_in.reshape(2, SQUARE, 2, share, 8 * unit), fsdp, 2), half)
    down_sum = sum_half(sum_fsdp(grad_down.reshape(2, 2, unit, D), fsdp, 1), half)

    branch_all = square_gather(grad_middle.astype(LOW))
    grad_out = dot32(attended_low, branch_all)
    out_sum = sum_fsdp(grad_out.reshape(2, 2, share, D), fsdp, 1)
    grad_att = dot32(out_mine, branch_all, ((1,), (1,))) * keep_t
    grad_t = grad_att.astype(LOW).reshape(2, HEAD_DIM, rows)
    delta = jnp.sum(
        grad_t.astype(f32) * attended_t.reshape(2, HEAD_DIM, rows), axis=1
    )
    dq_t, dk, dv = attend_back(
        half_flag,
        query_t,
        heads_t[:2].transpose(0, 2, 1),
        keys_r,
        keys_t,
        values_t.T,
        grad_t,
        grad_t.transpose(0, 2, 1),
        log_sum,
        delta,
    )
    pair = jnp.concatenate([dk, dv], axis=1)
    returned = lax.ppermute(
        pair[:KEYS].astype(LOW), "seq", [(i + SQUARE, i) for i in range(SQUARE)]
    )
    pair_t = (pair[KEYS:] + returned.astype(f32)).T
    scale = HEAD_DIM ** (-0.5)
    turned = turn(
        jnp.concatenate([dq_t, pair_t[None, :HEAD_DIM]], axis=0) * scale, cosine, -sine
    )
    grad_projected_t = jnp.concatenate(
        [turned.reshape(3 * HEAD_DIM, rows), pair_t[HEAD_DIM:]], axis=0
    ).astype(LOW)
    grad_mix = dot32(normed_low, grad_projected_t, ((0,), (1,)))
    mix_sum = sum_half(sum_fsdp(grad_mix.reshape(2, SQUARE, 2, share, 4 * HEAD_DIM), fsdp, 2), half)
    normed_part = dot32(grad_projected_t, mix_full, ((0,), (1,))).astype(LOW)
    grad_normed = square_scatter(normed_part)
    _, unit_attn, scale_attn = normalize(stream, gain_attn)
    grad_gain_attn, grad_input_norm = norm_backward(grad_normed, unit_attn, scale_attn, gain_attn)
    grad_tokens = grad_middle + grad_input_norm

    gain_blocks = jnp.pad(
        jnp.stack([grad_gain_attn, grad_gain_mlp]).reshape(2, FLEET, share).transpose(1, 0, 2),
        ((0, 0), (0, 6), (0, 128 - share)),
    )
    in_got, mix_got, out_got, gain_got = last_exchange(
        in_sum.astype(LOW), mix_sum.astype(LOW), out_sum.astype(LOW), gain_blocks
    )
    in_grad = (
        in_got.reshape(SQUARE, share, 2, 2, 2 * unit)
        .transpose(1, 2, 3, 0, 4)
        .reshape(1, share, 2 * FF)
        .astype(f32)
    )
    mix_got = mix_got.transpose(1, 0, 2)
    mix_grad = jnp.concatenate(
        [
            mix_got[:, :, :wide].reshape(share, D),
            mix_got[:, :, wide : wide + HEAD_DIM].reshape(share, key_width),
            mix_got[:, :, wide + HEAD_DIM :].reshape(share, key_width),
        ],
        axis=1,
    ).astype(f32)[None]
    out_grad = jnp.sum(out_got.astype(f32), axis=0)[None]
    down_grad = down_sum[None]
    norm_grad = jnp.sum(gain_got[:, :2, :share], axis=0)[None]
    squares = sum(
        jnp.sum(grad * grad) for grad in (mix_grad, out_grad, in_grad, down_grad, norm_grad)
    )
    total_squares = jnp.sum(share_all(jnp.broadcast_to(squares, (8, 128)))[:, 0, 0])
    grad_norm = jnp.sqrt(total_squares)
    clip_scale = CLIP_NORM / jnp.maximum(grad_norm, CLIP_NORM)
    results = [hidden_out, grad_tokens, grad_norm]
    for weight, first, second, grad, rate in (
        (mix_weight, mix_first, mix_second, mix_grad, LEARN_RATE),
        (out_weight, out_first, out_second, out_grad, OUT_RATE),
        (in_weight, in_first, in_second, in_grad, LEARN_RATE),
        (down_weight, down_first, down_second, down_grad, LEARN_RATE),
        (norm_gains, norm_first, norm_second, norm_grad, GAIN_RATE),
    ):
        new, moment, square = adam_update(weight, first, second, grad, clip_scale, rate)
        results += [grad, new, moment, square, new.astype(LOW)]
    return tuple(results)


def solution(mesh):
    squares = mesh.shape["seq"] == SEQ and mesh.shape["fsdp"] == 2
    return jax.shard_map(
        local_squares if squares else local,
        mesh=mesh,
        in_specs=(
            P(("seq", "fsdp"), None),
            P(("seq", "fsdp"), None),
            P(),
            P(None, ("seq", "fsdp"), None),
            P(None, ("seq", "fsdp"), None),
            P(None, ("seq", "fsdp"), None),
            P(None, ("seq", "fsdp"), None),
            P(None, None, ("seq", "fsdp")),
            P(None, ("seq", "fsdp"), None),
            P(None, ("seq", "fsdp"), None),
            P(None, ("seq", "fsdp"), None),
            P(None, ("seq", "fsdp"), None),
            P(None, None, ("seq", "fsdp")),
            P(None, ("seq", "fsdp"), None),
            P(None, ("seq", "fsdp"), None),
            P(None, ("seq", "fsdp"), None),
            P(None, ("seq", "fsdp"), None),
            P(None, None, ("seq", "fsdp")),
        ),
        out_specs=(
            P(("seq", "fsdp"), None),
            P(("seq", "fsdp"), None),
            P(),
            P(None, ("seq", "fsdp"), None),
            P(None, ("seq", "fsdp"), None),
            P(None, ("seq", "fsdp"), None),
            P(None, ("seq", "fsdp"), None),
            P(None, ("seq", "fsdp"), None),
            P(None, ("seq", "fsdp"), None),
            P(None, ("seq", "fsdp"), None),
            P(None, ("seq", "fsdp"), None),
            P(None, ("seq", "fsdp"), None),
            P(None, ("seq", "fsdp"), None),
            P(None, ("seq", "fsdp"), None),
            P(None, ("seq", "fsdp"), None),
            P(None, ("seq", "fsdp"), None),
            P(None, ("seq", "fsdp"), None),
            P(None, ("seq", "fsdp"), None),
            P(None, ("seq", "fsdp"), None),
            P(None, ("seq", "fsdp"), None),
            P(None, ("seq", "fsdp"), None),
            P(None, ("seq", "fsdp"), None),
            P(None, ("seq", "fsdp"), None),
            P(None, None, ("seq", "fsdp")),
            P(None, None, ("seq", "fsdp")),
            P(None, None, ("seq", "fsdp")),
            P(None, None, ("seq", "fsdp")),
            P(None, None, ("seq", "fsdp")),
        ),
        check_vma=False,
    )
```

```python
import functools

import jax
import jax.numpy as jnp
from jax import lax
from jax.experimental import pallas as pl
from jax.experimental.pallas import tpu as pltpu
from jax.sharding import PartitionSpec as P

D = 1536
HEADS = 16
KV_HEADS = 8
HEAD_DIM = 96
FF = 4096
LAYERS = 1
STEP_NUMBER = 10


EPS_NORM = 1e-05
ROPE_BASE = 100000.0
FLOOR_SCORE = -1e30
LEARN_RATE = 0.05
OUT_RATE = 0.2
GAIN_RATE = 2.0
BETA_ONE = 0.9
BETA_TWO = 0.99
EPS_ADAM = 1e-08
WEIGHT_DECAY = 0.1
CLIP_NORM = 1.0


def doc_layout(places, doc_lens):
    doc_ends = jnp.cumsum(doc_lens)
    passed = (places[:, None] >= doc_ends[None, :]).astype(jnp.int32)
    segment = jnp.sum(passed, axis=1)
    offset = jnp.sum(passed * doc_lens[None, :], axis=1)
    return (segment, places - offset)


def rotate(vectors, places, direction):
    half_dim = vectors.shape[-1] // 2
    inverse = ROPE_BASE ** (-jnp.arange(half_dim, dtype=jnp.float32) * 2.0 / vectors.shape[-1])
    angles = places.astype(jnp.float32)[:, None] * inverse[None, :]
    cosine = jnp.cos(angles)[:, None, :]
    sine_term = direction * jnp.sin(angles)[:, None, :]
    former = vectors[..., :half_dim]
    latter = vectors[..., half_dim:]
    return jnp.concatenate(
        [former * cosine - latter * sine_term, latter * cosine + former * sine_term], axis=-1
    )


def normalize(values, gain):
    scale_rows = lax.rsqrt(jnp.mean(values * values, axis=-1, keepdims=True) + EPS_NORM)
    unit_rows = values * scale_rows
    return (unit_rows * gain, unit_rows, scale_rows)


def norm_backward(grad_normed, unit_rows, scale_rows, gain):
    grad_gain = jnp.sum(grad_normed * unit_rows, axis=0)
    grad_unit = grad_normed * gain
    grad_values = scale_rows * (
        grad_unit - unit_rows * jnp.mean(grad_unit * unit_rows, axis=-1, keepdims=True)
    )
    return (grad_gain, grad_values)


def masked_scores(queries, key_block, first_key, query_places, query_segment, doc_lens):
    block_rows = key_block.shape[0]
    key_places = first_key + jnp.arange(block_rows, dtype=jnp.int32)
    key_segment, unused_places = doc_layout(key_places, doc_lens)
    allowed = (query_segment[:, None] == key_segment[None, :]) & (
        key_places[None, :] <= query_places[:, None]
    )
    key_heads = key_block.reshape(block_rows, KV_HEADS, HEAD_DIM)
    raw_scores = jnp.einsum(
        "qkgd,skd->qkgs", queries, key_heads, preferred_element_type=jnp.float32
    ) * HEAD_DIM ** (-0.5)
    return (jnp.where(allowed[:, None, None, :], raw_scores, FLOOR_SCORE), allowed)


def fold_block(carry, key_block, value_block, first_key, setting):
    queries, query_places, query_segment, doc_lens = setting
    running, totals, accumulated = carry
    block_rows = key_block.shape[0]
    scores, allowed = masked_scores(
        queries, key_block, first_key, query_places, query_segment, doc_lens
    )
    newest = jnp.maximum(running, jnp.max(scores, axis=-1))
    factor = jnp.exp(running - newest)
    weights = jnp.where(allowed[:, None, None, :], jnp.exp(scores - newest[..., None]), 0.0)
    totals = totals * factor + jnp.sum(weights, axis=-1)
    value_heads = value_block.reshape(block_rows, KV_HEADS, HEAD_DIM)
    accumulated = accumulated * factor[..., None] + jnp.einsum(
        "qkgs,skd->qkgd",
        weights.astype(jnp.bfloat16),
        value_heads,
        preferred_element_type=jnp.float32,
    )
    return (newest, totals, accumulated)


def fold_piece(carry, key_rows, value_rows, start, setting):
    total_rows = key_rows.shape[0]
    block_rows = 512

    def step(inner_state, number):
        first_key = start + number * block_rows
        key_block = lax.dynamic_slice_in_dim(key_rows, number * block_rows, block_rows, 0)
        value_block = lax.dynamic_slice_in_dim(value_rows, number * block_rows, block_rows, 0)
        state_out = fold_block(inner_state, key_block, value_block, first_key, setting)
        return (state_out, None)

    carry, unused_out = lax.scan(step, carry, jnp.arange(total_rows // block_rows, dtype=jnp.int32))
    return carry


def fetch_layer(mix_weight, out_weight, norm_gains, in_weight, down_weight, layer_index):
    mix_full, out_full, gain_full, in_full, down_full = (
        lax.all_gather(
            mix_weight[layer_index].astype(jnp.bfloat16), ("seq", "fsdp"), axis=0, tiled=True
        ),
        lax.all_gather(
            out_weight[layer_index].astype(jnp.bfloat16), ("seq", "fsdp"), axis=0, tiled=True
        ),
        lax.all_gather(
            norm_gains[layer_index].astype(jnp.bfloat16), ("seq", "fsdp"), axis=1, tiled=True
        ),
        lax.all_gather(
            in_weight[layer_index].astype(jnp.bfloat16), ("seq", "fsdp"), axis=0, tiled=True
        ),
        lax.all_gather(
            down_weight[layer_index].astype(jnp.bfloat16), ("seq", "fsdp"), axis=0, tiled=True
        ),
    )
    return ((mix_full, out_full, gain_full), (in_full, down_full))


def layer_forward(stream, attn_set, mlp_set, context):
    query_places, query_segment, positions, keep_rows, doc_lens = context
    mix_full, out_full, gain_full = attn_set
    in_full, down_full = mlp_set
    row_count = stream.shape[0]
    key_width = KV_HEADS * HEAD_DIM
    groups_per = HEADS // KV_HEADS
    gain_attn = gain_full[0].astype(jnp.float32)
    gain_mlp = gain_full[1].astype(jnp.float32)
    normed, unit_attn, scale_attn = normalize(stream, gain_attn)
    normed_low = normed.astype(jnp.bfloat16)
    projected = jnp.dot(normed_low, mix_full, preferred_element_type=jnp.float32)
    queries = (
        rotate(projected[:, :D].reshape(row_count, HEADS, HEAD_DIM), positions, 1.0)
        .astype(jnp.bfloat16)
        .reshape(row_count, KV_HEADS, groups_per, HEAD_DIM)
    )
    keys_low = (
        rotate(
            projected[:, D : D + key_width].reshape(row_count, KV_HEADS, HEAD_DIM), positions, 1.0
        )
        .astype(jnp.bfloat16)
        .reshape(row_count, key_width)
    )
    values_low = projected[:, D + key_width :].astype(jnp.bfloat16)
    setting = (queries, query_places, query_segment, doc_lens)
    key_all, value_all = (
        lax.all_gather(keys_low, "seq", axis=0, tiled=True),
        lax.all_gather(values_low, "seq", axis=0, tiled=True),
    )
    start_carry = (
        jnp.full((row_count, KV_HEADS, groups_per), FLOOR_SCORE, jnp.float32),
        jnp.zeros((row_count, KV_HEADS, groups_per), jnp.float32),
        jnp.zeros((row_count, KV_HEADS, groups_per, HEAD_DIM), jnp.float32),
    )
    running, totals, accumulated = fold_piece(start_carry, key_all, value_all, 0, setting)
    log_total = running + jnp.log(totals)
    attended = (accumulated / totals[..., None]).reshape(row_count, D) * keep_rows
    attended_low = attended.astype(jnp.bfloat16)
    middle = stream + jnp.dot(attended_low, out_full, preferred_element_type=jnp.float32)
    normed_two, unit_mlp, scale_mlp = normalize(middle, gain_mlp)
    normed_two_low = normed_two.astype(jnp.bfloat16)
    gate_up = jnp.dot(normed_two_low, in_full, preferred_element_type=jnp.float32)
    hidden_low = (jax.nn.silu(gate_up[:, :FF]) * gate_up[:, FF:]).astype(jnp.bfloat16)
    result = middle + jnp.dot(hidden_low, down_full, preferred_element_type=jnp.float32)
    kv_saved = (key_all, value_all)
    saved = (
        normed_low,
        unit_attn,
        scale_attn,
        queries,
        keys_low,
        values_low,
        log_total,
        attended,
        attended_low,
        unit_mlp,
        scale_mlp,
        normed_two_low,
        gate_up,
        hidden_low,
        kv_saved,
    )
    return (result, saved)


def layer_backward(grad_stream, saved, attn_set, mlp_set, context):
    query_places, query_segment, positions, keep_rows, doc_lens = context
    mix_full, out_full, gain_full = attn_set
    in_full, down_full = mlp_set
    (
        normed_low,
        unit_attn,
        scale_attn,
        queries,
        keys_low,
        values_low,
        log_total,
        attended,
        attended_low,
        unit_mlp,
        scale_mlp,
        normed_two_low,
        gate_up,
        hidden_low,
        kv_saved,
    ) = saved
    row_count = grad_stream.shape[0]
    key_width = KV_HEADS * HEAD_DIM
    groups_per = HEADS // KV_HEADS
    score_scale = HEAD_DIM ** (-0.5)
    gain_attn = gain_full[0].astype(jnp.float32)
    gain_mlp = gain_full[1].astype(jnp.float32)
    grad_branch = grad_stream.astype(jnp.bfloat16)
    grad_down = jnp.einsum("nf,nd->fd", hidden_low, grad_branch, preferred_element_type=jnp.float32)
    grad_hidden = jnp.einsum(
        "nd,fd->nf", grad_branch, down_full, preferred_element_type=jnp.float32
    )
    gate_part = gate_up[:, :FF]
    up_part = gate_up[:, FF:]
    sigmoid_gate = jax.nn.sigmoid(gate_part)
    grad_gate = grad_hidden * up_part * sigmoid_gate * (1.0 + gate_part * (1.0 - sigmoid_gate))
    grad_up = grad_hidden * gate_part * sigmoid_gate
    grad_gate_up = jnp.concatenate([grad_gate, grad_up], axis=1).astype(jnp.bfloat16)
    grad_in = jnp.einsum(
        "nd,nf->df", normed_two_low, grad_gate_up, preferred_element_type=jnp.float32
    )
    grad_normed_two = jnp.einsum(
        "nf,df->nd", grad_gate_up, in_full, preferred_element_type=jnp.float32
    )
    mlp_part = (
        lax.psum_scatter(grad_in, ("seq", "fsdp"), scatter_dimension=0, tiled=True),
        lax.psum_scatter(grad_down, ("seq", "fsdp"), scatter_dimension=0, tiled=True),
    )
    grad_gain_mlp, grad_middle_norm = norm_backward(grad_normed_two, unit_mlp, scale_mlp, gain_mlp)
    grad_middle = grad_stream + grad_middle_norm
    attn_branch = grad_middle.astype(jnp.bfloat16)
    grad_out = jnp.einsum(
        "nd,ne->de", attended_low, attn_branch, preferred_element_type=jnp.float32
    )
    grad_attended = (
        jnp.einsum("ne,de->nd", attn_branch, out_full, preferred_element_type=jnp.float32)
        * keep_rows
    )
    grad_heads = grad_attended.astype(jnp.bfloat16).reshape(
        row_count, KV_HEADS, groups_per, HEAD_DIM
    )
    row_delta = jnp.sum(
        grad_heads.astype(jnp.float32)
        * attended.reshape(row_count, KV_HEADS, groups_per, HEAD_DIM),
        axis=-1,
    )
    key_all, value_all = kv_saved
    total_keys = key_all.shape[0]
    block_rows = 512

    def back_step(grad_queries, number):
        first_key = number * block_rows
        key_block = lax.dynamic_slice_in_dim(key_all, first_key, block_rows, 0)
        value_block = lax.dynamic_slice_in_dim(value_all, first_key, block_rows, 0)
        scores, allowed = masked_scores(
            queries, key_block, first_key, query_places, query_segment, doc_lens
        )
        soft_weight = jnp.where(
            allowed[:, None, None, :], jnp.exp(scores - log_total[..., None]), 0.0
        )
        value_heads = value_block.reshape(block_rows, KV_HEADS, HEAD_DIM)
        key_heads = key_block.reshape(block_rows, KV_HEADS, HEAD_DIM)
        grad_weight = jnp.einsum(
            "qkgd,skd->qkgs", grad_heads, value_heads, preferred_element_type=jnp.float32
        )
        grad_score = (soft_weight * (grad_weight - row_delta[..., None])).astype(jnp.bfloat16)
        state_out = grad_queries + jnp.einsum(
            "qkgs,skd->qkgd", grad_score, key_heads, preferred_element_type=jnp.float32
        )
        grad_key = (
            jnp.einsum("qkgs,qkgd->skd", grad_score, queries, preferred_element_type=jnp.float32)
            * score_scale
        )
        grad_value = jnp.einsum(
            "qkgs,qkgd->skd",
            soft_weight.astype(jnp.bfloat16),
            grad_heads,
            preferred_element_type=jnp.float32,
        )
        return (
            state_out,
            jnp.concatenate(
                [
                    grad_key.reshape(block_rows, key_width),
                    grad_value.reshape(block_rows, key_width),
                ],
                axis=1,
            ),
        )

    start_grad = jnp.zeros((row_count, KV_HEADS, groups_per, HEAD_DIM), jnp.float32)
    grad_queries, pair_blocks = lax.scan(
        back_step, start_grad, jnp.arange(total_keys // block_rows, dtype=jnp.int32)
    )
    pair_terms = pair_blocks.reshape(total_keys, 2 * key_width)
    pair_sums = lax.psum_scatter(pair_terms, "seq", scatter_dimension=0, tiled=True)
    grad_rot_queries = rotate(
        (grad_queries * score_scale).reshape(row_count, HEADS, HEAD_DIM), positions, -1.0
    ).reshape(row_count, D)
    grad_rot_keys = rotate(
        pair_sums[:, :key_width].reshape(row_count, KV_HEADS, HEAD_DIM), positions, -1.0
    ).reshape(row_count, key_width)
    grad_projected = jnp.concatenate(
        [grad_rot_queries, grad_rot_keys, pair_sums[:, key_width:]], axis=1
    ).astype(jnp.bfloat16)
    grad_mix = jnp.einsum(
        "nd,nf->df", normed_low, grad_projected, preferred_element_type=jnp.float32
    )
    grad_normed = jnp.einsum(
        "nf,df->nd", grad_projected, mix_full, preferred_element_type=jnp.float32
    )
    grad_gain_attn, grad_input_norm = norm_backward(grad_normed, unit_attn, scale_attn, gain_attn)
    grad_gains = jnp.stack([grad_gain_attn, grad_gain_mlp])
    attn_part = (
        lax.psum_scatter(grad_mix, ("seq", "fsdp"), scatter_dimension=0, tiled=True),
        lax.psum_scatter(grad_out, ("seq", "fsdp"), scatter_dimension=0, tiled=True),
        lax.psum_scatter(grad_gains, ("seq", "fsdp"), scatter_dimension=1, tiled=True),
    )
    return (grad_middle + grad_input_norm, attn_part, mlp_part)


def adam_update(weight, first, second, grad, clip_scale, rate):
    clipped = grad * clip_scale
    first_new = BETA_ONE * first + (1.0 - BETA_ONE) * clipped
    second_new = BETA_TWO * second + (1.0 - BETA_TWO) * clipped * clipped
    first_hat = first_new / (1.0 - BETA_ONE**STEP_NUMBER)
    second_hat = second_new / (1.0 - BETA_TWO**STEP_NUMBER)
    updated = weight - rate * (
        first_hat / (jnp.sqrt(second_hat) + EPS_ADAM) + WEIGHT_DECAY * weight
    )
    return (updated, first_new, second_new)


def local(
    tokens,
    cotangent,
    lengths,
    mix_weight,
    out_weight,
    in_weight,
    down_weight,
    norm_gains,
    mix_first,
    out_first,
    in_first,
    down_first,
    norm_first,
    mix_second,
    out_second,
    in_second,
    down_second,
    norm_second,
):
    row_count = tokens.shape[0]
    group_index = lax.axis_index("fsdp")
    cycle_index = lax.axis_index("seq")
    doc_lens = lax.dynamic_index_in_dim(lengths, group_index, 0, keepdims=False)
    query_places = cycle_index * row_count + jnp.arange(row_count, dtype=jnp.int32)
    query_segment, positions = doc_layout(query_places, doc_lens)
    keep_rows = (query_segment < doc_lens.shape[0]).astype(jnp.float32)[:, None]
    context = (query_places, query_segment, positions, keep_rows, doc_lens)
    stream = tokens.astype(jnp.float32)
    layer_index = 0
    attn_set, mlp_set = fetch_layer(
        mix_weight, out_weight, norm_gains, in_weight, down_weight, layer_index
    )
    stream, saved = layer_forward(stream, attn_set, mlp_set, context)
    saved_list = [saved]
    weight_list = [(attn_set, mlp_set)]
    hidden_out = stream.astype(jnp.bfloat16)
    grad_stream = cotangent.astype(jnp.float32)
    attn_sums = [None] * LAYERS
    mlp_sums = [None] * LAYERS
    for layer_index in reversed(range(LAYERS)):
        attn_set, mlp_set = weight_list[layer_index]
        grad_stream, attn_part, mlp_part = layer_backward(
            grad_stream, saved_list[layer_index], attn_set, mlp_set, context
        )
        attn_sums[layer_index] = attn_part
        mlp_sums[layer_index] = mlp_part
    mix_grad = jnp.stack([attn_sums[0][0]])
    out_grad = jnp.stack([attn_sums[0][1]])
    norm_grad = jnp.stack([attn_sums[0][2]])
    in_grad = jnp.stack([mlp_sums[0][0]])
    down_grad = jnp.stack([mlp_sums[0][1]])
    squares = (
        jnp.sum(mix_grad * mix_grad)
        + jnp.sum(out_grad * out_grad)
        + jnp.sum(in_grad * in_grad)
        + jnp.sum(down_grad * down_grad)
        + jnp.sum(norm_grad * norm_grad)
    )
    total_squares = lax.psum(squares, ("seq", "fsdp"))
    grad_norm = jnp.sqrt(total_squares)
    clip_scale = CLIP_NORM / jnp.maximum(grad_norm, CLIP_NORM)
    mix_new, mix_moment, mix_square = adam_update(
        mix_weight, mix_first, mix_second, mix_grad, clip_scale, LEARN_RATE
    )
    out_new, out_moment, out_square = adam_update(
        out_weight, out_first, out_second, out_grad, clip_scale, OUT_RATE
    )
    in_new, in_moment, in_square = adam_update(
        in_weight, in_first, in_second, in_grad, clip_scale, LEARN_RATE
    )
    down_new, down_moment, down_square = adam_update(
        down_weight, down_first, down_second, down_grad, clip_scale, LEARN_RATE
    )
    norm_new, norm_moment, norm_square = adam_update(
        norm_gains, norm_first, norm_second, norm_grad, clip_scale, GAIN_RATE
    )
    return (
        hidden_out,
        grad_stream,
        grad_norm,
        mix_grad,
        mix_new,
        mix_moment,
        mix_square,
        mix_new.astype(jnp.bfloat16),
        out_grad,
        out_new,
        out_moment,
        out_square,
        out_new.astype(jnp.bfloat16),
        in_grad,
        in_new,
        in_moment,
        in_square,
        in_new.astype(jnp.bfloat16),
        down_grad,
        down_new,
        down_moment,
        down_square,
        down_new.astype(jnp.bfloat16),
        norm_grad,
        norm_new,
        norm_moment,
        norm_square,
        norm_new.astype(jnp.bfloat16),
    )


MESH = pl.DeviceIdType.MESH
ANY = pl.BlockSpec(memory_space=pl.ANY)
VMEM = pl.BlockSpec(memory_space=pltpu.VMEM)
LOW = jnp.bfloat16
SQUARE = 8
SEQ = 16
FLEET = 32
ROWS = 128
TOP_ROWS = 64
DOC_KINDS = 6
KEYS = 1024
BLOCK = 256
CORE, NEAR_Y, NEAR_Z = 1, 2, 4
LOG2E = 1.4426950408889634
SCALE2 = HEAD_DIM ** (-0.5) * LOG2E
WALL = 2.0**100


def flip(value, bits):
    for bit in (1, 2, 4, 8):
        if bits & bit:
            value = value + bit - 2 * bit * (lax.rem(lax.div(value, bit), 2))
    return value


class Place:
    def __init__(self):
        self.seq = lax.axis_index("seq")
        self.fsdp = lax.axis_index("fsdp")
        self.member = lax.rem(self.seq, SQUARE)
        self.half = lax.div(self.seq, SQUARE)
        self.rank = self.seq * 2 + self.fsdp

    def peer(self, bits):
        return (flip(self.seq, bits), self.fsdp)

    def slot(self, bits):
        return flip(self.member, bits)

    def after(self, step):
        rank = lax.rem(self.rank + step, FLEET)
        return rank, (lax.div(rank, 2), lax.rem(rank, 2))

    def twin(self):
        return (self.seq, 1 - self.fsdp)


def send(src, dst, sems, index, device):
    return pltpu.make_async_remote_copy(
        src_ref=src,
        dst_ref=dst,
        send_sem=sems[0].at[index],
        recv_sem=sems[1].at[index],
        device_id=device,
        device_id_type=MESH,
    )


def greet(devices):
    barrier = pltpu.get_barrier_semaphore()
    for device in devices:
        pl.semaphore_signal(barrier, inc=1, device_id=device, device_id_type=MESH)
    pl.semaphore_wait(barrier, len(devices))


def pair_sems(count):
    return [pltpu.SemaphoreType.DMA((count,)), pltpu.SemaphoreType.DMA((count,))]


class SquareGather:
    COPIES = 10

    def __init__(self, place, src, out, sems, local_sem, top_rows):
        p, h = place, top_rows
        own, ys, zs = p.slot(0), p.slot(NEAR_Y), p.slot(NEAR_Z)
        ds = p.slot(NEAR_Y | NEAR_Z)
        to_y, to_z, to_c = p.peer(NEAR_Y), p.peer(NEAR_Z), p.peer(CORE)
        top, low = pl.ds(0, h), pl.ds(h, ROWS - h)
        self.local = pltpu.make_async_copy(src, out.at[own], local_sem)
        self.y0 = send(src.at[top], out.at[own, top], sems, 0, to_y)
        self.y1 = send(src.at[low], out.at[own, low], sems, 1, to_y)
        self.z1 = send(src.at[low], out.at[own, low], sems, 2, to_z)
        self.z0 = send(src.at[top], out.at[own, top], sems, 3, to_z)
        self.fz = send(out.at[ys, top], out.at[ys, top], sems, 4, to_z)
        self.fy = send(out.at[zs, low], out.at[zs, low], sems, 5, to_y)
        self.c = [
            send(src, out.at[own], sems, 6, to_c),
            send(out.at[ys], out.at[ys], sems, 7, to_c),
            send(out.at[zs], out.at[zs], sems, 8, to_c),
            send(out.at[ds], out.at[ds], sems, 9, to_c),
        ]

    def start(self):
        for copy in (self.y0, self.z1, self.y1, self.z0, self.c[0], self.local):
            copy.start()

    def relay(self):
        self.y0.wait_recv()
        self.fz.start()
        self.z1.wait_recv()
        self.fy.start()

    def share(self):
        self.y1.wait_recv()
        self.c[1].start()
        self.z0.wait_recv()
        self.c[2].start()

    def finish(self):
        self.fz.wait_recv()
        self.fy.wait_recv()
        self.c[3].start()
        for copy in self.c:
            copy.wait_recv()
        for copy in [self.y0, self.y1, self.z0, self.z1, self.fz, self.fy] + self.c:
            copy.wait_send()
        self.local.wait()


def mix_spread(place, mix, mix_o, plane_s, cross_s, local_sem):
    twin = (place.seq, 1 - place.fsdp)
    first = [
        send(
            mix.at[lax.rem(flip(place.seq, bits), SQUARE)],
            mix_o.at[place.rank],
            plane_s,
            bits,
            (flip(place.seq, bits), place.fsdp),
        )
        for bits in range(1, SEQ)
    ]
    second = []
    for bits in range(SEQ):
        spot = flip(place.seq, bits) * 2 + place.fsdp
        second.append(send(mix_o.at[spot], mix_o.at[spot], cross_s, bits, twin))
    local = pltpu.make_async_copy(mix.at[place.member], mix_o.at[place.rank], local_sem)
    return first, second, local


def gather_kernel(src, out, send_sems, recv_sems, local_sem):
    place = Place()
    greet([place.peer(bits) for bits in (CORE, NEAR_Y, NEAR_Z)])
    gather = SquareGather(place, src, out, (send_sems, recv_sems), local_sem.at[0], TOP_ROWS)
    gather.start()
    gather.relay()
    gather.share()
    gather.finish()


def square_gather(block):
    return pl.pallas_call(
        gather_kernel,
        out_shape=jax.ShapeDtypeStruct((SQUARE,) + block.shape, block.dtype),
        in_specs=[ANY],
        out_specs=ANY,
        scratch_shapes=pair_sems(SquareGather.COPIES) + [pltpu.SemaphoreType.DMA((1,))],
        compiler_params=pltpu.CompilerParams(collective_id=1, has_side_effects=True),
        name="square_gather",
    )(block).reshape(SQUARE * block.shape[0], block.shape[1])


def add_rows(target, left, right, start, count):
    step = 16

    def body(number, _):
        rows = pl.ds(pl.multiple_of(start + number * step, step), step)
        target[rows] = (left[rows].astype(jnp.float32) + right[rows].astype(jnp.float32)).astype(
            target.dtype
        )
        return 0

    lax.fori_loop(0, count // step, body, 0)


class SquareScatter:
    def __init__(self, place, part, total, buffers, sems, top_rows):
        sib, away, passed, landed = buffers
        self.place, self.part, self.total = place, part, total
        self.sib, self.away, self.passed, self.landed = sib, away, passed, landed
        h = self.top_rows = top_rows
        top, low = pl.ds(0, h), pl.ds(h, ROWS - h)
        to_y, to_z, to_c = place.peer(NEAR_Y), place.peer(NEAR_Z), place.peer(CORE)
        self.order = (NEAR_Y | NEAR_Z, NEAR_Y, NEAR_Z, 0)
        self.cores = [
            send(part.at[place.slot(bits | CORE)], sib.at[number], sems, number, to_c)
            for number, bits in enumerate(self.order)
        ]
        self.d0 = send(away.at[0, top], passed.at[top], sems, 4, to_y)
        self.d1 = send(away.at[0, low], passed.at[low], sems, 5, to_z)
        self.y0 = send(away.at[1, top], landed.at[0, top], sems, 6, to_y)
        self.y1 = send(away.at[1, low], landed.at[0, low], sems, 7, to_y)
        self.z0 = send(away.at[2, top], landed.at[1, top], sems, 8, to_z)
        self.z1 = send(away.at[2, low], landed.at[1, low], sems, 9, to_z)

    @staticmethod
    def buffers(width):
        return [
            pltpu.VMEM((4, ROWS, width), LOW),
            pltpu.VMEM((3, ROWS, width), LOW),
            pltpu.VMEM((ROWS, width), LOW),
            pltpu.VMEM((2, ROWS, width), LOW),
        ]

    @staticmethod
    def scratch(width):
        return SquareScatter.buffers(width) + pair_sems(10)

    def start(self):
        for copy in self.cores:
            copy.start()

    def pair_up(self):
        for number, bits in enumerate(self.order):
            self.cores[number].wait_recv()
            target = self.away.at[number] if number < 3 else self.total
            add_rows(target, self.part.at[self.place.slot(bits)], self.sib.at[number], 0, ROWS)
            for copy in ((self.d0, self.d1), (self.y0,), (self.z1,), ())[number]:
                copy.start()

    def relay(self):
        h, rest = self.top_rows, ROWS - self.top_rows
        self.d0.wait_recv()
        add_rows(self.away.at[2], self.away.at[2], self.passed, 0, h)
        self.z0.start()
        self.d1.wait_recv()
        add_rows(self.away.at[1], self.away.at[1], self.passed, h, rest)
        self.y1.start()

    def finish(self):
        h, rest = self.top_rows, ROWS - self.top_rows
        total, landed = self.total, self.landed
        self.y0.wait_recv()
        add_rows(total, total, landed.at[0], 0, h)
        self.z1.wait_recv()
        add_rows(total, total, landed.at[1], h, rest)
        self.z0.wait_recv()
        add_rows(total, total, landed.at[1], 0, h)
        self.y1.wait_recv()
        add_rows(total, total, landed.at[0], h, rest)
        for copy in self.cores + [self.d0, self.d1, self.y0, self.y1, self.z0, self.z1]:
            copy.wait_send()


def scatter_kernel(part, total, *scratch):
    place = Place()
    greet([place.peer(bits) for bits in (CORE, NEAR_Y, NEAR_Z)])
    scatter = SquareScatter(place, part, total, scratch[:4], scratch[4:], TOP_ROWS)
    scatter.start()
    scatter.pair_up()
    scatter.relay()
    scatter.finish()


def square_scatter(part):
    width = part.shape[-1]
    return pl.pallas_call(
        scatter_kernel,
        out_shape=jax.ShapeDtypeStruct((ROWS, width), jnp.float32),
        in_specs=[VMEM],
        out_specs=VMEM,
        scratch_shapes=SquareScatter.scratch(width),
        compiler_params=pltpu.CompilerParams(
            collective_id=2, has_side_effects=True, vmem_limit_bytes=32 << 20
        ),
        name="square_scatter",
    )(part.reshape(SQUARE, ROWS, width))


def return_kernel(pair, part, pair_o, total, *scratch):
    place = Place()
    greet([place.peer(bits) for bits in (CORE, NEAR_Y, NEAR_Z, SQUARE)])
    down = send(pair, pair_o, scratch[:2], 0, place.peer(SQUARE))
    pl.when(place.half == 1)(down.start)
    scatter = SquareScatter(place, part, total, scratch[2:6], scratch[6:], TOP_ROWS)
    scatter.start()
    scatter.pair_up()
    scatter.relay()
    scatter.finish()
    pl.when(place.half == 1)(down.wait_send)
    pl.when(place.half == 0)(down.wait_recv)


def return_exchange(pair, part):
    width = part.shape[-1]
    shape = jax.ShapeDtypeStruct
    return pl.pallas_call(
        return_kernel,
        out_shape=(shape(pair.shape, LOW), shape((ROWS, width), jnp.float32)),
        in_specs=[ANY, VMEM],
        out_specs=(ANY, VMEM),
        scratch_shapes=pair_sems(1) + SquareScatter.scratch(width),
        compiler_params=pltpu.CompilerParams(
            collective_id=6, has_side_effects=True, vmem_limit_bytes=32 << 20
        ),
        name="return_exchange",
    )(pair, part.reshape(SQUARE, ROWS, width))


def last_kernel(
    part, mix, inn, out, total, mix_o, inn_o, out_o, crossed, staged, landed, *scratch
):
    place = Place()
    cross_s, plane_s, inn_s, out_s = (scratch[2 * i : 2 * i + 2] for i in range(4))
    local_sem = scratch[8]
    greet([(flip(place.seq, bits), place.fsdp) for bits in range(1, SEQ)] + [place.twin()])
    twin = place.twin()
    order = list(range(SEQ - 1, -1, -1))
    cross = {}
    for bits in order:
        target = flip(place.seq, bits)
        cross[bits] = send(mix.at[target, 1 - place.fsdp], crossed.at[target], cross_s, bits, twin)
        cross[bits].start()
    scatter = SquareScatter(place, part, total, scratch[9:13], scratch[13:], TOP_ROWS)
    scatter.start()
    copies = [
        send(inn.at[place.slot(bits)], inn_o.at[place.member], inn_s, bits, place.peer(bits))
        for bits in range(1, SQUARE)
    ]
    copies.append(
        pltpu.make_async_copy(inn.at[place.member], inn_o.at[place.member], local_sem.at[0])
    )

    def out_copy(number):
        owner = place.member * 2 + number
        remote = pltpu.make_async_remote_copy(
            src_ref=out.at[number],
            dst_ref=out_o.at[place.half],
            send_sem=out_s[0].at[number],
            recv_sem=out_s[1].at[place.half],
            device_id=(owner, place.fsdp),
            device_id_type=MESH,
        )
        local = pltpu.make_async_copy(out.at[number], out_o.at[place.half], local_sem.at[1])
        return remote, local, owner == place.seq

    scatter.pair_up()
    for number in range(2):
        remote, local, mine = out_copy(number)
        pl.when(mine)(local.start)
        pl.when(jnp.logical_not(mine))(remote.start)
    plane = {}
    for bits in order:
        target = flip(place.seq, bits)
        cross[bits].wait_recv()
        goal = staged.at[target] if bits else landed.at[place.seq]
        add_rows(goal, mix.at[target, place.fsdp], crossed.at[target], 0, mix.shape[2])
        if bits:
            plane[bits] = send(
                staged.at[target], landed.at[place.seq], plane_s, bits, (target, place.fsdp)
            )
            plane[bits].start()
        if bits == SQUARE:
            scatter.relay()
            for copy in copies:
                copy.start()
    scatter.finish()
    for bits in range(1, SEQ):
        plane[bits].wait_recv()

    def body(member, _):
        add_rows(mix_o.at[member], landed.at[member], landed.at[member + SQUARE], 0, mix.shape[2])
        return 0

    lax.fori_loop(0, SQUARE, body, 0)
    for bits in order:
        cross[bits].wait_send()
        if bits:
            plane[bits].wait_send()
    for copy in copies:
        copy.wait()
    for number in range(2):
        remote, local, mine = out_copy(number)
        pl.when(mine)(local.wait)
        pl.when(jnp.logical_not(mine))(remote.wait_send)
    for half in range(2):
        source_seq = half * SQUARE + lax.div(place.seq, 2)
        arrival = pltpu.make_async_remote_copy(
            src_ref=out.at[0],
            dst_ref=out_o.at[half],
            send_sem=out_s[0].at[half],
            recv_sem=out_s[1].at[half],
            device_id=(source_seq, place.fsdp),
            device_id_type=MESH,
        )
        pl.when(source_seq != place.seq)(arrival.wait_recv)


def last_exchange(part, mix, inn, out):
    shape = jax.ShapeDtypeStruct
    width = part.shape[-1]
    share, columns = mix.shape[2:]
    return pl.pallas_call(
        last_kernel,
        out_shape=(
            shape((ROWS, width), jnp.float32),
            shape((SQUARE, share, columns), jnp.float32),
            shape(inn.shape, LOW),
            shape(out.shape, LOW),
        ),
        in_specs=[VMEM, VMEM, ANY, ANY],
        out_specs=(VMEM, VMEM, ANY, ANY),
        scratch_shapes=[pltpu.VMEM((SEQ, share, columns), LOW)] * 3
        + pair_sems(SEQ)
        + pair_sems(SEQ)
        + pair_sems(SQUARE)
        + pair_sems(2)
        + [pltpu.SemaphoreType.DMA((2,))]
        + SquareScatter.scratch(width),
        compiler_params=pltpu.CompilerParams(
            collective_id=3, has_side_effects=True, vmem_limit_bytes=40 << 20
        ),
        name="last_exchange",
    )(part.reshape(SQUARE, ROWS, width), mix, inn, out)


def norm_kernel(gain, squares, gain_o, total_o, gains, sums, mine, *sems):
    place = Place()
    gain_s, sum_s = sems[0:2], sems[2:4]
    greet([place.after(step)[1] for step in range(1, FLEET)])
    copies = []
    for step in range(1, FLEET):
        rank, device = place.after(step)
        copies.append(send(gain.at[rank], gains.at[place.rank], gain_s, step, device))
        copies[-1].start()
    gains[place.rank] = gain[place.rank]
    for copy in copies:
        copy.wait()
    total = jnp.sum(gains[...], axis=0)
    gain_o[...] = total
    mine[...] = squares[...] + total * total
    copies = []
    for step in range(1, FLEET):
        rank, device = place.after(step)
        copies.append(send(mine, sums.at[place.rank], sum_s, step, device))
        copies[-1].start()
    sums[place.rank] = mine[...]
    for copy in copies:
        copy.wait()
    total_o[...] = jnp.sum(sums[...], axis=0)


def norm_exchange(gain, squares):
    shape = jax.ShapeDtypeStruct
    return pl.pallas_call(
        norm_kernel,
        out_shape=(shape(gain.shape[1:], jnp.float32), shape(squares.shape, jnp.float32)),
        in_specs=[VMEM] * 2,
        out_specs=(VMEM,) * 2,
        scratch_shapes=[pltpu.VMEM(gain.shape, jnp.float32)] * 2
        + [pltpu.VMEM(squares.shape, jnp.float32)]
        + pair_sems(FLEET)
        + pair_sems(FLEET),
        compiler_params=pltpu.CompilerParams(collective_id=4, has_side_effects=True),
        name="norm_exchange",
    )(gain, squares)


def dot32(left, right, dims=((1,), (0,))):
    return lax.dot_general(left, right, (dims, ((), ())), preferred_element_type=jnp.float32)


def block_of(number):
    return pl.ds(pl.multiple_of(number * BLOCK, BLOCK), BLOCK)


def later(number_of_columns):
    key_at = lax.broadcasted_iota(jnp.int32, (BLOCK, number_of_columns), 0)
    query_at = lax.rem(lax.broadcasted_iota(jnp.int32, (BLOCK, number_of_columns), 1), BLOCK)
    return key_at > query_at


class Mailbox:
    def __init__(self, sends, receives, locals_):
        self.sends, self.receives, self.locals_ = sends, receives, locals_
        self.taken, self.local_taken = 0, 0

    def take(self, count):
        start = self.taken
        self.taken += count
        spot = pl.ds(start, count)
        return (self.sends.at[spot], self.receives.at[spot])

    def local(self):
        self.local_taken += 1
        return self.locals_.at[self.local_taken - 1]


def token_layout(lengths, group, start, count):
    at = start + lax.broadcasted_iota(jnp.int32, (1, count), 1)
    segment = jnp.zeros((1, count), jnp.int32)
    offset = jnp.zeros((1, count), jnp.int32)
    end = jnp.int32(0)
    for number in range(lengths.shape[1]):
        length = lengths[group, number]
        end = end + length
        passed = (at >= end).astype(jnp.int32)
        segment = segment + passed
        offset = offset + passed * length
    return segment, at - offset


def wall_rows(segment):
    kind = lax.broadcasted_iota(jnp.int32, (32, segment.shape[1]), 0)
    return jnp.where((kind != segment) & (kind < DOC_KINDS), -WALL, 0.0)


def mark_rows(segment):
    kind = lax.broadcasted_iota(jnp.int32, (32, segment.shape[1]), 0)
    return jnp.where(kind == segment, 1.0, 0.0)


def turn_head(head, cosine, sine):
    former, latter = head[: HEAD_DIM // 2], head[HEAD_DIM // 2 :]
    return jnp.concatenate(
        [former * cosine - latter * sine, latter * cosine + former * sine], axis=0
    )


class WeightSpread:
    CHUNKS = 4

    def __init__(self, place, inn, down, in_o, down_o, mail):
        p = place
        twin, across = p.twin(), p.peer(SQUARE)
        self.square = [
            send(inn.at[p.slot(bits)], in_o.at[p.half, p.member, p.fsdp], box, 0, p.peer(bits))
            for bits in range(1, SQUARE)
            for box in (mail.take(1),)
        ]
        self.local = pltpu.make_async_copy(
            inn.at[p.member], in_o.at[p.half, p.member, p.fsdp], mail.local()
        )
        self.down_local = pltpu.make_async_copy(down, down_o.at[p.half, p.fsdp], mail.local())
        near = in_o.at[p.half, pl.ds(0, SQUARE), p.fsdp]
        self.near = send(near, near, mail.take(1), 0, twin)
        width = SQUARE // self.CHUNKS
        self.far, self.passed = [], []
        boxes, passed_boxes = mail.take(self.CHUNKS), mail.take(self.CHUNKS)
        for number in range(self.CHUNKS):
            rows = pl.ds(number * width, width)
            mine = in_o.at[p.half, rows, p.fsdp]
            other = in_o.at[1 - p.half, rows, p.fsdp]
            self.far.append(send(mine, mine, boxes, number, across))
            self.passed.append(send(other, other, passed_boxes, number, twin))
        boxes = mail.take(3)
        self.down_near = send(down, down_o.at[p.half, p.fsdp], boxes, 0, twin)
        self.down_far = send(down, down_o.at[p.half, p.fsdp], boxes, 1, across)
        other = down_o.at[1 - p.half, p.fsdp]
        self.down_passed = send(other, other, boxes, 2, twin)

    def start_square(self):
        for copy in self.square:
            copy.start()
        self.local.start()

    def square_done(self):
        for copy in self.square:
            copy.wait_recv()
        self.local.wait()

    def pass_on(self, number):
        self.far[number].wait_recv()
        self.passed[number].start()

    def finish(self):
        for copy in self.square + self.far:
            copy.wait_send()
        for copy in self.passed + [self.near]:
            copy.wait()
        self.down_far.wait_send()
        self.down_near.wait()
        self.down_passed.wait()
        self.down_local.wait()


def forward_kernel(
    lengths,
    frequency,
    tok,
    gain,
    mix,
    out,
    inn,
    down,
    mix_o,
    out_o,
    in_o,
    down_o,
    gain_o,
    normed_o,
    query_o,
    keys_o,
    values_o,
    pair_o,
    att_o,
    log_o,
    cos_o,
    sin_o,
    middle_o,
    two_o,
    tok_all,
    gains,
    top_s,
    sum_s,
    mixed_s,
    att_low,
    part,
    two,
    sib,
    away,
    passed,
    landed,
    sends,
    receives,
    locals_,
):
    f32 = jnp.float32
    place = Place()
    mail = Mailbox(sends, receives, locals_)
    twin = place.twin()
    blocks = KEYS // BLOCK
    greet([place.after(step)[1] for step in range(1, FLEET)])
    gather_tok = SquareGather(place, tok, tok_all, mail.take(10), mail.local(), TOP_ROWS)
    first, second, mix_local = mix_spread(
        place, mix, mix_o, mail.take(SEQ), mail.take(SEQ), mail.local()
    )
    mix_local.start()
    for bits in range(SEQ - 1, SQUARE - 1, -1):
        first[bits - 1].start()
    gather_tok.start()
    for bits in range(SQUARE - 1, 0, -1):
        first[bits - 1].start()
    gain_local = pltpu.make_async_copy(gain, gains.at[place.rank], mail.local())
    gain_local.start()
    gain_copies = []
    boxes = mail.take(FLEET)
    for step in range(1, FLEET):
        rank, device = place.after(step)
        gain_copies.append(send(gain, gains.at[place.rank], boxes, step, device))
        gain_copies[-1].start()

    keeper = lax.div(place.seq, 2)
    spot = lax.rem(place.seq, 2)
    out_boxes, out_local, twin_boxes = mail.take(2), mail.local(), mail.take(2)

    def out_copy(number):
        remote = pltpu.make_async_remote_copy(
            src_ref=out,
            dst_ref=out_o.at[spot, place.fsdp],
            send_sem=out_boxes[0].at[number],
            recv_sem=out_boxes[1].at[spot],
            device_id=(number * SQUARE + keeper, place.fsdp),
            device_id_type=MESH,
        )
        local = pltpu.make_async_copy(out, out_o.at[spot, place.fsdp], out_local)
        return remote, local, number * SQUARE + keeper == place.seq

    def out_arrival(number):
        source = place.member * 2 + number
        arrival = pltpu.make_async_remote_copy(
            src_ref=out,
            dst_ref=out_o.at[number, place.fsdp],
            send_sem=out_boxes[0].at[number],
            recv_sem=out_boxes[1].at[number],
            device_id=(source, place.fsdp),
            device_id_type=MESH,
        )
        return arrival, source == place.seq

    for number in range(2):
        remote, local, mine = out_copy(number)
        pl.when(mine)(local.start)
        pl.when(jnp.logical_not(mine))(remote.start)

    segment, position = token_layout(lengths, place.fsdp, place.half * KEYS, KEYS)
    angle = frequency[...] * position.astype(f32)
    cos_o[...] = jnp.cos(angle)
    sin_o[...] = jnp.sin(angle)
    keep = (segment < lengths.shape[1]).astype(f32)
    marks = mark_rows(segment).astype(LOW)
    for head in range(2):
        query_o[head, HEAD_DIM:, :] = marks
    walls = wall_rows(segment)

    gather_tok.relay()
    mix_local.wait()
    second[0].start()
    for bits in range(SQUARE - 1, 0, -1):
        first[bits - 1].wait_recv()
        second[bits].start()
    gather_tok.share()
    for bits in range(SEQ - 1, SQUARE - 1, -1):
        first[bits - 1].wait_recv()
        second[bits].start()
    spread = WeightSpread(place, inn, down, in_o, down_o, mail)
    spread.down_local.start()
    spread.down_near.start()
    spread.down_far.start()
    spread.start_square()
    gain_local.wait()
    for copy in gain_copies:
        copy.wait()
    gain_o[...] = jnp.zeros_like(gain_o)
    for rank in range(FLEET):
        lane = rank * (D // FLEET) // 128 * 128
        gain_o[:, lane : lane + 256] += gains[rank].astype(f32)
    gather_tok.finish()
    for copy in second:
        copy.wait_recv()

    up_boxes = mail.take(blocks)
    up = [
        send(pair_o.at[blocks + number], pair_o.at[number], up_boxes, number, place.peer(SQUARE))
        for number in range(blocks)
    ]
    for number in range(blocks):
        columns = pl.ds(number * BLOCK, BLOCK)
        halves = []
        for block in (2 * number, 2 * number + 1):
            x = tok_all[block].astype(f32)
            scale = lax.rsqrt(jnp.mean(x * x, axis=-1, keepdims=True) + EPS_NORM)
            low = (x * scale * gain_o[0:1, :D]).astype(LOW)
            normed_o[block] = low
            halves.append(dot32(low, mix_o[...].reshape(D, 4 * HEAD_DIM)).T)
        projected = jnp.concatenate(halves, axis=1)
        cosine, sine = cos_o[:, columns], sin_o[:, columns]
        for head in range(2):
            turned = turn_head(projected[head * HEAD_DIM : (head + 1) * HEAD_DIM], cosine, sine)
            query_o[head, :HEAD_DIM, columns] = turned.astype(LOW)
        key = turn_head(projected[2 * HEAD_DIM : 3 * HEAD_DIM], cosine, sine).astype(LOW)
        value = projected[3 * HEAD_DIM :].astype(LOW)
        pair_o[blocks + number, :HEAD_DIM] = key
        pair_o[blocks + number, HEAD_DIM:] = value
        pl.when(place.half == 0)(up[number].start)
        rows = pl.ds(KEYS + number * BLOCK, BLOCK)
        wall = walls[:, number * BLOCK : (number + 1) * BLOCK]
        keys_o[rows, :] = jnp.concatenate([key.astype(f32), wall], axis=0).T.astype(LOW)
        values_o[rows, :] = value.astype(f32).T.astype(LOW)

    def queries_of(number):
        columns = pl.ds(number * BLOCK, BLOCK)
        return jnp.concatenate([query_o[0, :, columns], query_o[1, :, columns]], axis=1)

    def fold(queries, spot, carry, diagonal=False):
        score = dot32(keys_o[block_of(spot), :], queries)
        if diagonal:
            score = jnp.where(later(2 * BLOCK), -WALL, score)
        top = jnp.max(score, axis=0, keepdims=True)
        if carry is not None:
            top = jnp.maximum(carry[0], top)
        weight = jnp.exp2((score - top) * SCALE2)
        total = jnp.sum(weight, axis=0, keepdims=True)
        mixed = dot32(pair_o[spot, HEAD_DIM:], weight.astype(LOW))
        if carry is not None:
            fade = jnp.exp2((carry[0] - top) * SCALE2)
            total = total + carry[1] * fade
            mixed = mixed + carry[2] * fade
        return (top, total, mixed)

    for number in range(blocks):
        queries = queries_of(number)
        carry = fold(queries, blocks + number, None, diagonal=True)
        carry = lax.fori_loop(
            blocks, blocks + number, functools.partial(fold, queries), carry
        )
        top_s[number : number + 1, :], sum_s[number : number + 1, :] = carry[:2]
        mixed_s[number] = carry[2]

    spread.square_done()
    spread.near.start()
    for number in range(2):
        remote, local, mine = out_copy(number)
        pl.when(mine)(local.wait)
        pl.when(jnp.logical_not(mine))(remote.wait_send)
    passing = []
    for number in range(2):
        arrival, mine = out_arrival(number)
        pl.when(jnp.logical_not(mine))(arrival.wait_recv)
        block = out_o.at[number, place.fsdp]
        passing.append(send(block, block, twin_boxes, number, twin))
        passing[-1].start()
    spread.down_far.wait_recv()
    spread.down_passed.start()

    @pl.when(place.half == 1)
    def _():
        other_segment, _ = token_layout(lengths, place.fsdp, 0, KEYS)
        other_walls = wall_rows(other_segment)
        for number in range(blocks):
            up[number].wait_recv()
            rows = pl.ds(number * BLOCK, BLOCK)
            wall = other_walls[:, number * BLOCK : (number + 1) * BLOCK]
            keys_o[rows, :] = (
                jnp.concatenate([pair_o[number, :HEAD_DIM].astype(f32), wall], axis=0)
                .T.astype(LOW)
            )
            values_o[rows, :] = pair_o[number, HEAD_DIM:].astype(f32).T.astype(LOW)

    @pl.when(place.half == 0)
    def _():
        for number in range(blocks):
            up[number].wait_send()
            pair_o[number] = jnp.zeros_like(pair_o[number])
        keys_o[pl.ds(0, KEYS), :] = jnp.zeros((KEYS, 128), LOW)
        values_o[pl.ds(0, KEYS), :] = jnp.zeros((KEYS, HEAD_DIM), LOW)

    for copy in spread.far:
        copy.start()
    for number in range(blocks):
        columns = pl.ds(number * BLOCK, BLOCK)
        carry = (top_s[number : number + 1, :], sum_s[number : number + 1, :], mixed_s[number])
        carry = lax.fori_loop(
            0,
            jnp.where(place.half == 1, blocks, 0),
            functools.partial(fold, queries_of(number)),
            carry,
        )
        top, total, mixed = carry
        mixed = mixed * (1.0 / total)
        level = top * SCALE2 + jnp.log2(total)
        for head in range(2):
            side = slice(head * BLOCK, (head + 1) * BLOCK)
            rows = pl.ds(head * HEAD_DIM, HEAD_DIM)
            kept = mixed[:, side] * keep[:, number * BLOCK : (number + 1) * BLOCK]
            att_o[rows, columns] = kept
            att_low[rows, columns] = kept.astype(LOW)
            log_o[pl.ds(head, 1), columns] = level[:, side]

    for copy in passing:
        copy.wait_recv()
    scatter = SquareScatter(
        place, part, middle_o, (sib, away, passed, landed), mail.take(10), TOP_ROWS
    )

    def out_block(slot):
        columns = pl.ds(pl.multiple_of(slot * ROWS, ROWS), ROWS)
        rows = att_low[:, columns].astype(f32).T.astype(LOW)
        part[slot] = dot32(rows, out_o[...].reshape(2 * HEAD_DIM, D)).astype(LOW)

    for number, bits in enumerate(scatter.order):
        out_block(place.slot(bits | CORE))
        scatter.cores[number].start()
    for bits in scatter.order:
        out_block(place.slot(bits))
    scatter.pair_up()
    spread.pass_on(0)
    scatter.relay()
    scatter.finish()
    middle = middle_o[...] + tok[...].astype(f32)
    middle_o[...] = middle
    scale = lax.rsqrt(jnp.mean(middle * middle, axis=-1, keepdims=True) + EPS_NORM)
    two[...] = (middle * scale * gain_o[1:2, :D]).astype(LOW)
    gather_two = SquareGather(place, two, two_o, mail.take(10), mail.local(), TOP_ROWS)
    gather_two.start()
    spread.pass_on(1)
    gather_two.relay()
    gather_two.share()
    spread.pass_on(2)
    gather_two.finish()
    spread.pass_on(3)
    spread.finish()
    for copy in first + second + passing:
        copy.wait_send()


def forward(lengths, frequency, tok, gain, mix, out, inn, down):
    shape = jax.ShapeDtypeStruct
    f32 = jnp.float32
    share, unit = out.shape[0], down.shape[0]
    blocks = KEYS // BLOCK
    return pl.pallas_call(
        forward_kernel,
        out_shape=(
            shape((FLEET,) + mix.shape[1:], LOW),
            shape((2, 2) + out.shape, LOW),
            shape((2, SQUARE, 2) + inn.shape[1:], LOW),
            shape((2, 2) + down.shape, LOW),
            shape((16, D + 128), f32),
            shape((SQUARE, ROWS, D), LOW),
            shape((2, 128, KEYS), LOW),
            shape((2 * KEYS, 128), LOW),
            shape((2 * KEYS, HEAD_DIM), LOW),
            shape((2 * blocks, 2 * HEAD_DIM, BLOCK), LOW),
            shape((2 * HEAD_DIM, KEYS), f32),
            shape((2, KEYS), f32),
            shape((HEAD_DIM // 2, KEYS), f32),
            shape((HEAD_DIM // 2, KEYS), f32),
            shape((ROWS, D), f32),
            shape((SQUARE, ROWS, D), LOW),
        ),
        in_specs=[pl.BlockSpec(memory_space=pltpu.SMEM), VMEM, VMEM, VMEM] + [ANY] * 4,
        out_specs=(VMEM, VMEM, ANY, ANY) + (VMEM,) * 12,
        scratch_shapes=[
            pltpu.VMEM((SQUARE, ROWS, D), LOW),
            pltpu.VMEM((FLEET,) + gain.shape, LOW),
            pltpu.VMEM((8, 2 * BLOCK), f32),
            pltpu.VMEM((8, 2 * BLOCK), f32),
            pltpu.VMEM((blocks, HEAD_DIM, 2 * BLOCK), f32),
            pltpu.VMEM((2 * HEAD_DIM, KEYS), LOW),
            pltpu.VMEM((SQUARE, ROWS, D), LOW),
            pltpu.VMEM((ROWS, D), LOW),
        ]
        + SquareScatter.buffers(D)
        + [
            pltpu.SemaphoreType.DMA((160,)),
            pltpu.SemaphoreType.DMA((160,)),
            pltpu.SemaphoreType.DMA((16,)),
        ],
        compiler_params=pltpu.CompilerParams(
            collective_id=0, has_side_effects=True, vmem_limit_bytes=56 << 20
        ),
        name="forward",
    )(lengths, frequency, tok, gain, mix, out, inn, down)


def attend_back_kernel(
    half, query_t, queries_r, keys, keys_t, values, grad_t, grad_r, log_sum, delta, dq_t, dk, dv
):
    first = jnp.where(half[0] == 1, 0, KEYS // BLOCK)
    dk[...] = jnp.zeros_like(dk)
    dv[...] = jnp.zeros_like(dv)
    for number in range(KEYS // BLOCK):
        columns = pl.ds(number * BLOCK, BLOCK)

        def both(ref, axis):
            if axis == 1:
                return jnp.concatenate([ref[0, :, columns], ref[1, :, columns]], axis=1)
            return jnp.concatenate([ref[0, columns, :], ref[1, columns, :]], axis=0)

        query_c, grad_c = both(query_t, 1), both(grad_t, 1)
        query_b, grad_b = both(queries_r, 0), both(grad_r, 0)
        level = jnp.concatenate([log_sum[0:1, columns], log_sum[1:2, columns]], axis=1)
        shift = jnp.concatenate([delta[0:1, columns], delta[1:2, columns]], axis=1)

        def fold(place, total, diagonal=False):
            rows = block_of(place)
            score = dot32(keys[rows, :], query_c)
            if diagonal:
                score = jnp.where(later(2 * BLOCK), -WALL, score)
            weight = jnp.exp2(score * SCALE2 - level)
            grad_weight = dot32(values[rows, :], grad_c)
            grad_score = (weight * (grad_weight - shift)).astype(LOW)
            dk[rows, :] += dot32(grad_score, query_b)
            dv[rows, :] += dot32(weight.astype(LOW), grad_b)
            return total + dot32(keys_t[:, rows], grad_score)

        last = KEYS // BLOCK + number
        total = fold(last, jnp.zeros((HEAD_DIM, 2 * BLOCK), jnp.float32), diagonal=True)
        total = lax.fori_loop(first, last, fold, total)
        for head in range(2):
            dq_t[head, :, columns] = total[:, head * BLOCK : (head + 1) * BLOCK]


def attend_back(half, *arrays):
    shape = jax.ShapeDtypeStruct
    return pl.pallas_call(
        attend_back_kernel,
        out_shape=(
            shape((2, HEAD_DIM, KEYS), jnp.float32),
            shape((2 * KEYS, HEAD_DIM), jnp.float32),
            shape((2 * KEYS, HEAD_DIM), jnp.float32),
        ),
        in_specs=[pl.BlockSpec(memory_space=pltpu.SMEM)] + [VMEM] * 9,
        out_specs=(VMEM,) * 3,
        compiler_params=pltpu.CompilerParams(vmem_limit_bytes=48 << 20),
        name="attend_back",
    )(half, *arrays)


def swap_fsdp(value):
    return lax.ppermute(value, "fsdp", [(0, 1), (1, 0)])


def swap_half(value):
    return lax.ppermute(value, "seq", [(i, i ^ SQUARE) for i in range(SEQ)])


def in_order(flag, mine, other, axis):
    return jnp.where(
        flag == 0, jnp.stack([mine, other], axis=axis), jnp.stack([other, mine], axis=axis)
    )


def four_parts(half, fsdp, block, axis):
    across = swap_half(block)
    near = in_order(fsdp, block, swap_fsdp(block), axis)
    far = in_order(fsdp, across, swap_fsdp(across), axis)
    return in_order(half, near, far, 0)


def keep_part(value, index, axis):
    mine = lax.dynamic_index_in_dim(value, index, axis, keepdims=False)
    other = lax.dynamic_index_in_dim(value, 1 - index, axis, keepdims=False)
    return mine, other


def sum_fsdp(value, fsdp, axis):
    mine, other = keep_part(value, fsdp, axis)
    return mine + swap_fsdp(other.astype(LOW)).astype(jnp.float32)


def sum_half(value, half):
    mine, other = keep_part(value, half, 0)
    return mine + swap_half(other.astype(LOW)).astype(jnp.float32)


def turn(values_t, cosine, sine):
    former, latter = values_t[:, : HEAD_DIM // 2], values_t[:, HEAD_DIM // 2 :]
    return jnp.concatenate(
        [former * cosine - latter * sine, latter * cosine + former * sine], axis=1
    )


def local_squares(
    tokens,
    cotangent,
    lengths,
    mix_weight,
    out_weight,
    in_weight,
    down_weight,
    norm_gains,
    mix_first,
    out_first,
    in_first,
    down_first,
    norm_first,
    mix_second,
    out_second,
    in_second,
    down_second,
    norm_second,
):
    f32 = jnp.float32
    fsdp = lax.axis_index("fsdp")
    seq = lax.axis_index("seq")
    half, member = seq // SQUARE, seq % SQUARE
    frequency = ROPE_BASE ** (-jnp.arange(HEAD_DIM // 2, dtype=f32) * 2.0 / HEAD_DIM)

    wide = 2 * HEAD_DIM
    key_width = KV_HEADS * HEAD_DIM
    mix_low = mix_weight[0].astype(LOW)
    share = mix_low.shape[0]
    mix_blocks = jnp.concatenate(
        [
            mix_low[:, :D].reshape(share, SQUARE, wide),
            mix_low[:, D : D + key_width].reshape(share, SQUARE, HEAD_DIM),
            mix_low[:, D + key_width :].reshape(share, SQUARE, HEAD_DIM),
        ],
        axis=2,
    ).transpose(1, 0, 2)
    unit = FF // FLEET
    in_blocks = (
        in_weight[0]
        .astype(LOW)
        .reshape(share, 2, 2, SQUARE, 2 * unit)
        .transpose(3, 0, 1, 2, 4)
        .reshape(SQUARE, share, 8 * unit)
    )
    out_low = out_weight[0].astype(LOW)
    down_low = down_weight[0].astype(LOW)
    rank = seq * 2 + fsdp
    gain_block = lax.dynamic_update_slice(
        jnp.zeros((16, 256), LOW), norm_gains[0].astype(LOW), (0, rank * share % 128)
    )
    (
        mix_full,
        out_mine,
        in_mine,
        down_mine,
        gains,
        normed_low,
        query_t,
        keys_r,
        values_r,
        pairs,
        attended_t,
        log_sum,
        cosine,
        sine,
        middle,
        two_all,
    ) = forward(
        lengths, frequency[:, None], tokens, gain_block, mix_blocks, out_low, in_blocks, down_low
    )
    rows = SQUARE * ROWS
    gain_attn, gain_mlp = gains[0, :D], gains[1, :D]
    mix_full = mix_full.reshape(D, 4 * HEAD_DIM)
    out_mine = out_mine.reshape(wide, D)
    in_mine = in_mine.reshape(D, 8 * unit)
    down_mine = down_mine.reshape(4 * unit, D)
    normed_low = normed_low.reshape(rows, D)
    two_all = two_all.reshape(rows, D)
    stream = tokens.astype(f32)
    cot_all = square_gather(cotangent)
    attended_low = attended_t.astype(LOW)
    places = half * KEYS + jnp.arange(KEYS, dtype=jnp.int32)
    doc_lens = lax.dynamic_index_in_dim(lengths, fsdp, 0, keepdims=False)
    keep_t = (places < jnp.sum(doc_lens)).astype(f32)[None, :]
    half_flag = half.astype(jnp.int32).reshape(1)

    _, unit_mlp, scale_mlp = normalize(middle, gain_mlp)
    gate_up = dot32(two_all, in_mine)
    gate, up = gate_up[:, : 4 * unit], gate_up[:, 4 * unit :]
    sigmoid_gate = jax.nn.sigmoid(gate)
    hidden_low = (gate * sigmoid_gate * up).astype(LOW)
    y_part = dot32(hidden_low, down_mine).astype(LOW)
    grad_hidden = dot32(cot_all, down_mine, ((1,), (1,)))
    grad_gate = grad_hidden * up * sigmoid_gate * (1.0 + gate * (1.0 - sigmoid_gate))
    grad_up = grad_hidden * gate * sigmoid_gate
    grad_gate_up = jnp.concatenate([grad_gate, grad_up], axis=1).astype(LOW)
    two_part = dot32(grad_gate_up, in_mine, ((1,), (1,))).astype(LOW)
    grad_normed_two = square_scatter(two_part)
    grad_down = dot32(hidden_low, cot_all, ((0,), (0,)))
    grad_in = dot32(two_all, grad_gate_up, ((0,), (0,)))
    grad_stream = cotangent.astype(f32)
    grad_gain_mlp, grad_middle_norm = norm_backward(grad_normed_two, unit_mlp, scale_mlp, gain_mlp)
    grad_middle = grad_stream + grad_middle_norm
    grad_in = grad_in.reshape(2, SQUARE, 2, share, 8 * unit)
    gate_x = sum_fsdp(grad_in[..., : 4 * unit], fsdp, 2)
    grad_up_in, gate_x = lax.optimization_barrier((grad_in[..., 4 * unit :], gate_x))
    up_x = sum_fsdp(grad_up_in, fsdp, 2)
    gate_sum = sum_half(gate_x, half)
    up_sum = sum_half(up_x, half)
    grad_down, up_x = lax.optimization_barrier((grad_down, up_x))
    down_x = sum_fsdp(grad_down.reshape(2, 2, unit, D), fsdp, 1)

    branch_all = square_gather(grad_middle.astype(LOW))
    grad_out = dot32(attended_low, branch_all)
    out_sum = sum_fsdp(grad_out.reshape(2, 2, share, D), fsdp, 1)
    grad_att = dot32(out_mine, branch_all, ((1,), (1,))) * keep_t
    grad_t = grad_att.astype(LOW).reshape(2, HEAD_DIM, rows)
    delta = jnp.sum(
        grad_t.astype(f32) * attended_t.reshape(2, HEAD_DIM, rows), axis=1
    )
    dq_t, dk, dv = attend_back(
        half_flag,
        query_t,
        query_t[:, :HEAD_DIM].transpose(0, 2, 1),
        keys_r,
        pairs[:, :HEAD_DIM].transpose(1, 0, 2).reshape(HEAD_DIM, 2 * KEYS),
        values_r,
        grad_t,
        grad_t.transpose(0, 2, 1),
        log_sum,
        delta,
    )
    pair = jnp.concatenate([dk, dv], axis=1)
    returned, y_sum = return_exchange(pair[:KEYS].astype(LOW), y_part)
    hidden_out = (middle + y_sum).astype(LOW)
    down_x, returned = lax.optimization_barrier((down_x, returned))
    down_sum = sum_half(down_x, half)
    pair_t = (pair[KEYS:] + jnp.where(half == 0, returned.astype(f32), 0.0)).T
    scale = HEAD_DIM ** (-0.5)
    turned = turn(
        jnp.concatenate([dq_t, pair_t[None, :HEAD_DIM]], axis=0) * scale, cosine, -sine
    )
    grad_projected_t = jnp.concatenate(
        [turned.reshape(3 * HEAD_DIM, rows), pair_t[HEAD_DIM:]], axis=0
    ).astype(LOW)
    grad_mix = dot32(normed_low, grad_projected_t, ((0,), (1,))).astype(LOW)
    normed_part = dot32(grad_projected_t, mix_full, ((0,), (1,))).astype(LOW)
    in_sum = jnp.concatenate([gate_sum.astype(LOW), up_sum.astype(LOW)], axis=-1)
    grad_normed, mix_got, in_got, out_got = last_exchange(
        normed_part,
        grad_mix.reshape(SEQ, 2, share, 4 * HEAD_DIM),
        in_sum,
        out_sum.astype(LOW),
    )
    _, unit_attn, scale_attn = normalize(stream, gain_attn)
    grad_gain_attn, grad_input_norm = norm_backward(grad_normed, unit_attn, scale_attn, gain_attn)
    grad_tokens = grad_middle + grad_input_norm

    gain_blocks = jnp.pad(
        jnp.stack([grad_gain_attn, grad_gain_mlp]).reshape(2, FLEET, share).transpose(1, 0, 2),
        ((0, 0), (0, 6), (0, 128 - share)),
    )
    in_grad = (
        in_got.reshape(SQUARE, share, 2, 2, 2 * unit)
        .transpose(1, 2, 3, 0, 4)
        .reshape(1, share, 2 * FF)
        .astype(f32)
    )
    mix_got = mix_got.transpose(1, 0, 2)
    mix_grad = jnp.concatenate(
        [
            mix_got[:, :, :wide].reshape(share, D),
            mix_got[:, :, wide : wide + HEAD_DIM].reshape(share, key_width),
            mix_got[:, :, wide + HEAD_DIM :].reshape(share, key_width),
        ],
        axis=1,
    )[None]
    out_grad = jnp.sum(out_got.astype(f32), axis=0)[None]
    down_grad = down_sum[None]
    squares = sum(jnp.sum(grad * grad) for grad in (mix_grad, out_grad, in_grad, down_grad))
    corner = jnp.zeros((8, 128), f32).at[0, 127].set(squares)
    norm_got, totals = norm_exchange(gain_blocks, corner)
    norm_grad = norm_got[None, :2, :share]
    grad_norm = jnp.sqrt(jnp.sum(totals))
    clip_scale = CLIP_NORM / jnp.maximum(grad_norm, CLIP_NORM)
    results = [hidden_out, grad_tokens, grad_norm]
    for weight, first, second, grad, rate in (
        (mix_weight, mix_first, mix_second, mix_grad, LEARN_RATE),
        (out_weight, out_first, out_second, out_grad, OUT_RATE),
        (in_weight, in_first, in_second, in_grad, LEARN_RATE),
        (down_weight, down_first, down_second, down_grad, LEARN_RATE),
        (norm_gains, norm_first, norm_second, norm_grad, GAIN_RATE),
    ):
        new, moment, square = adam_update(weight, first, second, grad, clip_scale, rate)
        results += [grad, new, moment, square, new.astype(LOW)]
    return tuple(results)


def solution(mesh):
    squares = mesh.shape["seq"] == SEQ and mesh.shape["fsdp"] == 2
    return jax.shard_map(
        local_squares if squares else local,
        mesh=mesh,
        in_specs=(
            P(("seq", "fsdp"), None),
            P(("seq", "fsdp"), None),
            P(),
            P(None, ("seq", "fsdp"), None),
            P(None, ("seq", "fsdp"), None),
            P(None, ("seq", "fsdp"), None),
            P(None, ("seq", "fsdp"), None),
            P(None, None, ("seq", "fsdp")),
            P(None, ("seq", "fsdp"), None),
            P(None, ("seq", "fsdp"), None),
            P(None, ("seq", "fsdp"), None),
            P(None, ("seq", "fsdp"), None),
            P(None, None, ("seq", "fsdp")),
            P(None, ("seq", "fsdp"), None),
            P(None, ("seq", "fsdp"), None),
            P(None, ("seq", "fsdp"), None),
            P(None, ("seq", "fsdp"), None),
            P(None, None, ("seq", "fsdp")),
        ),
        out_specs=(
            P(("seq", "fsdp"), None),
            P(("seq", "fsdp"), None),
            P(),
            P(None, ("seq", "fsdp"), None),
            P(None, ("seq", "fsdp"), None),
            P(None, ("seq", "fsdp"), None),
            P(None, ("seq", "fsdp"), None),
            P(None, ("seq", "fsdp"), None),
            P(None, ("seq", "fsdp"), None),
            P(None, ("seq", "fsdp"), None),
            P(None, ("seq", "fsdp"), None),
            P(None, ("seq", "fsdp"), None),
            P(None, ("seq", "fsdp"), None),
            P(None, ("seq", "fsdp"), None),
            P(None, ("seq", "fsdp"), None),
            P(None, ("seq", "fsdp"), None),
            P(None, ("seq", "fsdp"), None),
            P(None, ("seq", "fsdp"), None),
            P(None, ("seq", "fsdp"), None),
            P(None, ("seq", "fsdp"), None),
            P(None, ("seq", "fsdp"), None),
            P(None, ("seq", "fsdp"), None),
            P(None, ("seq", "fsdp"), None),
            P(None, None, ("seq", "fsdp")),
            P(None, None, ("seq", "fsdp")),
            P(None, None, ("seq", "fsdp")),
            P(None, None, ("seq", "fsdp")),
            P(None, None, ("seq", "fsdp")),
        ),
        check_vma=False,
    )
```

```python
import functools

import jax
import jax.numpy as jnp
from jax import lax
from jax.experimental import pallas as pl
from jax.experimental.pallas import tpu as pltpu
from jax.sharding import PartitionSpec as P

D = 1536
HEADS = 16
KV_HEADS = 8
HEAD_DIM = 96
FF = 4096
LAYERS = 1
STEP_NUMBER = 10


EPS_NORM = 1e-05
ROPE_BASE = 100000.0
FLOOR_SCORE = -1e30
LEARN_RATE = 0.05
OUT_RATE = 0.2
GAIN_RATE = 2.0
BETA_ONE = 0.9
BETA_TWO = 0.99
EPS_ADAM = 1e-08
WEIGHT_DECAY = 0.1
CLIP_NORM = 1.0


def doc_layout(places, doc_lens):
    doc_ends = jnp.cumsum(doc_lens)
    passed = (places[:, None] >= doc_ends[None, :]).astype(jnp.int32)
    segment = jnp.sum(passed, axis=1)
    offset = jnp.sum(passed * doc_lens[None, :], axis=1)
    return (segment, places - offset)


def rotate(vectors, places, direction):
    half_dim = vectors.shape[-1] // 2
    inverse = ROPE_BASE ** (-jnp.arange(half_dim, dtype=jnp.float32) * 2.0 / vectors.shape[-1])
    angles = places.astype(jnp.float32)[:, None] * inverse[None, :]
    cosine = jnp.cos(angles)[:, None, :]
    sine_term = direction * jnp.sin(angles)[:, None, :]
    former = vectors[..., :half_dim]
    latter = vectors[..., half_dim:]
    return jnp.concatenate(
        [former * cosine - latter * sine_term, latter * cosine + former * sine_term], axis=-1
    )


def normalize(values, gain):
    scale_rows = lax.rsqrt(jnp.mean(values * values, axis=-1, keepdims=True) + EPS_NORM)
    unit_rows = values * scale_rows
    return (unit_rows * gain, unit_rows, scale_rows)


def norm_backward(grad_normed, unit_rows, scale_rows, gain):
    grad_gain = jnp.sum(grad_normed * unit_rows, axis=0)
    grad_unit = grad_normed * gain
    grad_values = scale_rows * (
        grad_unit - unit_rows * jnp.mean(grad_unit * unit_rows, axis=-1, keepdims=True)
    )
    return (grad_gain, grad_values)


def masked_scores(queries, key_block, first_key, query_places, query_segment, doc_lens):
    block_rows = key_block.shape[0]
    key_places = first_key + jnp.arange(block_rows, dtype=jnp.int32)
    key_segment, unused_places = doc_layout(key_places, doc_lens)
    allowed = (query_segment[:, None] == key_segment[None, :]) & (
        key_places[None, :] <= query_places[:, None]
    )
    key_heads = key_block.reshape(block_rows, KV_HEADS, HEAD_DIM)
    raw_scores = jnp.einsum(
        "qkgd,skd->qkgs", queries, key_heads, preferred_element_type=jnp.float32
    ) * HEAD_DIM ** (-0.5)
    return (jnp.where(allowed[:, None, None, :], raw_scores, FLOOR_SCORE), allowed)


def fold_block(carry, key_block, value_block, first_key, setting):
    queries, query_places, query_segment, doc_lens = setting
    running, totals, accumulated = carry
    block_rows = key_block.shape[0]
    scores, allowed = masked_scores(
        queries, key_block, first_key, query_places, query_segment, doc_lens
    )
    newest = jnp.maximum(running, jnp.max(scores, axis=-1))
    factor = jnp.exp(running - newest)
    weights = jnp.where(allowed[:, None, None, :], jnp.exp(scores - newest[..., None]), 0.0)
    totals = totals * factor + jnp.sum(weights, axis=-1)
    value_heads = value_block.reshape(block_rows, KV_HEADS, HEAD_DIM)
    accumulated = accumulated * factor[..., None] + jnp.einsum(
        "qkgs,skd->qkgd",
        weights.astype(jnp.bfloat16),
        value_heads,
        preferred_element_type=jnp.float32,
    )
    return (newest, totals, accumulated)


def fold_piece(carry, key_rows, value_rows, start, setting):
    total_rows = key_rows.shape[0]
    block_rows = 512

    def step(inner_state, number):
        first_key = start + number * block_rows
        key_block = lax.dynamic_slice_in_dim(key_rows, number * block_rows, block_rows, 0)
        value_block = lax.dynamic_slice_in_dim(value_rows, number * block_rows, block_rows, 0)
        state_out = fold_block(inner_state, key_block, value_block, first_key, setting)
        return (state_out, None)

    carry, unused_out = lax.scan(step, carry, jnp.arange(total_rows // block_rows, dtype=jnp.int32))
    return carry


def fetch_layer(mix_weight, out_weight, norm_gains, in_weight, down_weight, layer_index):
    mix_full, out_full, gain_full, in_full, down_full = (
        lax.all_gather(
            mix_weight[layer_index].astype(jnp.bfloat16), ("seq", "fsdp"), axis=0, tiled=True
        ),
        lax.all_gather(
            out_weight[layer_index].astype(jnp.bfloat16), ("seq", "fsdp"), axis=0, tiled=True
        ),
        lax.all_gather(
            norm_gains[layer_index].astype(jnp.bfloat16), ("seq", "fsdp"), axis=1, tiled=True
        ),
        lax.all_gather(
            in_weight[layer_index].astype(jnp.bfloat16), ("seq", "fsdp"), axis=0, tiled=True
        ),
        lax.all_gather(
            down_weight[layer_index].astype(jnp.bfloat16), ("seq", "fsdp"), axis=0, tiled=True
        ),
    )
    return ((mix_full, out_full, gain_full), (in_full, down_full))


def layer_forward(stream, attn_set, mlp_set, context):
    query_places, query_segment, positions, keep_rows, doc_lens = context
    mix_full, out_full, gain_full = attn_set
    in_full, down_full = mlp_set
    row_count = stream.shape[0]
    key_width = KV_HEADS * HEAD_DIM
    groups_per = HEADS // KV_HEADS
    gain_attn = gain_full[0].astype(jnp.float32)
    gain_mlp = gain_full[1].astype(jnp.float32)
    normed, unit_attn, scale_attn = normalize(stream, gain_attn)
    normed_low = normed.astype(jnp.bfloat16)
    projected = jnp.dot(normed_low, mix_full, preferred_element_type=jnp.float32)
    queries = (
        rotate(projected[:, :D].reshape(row_count, HEADS, HEAD_DIM), positions, 1.0)
        .astype(jnp.bfloat16)
        .reshape(row_count, KV_HEADS, groups_per, HEAD_DIM)
    )
    keys_low = (
        rotate(
            projected[:, D : D + key_width].reshape(row_count, KV_HEADS, HEAD_DIM), positions, 1.0
        )
        .astype(jnp.bfloat16)
        .reshape(row_count, key_width)
    )
    values_low = projected[:, D + key_width :].astype(jnp.bfloat16)
    setting = (queries, query_places, query_segment, doc_lens)
    key_all, value_all = (
        lax.all_gather(keys_low, "seq", axis=0, tiled=True),
        lax.all_gather(values_low, "seq", axis=0, tiled=True),
    )
    start_carry = (
        jnp.full((row_count, KV_HEADS, groups_per), FLOOR_SCORE, jnp.float32),
        jnp.zeros((row_count, KV_HEADS, groups_per), jnp.float32),
        jnp.zeros((row_count, KV_HEADS, groups_per, HEAD_DIM), jnp.float32),
    )
    running, totals, accumulated = fold_piece(start_carry, key_all, value_all, 0, setting)
    log_total = running + jnp.log(totals)
    attended = (accumulated / totals[..., None]).reshape(row_count, D) * keep_rows
    attended_low = attended.astype(jnp.bfloat16)
    middle = stream + jnp.dot(attended_low, out_full, preferred_element_type=jnp.float32)
    normed_two, unit_mlp, scale_mlp = normalize(middle, gain_mlp)
    normed_two_low = normed_two.astype(jnp.bfloat16)
    gate_up = jnp.dot(normed_two_low, in_full, preferred_element_type=jnp.float32)
    hidden_low = (jax.nn.silu(gate_up[:, :FF]) * gate_up[:, FF:]).astype(jnp.bfloat16)
    result = middle + jnp.dot(hidden_low, down_full, preferred_element_type=jnp.float32)
    kv_saved = (key_all, value_all)
    saved = (
        normed_low,
        unit_attn,
        scale_attn,
        queries,
        keys_low,
        values_low,
        log_total,
        attended,
        attended_low,
        unit_mlp,
        scale_mlp,
        normed_two_low,
        gate_up,
        hidden_low,
        kv_saved,
    )
    return (result, saved)


def layer_backward(grad_stream, saved, attn_set, mlp_set, context):
    query_places, query_segment, positions, keep_rows, doc_lens = context
    mix_full, out_full, gain_full = attn_set
    in_full, down_full = mlp_set
    (
        normed_low,
        unit_attn,
        scale_attn,
        queries,
        keys_low,
        values_low,
        log_total,
        attended,
        attended_low,
        unit_mlp,
        scale_mlp,
        normed_two_low,
        gate_up,
        hidden_low,
        kv_saved,
    ) = saved
    row_count = grad_stream.shape[0]
    key_width = KV_HEADS * HEAD_DIM
    groups_per = HEADS // KV_HEADS
    score_scale = HEAD_DIM ** (-0.5)
    gain_attn = gain_full[0].astype(jnp.float32)
    gain_mlp = gain_full[1].astype(jnp.float32)
    grad_branch = grad_stream.astype(jnp.bfloat16)
    grad_down = jnp.einsum("nf,nd->fd", hidden_low, grad_branch, preferred_element_type=jnp.float32)
    grad_hidden = jnp.einsum(
        "nd,fd->nf", grad_branch, down_full, preferred_element_type=jnp.float32
    )
    gate_part = gate_up[:, :FF]
    up_part = gate_up[:, FF:]
    sigmoid_gate = jax.nn.sigmoid(gate_part)
    grad_gate = grad_hidden * up_part * sigmoid_gate * (1.0 + gate_part * (1.0 - sigmoid_gate))
    grad_up = grad_hidden * gate_part * sigmoid_gate
    grad_gate_up = jnp.concatenate([grad_gate, grad_up], axis=1).astype(jnp.bfloat16)
    grad_in = jnp.einsum(
        "nd,nf->df", normed_two_low, grad_gate_up, preferred_element_type=jnp.float32
    )
    grad_normed_two = jnp.einsum(
        "nf,df->nd", grad_gate_up, in_full, preferred_element_type=jnp.float32
    )
    mlp_part = (
        lax.psum_scatter(grad_in, ("seq", "fsdp"), scatter_dimension=0, tiled=True),
        lax.psum_scatter(grad_down, ("seq", "fsdp"), scatter_dimension=0, tiled=True),
    )
    grad_gain_mlp, grad_middle_norm = norm_backward(grad_normed_two, unit_mlp, scale_mlp, gain_mlp)
    grad_middle = grad_stream + grad_middle_norm
    attn_branch = grad_middle.astype(jnp.bfloat16)
    grad_out = jnp.einsum(
        "nd,ne->de", attended_low, attn_branch, preferred_element_type=jnp.float32
    )
    grad_attended = (
        jnp.einsum("ne,de->nd", attn_branch, out_full, preferred_element_type=jnp.float32)
        * keep_rows
    )
    grad_heads = grad_attended.astype(jnp.bfloat16).reshape(
        row_count, KV_HEADS, groups_per, HEAD_DIM
    )
    row_delta = jnp.sum(
        grad_heads.astype(jnp.float32)
        * attended.reshape(row_count, KV_HEADS, groups_per, HEAD_DIM),
        axis=-1,
    )
    key_all, value_all = kv_saved
    total_keys = key_all.shape[0]
    block_rows = 512

    def back_step(grad_queries, number):
        first_key = number * block_rows
        key_block = lax.dynamic_slice_in_dim(key_all, first_key, block_rows, 0)
        value_block = lax.dynamic_slice_in_dim(value_all, first_key, block_rows, 0)
        scores, allowed = masked_scores(
            queries, key_block, first_key, query_places, query_segment, doc_lens
        )
        soft_weight = jnp.where(
            allowed[:, None, None, :], jnp.exp(scores - log_total[..., None]), 0.0
        )
        value_heads = value_block.reshape(block_rows, KV_HEADS, HEAD_DIM)
        key_heads = key_block.reshape(block_rows, KV_HEADS, HEAD_DIM)
        grad_weight = jnp.einsum(
            "qkgd,skd->qkgs", grad_heads, value_heads, preferred_element_type=jnp.float32
        )
        grad_score = (soft_weight * (grad_weight - row_delta[..., None])).astype(jnp.bfloat16)
        state_out = grad_queries + jnp.einsum(
            "qkgs,skd->qkgd", grad_score, key_heads, preferred_element_type=jnp.float32
        )
        grad_key = (
            jnp.einsum("qkgs,qkgd->skd", grad_score, queries, preferred_element_type=jnp.float32)
            * score_scale
        )
        grad_value = jnp.einsum(
            "qkgs,qkgd->skd",
            soft_weight.astype(jnp.bfloat16),
            grad_heads,
            preferred_element_type=jnp.float32,
        )
        return (
            state_out,
            jnp.concatenate(
                [
                    grad_key.reshape(block_rows, key_width),
                    grad_value.reshape(block_rows, key_width),
                ],
                axis=1,
            ),
        )

    start_grad = jnp.zeros((row_count, KV_HEADS, groups_per, HEAD_DIM), jnp.float32)
    grad_queries, pair_blocks = lax.scan(
        back_step, start_grad, jnp.arange(total_keys // block_rows, dtype=jnp.int32)
    )
    pair_terms = pair_blocks.reshape(total_keys, 2 * key_width)
    pair_sums = lax.psum_scatter(pair_terms, "seq", scatter_dimension=0, tiled=True)
    grad_rot_queries = rotate(
        (grad_queries * score_scale).reshape(row_count, HEADS, HEAD_DIM), positions, -1.0
    ).reshape(row_count, D)
    grad_rot_keys = rotate(
        pair_sums[:, :key_width].reshape(row_count, KV_HEADS, HEAD_DIM), positions, -1.0
    ).reshape(row_count, key_width)
    grad_projected = jnp.concatenate(
        [grad_rot_queries, grad_rot_keys, pair_sums[:, key_width:]], axis=1
    ).astype(jnp.bfloat16)
    grad_mix = jnp.einsum(
        "nd,nf->df", normed_low, grad_projected, preferred_element_type=jnp.float32
    )
    grad_normed = jnp.einsum(
        "nf,df->nd", grad_projected, mix_full, preferred_element_type=jnp.float32
    )
    grad_gain_attn, grad_input_norm = norm_backward(grad_normed, unit_attn, scale_attn, gain_attn)
    grad_gains = jnp.stack([grad_gain_attn, grad_gain_mlp])
    attn_part = (
        lax.psum_scatter(grad_mix, ("seq", "fsdp"), scatter_dimension=0, tiled=True),
        lax.psum_scatter(grad_out, ("seq", "fsdp"), scatter_dimension=0, tiled=True),
        lax.psum_scatter(grad_gains, ("seq", "fsdp"), scatter_dimension=1, tiled=True),
    )
    return (grad_middle + grad_input_norm, attn_part, mlp_part)


def adam_update(weight, first, second, grad, clip_scale, rate):
    clipped = grad * clip_scale
    first_new = BETA_ONE * first + (1.0 - BETA_ONE) * clipped
    second_new = BETA_TWO * second + (1.0 - BETA_TWO) * clipped * clipped
    first_hat = first_new / (1.0 - BETA_ONE**STEP_NUMBER)
    second_hat = second_new / (1.0 - BETA_TWO**STEP_NUMBER)
    updated = weight - rate * (
        first_hat / (jnp.sqrt(second_hat) + EPS_ADAM) + WEIGHT_DECAY * weight
    )
    return (updated, first_new, second_new)


def local(
    tokens,
    cotangent,
    lengths,
    mix_weight,
    out_weight,
    in_weight,
    down_weight,
    norm_gains,
    mix_first,
    out_first,
    in_first,
    down_first,
    norm_first,
    mix_second,
    out_second,
    in_second,
    down_second,
    norm_second,
):
    row_count = tokens.shape[0]
    group_index = lax.axis_index("fsdp")
    cycle_index = lax.axis_index("seq")
    doc_lens = lax.dynamic_index_in_dim(lengths, group_index, 0, keepdims=False)
    query_places = cycle_index * row_count + jnp.arange(row_count, dtype=jnp.int32)
    query_segment, positions = doc_layout(query_places, doc_lens)
    keep_rows = (query_segment < doc_lens.shape[0]).astype(jnp.float32)[:, None]
    context = (query_places, query_segment, positions, keep_rows, doc_lens)
    stream = tokens.astype(jnp.float32)
    layer_index = 0
    attn_set, mlp_set = fetch_layer(
        mix_weight, out_weight, norm_gains, in_weight, down_weight, layer_index
    )
    stream, saved = layer_forward(stream, attn_set, mlp_set, context)
    saved_list = [saved]
    weight_list = [(attn_set, mlp_set)]
    hidden_out = stream.astype(jnp.bfloat16)
    grad_stream = cotangent.astype(jnp.float32)
    attn_sums = [None] * LAYERS
    mlp_sums = [None] * LAYERS
    for layer_index in reversed(range(LAYERS)):
        attn_set, mlp_set = weight_list[layer_index]
        grad_stream, attn_part, mlp_part = layer_backward(
            grad_stream, saved_list[layer_index], attn_set, mlp_set, context
        )
        attn_sums[layer_index] = attn_part
        mlp_sums[layer_index] = mlp_part
    mix_grad = jnp.stack([attn_sums[0][0]])
    out_grad = jnp.stack([attn_sums[0][1]])
    norm_grad = jnp.stack([attn_sums[0][2]])
    in_grad = jnp.stack([mlp_sums[0][0]])
    down_grad = jnp.stack([mlp_sums[0][1]])
    squares = (
        jnp.sum(mix_grad * mix_grad)
        + jnp.sum(out_grad * out_grad)
        + jnp.sum(in_grad * in_grad)
        + jnp.sum(down_grad * down_grad)
        + jnp.sum(norm_grad * norm_grad)
    )
    total_squares = lax.psum(squares, ("seq", "fsdp"))
    grad_norm = jnp.sqrt(total_squares)
    clip_scale = CLIP_NORM / jnp.maximum(grad_norm, CLIP_NORM)
    mix_new, mix_moment, mix_square = adam_update(
        mix_weight, mix_first, mix_second, mix_grad, clip_scale, LEARN_RATE
    )
    out_new, out_moment, out_square = adam_update(
        out_weight, out_first, out_second, out_grad, clip_scale, OUT_RATE
    )
    in_new, in_moment, in_square = adam_update(
        in_weight, in_first, in_second, in_grad, clip_scale, LEARN_RATE
    )
    down_new, down_moment, down_square = adam_update(
        down_weight, down_first, down_second, down_grad, clip_scale, LEARN_RATE
    )
    norm_new, norm_moment, norm_square = adam_update(
        norm_gains, norm_first, norm_second, norm_grad, clip_scale, GAIN_RATE
    )
    return (
        hidden_out,
        grad_stream,
        grad_norm,
        mix_grad,
        mix_new,
        mix_moment,
        mix_square,
        mix_new.astype(jnp.bfloat16),
        out_grad,
        out_new,
        out_moment,
        out_square,
        out_new.astype(jnp.bfloat16),
        in_grad,
        in_new,
        in_moment,
        in_square,
        in_new.astype(jnp.bfloat16),
        down_grad,
        down_new,
        down_moment,
        down_square,
        down_new.astype(jnp.bfloat16),
        norm_grad,
        norm_new,
        norm_moment,
        norm_square,
        norm_new.astype(jnp.bfloat16),
    )


MESH = pl.DeviceIdType.MESH
ANY = pl.BlockSpec(memory_space=pl.ANY)
VMEM = pl.BlockSpec(memory_space=pltpu.VMEM)
LOW = jnp.bfloat16
SQUARE = 8
SEQ = 16
FLEET = 32
ROWS = 128
TOP_ROWS = 64
DOC_KINDS = 6
KEYS = 1024
BLOCK = 256
CORE, NEAR_Y, NEAR_Z = 1, 2, 4
LOG2E = 1.4426950408889634
SCALE2 = HEAD_DIM ** (-0.5) * LOG2E
WALL = 2.0**100


def flip(value, bits):
    for bit in (1, 2, 4, 8):
        if bits & bit:
            value = value + bit - 2 * bit * (lax.rem(lax.div(value, bit), 2))
    return value


class Place:
    def __init__(self):
        self.seq = lax.axis_index("seq")
        self.fsdp = lax.axis_index("fsdp")
        self.member = lax.rem(self.seq, SQUARE)
        self.half = lax.div(self.seq, SQUARE)
        self.rank = self.seq * 2 + self.fsdp

    def peer(self, bits):
        return (flip(self.seq, bits), self.fsdp)

    def slot(self, bits):
        return flip(self.member, bits)

    def after(self, step):
        rank = lax.rem(self.rank + step, FLEET)
        return rank, (lax.div(rank, 2), lax.rem(rank, 2))

    def twin(self):
        return (self.seq, 1 - self.fsdp)


def send(src, dst, sems, index, device):
    return pltpu.make_async_remote_copy(
        src_ref=src,
        dst_ref=dst,
        send_sem=sems[0].at[index],
        recv_sem=sems[1].at[index],
        device_id=device,
        device_id_type=MESH,
    )


def greet(devices):
    barrier = pltpu.get_barrier_semaphore()
    for device in devices:
        pl.semaphore_signal(barrier, inc=1, device_id=device, device_id_type=MESH)
    pl.semaphore_wait(barrier, len(devices))


class SquareGather:
    COPIES = 10

    def __init__(self, place, src, out, sems, local_sem, top_rows):
        p, h = place, top_rows
        own, ys, zs = p.slot(0), p.slot(NEAR_Y), p.slot(NEAR_Z)
        ds = p.slot(NEAR_Y | NEAR_Z)
        to_y, to_z, to_c = p.peer(NEAR_Y), p.peer(NEAR_Z), p.peer(CORE)
        top, low = pl.ds(0, h), pl.ds(h, ROWS - h)
        self.local = pltpu.make_async_copy(src, out.at[own], local_sem)
        self.y0 = send(src.at[top], out.at[own, top], sems, 0, to_y)
        self.y1 = send(src.at[low], out.at[own, low], sems, 1, to_y)
        self.z1 = send(src.at[low], out.at[own, low], sems, 2, to_z)
        self.z0 = send(src.at[top], out.at[own, top], sems, 3, to_z)
        self.fz = send(out.at[ys, top], out.at[ys, top], sems, 4, to_z)
        self.fy = send(out.at[zs, low], out.at[zs, low], sems, 5, to_y)
        self.c = [
            send(src, out.at[own], sems, 6, to_c),
            send(out.at[ys], out.at[ys], sems, 7, to_c),
            send(out.at[zs], out.at[zs], sems, 8, to_c),
            send(out.at[ds], out.at[ds], sems, 9, to_c),
        ]

    def start(self):
        for copy in (self.y0, self.z1, self.y1, self.z0, self.c[0], self.local):
            copy.start()

    def relay(self):
        self.y0.wait_recv()
        self.fz.start()
        self.z1.wait_recv()
        self.fy.start()

    def share(self):
        self.y1.wait_recv()
        self.c[1].start()
        self.z0.wait_recv()
        self.c[2].start()

    def finish(self):
        self.fz.wait_recv()
        self.fy.wait_recv()
        self.c[3].start()
        for copy in self.c:
            copy.wait_recv()
        for copy in [self.y0, self.y1, self.z0, self.z1, self.fz, self.fy] + self.c:
            copy.wait_send()
        self.local.wait()


def mix_spread(place, mix, mix_o, plane_s, cross_s, local_sem):
    twin = (place.seq, 1 - place.fsdp)
    first = [
        send(
            mix.at[lax.rem(flip(place.seq, bits), SQUARE)],
            mix_o.at[place.rank],
            plane_s,
            bits,
            (flip(place.seq, bits), place.fsdp),
        )
        for bits in range(1, SEQ)
    ]
    second = []
    for bits in range(SEQ):
        spot = flip(place.seq, bits) * 2 + place.fsdp
        second.append(send(mix_o.at[spot], mix_o.at[spot], cross_s, bits, twin))
    local = pltpu.make_async_copy(mix.at[place.member], mix_o.at[place.rank], local_sem)
    return first, second, local


def add_rows(target, left, right, start, count):
    step = 16

    def body(number, _):
        rows = pl.ds(pl.multiple_of(start + number * step, step), step)
        target[rows] = (left[rows].astype(jnp.float32) + right[rows].astype(jnp.float32)).astype(
            target.dtype
        )
        return 0

    lax.fori_loop(0, count // step, body, 0)


class SquareScatter:
    def __init__(self, place, part, total, buffers, sems, top_rows):
        sib, away, passed, landed = buffers
        self.place, self.part, self.total = place, part, total
        self.sib, self.away, self.passed, self.landed = sib, away, passed, landed
        h = self.top_rows = top_rows
        top, low = pl.ds(0, h), pl.ds(h, ROWS - h)
        to_y, to_z, to_c = place.peer(NEAR_Y), place.peer(NEAR_Z), place.peer(CORE)
        self.order = (NEAR_Y | NEAR_Z, NEAR_Y, NEAR_Z, 0)
        self.cores = [
            send(part.at[place.slot(bits | CORE)], sib.at[number], sems, number, to_c)
            for number, bits in enumerate(self.order)
        ]
        self.d0 = send(away.at[0, top], passed.at[top], sems, 4, to_y)
        self.d1 = send(away.at[0, low], passed.at[low], sems, 5, to_z)
        self.y0 = send(away.at[1, top], landed.at[0, top], sems, 6, to_y)
        self.y1 = send(away.at[1, low], landed.at[0, low], sems, 7, to_y)
        self.z0 = send(away.at[2, top], landed.at[1, top], sems, 8, to_z)
        self.z1 = send(away.at[2, low], landed.at[1, low], sems, 9, to_z)

    @staticmethod
    def buffers(width):
        return [
            pltpu.VMEM((4, ROWS, width), LOW),
            pltpu.VMEM((3, ROWS, width), LOW),
            pltpu.VMEM((ROWS, width), LOW),
            pltpu.VMEM((2, ROWS, width), LOW),
        ]

    def start(self):
        for copy in self.cores:
            copy.start()

    def pair_one(self, number):
        self.cores[number].wait_recv()
        target = self.away.at[number] if number < 3 else self.total
        mine = self.part.at[self.place.slot(self.order[number])]
        add_rows(target, mine, self.sib.at[number], 0, ROWS)
        for copy in ((self.d0, self.d1), (self.y0,), (self.z1,), ())[number]:
            copy.start()

    def pair_up(self):
        for number in range(4):
            self.pair_one(number)

    def relay(self):
        h, rest = self.top_rows, ROWS - self.top_rows
        self.d0.wait_recv()
        add_rows(self.away.at[2], self.away.at[2], self.passed, 0, h)
        self.z0.start()
        self.d1.wait_recv()
        add_rows(self.away.at[1], self.away.at[1], self.passed, h, rest)
        self.y1.start()

    def finish(self):
        h, rest = self.top_rows, ROWS - self.top_rows
        total, landed = self.total, self.landed
        self.y0.wait_recv()
        add_rows(total, total, landed.at[0], 0, h)
        self.z1.wait_recv()
        add_rows(total, total, landed.at[1], h, rest)
        self.z0.wait_recv()
        add_rows(total, total, landed.at[1], 0, h)
        self.y1.wait_recv()
        add_rows(total, total, landed.at[0], h, rest)
        for copy in self.cores + [self.d0, self.d1, self.y0, self.y1, self.z0, self.z1]:
            copy.wait_send()


def dot32(left, right, dims=((1,), (0,))):
    return lax.dot_general(left, right, (dims, ((), ())), preferred_element_type=jnp.float32)


def block_of(number):
    return pl.ds(pl.multiple_of(number * BLOCK, BLOCK), BLOCK)


def later(number_of_columns):
    key_at = lax.broadcasted_iota(jnp.int32, (BLOCK, number_of_columns), 0)
    query_at = lax.rem(lax.broadcasted_iota(jnp.int32, (BLOCK, number_of_columns), 1), BLOCK)
    return key_at > query_at


class Mailbox:
    def __init__(self, sends, receives, locals_):
        self.sends, self.receives, self.locals_ = sends, receives, locals_
        self.taken, self.local_taken = 0, 0

    def take(self, count):
        start = self.taken
        self.taken += count
        spot = pl.ds(start, count)
        return (self.sends.at[spot], self.receives.at[spot])

    def local(self):
        self.local_taken += 1
        return self.locals_.at[self.local_taken - 1]


def token_layout(lengths, group, start, count):
    at = start + lax.broadcasted_iota(jnp.int32, (1, count), 1)
    segment = jnp.zeros((1, count), jnp.int32)
    offset = jnp.zeros((1, count), jnp.int32)
    end = jnp.int32(0)
    for number in range(lengths.shape[1]):
        length = lengths[group, number]
        end = end + length
        passed = (at >= end).astype(jnp.int32)
        segment = segment + passed
        offset = offset + passed * length
    return segment, at - offset


def wall_rows(segment):
    kind = lax.broadcasted_iota(jnp.int32, (32, segment.shape[1]), 0)
    return jnp.where((kind != segment) & (kind < DOC_KINDS), -WALL, 0.0)


def mark_rows(segment):
    kind = lax.broadcasted_iota(jnp.int32, (32, segment.shape[1]), 0)
    return jnp.where(kind == segment, 1.0, 0.0)


def turn_head(head, cosine, sine):
    former, latter = head[: HEAD_DIM // 2], head[HEAD_DIM // 2 :]
    return jnp.concatenate(
        [former * cosine - latter * sine, latter * cosine + former * sine], axis=0
    )


class WeightSpread:
    CHUNKS = 4

    def __init__(self, place, inn, down, in_o, down_o, mail):
        p = place
        twin, across = p.twin(), p.peer(SQUARE)
        self.square = [
            send(inn.at[p.slot(bits)], in_o.at[p.half, p.member, p.fsdp], box, 0, p.peer(bits))
            for bits in range(1, SQUARE)
            for box in (mail.take(1),)
        ]
        self.local = pltpu.make_async_copy(
            inn.at[p.member], in_o.at[p.half, p.member, p.fsdp], mail.local()
        )
        self.down_local = pltpu.make_async_copy(down, down_o.at[p.half, p.fsdp], mail.local())
        near = in_o.at[p.half, pl.ds(0, SQUARE), p.fsdp]
        self.near = send(near, near, mail.take(1), 0, twin)
        width = SQUARE // self.CHUNKS
        self.far, self.passed = [], []
        boxes, passed_boxes = mail.take(self.CHUNKS), mail.take(self.CHUNKS)
        for number in range(self.CHUNKS):
            rows = pl.ds(number * width, width)
            mine = in_o.at[p.half, rows, p.fsdp]
            other = in_o.at[1 - p.half, rows, p.fsdp]
            self.far.append(send(mine, mine, boxes, number, across))
            self.passed.append(send(other, other, passed_boxes, number, twin))
        boxes = mail.take(3)
        self.down_near = send(down, down_o.at[p.half, p.fsdp], boxes, 0, twin)
        self.down_far = send(down, down_o.at[p.half, p.fsdp], boxes, 1, across)
        other = down_o.at[1 - p.half, p.fsdp]
        self.down_passed = send(other, other, boxes, 2, twin)

    def start_square(self):
        for copy in self.square:
            copy.start()
        self.local.start()

    def square_done(self):
        for copy in self.square:
            copy.wait_recv()
        self.local.wait()

    def pass_on(self, number):
        self.far[number].wait_recv()
        self.passed[number].start()

    def finish(self):
        for copy in self.square + self.far:
            copy.wait_send()
        for copy in self.passed + [self.near]:
            copy.wait()
        self.down_far.wait_send()
        self.down_near.wait()
        self.down_passed.wait()
        self.down_local.wait()


def forward_kernel(
    lengths,
    frequency,
    tok,
    gain,
    mix,
    out,
    inn,
    down,
    cot,
    mix_o,
    out_o,
    in_o,
    down_o,
    gain_o,
    normed_o,
    query_o,
    keys_o,
    values_o,
    pair_o,
    att_o,
    log_o,
    cos_o,
    sin_o,
    middle_o,
    two_o,
    cot_o,
    tok_all,
    gains,
    top_s,
    sum_s,
    mixed_s,
    att_low,
    part,
    two,
    sib,
    away,
    passed,
    landed,
    sends,
    receives,
    locals_,
):
    f32 = jnp.float32
    place = Place()
    mail = Mailbox(sends, receives, locals_)
    twin = place.twin()
    blocks = KEYS // BLOCK
    greet([place.after(step)[1] for step in range(1, FLEET)])
    gather_tok = SquareGather(place, tok, tok_all, mail.take(10), mail.local(), TOP_ROWS)
    first, second, mix_local = mix_spread(
        place, mix, mix_o, mail.take(SEQ), mail.take(SEQ), mail.local()
    )
    mix_local.start()
    for bits in range(SEQ - 1, SQUARE - 1, -1):
        first[bits - 1].start()
    gather_tok.start()
    for bits in range(SQUARE - 1, 0, -1):
        first[bits - 1].start()
    gain_local = pltpu.make_async_copy(gain, gains.at[place.rank], mail.local())
    gain_local.start()
    gain_copies = []
    boxes = mail.take(FLEET)
    for step in range(1, FLEET):
        rank, device = place.after(step)
        gain_copies.append(send(gain, gains.at[place.rank], boxes, step, device))
        gain_copies[-1].start()

    keeper = lax.div(place.seq, 2)
    spot = lax.rem(place.seq, 2)
    out_boxes, out_local, twin_boxes = mail.take(2), mail.local(), mail.take(2)

    def out_copy(number):
        remote = pltpu.make_async_remote_copy(
            src_ref=out,
            dst_ref=out_o.at[spot, place.fsdp],
            send_sem=out_boxes[0].at[number],
            recv_sem=out_boxes[1].at[spot],
            device_id=(number * SQUARE + keeper, place.fsdp),
            device_id_type=MESH,
        )
        local = pltpu.make_async_copy(out, out_o.at[spot, place.fsdp], out_local)
        return remote, local, number * SQUARE + keeper == place.seq

    def out_arrival(number):
        source = place.member * 2 + number
        arrival = pltpu.make_async_remote_copy(
            src_ref=out,
            dst_ref=out_o.at[number, place.fsdp],
            send_sem=out_boxes[0].at[number],
            recv_sem=out_boxes[1].at[number],
            device_id=(source, place.fsdp),
            device_id_type=MESH,
        )
        return arrival, source == place.seq

    for number in range(2):
        remote, local, mine = out_copy(number)
        pl.when(mine)(local.start)
        pl.when(jnp.logical_not(mine))(remote.start)

    segment, position = token_layout(lengths, place.fsdp, place.half * KEYS, KEYS)
    angle = frequency[...] * position.astype(f32)
    cos_o[...] = jnp.cos(angle)
    sin_o[...] = jnp.sin(angle)
    keep = (segment < lengths.shape[1]).astype(f32)
    marks = mark_rows(segment).astype(LOW)
    for head in range(2):
        query_o[head, HEAD_DIM:, :] = marks
    walls = wall_rows(segment)

    gather_tok.relay()
    mix_local.wait()
    second[0].start()
    for bits in range(SQUARE - 1, 0, -1):
        first[bits - 1].wait_recv()
        second[bits].start()
    gather_tok.share()
    for bits in range(SEQ - 1, SQUARE - 1, -1):
        first[bits - 1].wait_recv()
        second[bits].start()
    spread = WeightSpread(place, inn, down, in_o, down_o, mail)
    spread.down_local.start()
    spread.down_near.start()
    spread.down_far.start()
    spread.start_square()
    gain_local.wait()
    for copy in gain_copies:
        copy.wait()
    gain_o[...] = jnp.zeros_like(gain_o)
    for rank in range(FLEET):
        lane = rank * (D // FLEET) // 128 * 128
        gain_o[:, lane : lane + 256] += gains[rank].astype(f32)
    gather_tok.finish()
    for copy in second:
        copy.wait_recv()

    up_boxes = mail.take(blocks)
    up = [
        send(pair_o.at[blocks + number], pair_o.at[number], up_boxes, number, place.peer(SQUARE))
        for number in range(blocks)
    ]
    for number in range(blocks):
        columns = pl.ds(number * BLOCK, BLOCK)
        halves = []
        for block in (2 * number, 2 * number + 1):
            x = tok_all[block].astype(f32)
            scale = lax.rsqrt(jnp.mean(x * x, axis=-1, keepdims=True) + EPS_NORM)
            low = (x * scale * gain_o[0:1, :D]).astype(LOW)
            normed_o[block] = low
            halves.append(dot32(low, mix_o[...].reshape(D, 4 * HEAD_DIM)).T)
        projected = jnp.concatenate(halves, axis=1)
        cosine, sine = cos_o[:, columns], sin_o[:, columns]
        for head in range(2):
            turned = turn_head(projected[head * HEAD_DIM : (head + 1) * HEAD_DIM], cosine, sine)
            query_o[head, :HEAD_DIM, columns] = turned.astype(LOW)
        key = turn_head(projected[2 * HEAD_DIM : 3 * HEAD_DIM], cosine, sine).astype(LOW)
        value = projected[3 * HEAD_DIM :].astype(LOW)
        pair_o[blocks + number, :HEAD_DIM] = key
        pair_o[blocks + number, HEAD_DIM:] = value
        pl.when(place.half == 0)(up[number].start)
        rows = pl.ds(KEYS + number * BLOCK, BLOCK)
        wall = walls[:, number * BLOCK : (number + 1) * BLOCK]
        keys_o[rows, :] = jnp.concatenate([key.astype(f32), wall], axis=0).T.astype(LOW)
        values_o[rows, :] = value.astype(f32).T.astype(LOW)

    def queries_of(number):
        columns = pl.ds(number * BLOCK, BLOCK)
        return jnp.concatenate([query_o[0, :, columns], query_o[1, :, columns]], axis=1)

    def fold(queries, spot, carry, diagonal=False):
        score = dot32(keys_o[block_of(spot), :], queries)
        if diagonal:
            score = jnp.where(later(2 * BLOCK), -WALL, score)
        top = jnp.max(score, axis=0, keepdims=True)
        if carry is not None:
            top = jnp.maximum(carry[0], top)
        weight = jnp.exp2((score - top) * SCALE2)
        total = jnp.sum(weight, axis=0, keepdims=True)
        mixed = dot32(pair_o[spot, HEAD_DIM:], weight.astype(LOW))
        if carry is not None:
            fade = jnp.exp2((carry[0] - top) * SCALE2)
            total = total + carry[1] * fade
            mixed = mixed + carry[2] * fade
        return (top, total, mixed)

    for number in range(blocks):
        queries = queries_of(number)
        carry = fold(queries, blocks + number, None, diagonal=True)
        carry = lax.fori_loop(
            blocks, blocks + number, functools.partial(fold, queries), carry
        )
        top_s[number : number + 1, :], sum_s[number : number + 1, :] = carry[:2]
        mixed_s[number] = carry[2]

    spread.square_done()
    spread.near.start()
    for number in range(2):
        remote, local, mine = out_copy(number)
        pl.when(mine)(local.wait)
        pl.when(jnp.logical_not(mine))(remote.wait_send)
    passing = []
    for number in range(2):
        arrival, mine = out_arrival(number)
        pl.when(jnp.logical_not(mine))(arrival.wait_recv)
        block = out_o.at[number, place.fsdp]
        passing.append(send(block, block, twin_boxes, number, twin))
        passing[-1].start()
    spread.down_far.wait_recv()
    spread.down_passed.start()

    @pl.when(place.half == 1)
    def _():
        other_segment, _ = token_layout(lengths, place.fsdp, 0, KEYS)
        other_walls = wall_rows(other_segment)
        for number in range(blocks):
            up[number].wait_recv()
            rows = pl.ds(number * BLOCK, BLOCK)
            wall = other_walls[:, number * BLOCK : (number + 1) * BLOCK]
            keys_o[rows, :] = (
                jnp.concatenate([pair_o[number, :HEAD_DIM].astype(f32), wall], axis=0)
                .T.astype(LOW)
            )
            values_o[rows, :] = pair_o[number, HEAD_DIM:].astype(f32).T.astype(LOW)

    @pl.when(place.half == 0)
    def _():
        for number in range(blocks):
            up[number].wait_send()
            pair_o[number] = jnp.zeros_like(pair_o[number])
        keys_o[pl.ds(0, KEYS), :] = jnp.zeros((KEYS, 128), LOW)
        values_o[pl.ds(0, KEYS), :] = jnp.zeros((KEYS, HEAD_DIM), LOW)

    for copy in spread.far:
        copy.start()
    for number in range(blocks):
        columns = pl.ds(number * BLOCK, BLOCK)
        carry = (top_s[number : number + 1, :], sum_s[number : number + 1, :], mixed_s[number])
        carry = lax.fori_loop(
            0,
            jnp.where(place.half == 1, blocks, 0),
            functools.partial(fold, queries_of(number)),
            carry,
        )
        top, total, mixed = carry
        mixed = mixed * (1.0 / total)
        level = top * SCALE2 + jnp.log2(total)
        for head in range(2):
            side = slice(head * BLOCK, (head + 1) * BLOCK)
            rows = pl.ds(head * HEAD_DIM, HEAD_DIM)
            kept = mixed[:, side] * keep[:, number * BLOCK : (number + 1) * BLOCK]
            att_o[rows, columns] = kept
            att_low[rows, columns] = kept.astype(LOW)
            log_o[pl.ds(head, 1), columns] = level[:, side]

    for copy in passing:
        copy.wait_recv()
    scatter = SquareScatter(
        place, part, middle_o, (sib, away, passed, landed), mail.take(10), TOP_ROWS
    )

    def out_block(slot):
        columns = pl.ds(pl.multiple_of(slot * ROWS, ROWS), ROWS)
        rows = att_low[:, columns].astype(f32).T.astype(LOW)
        part[slot] = dot32(rows, out_o[...].reshape(2 * HEAD_DIM, D)).astype(LOW)

    for number, bits in enumerate(scatter.order):
        out_block(place.slot(bits | CORE))
        scatter.cores[number].start()
    for bits in scatter.order:
        out_block(place.slot(bits))
    scatter.pair_up()
    spread.pass_on(0)
    scatter.relay()
    scatter.finish()
    middle = middle_o[...] + tok[...].astype(f32)
    middle_o[...] = middle
    scale = lax.rsqrt(jnp.mean(middle * middle, axis=-1, keepdims=True) + EPS_NORM)
    two[...] = (middle * scale * gain_o[1:2, :D]).astype(LOW)
    gather_two = SquareGather(place, two, two_o, mail.take(10), mail.local(), TOP_ROWS)
    gather_two.start()
    gather_cot = SquareGather(place, cot, cot_o, mail.take(10), mail.local(), TOP_ROWS)
    spread.pass_on(1)
    gather_two.relay()
    gather_cot.start()
    gather_two.share()
    spread.pass_on(2)
    gather_two.finish()
    gather_cot.relay()
    gather_cot.share()
    spread.pass_on(3)
    gather_cot.finish()
    spread.finish()
    for copy in first + second + passing:
        copy.wait_send()


def forward(lengths, frequency, tok, gain, mix, out, inn, down, cot):
    shape = jax.ShapeDtypeStruct
    f32 = jnp.float32
    share, unit = out.shape[0], down.shape[0]
    blocks = KEYS // BLOCK
    return pl.pallas_call(
        forward_kernel,
        out_shape=(
            shape((FLEET,) + mix.shape[1:], LOW),
            shape((2, 2) + out.shape, LOW),
            shape((2, SQUARE, 2) + inn.shape[1:], LOW),
            shape((2, 2) + down.shape, LOW),
            shape((16, D + 128), f32),
            shape((SQUARE, ROWS, D), LOW),
            shape((2, 128, KEYS), LOW),
            shape((2 * KEYS, 128), LOW),
            shape((2 * KEYS, HEAD_DIM), LOW),
            shape((2 * blocks, 2 * HEAD_DIM, BLOCK), LOW),
            shape((2 * HEAD_DIM, KEYS), f32),
            shape((2, KEYS), f32),
            shape((HEAD_DIM // 2, KEYS), f32),
            shape((HEAD_DIM // 2, KEYS), f32),
            shape((ROWS, D), f32),
            shape((SQUARE, ROWS, D), LOW),
            shape((SQUARE, ROWS, D), LOW),
        ),
        in_specs=[pl.BlockSpec(memory_space=pltpu.SMEM), VMEM, VMEM, VMEM] + [ANY] * 5,
        out_specs=(VMEM, VMEM, ANY, ANY) + (VMEM,) * 13,
        scratch_shapes=[
            pltpu.VMEM((SQUARE, ROWS, D), LOW),
            pltpu.VMEM((FLEET,) + gain.shape, LOW),
            pltpu.VMEM((8, 2 * BLOCK), f32),
            pltpu.VMEM((8, 2 * BLOCK), f32),
            pltpu.VMEM((blocks, HEAD_DIM, 2 * BLOCK), f32),
            pltpu.VMEM((2 * HEAD_DIM, KEYS), LOW),
            pltpu.VMEM((SQUARE, ROWS, D), LOW),
            pltpu.VMEM((ROWS, D), LOW),
        ]
        + SquareScatter.buffers(D)
        + [
            pltpu.SemaphoreType.DMA((160,)),
            pltpu.SemaphoreType.DMA((160,)),
            pltpu.SemaphoreType.DMA((16,)),
        ],
        compiler_params=pltpu.CompilerParams(
            collective_id=0, has_side_effects=True, vmem_limit_bytes=56 << 20
        ),
        name="forward",
    )(lengths, frequency, tok, gain, mix, out, inn, down, cot)


def norm_back(grad, values, gain):
    scale = lax.rsqrt(jnp.mean(values * values, axis=-1, keepdims=True) + EPS_NORM)
    unit = values * scale
    grad_gain = jnp.sum(grad * unit, axis=0, keepdims=True)
    grad_unit = grad * gain
    centre = jnp.mean(grad_unit * unit, axis=-1, keepdims=True)
    return grad_gain, scale * (grad_unit - unit * centre)


def add_blocks(target, left, right, count):
    for number in range(count):
        add_rows(target.at[number], left.at[number], right.at[number], 0, target.shape[1])


def square_sum(ref):
    value = ref[...].astype(jnp.float32)
    return jnp.sum(value * value)


def backward_kernel(
    lengths,
    tok,
    cot,
    middle,
    gain_far,
    mix_far,
    out_far,
    inn_far,
    down_far,
    normed_far,
    query_far,
    keys_far,
    values_far,
    pair_far,
    att_far,
    log_sum_far,
    cosine_far,
    sine_far,
    two_all_far,
    cot_all_far,
    hidden_o,
    tokens_o,
    mix_o,
    out_o,
    in_o,
    down_o,
    gain_o,
    total_o,
    gain,
    mix,
    out,
    inn,
    down,
    query,
    keys,
    values,
    pair,
    att,
    log_sum,
    cosine,
    sine,
    two_all,
    cot_all,
    part,
    hidden,
    gate_grad,
    gin,
    gin_x,
    gin_z,
    gdown,
    gdown_x,
    gdown_z,
    gout,
    gout_x,
    out_got,
    total,
    grad_mid,
    branch,
    branch_all,
    y_total,
    grad_t,
    query_c,
    grad_c,
    query_r,
    grad_r,
    level_s,
    shift_s,
    dq_s,
    back,
    back_in,
    gproj_t,
    gproj_r,
    gmix,
    crossed,
    staged,
    landed_mix,
    gain_v,
    gain_w,
    sums,
    mine_s,
    sib_a,
    away_a,
    passed_a,
    landed_a,
    sib_b,
    away_b,
    passed_b,
    landed_b,
    sends,
    receives,
    locals_,
):
    f32 = jnp.float32
    place = Place()
    half, fsdp, member = place.half, place.fsdp, place.member
    mail = Mailbox(sends, receives, locals_)
    twin, across = place.twin(), place.peer(SQUARE)
    blocks = KEYS // BLOCK
    rows_all = SQUARE * ROWS
    units = hidden.shape[1]
    loads = {}
    for name, src, dst in (
        ("inn", inn_far, inn),
        ("two_all", two_all_far, two_all),
        ("down", down_far, down),
        ("cot_all", cot_all_far, cot_all),
        ("gain", gain_far, gain),
        ("out", out_far, out),
        ("att", att_far, att),
        ("query", query_far, query),
        ("log_sum", log_sum_far, log_sum),
        ("keys", keys_far, keys),
        ("values", values_far, values),
        ("pair", pair_far, pair),
        ("cosine", cosine_far, cosine),
        ("sine", sine_far, sine),
        ("mix", mix_far, mix),
    ):
        loads[name] = pltpu.make_async_copy(src, dst, mail.local())
        loads[name].start()
    greet([place.after(step)[1] for step in range(1, FLEET)])
    buffers_a = (sib_a, away_a, passed_a, landed_a)
    buffers_b = (sib_b, away_b, passed_b, landed_b)

    scatter = SquareScatter(place, part, total, buffers_a, mail.take(10), TOP_ROWS)

    def feed_forward(chip):
        pair_of = pl.ds(chip * 2, 2)
        rows = pl.ds(pl.multiple_of(chip * 2 * ROWS, 2 * ROWS), 2 * ROWS)
        gate_up = dot32(two_all[pair_of].reshape(2 * ROWS, D), inn[...])
        gate, up = gate_up[:, :units], gate_up[:, units:]
        sigmoid = 1.0 / (1.0 + jnp.exp(-gate))
        silu = gate * sigmoid
        low = (silu * up).astype(LOW)
        hidden[rows, :] = low
        grad_hidden = dot32(cot_all[pair_of].reshape(2 * ROWS, D), down[...], ((1,), (1,)))
        grad_gate = grad_hidden * up * sigmoid * (1.0 + gate * (1.0 - sigmoid))
        grad_up = grad_hidden * silu
        low = jnp.concatenate([grad_gate, grad_up], axis=1).astype(LOW)
        gate_grad[rows, :] = low
        part[pair_of] = dot32(low, inn[...], ((1,), (1,))).astype(LOW).reshape(2, ROWS, D)

    for name in ("inn", "two_all", "down", "cot_all"):
        loads[name].wait()
    for number, bits in enumerate(scatter.order):
        feed_forward(lax.div(place.slot(bits), 2))
        scatter.cores[number].start()
        if number:
            scatter.pair_one(number - 1)
    scatter.pair_one(3)

    in_boxes, far_boxes = mail.take(4), mail.take(2)
    in_cross, in_far = {}, {}
    down_boxes, down_far_box = mail.take(2), mail.take(1)
    down_cross = {}
    width = SQUARE // 2

    def in_grads(away, number):
        which = 1 - half if away else half
        spot = pl.ds(number * width, width)
        lanes = pl.ds(pl.multiple_of((which * 2 + number) * (D // 4), 128), D // 4)
        left = two_all[:, :, lanes].reshape(rows_all, D // 4)
        grad = dot32(left, gate_grad[...], ((0,), (0,)))
        gin[which, spot] = grad.astype(LOW).reshape(width, 2, D // FLEET, 2 * units)
        copy = send(
            gin.at[which, spot, 1 - fsdp], gin_x.at[which, spot], in_boxes, away * 2 + number, twin
        )
        copy.start()
        in_cross[away, number] = copy

    def down_grads(away):
        which = 1 - half if away else half
        lanes = pl.ds(pl.multiple_of(which * (units // 2), 128), units // 2)
        left = hidden[:, lanes]
        right = cot_all[...].reshape(rows_all, D)
        grad = dot32(left, right, ((0,), (0,)))
        gdown[which] = grad.astype(LOW).reshape(2, units // 4, D)
        copy = send(gdown.at[which, 1 - fsdp], gdown_x.at[which], down_boxes, away, twin)
        copy.start()
        down_cross[away] = copy

    in_grads(1, 0)
    in_grads(1, 1)
    scatter.relay()
    down_grads(1)
    in_grads(0, 0)
    in_grads(0, 1)
    down_grads(0)
    scatter.finish()
    loads["gain"].wait()
    gain_v[...] = jnp.zeros_like(gain_v)
    gain_mlp, grad_norm = norm_back(total[...], middle[...], gain[1:2, :D])
    gain_v[1:2, :D] = gain_mlp
    grad_middle = cot[...].astype(f32) + grad_norm
    grad_mid[...] = grad_middle
    branch[...] = grad_middle.astype(LOW)
    gather = SquareGather(place, branch, branch_all, mail.take(10), mail.local(), TOP_ROWS)
    gather.start()

    def in_onward(number):
        spot = pl.ds(number * width, width)
        in_cross[1, number].wait_recv()
        mine = gin.at[1 - half, spot, fsdp]
        add_blocks(mine, mine, gin_x.at[1 - half, spot], width)
        in_far[number] = send(mine, gin_z.at[spot], far_boxes, number, across)
        in_far[number].start()

    in_onward(0)
    gather.relay()
    for number in range(SQUARE // 2):
        rows = pl.ds(number * 2 * ROWS, 2 * ROWS)
        y_rows = dot32(hidden[rows, :], down[...]).astype(LOW)
        part[pl.ds(number * 2, 2)] = y_rows.reshape(2, ROWS, D)
    in_onward(1)
    gather.share()
    for name in ("out", "att", "query", "log_sum", "keys", "values", "pair", "cosine", "sine"):
        loads[name].wait()
    loads["mix"].wait()

    segment, _ = token_layout(lengths, fsdp, half * KEYS, KEYS)
    keep = (segment < lengths.shape[1]).astype(f32)
    gather.finish()
    scatter_y = SquareScatter(place, part, y_total, buffers_a, mail.take(10), TOP_ROWS)
    scatter_y.start()
    branch_rows = branch_all[...].reshape(rows_all, D)
    grad_att = dot32(out[...].reshape(2 * HEAD_DIM, D), branch_rows, ((1,), (1,))) * keep
    grad_low = grad_att.astype(LOW)
    delta = grad_low.astype(f32) * att[...]
    for head in range(2):
        rows = slice(head * HEAD_DIM, (head + 1) * HEAD_DIM)
        grad_t[head] = grad_low[rows]
        shift = jnp.sum(delta[rows], axis=0, keepdims=True)
        for number in range(blocks):
            columns = pl.ds(number * BLOCK, BLOCK)
            side = pl.ds(head * BLOCK, BLOCK)
            query_c[number, :, side] = query[head, :, columns]
            grad_c[number, :, side] = grad_t[head, :, columns]
            query_r[number, side, :] = query[head, :, columns].astype(f32).T.astype(LOW)
            grad_r[number, side, :] = grad_t[head, :, columns].astype(f32).T.astype(LOW)
            level_s[number, :, side] = jnp.broadcast_to(
                log_sum[pl.ds(head, 1), columns], (8, BLOCK)
            )
            shift_s[number, :, side] = jnp.broadcast_to(
                shift[:, number * BLOCK : (number + 1) * BLOCK], (8, BLOCK)
            )
    scatter_y.pair_up()

    dq_s[...] = jnp.zeros_like(dq_s)

    def fold(spot, number, carry, diagonal=False):
        grad_key, grad_value = carry
        rows = block_of(spot)
        score = dot32(keys[rows, :], query_c[number])
        if diagonal:
            score = jnp.where(later(2 * BLOCK), -WALL, score)
        weight = jnp.exp2(score * SCALE2 - level_s[number, 0:1, :])
        grad_weight = dot32(values[rows, :], grad_c[number])
        grad_score = (weight * (grad_weight - shift_s[number, 0:1, :])).astype(LOW)
        dq_s[number] += dot32(pair[spot, :HEAD_DIM], grad_score)
        grad_key = grad_key + dot32(grad_score, query_r[number])
        grad_value = grad_value + dot32(weight.astype(LOW), grad_r[number])
        return grad_key, grad_value

    none = (jnp.zeros((BLOCK, 128), f32), jnp.zeros((BLOCK, HEAD_DIM), f32))
    back_boxes = mail.take(blocks)
    returns = [
        send(back.at[number], back_in.at[number], back_boxes, number, across)
        for number in range(blocks)
    ]

    @pl.when(half == 1)
    def _():
        for number in range(blocks):
            grad_key, grad_value = lax.fori_loop(
                0, blocks, functools.partial(fold, number), none
            )
            back[number, :HEAD_DIM] = grad_key.T[:HEAD_DIM].astype(LOW)
            back[number, HEAD_DIM:] = grad_value.T.astype(LOW)
            returns[number].start()

    scatter_y.relay()
    down_cross[1].wait_recv()
    down_mine = gdown.at[1 - half, fsdp]
    add_rows(down_mine, down_mine, gdown_x.at[1 - half], 0, units // 4)
    down_far = send(down_mine, gdown_z, down_far_box, 0, across)

    out_boxes, owner_boxes = mail.take(1), mail.take(2)
    out_local = mail.local()
    grad_out = dot32(att[...].astype(LOW), branch_all[...].reshape(rows_all, D))
    gout[...] = grad_out.astype(LOW).reshape(2, 2, D // FLEET, D)
    out_cross = send(gout.at[pl.ds(0, 2), 1 - fsdp], gout_x, out_boxes, 0, twin)
    out_cross.start()

    for number in range(blocks):
        carry = fold(blocks + number, number, none, diagonal=True)
        grad_key, grad_value = lax.fori_loop(
            number + 1, blocks, functools.partial(fold, blocks + number), carry
        )
        columns = pl.ds(number * BLOCK, BLOCK)
        gproj_t[pl.ds(2 * HEAD_DIM, HEAD_DIM), columns] = grad_key.T[:HEAD_DIM]
        gproj_t[pl.ds(3 * HEAD_DIM, HEAD_DIM), columns] = grad_value.T
    scatter_y.finish()
    normed_load = pltpu.make_async_copy(normed_far, part, mail.local())
    normed_load.start()
    hidden_o[...] = (middle[...] + y_total[...]).astype(LOW)

    square_boxes = mail.take(SQUARE)
    in_local = mail.local()
    in_square = []
    for number in range(2):
        spot = pl.ds(number * width, width)
        in_cross[0, number].wait_recv()
        mine = gin.at[half, spot, fsdp]
        add_blocks(mine, mine, gin_x.at[half, spot], width)

    @pl.when(half == 0)
    def _():
        for number in range(blocks):
            returns[number].wait_recv()
            columns = pl.ds(number * BLOCK, BLOCK)
            rows = pl.ds(2 * HEAD_DIM, 2 * HEAD_DIM)
            gproj_t[rows, columns] = gproj_t[rows, columns] + back_in[number].astype(f32)

    @pl.when(half == 1)
    def _():
        for number in range(blocks):
            returns[number].wait_send()

    down_far.start()
    factor = HEAD_DIM ** (-0.5)
    for number in range(blocks):
        columns = pl.ds(number * BLOCK, BLOCK)
        cos_b, sin_b = cosine[:, columns], -sine[:, columns]
        pieces = []
        for head in range(2):
            dq = dq_s[number, :, head * BLOCK : (head + 1) * BLOCK]
            pieces.append(turn_head(dq * factor, cos_b, sin_b))
        dk = gproj_t[pl.ds(2 * HEAD_DIM, HEAD_DIM), columns]
        pieces.append(turn_head(dk * factor, cos_b, sin_b))
        pieces.append(gproj_t[pl.ds(3 * HEAD_DIM, HEAD_DIM), columns])
        gproj_r[columns, :] = jnp.concatenate(pieces, axis=0).T.astype(LOW)

    cross_boxes, plane_boxes = mail.take(SEQ), mail.take(SEQ)
    share = D // FLEET
    normed_load.wait()
    for number in range(4):
        left = part[:, :, pl.ds(number * (D // 4), D // 4)].reshape(rows_all, D // 4)
        grad = dot32(left, gproj_r[...], ((0,), (0,)))
        gmix[pl.ds(number * 4, 4)] = grad.astype(LOW).reshape(4, 2, share, 4 * HEAD_DIM)
    order = list(range(SEQ - 1, -1, -1))
    cross = {}
    for bits in order:
        target = flip(place.seq, bits)
        cross[bits] = send(gmix.at[target, 1 - fsdp], crossed.at[target], cross_boxes, bits, twin)
        cross[bits].start()
    scatter_n = SquareScatter(place, part, total, buffers_b, mail.take(10), TOP_ROWS)
    for number, bits in enumerate(scatter_n.order):
        chip = lax.div(place.slot(bits), 2)
        rows = pl.ds(pl.multiple_of(chip * 2 * ROWS, 2 * ROWS), 2 * ROWS)
        grad = dot32(gproj_r[rows, :], mix[...].reshape(D, 4 * HEAD_DIM), ((1,), (1,)))
        part[pl.ds(chip * 2, 2)] = grad.astype(LOW).reshape(2, ROWS, D)
        scatter_n.cores[number].start()
    scatter_n.pair_up()

    def out_copy(number):
        owner = member * 2 + number
        remote = pltpu.make_async_remote_copy(
            src_ref=gout.at[number, fsdp],
            dst_ref=out_got.at[half],
            send_sem=owner_boxes[0].at[number],
            recv_sem=owner_boxes[1].at[half],
            device_id=(owner, fsdp),
            device_id_type=MESH,
        )
        local = pltpu.make_async_copy(gout.at[number, fsdp], out_got.at[half], out_local)
        return remote, local, owner == place.seq

    out_cross.wait_recv()
    for number in range(2):
        mine = gout.at[number, fsdp]
        add_rows(mine, mine, gout_x.at[number], 0, share)
        remote, local, own_block = out_copy(number)
        pl.when(own_block)(local.start)
        pl.when(jnp.logical_not(own_block))(remote.start)
    plane = {}
    for bits in order:
        target = flip(place.seq, bits)
        cross[bits].wait_recv()
        goal = staged.at[target] if bits else landed_mix.at[place.seq]
        add_rows(goal, gmix.at[target, fsdp], crossed.at[target], 0, share)
        if bits:
            plane[bits] = send(
                staged.at[target], landed_mix.at[place.seq], plane_boxes, bits, (target, fsdp)
            )
            plane[bits].start()
        if bits == SQUARE:
            scatter_n.relay()
    for number in range(2):
        spot = pl.ds(number * width, width)
        in_far[number].wait_recv()
        mine = gin.at[half, spot, fsdp]
        add_blocks(mine, mine, gin_z.at[spot], width)
    in_keep = pltpu.make_async_copy(gin.at[half, member, fsdp], in_o.at[member], in_local)
    in_keep.start()
    for bits in range(1, SQUARE):
        copy = send(
            gin.at[half, place.slot(bits), fsdp],
            in_o.at[member],
            square_boxes,
            bits,
            place.peer(bits),
        )
        copy.start()
        in_square.append(copy)
    down_cross[0].wait_recv()
    down_own = gdown.at[half, fsdp]
    add_rows(down_own, down_own, gdown_x.at[half], 0, units // 4)
    scatter_n.finish()
    gain_attn, grad_norm = norm_back(total[...], tok[...].astype(f32), gain[0:1, :D])
    gain_v[0:1, :D] = gain_attn
    tokens_o[...] = grad_mid[...] + grad_norm
    gain_boxes, sum_boxes = mail.take(FLEET), mail.take(FLEET)
    gain_copies = []
    for step in range(1, FLEET):
        rank, device = place.after(step)
        lane = pl.multiple_of(lax.div(rank * share, 128) * 128, 128)
        gain_copies.append(
            send(
                gain_v.at[:, pl.ds(lane, 256)], gain_w.at[place.rank], gain_boxes, step, device
            )
        )
        gain_copies[-1].start()
    lane = pl.multiple_of(lax.div(place.rank * share, 128) * 128, 128)
    gain_w[place.rank] = gain_v[:, pl.ds(lane, 256)]
    for bits in range(1, SEQ):
        plane[bits].wait_recv()
    for number in range(SQUARE):
        add_rows(mix_o.at[number], landed_mix.at[number], landed_mix.at[number + SQUARE], 0, share)
    for number in range(2):
        source = number * SQUARE + lax.div(place.seq, 2)
        arrival = pltpu.make_async_remote_copy(
            src_ref=gout.at[0, 0],
            dst_ref=out_got.at[number],
            send_sem=owner_boxes[0].at[number],
            recv_sem=owner_boxes[1].at[number],
            device_id=(source, fsdp),
            device_id_type=MESH,
        )
        pl.when(source != place.seq)(arrival.wait_recv)
        remote, local, own_block = out_copy(number)
        pl.when(own_block)(local.wait)
    add_rows(out_o, out_got.at[0], out_got.at[1], 0, share)
    down_far.wait_recv()
    add_rows(down_o, down_own, gdown_z, 0, units // 4)
    squares = square_sum(mix_o) + square_sum(out_o) + square_sum(down_o)
    in_keep.wait()
    for copy in in_square:
        copy.wait_recv()
    squares = squares + square_sum(in_o)
    for copy in gain_copies:
        copy.wait()
    window = gain_w[0]
    for rank in range(1, FLEET):
        window = window + gain_w[rank]
    gain_o[...] = window
    start = lax.rem(place.rank * share, 128)
    at = lax.broadcasted_iota(jnp.int32, window.shape, 1)
    window = jnp.where((at >= start) & (at < start + share), window, 0.0)
    squares = squares + jnp.sum(window * window)
    mine_s[...] = jnp.broadcast_to(squares, mine_s.shape)
    sums[place.rank] = mine_s[...]
    copies = []
    for step in range(1, FLEET):
        rank, device = place.after(step)
        copies.append(send(mine_s, sums.at[place.rank], sum_boxes, step, device))
        copies[-1].start()
    for copy in copies:
        copy.wait()
    result = sums[0]
    for rank in range(1, FLEET):
        result = result + sums[rank]
    total_o[...] = result
    for copy in list(in_cross.values()) + list(in_far.values()) + list(down_cross.values()):
        copy.wait_send()
    for copy in [down_far, out_cross] + in_square + list(cross.values()) + list(plane.values()):
        copy.wait_send()
    for number in range(2):
        remote, local, own_block = out_copy(number)
        pl.when(jnp.logical_not(own_block))(remote.wait_send)


def backward(arrays):
    shape = jax.ShapeDtypeStruct
    f32 = jnp.float32
    blocks = KEYS // BLOCK
    share, unit = D // FLEET, FF // FLEET
    low = lambda *size: pltpu.VMEM(size, LOW)
    full = lambda *size: pltpu.VMEM(size, f32)
    stage = low(SEQ, share, 4 * HEAD_DIM)
    return pl.pallas_call(
        backward_kernel,
        out_shape=(
            shape((ROWS, D), LOW),
            shape((ROWS, D), f32),
            shape((SQUARE, share, 4 * HEAD_DIM), f32),
            shape((share, D), f32),
            shape((SQUARE, share, 8 * unit), LOW),
            shape((unit, D), f32),
            shape((8, 256), f32),
            shape((8, 128), f32),
        ),
        in_specs=[pl.BlockSpec(memory_space=pltpu.SMEM)] + [VMEM] * 3 + [ANY] * (len(arrays) - 4),
        out_specs=(VMEM,) * 8,
        scratch_shapes=[pltpu.VMEM(a.shape, a.dtype) for i, a in enumerate(arrays) if i > 3 and i != 9]
        + [
            low(SQUARE, ROWS, D),
            low(KEYS, 4 * unit),
            low(KEYS, 8 * unit),
            low(2, SQUARE, 2, share, 8 * unit),
            low(2, SQUARE, share, 8 * unit),
            low(SQUARE, share, 8 * unit),
            low(2, 2, unit, D),
            low(2, unit, D),
            low(unit, D),
            low(2, 2, share, D),
            low(2, share, D),
            low(2, share, D),
            full(ROWS, D),
            full(ROWS, D),
            low(ROWS, D),
            low(SQUARE, ROWS, D),
            full(ROWS, D),
            low(2, HEAD_DIM, KEYS),
            low(blocks, 128, 2 * BLOCK),
            low(blocks, HEAD_DIM, 2 * BLOCK),
            low(blocks, 2 * BLOCK, 128),
            low(blocks, 2 * BLOCK, HEAD_DIM),
            full(blocks, 8, 2 * BLOCK),
            full(blocks, 8, 2 * BLOCK),
            full(blocks, HEAD_DIM, 2 * BLOCK),
            low(blocks, 2 * HEAD_DIM, BLOCK),
            low(blocks, 2 * HEAD_DIM, BLOCK),
            full(4 * HEAD_DIM, KEYS),
            low(KEYS, 4 * HEAD_DIM),
            low(SEQ, 2, share, 4 * HEAD_DIM),
            stage,
            stage,
            stage,
            full(8, D + 128),
            full(FLEET, 8, 256),
            full(FLEET, 8, 128),
            full(8, 128),
        ]
        + SquareScatter.buffers(D)
        + SquareScatter.buffers(D)
        + [
            pltpu.SemaphoreType.DMA((180,)),
            pltpu.SemaphoreType.DMA((180,)),
            pltpu.SemaphoreType.DMA((24,)),
        ],
        compiler_params=pltpu.CompilerParams(
            collective_id=1, has_side_effects=True, vmem_limit_bytes=62 << 20
        ),
        name="backward",
    )(*arrays)


def local_squares(
    tokens,
    cotangent,
    lengths,
    mix_weight,
    out_weight,
    in_weight,
    down_weight,
    norm_gains,
    mix_first,
    out_first,
    in_first,
    down_first,
    norm_first,
    mix_second,
    out_second,
    in_second,
    down_second,
    norm_second,
):
    f32 = jnp.float32
    fsdp = lax.axis_index("fsdp")
    seq = lax.axis_index("seq")
    frequency = ROPE_BASE ** (-jnp.arange(HEAD_DIM // 2, dtype=f32) * 2.0 / HEAD_DIM)

    wide = 2 * HEAD_DIM
    key_width = KV_HEADS * HEAD_DIM
    mix_low = mix_weight[0].astype(LOW)
    share = mix_low.shape[0]
    mix_blocks = jnp.concatenate(
        [
            mix_low[:, :D].reshape(share, SQUARE, wide),
            mix_low[:, D : D + key_width].reshape(share, SQUARE, HEAD_DIM),
            mix_low[:, D + key_width :].reshape(share, SQUARE, HEAD_DIM),
        ],
        axis=2,
    ).transpose(1, 0, 2)
    unit = FF // FLEET
    in_blocks = (
        in_weight[0]
        .astype(LOW)
        .reshape(share, 2, 2, SQUARE, 2 * unit)
        .transpose(3, 0, 1, 2, 4)
        .reshape(SQUARE, share, 8 * unit)
    )
    out_low = out_weight[0].astype(LOW)
    down_low = down_weight[0].astype(LOW)
    rank = seq * 2 + fsdp
    gain_block = lax.dynamic_update_slice(
        jnp.zeros((16, 256), LOW), norm_gains[0].astype(LOW), (0, rank * share % 128)
    )
    (
        mix_full,
        out_mine,
        in_mine,
        down_mine,
        gains,
        normed_low,
        query_t,
        keys_r,
        values_r,
        pairs,
        attended_t,
        log_sum,
        cosine,
        sine,
        middle,
        two_all,
        cot_all,
    ) = forward(
        lengths,
        frequency[:, None],
        tokens,
        gain_block,
        mix_blocks,
        out_low,
        in_blocks,
        down_low,
        cotangent,
    )
    hidden_out, grad_tokens, mix_got, out_got, in_got, down_got, gain_got, totals = backward(
        [
            lengths,
            tokens,
            cotangent,
            middle,
            gains,
            mix_full,
            out_mine,
            in_mine.reshape(D, 8 * unit),
            down_mine.reshape(4 * unit, D),
            normed_low,
            query_t,
            keys_r,
            values_r,
            pairs,
            attended_t,
            log_sum,
            cosine,
            sine,
            two_all,
            cot_all,
        ]
    )

    in_grad = (
        in_got.reshape(SQUARE, share, 2, 2, 2 * unit)
        .transpose(1, 2, 3, 0, 4)
        .reshape(1, share, 2 * FF)
        .astype(f32)
    )
    mix_got = mix_got.transpose(1, 0, 2)
    mix_grad = jnp.concatenate(
        [
            mix_got[:, :, :wide].reshape(share, D),
            mix_got[:, :, wide : wide + HEAD_DIM].reshape(share, key_width),
            mix_got[:, :, wide + HEAD_DIM :].reshape(share, key_width),
        ],
        axis=1,
    )[None]
    out_grad = out_got[None]
    down_grad = down_got[None]
    norm_grad = lax.dynamic_slice(gain_got[:2], (0, rank * share % 128), (2, share))[None]
    grad_norm = jnp.sqrt(totals[0, 0])
    clip_scale = CLIP_NORM / jnp.maximum(grad_norm, CLIP_NORM)
    results = [hidden_out, grad_tokens, grad_norm]
    for weight, first, second, grad, rate in (
        (mix_weight, mix_first, mix_second, mix_grad, LEARN_RATE),
        (out_weight, out_first, out_second, out_grad, OUT_RATE),
        (in_weight, in_first, in_second, in_grad, LEARN_RATE),
        (down_weight, down_first, down_second, down_grad, LEARN_RATE),
        (norm_gains, norm_first, norm_second, norm_grad, GAIN_RATE),
    ):
        new, moment, square = adam_update(weight, first, second, grad, clip_scale, rate)
        results += [grad, new, moment, square, new.astype(LOW)]
    return tuple(results)


def solution(mesh):
    squares = mesh.shape["seq"] == SEQ and mesh.shape["fsdp"] == 2
    return jax.shard_map(
        local_squares if squares else local,
        mesh=mesh,
        in_specs=(
            P(("seq", "fsdp"), None),
            P(("seq", "fsdp"), None),
            P(),
            P(None, ("seq", "fsdp"), None),
            P(None, ("seq", "fsdp"), None),
            P(None, ("seq", "fsdp"), None),
            P(None, ("seq", "fsdp"), None),
            P(None, None, ("seq", "fsdp")),
            P(None, ("seq", "fsdp"), None),
            P(None, ("seq", "fsdp"), None),
            P(None, ("seq", "fsdp"), None),
            P(None, ("seq", "fsdp"), None),
            P(None, None, ("seq", "fsdp")),
            P(None, ("seq", "fsdp"), None),
            P(None, ("seq", "fsdp"), None),
            P(None, ("seq", "fsdp"), None),
            P(None, ("seq", "fsdp"), None),
            P(None, None, ("seq", "fsdp")),
        ),
        out_specs=(
            P(("seq", "fsdp"), None),
            P(("seq", "fsdp"), None),
            P(),
            P(None, ("seq", "fsdp"), None),
            P(None, ("seq", "fsdp"), None),
            P(None, ("seq", "fsdp"), None),
            P(None, ("seq", "fsdp"), None),
            P(None, ("seq", "fsdp"), None),
            P(None, ("seq", "fsdp"), None),
            P(None, ("seq", "fsdp"), None),
            P(None, ("seq", "fsdp"), None),
            P(None, ("seq", "fsdp"), None),
            P(None, ("seq", "fsdp"), None),
            P(None, ("seq", "fsdp"), None),
            P(None, ("seq", "fsdp"), None),
            P(None, ("seq", "fsdp"), None),
            P(None, ("seq", "fsdp"), None),
            P(None, ("seq", "fsdp"), None),
            P(None, ("seq", "fsdp"), None),
            P(None, ("seq", "fsdp"), None),
            P(None, ("seq", "fsdp"), None),
            P(None, ("seq", "fsdp"), None),
            P(None, ("seq", "fsdp"), None),
            P(None, None, ("seq", "fsdp")),
            P(None, None, ("seq", "fsdp")),
            P(None, None, ("seq", "fsdp")),
            P(None, None, ("seq", "fsdp")),
            P(None, None, ("seq", "fsdp")),
        ),
        check_vma=False,
    )
```

```python
import functools

import jax
import jax.numpy as jnp
from jax import lax
from jax.experimental import pallas as pl
from jax.experimental.pallas import tpu as pltpu
from jax.sharding import PartitionSpec as P

D = 1536
HEADS = 16
KV_HEADS = 8
HEAD_DIM = 96
FF = 4096
LAYERS = 1
STEP_NUMBER = 10


EPS_NORM = 1e-05
ROPE_BASE = 100000.0
FLOOR_SCORE = -1e30
LEARN_RATE = 0.05
OUT_RATE = 0.2
GAIN_RATE = 2.0
BETA_ONE = 0.9
BETA_TWO = 0.99
EPS_ADAM = 1e-08
WEIGHT_DECAY = 0.1
CLIP_NORM = 1.0


def doc_layout(places, doc_lens):
    doc_ends = jnp.cumsum(doc_lens)
    passed = (places[:, None] >= doc_ends[None, :]).astype(jnp.int32)
    segment = jnp.sum(passed, axis=1)
    offset = jnp.sum(passed * doc_lens[None, :], axis=1)
    return (segment, places - offset)


def rotate(vectors, places, direction):
    half_dim = vectors.shape[-1] // 2
    inverse = ROPE_BASE ** (-jnp.arange(half_dim, dtype=jnp.float32) * 2.0 / vectors.shape[-1])
    angles = places.astype(jnp.float32)[:, None] * inverse[None, :]
    cosine = jnp.cos(angles)[:, None, :]
    sine_term = direction * jnp.sin(angles)[:, None, :]
    former = vectors[..., :half_dim]
    latter = vectors[..., half_dim:]
    return jnp.concatenate(
        [former * cosine - latter * sine_term, latter * cosine + former * sine_term], axis=-1
    )


def normalize(values, gain):
    scale_rows = lax.rsqrt(jnp.mean(values * values, axis=-1, keepdims=True) + EPS_NORM)
    unit_rows = values * scale_rows
    return (unit_rows * gain, unit_rows, scale_rows)


def norm_backward(grad_normed, unit_rows, scale_rows, gain):
    grad_gain = jnp.sum(grad_normed * unit_rows, axis=0)
    grad_unit = grad_normed * gain
    grad_values = scale_rows * (
        grad_unit - unit_rows * jnp.mean(grad_unit * unit_rows, axis=-1, keepdims=True)
    )
    return (grad_gain, grad_values)


def masked_scores(queries, key_block, first_key, query_places, query_segment, doc_lens):
    block_rows = key_block.shape[0]
    key_places = first_key + jnp.arange(block_rows, dtype=jnp.int32)
    key_segment, unused_places = doc_layout(key_places, doc_lens)
    allowed = (query_segment[:, None] == key_segment[None, :]) & (
        key_places[None, :] <= query_places[:, None]
    )
    key_heads = key_block.reshape(block_rows, KV_HEADS, HEAD_DIM)
    raw_scores = jnp.einsum(
        "qkgd,skd->qkgs", queries, key_heads, preferred_element_type=jnp.float32
    ) * HEAD_DIM ** (-0.5)
    return (jnp.where(allowed[:, None, None, :], raw_scores, FLOOR_SCORE), allowed)


def fold_block(carry, key_block, value_block, first_key, setting):
    queries, query_places, query_segment, doc_lens = setting
    running, totals, accumulated = carry
    block_rows = key_block.shape[0]
    scores, allowed = masked_scores(
        queries, key_block, first_key, query_places, query_segment, doc_lens
    )
    newest = jnp.maximum(running, jnp.max(scores, axis=-1))
    factor = jnp.exp(running - newest)
    weights = jnp.where(allowed[:, None, None, :], jnp.exp(scores - newest[..., None]), 0.0)
    totals = totals * factor + jnp.sum(weights, axis=-1)
    value_heads = value_block.reshape(block_rows, KV_HEADS, HEAD_DIM)
    accumulated = accumulated * factor[..., None] + jnp.einsum(
        "qkgs,skd->qkgd",
        weights.astype(jnp.bfloat16),
        value_heads,
        preferred_element_type=jnp.float32,
    )
    return (newest, totals, accumulated)


def fold_piece(carry, key_rows, value_rows, start, setting):
    total_rows = key_rows.shape[0]
    block_rows = 512

    def step(inner_state, number):
        first_key = start + number * block_rows
        key_block = lax.dynamic_slice_in_dim(key_rows, number * block_rows, block_rows, 0)
        value_block = lax.dynamic_slice_in_dim(value_rows, number * block_rows, block_rows, 0)
        state_out = fold_block(inner_state, key_block, value_block, first_key, setting)
        return (state_out, None)

    carry, unused_out = lax.scan(step, carry, jnp.arange(total_rows // block_rows, dtype=jnp.int32))
    return carry


def fetch_layer(mix_weight, out_weight, norm_gains, in_weight, down_weight, layer_index):
    mix_full, out_full, gain_full, in_full, down_full = (
        lax.all_gather(
            mix_weight[layer_index].astype(jnp.bfloat16), ("seq", "fsdp"), axis=0, tiled=True
        ),
        lax.all_gather(
            out_weight[layer_index].astype(jnp.bfloat16), ("seq", "fsdp"), axis=0, tiled=True
        ),
        lax.all_gather(
            norm_gains[layer_index].astype(jnp.bfloat16), ("seq", "fsdp"), axis=1, tiled=True
        ),
        lax.all_gather(
            in_weight[layer_index].astype(jnp.bfloat16), ("seq", "fsdp"), axis=0, tiled=True
        ),
        lax.all_gather(
            down_weight[layer_index].astype(jnp.bfloat16), ("seq", "fsdp"), axis=0, tiled=True
        ),
    )
    return ((mix_full, out_full, gain_full), (in_full, down_full))


def layer_forward(stream, attn_set, mlp_set, context):
    query_places, query_segment, positions, keep_rows, doc_lens = context
    mix_full, out_full, gain_full = attn_set
    in_full, down_full = mlp_set
    row_count = stream.shape[0]
    key_width = KV_HEADS * HEAD_DIM
    groups_per = HEADS // KV_HEADS
    gain_attn = gain_full[0].astype(jnp.float32)
    gain_mlp = gain_full[1].astype(jnp.float32)
    normed, unit_attn, scale_attn = normalize(stream, gain_attn)
    normed_low = normed.astype(jnp.bfloat16)
    projected = jnp.dot(normed_low, mix_full, preferred_element_type=jnp.float32)
    queries = (
        rotate(projected[:, :D].reshape(row_count, HEADS, HEAD_DIM), positions, 1.0)
        .astype(jnp.bfloat16)
        .reshape(row_count, KV_HEADS, groups_per, HEAD_DIM)
    )
    keys_low = (
        rotate(
            projected[:, D : D + key_width].reshape(row_count, KV_HEADS, HEAD_DIM), positions, 1.0
        )
        .astype(jnp.bfloat16)
        .reshape(row_count, key_width)
    )
    values_low = projected[:, D + key_width :].astype(jnp.bfloat16)
    setting = (queries, query_places, query_segment, doc_lens)
    key_all, value_all = (
        lax.all_gather(keys_low, "seq", axis=0, tiled=True),
        lax.all_gather(values_low, "seq", axis=0, tiled=True),
    )
    start_carry = (
        jnp.full((row_count, KV_HEADS, groups_per), FLOOR_SCORE, jnp.float32),
        jnp.zeros((row_count, KV_HEADS, groups_per), jnp.float32),
        jnp.zeros((row_count, KV_HEADS, groups_per, HEAD_DIM), jnp.float32),
    )
    running, totals, accumulated = fold_piece(start_carry, key_all, value_all, 0, setting)
    log_total = running + jnp.log(totals)
    attended = (accumulated / totals[..., None]).reshape(row_count, D) * keep_rows
    attended_low = attended.astype(jnp.bfloat16)
    middle = stream + jnp.dot(attended_low, out_full, preferred_element_type=jnp.float32)
    normed_two, unit_mlp, scale_mlp = normalize(middle, gain_mlp)
    normed_two_low = normed_two.astype(jnp.bfloat16)
    gate_up = jnp.dot(normed_two_low, in_full, preferred_element_type=jnp.float32)
    hidden_low = (jax.nn.silu(gate_up[:, :FF]) * gate_up[:, FF:]).astype(jnp.bfloat16)
    result = middle + jnp.dot(hidden_low, down_full, preferred_element_type=jnp.float32)
    kv_saved = (key_all, value_all)
    saved = (
        normed_low,
        unit_attn,
        scale_attn,
        queries,
        keys_low,
        values_low,
        log_total,
        attended,
        attended_low,
        unit_mlp,
        scale_mlp,
        normed_two_low,
        gate_up,
        hidden_low,
        kv_saved,
    )
    return (result, saved)


def layer_backward(grad_stream, saved, attn_set, mlp_set, context):
    query_places, query_segment, positions, keep_rows, doc_lens = context
    mix_full, out_full, gain_full = attn_set
    in_full, down_full = mlp_set
    (
        normed_low,
        unit_attn,
        scale_attn,
        queries,
        keys_low,
        values_low,
        log_total,
        attended,
        attended_low,
        unit_mlp,
        scale_mlp,
        normed_two_low,
        gate_up,
        hidden_low,
        kv_saved,
    ) = saved
    row_count = grad_stream.shape[0]
    key_width = KV_HEADS * HEAD_DIM
    groups_per = HEADS // KV_HEADS
    score_scale = HEAD_DIM ** (-0.5)
    gain_attn = gain_full[0].astype(jnp.float32)
    gain_mlp = gain_full[1].astype(jnp.float32)
    grad_branch = grad_stream.astype(jnp.bfloat16)
    grad_down = jnp.einsum("nf,nd->fd", hidden_low, grad_branch, preferred_element_type=jnp.float32)
    grad_hidden = jnp.einsum(
        "nd,fd->nf", grad_branch, down_full, preferred_element_type=jnp.float32
    )
    gate_part = gate_up[:, :FF]
    up_part = gate_up[:, FF:]
    sigmoid_gate = jax.nn.sigmoid(gate_part)
    grad_gate = grad_hidden * up_part * sigmoid_gate * (1.0 + gate_part * (1.0 - sigmoid_gate))
    grad_up = grad_hidden * gate_part * sigmoid_gate
    grad_gate_up = jnp.concatenate([grad_gate, grad_up], axis=1).astype(jnp.bfloat16)
    grad_in = jnp.einsum(
        "nd,nf->df", normed_two_low, grad_gate_up, preferred_element_type=jnp.float32
    )
    grad_normed_two = jnp.einsum(
        "nf,df->nd", grad_gate_up, in_full, preferred_element_type=jnp.float32
    )
    mlp_part = (
        lax.psum_scatter(grad_in, ("seq", "fsdp"), scatter_dimension=0, tiled=True),
        lax.psum_scatter(grad_down, ("seq", "fsdp"), scatter_dimension=0, tiled=True),
    )
    grad_gain_mlp, grad_middle_norm = norm_backward(grad_normed_two, unit_mlp, scale_mlp, gain_mlp)
    grad_middle = grad_stream + grad_middle_norm
    attn_branch = grad_middle.astype(jnp.bfloat16)
    grad_out = jnp.einsum(
        "nd,ne->de", attended_low, attn_branch, preferred_element_type=jnp.float32
    )
    grad_attended = (
        jnp.einsum("ne,de->nd", attn_branch, out_full, preferred_element_type=jnp.float32)
        * keep_rows
    )
    grad_heads = grad_attended.astype(jnp.bfloat16).reshape(
        row_count, KV_HEADS, groups_per, HEAD_DIM
    )
    row_delta = jnp.sum(
        grad_heads.astype(jnp.float32)
        * attended.reshape(row_count, KV_HEADS, groups_per, HEAD_DIM),
        axis=-1,
    )
    key_all, value_all = kv_saved
    total_keys = key_all.shape[0]
    block_rows = 512

    def back_step(grad_queries, number):
        first_key = number * block_rows
        key_block = lax.dynamic_slice_in_dim(key_all, first_key, block_rows, 0)
        value_block = lax.dynamic_slice_in_dim(value_all, first_key, block_rows, 0)
        scores, allowed = masked_scores(
            queries, key_block, first_key, query_places, query_segment, doc_lens
        )
        soft_weight = jnp.where(
            allowed[:, None, None, :], jnp.exp(scores - log_total[..., None]), 0.0
        )
        value_heads = value_block.reshape(block_rows, KV_HEADS, HEAD_DIM)
        key_heads = key_block.reshape(block_rows, KV_HEADS, HEAD_DIM)
        grad_weight = jnp.einsum(
            "qkgd,skd->qkgs", grad_heads, value_heads, preferred_element_type=jnp.float32
        )
        grad_score = (soft_weight * (grad_weight - row_delta[..., None])).astype(jnp.bfloat16)
        state_out = grad_queries + jnp.einsum(
            "qkgs,skd->qkgd", grad_score, key_heads, preferred_element_type=jnp.float32
        )
        grad_key = (
            jnp.einsum("qkgs,qkgd->skd", grad_score, queries, preferred_element_type=jnp.float32)
            * score_scale
        )
        grad_value = jnp.einsum(
            "qkgs,qkgd->skd",
            soft_weight.astype(jnp.bfloat16),
            grad_heads,
            preferred_element_type=jnp.float32,
        )
        return (
            state_out,
            jnp.concatenate(
                [
                    grad_key.reshape(block_rows, key_width),
                    grad_value.reshape(block_rows, key_width),
                ],
                axis=1,
            ),
        )

    start_grad = jnp.zeros((row_count, KV_HEADS, groups_per, HEAD_DIM), jnp.float32)
    grad_queries, pair_blocks = lax.scan(
        back_step, start_grad, jnp.arange(total_keys // block_rows, dtype=jnp.int32)
    )
    pair_terms = pair_blocks.reshape(total_keys, 2 * key_width)
    pair_sums = lax.psum_scatter(pair_terms, "seq", scatter_dimension=0, tiled=True)
    grad_rot_queries = rotate(
        (grad_queries * score_scale).reshape(row_count, HEADS, HEAD_DIM), positions, -1.0
    ).reshape(row_count, D)
    grad_rot_keys = rotate(
        pair_sums[:, :key_width].reshape(row_count, KV_HEADS, HEAD_DIM), positions, -1.0
    ).reshape(row_count, key_width)
    grad_projected = jnp.concatenate(
        [grad_rot_queries, grad_rot_keys, pair_sums[:, key_width:]], axis=1
    ).astype(jnp.bfloat16)
    grad_mix = jnp.einsum(
        "nd,nf->df", normed_low, grad_projected, preferred_element_type=jnp.float32
    )
    grad_normed = jnp.einsum(
        "nf,df->nd", grad_projected, mix_full, preferred_element_type=jnp.float32
    )
    grad_gain_attn, grad_input_norm = norm_backward(grad_normed, unit_attn, scale_attn, gain_attn)
    grad_gains = jnp.stack([grad_gain_attn, grad_gain_mlp])
    attn_part = (
        lax.psum_scatter(grad_mix, ("seq", "fsdp"), scatter_dimension=0, tiled=True),
        lax.psum_scatter(grad_out, ("seq", "fsdp"), scatter_dimension=0, tiled=True),
        lax.psum_scatter(grad_gains, ("seq", "fsdp"), scatter_dimension=1, tiled=True),
    )
    return (grad_middle + grad_input_norm, attn_part, mlp_part)


def adam_update(weight, first, second, grad, clip_scale, rate):
    clipped = grad * clip_scale
    first_new = BETA_ONE * first + (1.0 - BETA_ONE) * clipped
    second_new = BETA_TWO * second + (1.0 - BETA_TWO) * clipped * clipped
    first_hat = first_new / (1.0 - BETA_ONE**STEP_NUMBER)
    second_hat = second_new / (1.0 - BETA_TWO**STEP_NUMBER)
    updated = weight - rate * (
        first_hat / (jnp.sqrt(second_hat) + EPS_ADAM) + WEIGHT_DECAY * weight
    )
    return (updated, first_new, second_new)


def local(
    tokens,
    cotangent,
    lengths,
    mix_weight,
    out_weight,
    in_weight,
    down_weight,
    norm_gains,
    mix_first,
    out_first,
    in_first,
    down_first,
    norm_first,
    mix_second,
    out_second,
    in_second,
    down_second,
    norm_second,
):
    row_count = tokens.shape[0]
    group_index = lax.axis_index("fsdp")
    cycle_index = lax.axis_index("seq")
    doc_lens = lax.dynamic_index_in_dim(lengths, group_index, 0, keepdims=False)
    query_places = cycle_index * row_count + jnp.arange(row_count, dtype=jnp.int32)
    query_segment, positions = doc_layout(query_places, doc_lens)
    keep_rows = (query_segment < doc_lens.shape[0]).astype(jnp.float32)[:, None]
    context = (query_places, query_segment, positions, keep_rows, doc_lens)
    stream = tokens.astype(jnp.float32)
    layer_index = 0
    attn_set, mlp_set = fetch_layer(
        mix_weight, out_weight, norm_gains, in_weight, down_weight, layer_index
    )
    stream, saved = layer_forward(stream, attn_set, mlp_set, context)
    saved_list = [saved]
    weight_list = [(attn_set, mlp_set)]
    hidden_out = stream.astype(jnp.bfloat16)
    grad_stream = cotangent.astype(jnp.float32)
    attn_sums = [None] * LAYERS
    mlp_sums = [None] * LAYERS
    for layer_index in reversed(range(LAYERS)):
        attn_set, mlp_set = weight_list[layer_index]
        grad_stream, attn_part, mlp_part = layer_backward(
            grad_stream, saved_list[layer_index], attn_set, mlp_set, context
        )
        attn_sums[layer_index] = attn_part
        mlp_sums[layer_index] = mlp_part
    mix_grad = jnp.stack([attn_sums[0][0]])
    out_grad = jnp.stack([attn_sums[0][1]])
    norm_grad = jnp.stack([attn_sums[0][2]])
    in_grad = jnp.stack([mlp_sums[0][0]])
    down_grad = jnp.stack([mlp_sums[0][1]])
    squares = (
        jnp.sum(mix_grad * mix_grad)
        + jnp.sum(out_grad * out_grad)
        + jnp.sum(in_grad * in_grad)
        + jnp.sum(down_grad * down_grad)
        + jnp.sum(norm_grad * norm_grad)
    )
    total_squares = lax.psum(squares, ("seq", "fsdp"))
    grad_norm = jnp.sqrt(total_squares)
    clip_scale = CLIP_NORM / jnp.maximum(grad_norm, CLIP_NORM)
    mix_new, mix_moment, mix_square = adam_update(
        mix_weight, mix_first, mix_second, mix_grad, clip_scale, LEARN_RATE
    )
    out_new, out_moment, out_square = adam_update(
        out_weight, out_first, out_second, out_grad, clip_scale, OUT_RATE
    )
    in_new, in_moment, in_square = adam_update(
        in_weight, in_first, in_second, in_grad, clip_scale, LEARN_RATE
    )
    down_new, down_moment, down_square = adam_update(
        down_weight, down_first, down_second, down_grad, clip_scale, LEARN_RATE
    )
    norm_new, norm_moment, norm_square = adam_update(
        norm_gains, norm_first, norm_second, norm_grad, clip_scale, GAIN_RATE
    )
    return (
        hidden_out,
        grad_stream,
        grad_norm,
        mix_grad,
        mix_new,
        mix_moment,
        mix_square,
        mix_new.astype(jnp.bfloat16),
        out_grad,
        out_new,
        out_moment,
        out_square,
        out_new.astype(jnp.bfloat16),
        in_grad,
        in_new,
        in_moment,
        in_square,
        in_new.astype(jnp.bfloat16),
        down_grad,
        down_new,
        down_moment,
        down_square,
        down_new.astype(jnp.bfloat16),
        norm_grad,
        norm_new,
        norm_moment,
        norm_square,
        norm_new.astype(jnp.bfloat16),
    )


MESH = pl.DeviceIdType.MESH
ANY = pl.BlockSpec(memory_space=pl.ANY)
VMEM = pl.BlockSpec(memory_space=pltpu.VMEM)
LOW = jnp.bfloat16
SQUARE = 8
SEQ = 16
FLEET = 32
ROWS = 128
GATHER_TOP = 64
SCATTER_TOP = 64
DOC_KINDS = 6
KEYS = 1024
BLOCK = 256
CORE, NEAR_Y, NEAR_Z = 1, 2, 4
LOG2E = 1.4426950408889634
SCALE2 = HEAD_DIM ** (-0.5) * LOG2E
WALL = 2.0**100


def flip(value, bits):
    for bit in (1, 2, 4, 8):
        if bits & bit:
            value = value + bit - 2 * bit * (lax.rem(lax.div(value, bit), 2))
    return value


class Place:
    def __init__(self):
        self.seq = lax.axis_index("seq")
        self.fsdp = lax.axis_index("fsdp")
        self.member = lax.rem(self.seq, SQUARE)
        self.half = lax.div(self.seq, SQUARE)
        self.rank = self.seq * 2 + self.fsdp

    def peer(self, bits):
        return (flip(self.seq, bits), self.fsdp)

    def slot(self, bits):
        return flip(self.member, bits)

    def after(self, step):
        rank = lax.rem(self.rank + step, FLEET)
        return rank, (lax.div(rank, 2), lax.rem(rank, 2))

    def twin(self):
        return (self.seq, 1 - self.fsdp)


def send(src, dst, sems, index, device):
    return pltpu.make_async_remote_copy(
        src_ref=src,
        dst_ref=dst,
        send_sem=sems[0].at[index],
        recv_sem=sems[1].at[index],
        device_id=device,
        device_id_type=MESH,
    )


def greet(devices):
    barrier = pltpu.get_barrier_semaphore()
    for device in devices:
        pl.semaphore_signal(barrier, inc=1, device_id=device, device_id_type=MESH)
    pl.semaphore_wait(barrier, len(devices))


class SquareGather:
    COPIES = 10

    def __init__(self, place, src, out, sems, local_sem, top_rows):
        p, h = place, top_rows
        own, ys, zs = p.slot(0), p.slot(NEAR_Y), p.slot(NEAR_Z)
        ds = p.slot(NEAR_Y | NEAR_Z)
        to_y, to_z, to_c = p.peer(NEAR_Y), p.peer(NEAR_Z), p.peer(CORE)
        top, low = pl.ds(0, h), pl.ds(h, ROWS - h)
        self.local = pltpu.make_async_copy(src, out.at[own], local_sem)
        self.y0 = send(src.at[top], out.at[own, top], sems, 0, to_y)
        self.y1 = send(src.at[low], out.at[own, low], sems, 1, to_y)
        self.z1 = send(src.at[low], out.at[own, low], sems, 2, to_z)
        self.z0 = send(src.at[top], out.at[own, top], sems, 3, to_z)
        self.fz = send(out.at[ys, top], out.at[ys, top], sems, 4, to_z)
        self.fy = send(out.at[zs, low], out.at[zs, low], sems, 5, to_y)
        self.c = [
            send(src, out.at[own], sems, 6, to_c),
            send(out.at[ys], out.at[ys], sems, 7, to_c),
            send(out.at[zs], out.at[zs], sems, 8, to_c),
            send(out.at[ds], out.at[ds], sems, 9, to_c),
        ]

    def start(self):
        for copy in (self.y0, self.z1, self.y1, self.z0, self.c[0], self.local):
            copy.start()

    def relay(self):
        self.y0.wait_recv()
        self.fz.start()
        self.z1.wait_recv()
        self.fy.start()

    def share(self):
        self.y1.wait_recv()
        self.c[1].start()
        self.z0.wait_recv()
        self.c[2].start()

    def finish(self):
        self.fz.wait_recv()
        self.fy.wait_recv()
        self.c[3].start()
        for copy in self.c:
            copy.wait_recv()
        for copy in [self.y0, self.y1, self.z0, self.z1, self.fz, self.fy] + self.c:
            copy.wait_send()
        self.local.wait()


def mix_spread(place, mix, mix_o, plane_s, cross_s, local_sem):
    twin = (place.seq, 1 - place.fsdp)
    first = [
        send(
            mix.at[lax.rem(flip(place.seq, bits), SQUARE)],
            mix_o.at[place.rank],
            plane_s,
            bits,
            (flip(place.seq, bits), place.fsdp),
        )
        for bits in range(1, SEQ)
    ]
    second = []
    for bits in range(SEQ):
        spot = flip(place.seq, bits) * 2 + place.fsdp
        second.append(send(mix_o.at[spot], mix_o.at[spot], cross_s, bits, twin))
    local = pltpu.make_async_copy(mix.at[place.member], mix_o.at[place.rank], local_sem)
    return first, second, local


def add_rows(target, left, right, start, count):
    step = 16

    def body(number, _):
        rows = pl.ds(pl.multiple_of(start + number * step, step), step)
        target[rows] = (left[rows].astype(jnp.float32) + right[rows].astype(jnp.float32)).astype(
            target.dtype
        )
        return 0

    lax.fori_loop(0, count // step, body, 0)


class SquareScatter:
    def __init__(self, place, part, total, buffers, sems, top_rows):
        sib, away, passed, landed = buffers
        self.place, self.part, self.total = place, part, total
        self.sib, self.away, self.passed, self.landed = sib, away, passed, landed
        h = self.top_rows = top_rows
        top, low = pl.ds(0, h), pl.ds(h, ROWS - h)
        to_y, to_z, to_c = place.peer(NEAR_Y), place.peer(NEAR_Z), place.peer(CORE)
        self.order = (NEAR_Y | NEAR_Z, NEAR_Y, NEAR_Z, 0)
        self.cores = [
            send(part.at[place.slot(bits | CORE)], sib.at[number], sems, number, to_c)
            for number, bits in enumerate(self.order)
        ]
        self.d0 = send(away.at[0, top], passed.at[top], sems, 4, to_y)
        self.d1 = send(away.at[0, low], passed.at[low], sems, 5, to_z)
        self.y0 = send(away.at[1, top], landed.at[0, top], sems, 6, to_y)
        self.y1 = send(away.at[1, low], landed.at[0, low], sems, 7, to_y)
        self.z0 = send(away.at[2, top], landed.at[1, top], sems, 8, to_z)
        self.z1 = send(away.at[2, low], landed.at[1, low], sems, 9, to_z)

    @staticmethod
    def buffers(width):
        return [
            pltpu.VMEM((4, ROWS, width), LOW),
            pltpu.VMEM((3, ROWS, width), LOW),
            pltpu.VMEM((ROWS, width), LOW),
            pltpu.VMEM((2, ROWS, width), LOW),
        ]

    def start(self):
        for copy in self.cores:
            copy.start()

    def pair_one(self, number):
        self.cores[number].wait_recv()
        target = self.away.at[number] if number < 3 else self.total
        mine = self.part.at[self.place.slot(self.order[number])]
        add_rows(target, mine, self.sib.at[number], 0, ROWS)
        for copy in ((self.d0, self.d1), (self.y0,), (self.z1,), ())[number]:
            copy.start()

    def pair_up(self):
        for number in range(4):
            self.pair_one(number)

    def relay(self):
        h, rest = self.top_rows, ROWS - self.top_rows
        self.d0.wait_recv()
        add_rows(self.away.at[2], self.away.at[2], self.passed, 0, h)
        self.z0.start()
        self.d1.wait_recv()
        add_rows(self.away.at[1], self.away.at[1], self.passed, h, rest)
        self.y1.start()

    def finish(self):
        h, rest = self.top_rows, ROWS - self.top_rows
        total, landed = self.total, self.landed
        self.y0.wait_recv()
        add_rows(total, total, landed.at[0], 0, h)
        self.z1.wait_recv()
        add_rows(total, total, landed.at[1], h, rest)
        self.z0.wait_recv()
        add_rows(total, total, landed.at[1], 0, h)
        self.y1.wait_recv()
        add_rows(total, total, landed.at[0], h, rest)
        for copy in self.cores + [self.d0, self.d1, self.y0, self.y1, self.z0, self.z1]:
            copy.wait_send()


def dot32(left, right, dims=((1,), (0,))):
    return lax.dot_general(left, right, (dims, ((), ())), preferred_element_type=jnp.float32)


def block_of(number):
    return pl.ds(pl.multiple_of(number * BLOCK, BLOCK), BLOCK)


def later(number_of_columns):
    key_at = lax.broadcasted_iota(jnp.int32, (BLOCK, number_of_columns), 0)
    query_at = lax.rem(lax.broadcasted_iota(jnp.int32, (BLOCK, number_of_columns), 1), BLOCK)
    return key_at > query_at


class Mailbox:
    def __init__(self, sends, receives, locals_):
        self.sends, self.receives, self.locals_ = sends, receives, locals_
        self.taken, self.local_taken = 0, 0

    def take(self, count):
        start = self.taken
        self.taken += count
        spot = pl.ds(start, count)
        return (self.sends.at[spot], self.receives.at[spot])

    def local(self):
        self.local_taken += 1
        return self.locals_.at[self.local_taken - 1]


def token_layout(lengths, group, start, count):
    at = start + lax.broadcasted_iota(jnp.int32, (1, count), 1)
    segment = jnp.zeros((1, count), jnp.int32)
    offset = jnp.zeros((1, count), jnp.int32)
    end = jnp.int32(0)
    for number in range(lengths.shape[1]):
        length = lengths[group, number]
        end = end + length
        passed = (at >= end).astype(jnp.int32)
        segment = segment + passed
        offset = offset + passed * length
    return segment, at - offset


def wall_rows(segment):
    kind = lax.broadcasted_iota(jnp.int32, (32, segment.shape[1]), 0)
    return jnp.where((kind != segment) & (kind < DOC_KINDS), -WALL, 0.0)


def mark_rows(segment):
    kind = lax.broadcasted_iota(jnp.int32, (32, segment.shape[1]), 0)
    return jnp.where(kind == segment, 1.0, 0.0)


def turn_head(head, cosine, sine):
    former, latter = head[: HEAD_DIM // 2], head[HEAD_DIM // 2 :]
    return jnp.concatenate(
        [former * cosine - latter * sine, latter * cosine + former * sine], axis=0
    )


class WeightSpread:
    CHUNKS = 4

    def __init__(self, place, inn, down, in_o, down_o, mail):
        p = place
        twin, across = p.twin(), p.peer(SQUARE)
        self.square = [
            send(inn.at[p.slot(bits)], in_o.at[p.half, p.member, p.fsdp], box, 0, p.peer(bits))
            for bits in range(1, SQUARE)
            for box in (mail.take(1),)
        ]
        self.local = pltpu.make_async_copy(
            inn.at[p.member], in_o.at[p.half, p.member, p.fsdp], mail.local()
        )
        self.down_local = pltpu.make_async_copy(down, down_o.at[p.half, p.fsdp], mail.local())
        near = in_o.at[p.half, pl.ds(0, SQUARE), p.fsdp]
        self.near = send(near, near, mail.take(1), 0, twin)
        width = SQUARE // self.CHUNKS
        self.far, self.passed = [], []
        boxes, passed_boxes = mail.take(self.CHUNKS), mail.take(self.CHUNKS)
        for number in range(self.CHUNKS):
            rows = pl.ds(number * width, width)
            mine = in_o.at[p.half, rows, p.fsdp]
            other = in_o.at[1 - p.half, rows, p.fsdp]
            self.far.append(send(mine, mine, boxes, number, across))
            self.passed.append(send(other, other, passed_boxes, number, twin))
        boxes = mail.take(3)
        self.down_near = send(down, down_o.at[p.half, p.fsdp], boxes, 0, twin)
        self.down_far = send(down, down_o.at[p.half, p.fsdp], boxes, 1, across)
        other = down_o.at[1 - p.half, p.fsdp]
        self.down_passed = send(other, other, boxes, 2, twin)

    def start_square(self):
        for copy in self.square:
            copy.start()
        self.local.start()

    def square_done(self):
        for copy in self.square:
            copy.wait_recv()
        self.local.wait()

    def pass_on(self, number):
        self.far[number].wait_recv()
        self.passed[number].start()

    def arrived(self):
        for copy in self.passed + [self.near, self.down_near, self.down_passed]:
            copy.wait_recv()
        self.down_local.wait()

    def drain(self):
        for copy in self.square + self.far + self.passed:
            copy.wait_send()
        for copy in (self.near, self.down_far, self.down_near, self.down_passed):
            copy.wait_send()


def forward_part(place, mail, r):
    lengths, frequency, tok, gain, mix, out, inn, down, cot = (
        r.lengths, r.frequency, r.tok, r.gain_in, r.mix_in, r.out_in, r.inn_in, r.down_in, r.cot
    )
    mix_o, out_o, gain_o, pair_o, att_o = r.mix, r.out, r.gain, r.pair, r.att
    keys_o, values_o, cos_o, sin_o = r.keys, r.values, r.cosine, r.sine
    tok_all, gains, query_c, part, two = r.tok_all, r.gains, r.query_c, r.part, r.two
    top_s, sum_s, mixed_s, att_low, middle_o = r.top_s, r.sum_s, r.dq_s, r.att_low, r.middle
    f32 = jnp.float32
    twin = place.twin()
    blocks = KEYS // BLOCK
    greet([place.after(step)[1] for step in range(1, FLEET)])
    gather_tok = SquareGather(place, tok, tok_all, mail.take(10), mail.local(), GATHER_TOP)
    first, second, mix_local = mix_spread(
        place, mix, mix_o, mail.take(SEQ), mail.take(SEQ), mail.local()
    )
    mix_local.start()
    for bits in range(SEQ - 1, SQUARE - 1, -1):
        first[bits - 1].start()
    gather_tok.start()
    for bits in range(SQUARE - 1, 0, -1):
        first[bits - 1].start()
    gain_local = pltpu.make_async_copy(gain, gains.at[place.rank], mail.local())
    gain_local.start()
    gain_copies = []
    boxes = mail.take(FLEET)
    for step in range(1, FLEET):
        rank, device = place.after(step)
        gain_copies.append(send(gain, gains.at[place.rank], boxes, step, device))
        gain_copies[-1].start()

    keeper = lax.div(place.seq, 2)
    spot = lax.rem(place.seq, 2)
    out_boxes, out_local, twin_boxes = mail.take(2), mail.local(), mail.take(2)

    def out_copy(number):
        remote = pltpu.make_async_remote_copy(
            src_ref=out,
            dst_ref=out_o.at[spot, place.fsdp],
            send_sem=out_boxes[0].at[number],
            recv_sem=out_boxes[1].at[spot],
            device_id=(number * SQUARE + keeper, place.fsdp),
            device_id_type=MESH,
        )
        local = pltpu.make_async_copy(out, out_o.at[spot, place.fsdp], out_local)
        return remote, local, number * SQUARE + keeper == place.seq

    def out_arrival(number):
        source = place.member * 2 + number
        arrival = pltpu.make_async_remote_copy(
            src_ref=out,
            dst_ref=out_o.at[number, place.fsdp],
            send_sem=out_boxes[0].at[number],
            recv_sem=out_boxes[1].at[number],
            device_id=(source, place.fsdp),
            device_id_type=MESH,
        )
        return arrival, source == place.seq

    for number in range(2):
        remote, local, mine = out_copy(number)
        pl.when(mine)(local.start)
        pl.when(jnp.logical_not(mine))(remote.start)

    segment, position = token_layout(lengths, place.fsdp, place.half * KEYS, KEYS)
    angle = frequency[...] * position.astype(f32)
    cos_o[...] = jnp.cos(angle)
    sin_o[...] = jnp.sin(angle)
    keep = (segment < lengths.shape[1]).astype(f32)
    marks = mark_rows(segment).astype(LOW)
    for number in range(blocks):
        mark = marks[:, number * BLOCK : (number + 1) * BLOCK]
        query_c[number, HEAD_DIM:, :] = jnp.concatenate([mark, mark], axis=1)
    walls = wall_rows(segment)

    gather_tok.relay()
    mix_local.wait()
    second[0].start()
    for bits in range(SQUARE - 1, 0, -1):
        first[bits - 1].wait_recv()
        second[bits].start()
    gather_tok.share()
    for bits in range(SEQ - 1, SQUARE - 1, -1):
        first[bits - 1].wait_recv()
        second[bits].start()
    spread = WeightSpread(place, inn, down, r.inn, r.down, mail)
    spread.down_local.start()
    spread.start_square()
    gather_cot = SquareGather(place, cot, r.cot_all, mail.take(10), mail.local(), GATHER_TOP)
    gather_cot.start()
    gain_local.wait()
    for copy in gain_copies:
        copy.wait()
    gain_o[...] = jnp.zeros_like(gain_o)
    for rank in range(FLEET):
        lane = rank * (D // FLEET) // 128 * 128
        gain_o[:, lane : lane + 256] += gains[rank].astype(f32)
    gather_tok.finish()
    for copy in second:
        copy.wait_recv()

    up_boxes = mail.take(blocks)
    up = [
        send(pair_o.at[blocks + number], pair_o.at[number], up_boxes, number, place.peer(SQUARE))
        for number in range(blocks)
    ]
    for number in range(blocks):
        columns = pl.ds(number * BLOCK, BLOCK)
        halves = []
        for block in (2 * number, 2 * number + 1):
            x = tok_all[block].astype(f32)
            scale = lax.rsqrt(jnp.mean(x * x, axis=-1, keepdims=True) + EPS_NORM)
            low = (x * scale * gain_o[0:1, :D]).astype(LOW)
            tok_all[block] = low
            halves.append(dot32(low, mix_o[...].reshape(D, 4 * HEAD_DIM)).T)
        projected = jnp.concatenate(halves, axis=1)
        cosine, sine = cos_o[:, columns], sin_o[:, columns]
        for head in range(2):
            turned = turn_head(projected[head * HEAD_DIM : (head + 1) * HEAD_DIM], cosine, sine)
            side = pl.ds(head * BLOCK, BLOCK)
            query_c[number, :HEAD_DIM, side] = turned.astype(LOW)
        key = turn_head(projected[2 * HEAD_DIM : 3 * HEAD_DIM], cosine, sine).astype(LOW)
        value = projected[3 * HEAD_DIM :].astype(LOW)
        pair_o[blocks + number, :HEAD_DIM] = key
        pair_o[blocks + number, HEAD_DIM:] = value
        pl.when(place.half == 0)(up[number].start)
        rows = pl.ds(KEYS + number * BLOCK, BLOCK)
        wall = walls[:, number * BLOCK : (number + 1) * BLOCK]
        keys_o[rows, :] = jnp.concatenate([key.astype(f32), wall], axis=0).T.astype(LOW)
        values_o[rows, :] = value.astype(f32).T.astype(LOW)

    for number in range(2):
        remote, local, mine = out_copy(number)
        pl.when(mine)(local.wait)
        pl.when(jnp.logical_not(mine))(remote.wait_send)
    passing = []
    for number in range(2):
        arrival, mine = out_arrival(number)
        pl.when(jnp.logical_not(mine))(arrival.wait_recv)
        block = out_o.at[number, place.fsdp]
        passing.append(send(block, block, twin_boxes, number, twin))
        passing[-1].start()
    spread.square_done()
    spread.near.start()
    spread.down_near.start()
    for copy in spread.far:
        pl.when(place.half == 1)(copy.start)

    normed_out = pltpu.make_async_copy(tok_all, r.normed, mail.local())
    normed_out.start()
    gather_cot.relay()
    gather_cot.share()

    def fold(queries, spot, carry, diagonal=False):
        score = dot32(keys_o[block_of(spot), :], queries)
        if diagonal:
            score = jnp.where(later(2 * BLOCK), -WALL, score)
        top = jnp.max(score, axis=0, keepdims=True)
        if carry is not None:
            top = jnp.maximum(carry[0], top)
        weight = jnp.exp2((score - top) * SCALE2)
        total = jnp.sum(weight, axis=0, keepdims=True)
        mixed = dot32(pair_o[spot, HEAD_DIM:], weight.astype(LOW))
        if carry is not None:
            fade = jnp.exp2((carry[0] - top) * SCALE2)
            total = total + carry[1] * fade
            mixed = mixed + carry[2] * fade
        return (top, total, mixed)

    for number in range(blocks):
        queries = query_c[number]
        carry = fold(queries, blocks + number, None, diagonal=True)
        carry = lax.fori_loop(
            blocks, blocks + number, functools.partial(fold, queries), carry
        )
        top_s[number : number + 1, :], sum_s[number : number + 1, :] = carry[:2]
        mixed_s[number] = carry[2]

    spread.down_far.start()

    @pl.when(place.half == 1)
    def _():
        other_segment, _ = token_layout(lengths, place.fsdp, 0, KEYS)
        other_walls = wall_rows(other_segment)
        for number in range(blocks):
            up[number].wait_recv()
            rows = pl.ds(number * BLOCK, BLOCK)
            wall = other_walls[:, number * BLOCK : (number + 1) * BLOCK]
            keys_o[rows, :] = (
                jnp.concatenate([pair_o[number, :HEAD_DIM].astype(f32), wall], axis=0)
                .T.astype(LOW)
            )
            values_o[rows, :] = pair_o[number, HEAD_DIM:].astype(f32).T.astype(LOW)

    @pl.when(place.half == 0)
    def _():
        for number in range(blocks):
            up[number].wait_send()
            pair_o[number] = jnp.zeros_like(pair_o[number])
        keys_o[pl.ds(0, KEYS), :] = jnp.zeros((KEYS, 128), LOW)
        values_o[pl.ds(0, KEYS), :] = jnp.zeros((KEYS, HEAD_DIM), LOW)

    for copy in spread.far:
        pl.when(place.half == 0)(copy.start)
    for number in range(blocks):
        columns = pl.ds(number * BLOCK, BLOCK)
        carry = (top_s[number : number + 1, :], sum_s[number : number + 1, :], mixed_s[number])
        carry = lax.fori_loop(
            0,
            jnp.where(place.half == 1, blocks, 0),
            functools.partial(fold, query_c[number]),
            carry,
        )
        top, total, mixed = carry
        mixed = mixed * (1.0 / total)
        level = top * SCALE2 + jnp.log2(total)
        r.level_s[number] = jnp.broadcast_to(level, (8, 2 * BLOCK))
        for head in range(2):
            side = slice(head * BLOCK, (head + 1) * BLOCK)
            rows = pl.ds(head * HEAD_DIM, HEAD_DIM)
            kept = mixed[:, side] * keep[:, number * BLOCK : (number + 1) * BLOCK]
            att_o[rows, columns] = kept
            att_low[rows, columns] = kept.astype(LOW)

    for copy in passing:
        copy.wait_recv()
    normed_out.wait()
    scatter = SquareScatter(
        place, part, middle_o, r.buffers_a, mail.take(10), SCATTER_TOP
    )

    def out_block(slot):
        columns = pl.ds(pl.multiple_of(slot * ROWS, ROWS), ROWS)
        rows = att_low[:, columns].astype(f32).T.astype(LOW)
        part[slot] = dot32(rows, out_o[...].reshape(2 * HEAD_DIM, D)).astype(LOW)

    for number, bits in enumerate(scatter.order):
        out_block(place.slot(bits | CORE))
        scatter.cores[number].start()
    for bits in scatter.order:
        out_block(place.slot(bits))
    scatter.pair_up()
    spread.down_far.wait_recv()
    spread.down_passed.start()
    spread.pass_on(0)
    scatter.relay()
    scatter.finish()
    middle = middle_o[...] + tok[...].astype(f32)
    middle_o[...] = middle
    scale = lax.rsqrt(jnp.mean(middle * middle, axis=-1, keepdims=True) + EPS_NORM)
    two[...] = (middle * scale * gain_o[1:2, :D]).astype(LOW)
    gather_two = SquareGather(place, two, r.two_all, mail.take(10), mail.local(), GATHER_TOP)
    gather_two.start()
    spread.pass_on(1)
    gather_two.relay()
    gather_two.share()
    spread.pass_on(2)
    gather_two.finish()
    gather_cot.finish()
    spread.pass_on(3)
    spread.arrived()

    def drain():
        spread.drain()
        for copy in first + second + passing:
            copy.wait_send()

    return keep, drain


def norm_back(grad, values, gain):
    scale = lax.rsqrt(jnp.mean(values * values, axis=-1, keepdims=True) + EPS_NORM)
    unit = values * scale
    grad_gain = jnp.sum(grad * unit, axis=0, keepdims=True)
    grad_unit = grad * gain
    centre = jnp.mean(grad_unit * unit, axis=-1, keepdims=True)
    return grad_gain, scale * (grad_unit - unit * centre)


def add_blocks(target, left, right, count):
    for number in range(count):
        add_rows(target.at[number], left.at[number], right.at[number], 0, target.shape[1])


def square_sum(ref):
    value = ref[...].astype(jnp.float32)
    return jnp.sum(value * value)


def backward_part(place, mail, r, keep):
    tok, cot, middle, gain, mix, out = r.tok, r.cot, r.middle, r.gain, r.mix, r.out
    inn, down, keys, values, pair, att = r.inn, r.down, r.keys, r.values, r.pair, r.att
    cosine, sine, two_all, cot_all = r.cosine, r.sine, r.two_all, r.cot_all
    part, hidden, gate_grad, total, grad_mid = r.part, r.hidden, r.gate_grad, r.total, r.grad_mid
    gin, gin_x, gin_z, gdown, gdown_x, gdown_z = (
        r.gin, r.gin_x, r.gin_z, r.gdown, r.gdown_x, r.gdown_z
    )
    gout, gout_x, out_got, branch, branch_all = r.gout, r.gout_x, r.out_got, r.two, r.tok_all
    query_c, grad_c, query_r, grad_r = r.query_c, r.grad_c, r.query_r, r.grad_r
    level_s, shift_s, dq_s, back, back_in = r.level_s, r.shift_s, r.dq_s, r.back, r.back_in
    gproj_t, gproj_r, gmix, crossed = r.gproj_t, r.gproj_r, r.gmix, r.crossed
    landed_mix, gain_v, gain_w, sums, mine_s = r.landed_mix, r.gain_v, r.gain_w, r.sums, r.mine_s
    hidden_o, tokens_o, mix_o, out_o = r.hidden_o, r.tokens_o, r.mix_o, r.out_o
    in_o, down_o, gain_o, total_o = r.in_o, r.down_o, r.gain_o, r.total_o
    f32 = jnp.float32
    half, fsdp, member = place.half, place.fsdp, place.member
    twin, across = place.twin(), place.peer(SQUARE)
    blocks = KEYS // BLOCK
    rows_all = SQUARE * ROWS
    units = hidden.shape[1]
    buffers_a, buffers_b = r.buffers_a, r.buffers_b

    scatter = SquareScatter(place, part, total, buffers_a, mail.take(10), SCATTER_TOP)

    def feed_forward(chip):
        pair_of = pl.ds(chip * 2, 2)
        rows = pl.ds(pl.multiple_of(chip * 2 * ROWS, 2 * ROWS), 2 * ROWS)
        gate_up = dot32(two_all[pair_of].reshape(2 * ROWS, D), inn[...].reshape(D, 2 * units))
        gate, up = gate_up[:, :units], gate_up[:, units:]
        sigmoid = 1.0 / (1.0 + jnp.exp(-gate))
        silu = gate * sigmoid
        low = (silu * up).astype(LOW)
        hidden[rows, :] = low
        grad_hidden = dot32(cot_all[pair_of].reshape(2 * ROWS, D), down[...].reshape(units, D), ((1,), (1,)))
        grad_gate = grad_hidden * up * sigmoid * (1.0 + gate * (1.0 - sigmoid))
        grad_up = grad_hidden * silu
        low = jnp.concatenate([grad_gate, grad_up], axis=1).astype(LOW)
        gate_grad[rows, :] = low
        part[pair_of] = dot32(low, inn[...].reshape(D, 2 * units), ((1,), (1,))).astype(LOW).reshape(2, ROWS, D)

    for number, bits in enumerate(scatter.order):
        feed_forward(lax.div(place.slot(bits), 2))
        scatter.cores[number].start()
        if number:
            scatter.pair_one(number - 1)
    scatter.pair_one(3)

    in_boxes, far_boxes = mail.take(4), mail.take(2)
    in_cross, in_far = {}, {}
    down_boxes, down_far_box = mail.take(2), mail.take(1)
    down_cross = {}
    width = SQUARE // 2

    def in_grads(away, number):
        which = 1 - half if away else half
        spot = pl.ds(number * width, width)
        lanes = pl.ds(pl.multiple_of((which * 2 + number) * (D // 4), 128), D // 4)
        left = two_all[:, :, lanes].reshape(rows_all, D // 4)
        grad = dot32(left, gate_grad[...], ((0,), (0,)))
        gin[which, spot] = grad.astype(LOW).reshape(width, 2, D // FLEET, 2 * units)
        copy = send(
            gin.at[which, spot, 1 - fsdp], gin_x.at[which, spot], in_boxes, away * 2 + number, twin
        )
        copy.start()
        in_cross[away, number] = copy

    def down_grads(away):
        which = 1 - half if away else half
        lanes = pl.ds(pl.multiple_of(which * (units // 2), 128), units // 2)
        left = hidden[:, lanes]
        right = cot_all[...].reshape(rows_all, D)
        grad = dot32(left, right, ((0,), (0,)))
        gdown[which] = grad.astype(LOW).reshape(2, units // 4, D)
        copy = send(gdown.at[which, 1 - fsdp], gdown_x.at[which], down_boxes, away, twin)
        copy.start()
        down_cross[away] = copy

    in_grads(1, 0)
    in_grads(1, 1)
    scatter.relay()
    down_grads(1)
    in_grads(0, 0)
    in_grads(0, 1)
    down_grads(0)
    scatter.finish()
    gain_v[...] = jnp.zeros_like(gain_v)
    gain_mlp, grad_norm = norm_back(total[...], middle[...], gain[1:2, :D])
    gain_v[1:2, :D] = gain_mlp
    grad_middle = cot[...].astype(f32) + grad_norm
    grad_mid[...] = grad_middle
    branch[...] = grad_middle.astype(LOW)
    gather = SquareGather(place, branch, branch_all, mail.take(10), mail.local(), GATHER_TOP)
    gather.start()

    def in_onward(number):
        spot = pl.ds(number * width, width)
        in_cross[1, number].wait_recv()
        mine = gin.at[1 - half, spot, fsdp]
        add_blocks(mine, mine, gin_x.at[1 - half, spot], width)
        in_far[number] = send(mine, gin_z.at[spot], far_boxes, number, across)
        in_far[number].start()

    in_onward(0)
    gather.relay()
    for number in range(SQUARE // 2):
        rows = pl.ds(number * 2 * ROWS, 2 * ROWS)
        y_rows = dot32(hidden[rows, :], down[...].reshape(units, D)).astype(LOW)
        part[pl.ds(number * 2, 2)] = y_rows.reshape(2, ROWS, D)
    in_onward(1)
    gather.share()

    gather.finish()
    scatter_y = SquareScatter(place, part, total, buffers_a, mail.take(10), SCATTER_TOP)
    scatter_y.start()
    branch_rows = branch_all[...].reshape(rows_all, D)
    grad_att = dot32(out[...].reshape(2 * HEAD_DIM, D), branch_rows, ((1,), (1,))) * keep
    grad_low = grad_att.astype(LOW)
    delta = grad_low.astype(f32) * att[...]
    for head in range(2):
        rows = slice(head * HEAD_DIM, (head + 1) * HEAD_DIM)
        grad_head = grad_low[rows]
        shift = jnp.sum(delta[rows], axis=0, keepdims=True)
        for number in range(blocks):
            side = pl.ds(head * BLOCK, BLOCK)
            grad_block = grad_head[:, number * BLOCK : (number + 1) * BLOCK]
            grad_c[number, :, side] = grad_block
            query_r[number, side, :] = query_c[number, :, side].astype(f32).T.astype(LOW)
            grad_r[number, side, :] = grad_block.astype(f32).T.astype(LOW)
            shift_s[number, :, side] = jnp.broadcast_to(
                shift[:, number * BLOCK : (number + 1) * BLOCK], (8, BLOCK)
            )
    scatter_y.pair_up()

    dq_s[...] = jnp.zeros_like(dq_s)

    def fold(spot, number, carry, diagonal=False):
        grad_key, grad_value = carry
        rows = block_of(spot)
        score = dot32(keys[rows, :], query_c[number])
        if diagonal:
            score = jnp.where(later(2 * BLOCK), -WALL, score)
        weight = jnp.exp2(score * SCALE2 - level_s[number, 0:1, :])
        grad_weight = dot32(values[rows, :], grad_c[number])
        grad_score = (weight * (grad_weight - shift_s[number, 0:1, :])).astype(LOW)
        dq_s[number] += dot32(pair[spot, :HEAD_DIM], grad_score)
        grad_key = grad_key + dot32(grad_score, query_r[number])
        grad_value = grad_value + dot32(weight.astype(LOW), grad_r[number])
        return grad_key, grad_value

    none = (jnp.zeros((BLOCK, 128), f32), jnp.zeros((BLOCK, HEAD_DIM), f32))
    back_boxes = mail.take(blocks)
    returns = [
        send(back.at[number], back_in.at[number], back_boxes, number, across)
        for number in range(blocks)
    ]

    @pl.when(half == 1)
    def _():
        for number in range(blocks):
            grad_key, grad_value = lax.fori_loop(
                0, blocks, functools.partial(fold, number), none
            )
            back[number, :HEAD_DIM] = grad_key.T[:HEAD_DIM].astype(LOW)
            back[number, HEAD_DIM:] = grad_value.T.astype(LOW)
            returns[number].start()

    scatter_y.relay()
    down_cross[1].wait_recv()
    down_mine = gdown.at[1 - half, fsdp]
    add_rows(down_mine, down_mine, gdown_x.at[1 - half], 0, units // 4)
    down_far = send(down_mine, gdown_z, down_far_box, 0, across)

    out_boxes, owner_boxes = mail.take(1), mail.take(2)
    out_local = mail.local()
    grad_out = dot32(r.att_low[...], branch_all[...].reshape(rows_all, D))
    gout[...] = grad_out.astype(LOW).reshape(2, 2, D // FLEET, D)
    out_cross = send(gout.at[pl.ds(0, 2), 1 - fsdp], gout_x, out_boxes, 0, twin)
    out_cross.start()

    for number in range(blocks):
        carry = fold(blocks + number, number, none, diagonal=True)
        grad_key, grad_value = lax.fori_loop(
            number + 1, blocks, functools.partial(fold, blocks + number), carry
        )
        columns = pl.ds(number * BLOCK, BLOCK)
        gproj_t[pl.ds(0, HEAD_DIM), columns] = grad_key.T[:HEAD_DIM]
        gproj_t[pl.ds(HEAD_DIM, HEAD_DIM), columns] = grad_value.T
    scatter_y.finish()
    normed_load = pltpu.make_async_copy(r.normed, part, mail.local())
    normed_load.start()
    hidden_o[...] = (middle[...] + total[...]).astype(LOW)

    square_boxes = mail.take(SQUARE)
    in_local = mail.local()
    in_square = []
    for number in range(2):
        spot = pl.ds(number * width, width)
        in_cross[0, number].wait_recv()
        mine = gin.at[half, spot, fsdp]
        add_blocks(mine, mine, gin_x.at[half, spot], width)

    @pl.when(half == 0)
    def _():
        for number in range(blocks):
            returns[number].wait_recv()
            columns = pl.ds(number * BLOCK, BLOCK)
            gproj_t[:, columns] = gproj_t[:, columns] + back_in[number].astype(f32)

    @pl.when(half == 1)
    def _():
        for number in range(blocks):
            returns[number].wait_send()

    down_far.start()
    factor = HEAD_DIM ** (-0.5)
    for number in range(blocks):
        columns = pl.ds(number * BLOCK, BLOCK)
        cos_b, sin_b = cosine[:, columns], -sine[:, columns]
        pieces = []
        for head in range(2):
            dq = dq_s[number, :, head * BLOCK : (head + 1) * BLOCK]
            pieces.append(turn_head(dq * factor, cos_b, sin_b))
        dk = gproj_t[pl.ds(0, HEAD_DIM), columns]
        pieces.append(turn_head(dk * factor, cos_b, sin_b))
        pieces.append(gproj_t[pl.ds(HEAD_DIM, HEAD_DIM), columns])
        gproj_r[columns, :] = jnp.concatenate(pieces, axis=0).T.astype(LOW)

    cross_boxes, plane_boxes = mail.take(SEQ), mail.take(SEQ)
    share = D // FLEET
    normed_load.wait()
    for number in range(4):
        left = part[:, :, pl.ds(number * (D // 4), D // 4)].reshape(rows_all, D // 4)
        grad = dot32(left, gproj_r[...], ((0,), (0,)))
        gmix[pl.ds(number * 4, 4)] = grad.astype(LOW).reshape(4, 2, share, 4 * HEAD_DIM)
    order = list(range(SEQ - 1, -1, -1))
    cross = {}
    for bits in order:
        target = flip(place.seq, bits)
        cross[bits] = send(gmix.at[target, 1 - fsdp], crossed.at[target], cross_boxes, bits, twin)
        cross[bits].start()
    scatter_n = SquareScatter(place, part, total, buffers_b, mail.take(10), SCATTER_TOP)
    for number, bits in enumerate(scatter_n.order):
        chip = lax.div(place.slot(bits), 2)
        rows = pl.ds(pl.multiple_of(chip * 2 * ROWS, 2 * ROWS), 2 * ROWS)
        grad = dot32(gproj_r[rows, :], mix[...].reshape(D, 4 * HEAD_DIM), ((1,), (1,)))
        part[pl.ds(chip * 2, 2)] = grad.astype(LOW).reshape(2, ROWS, D)
        scatter_n.cores[number].start()
    scatter_n.pair_up()

    def out_copy(number):
        owner = member * 2 + number
        remote = pltpu.make_async_remote_copy(
            src_ref=gout.at[number, fsdp],
            dst_ref=out_got.at[half],
            send_sem=owner_boxes[0].at[number],
            recv_sem=owner_boxes[1].at[half],
            device_id=(owner, fsdp),
            device_id_type=MESH,
        )
        local = pltpu.make_async_copy(gout.at[number, fsdp], out_got.at[half], out_local)
        return remote, local, owner == place.seq

    out_cross.wait_recv()
    for number in range(2):
        mine = gout.at[number, fsdp]
        add_rows(mine, mine, gout_x.at[number], 0, share)
        remote, local, own_block = out_copy(number)
        pl.when(own_block)(local.start)
        pl.when(jnp.logical_not(own_block))(remote.start)
    plane = {}
    for bits in order:
        target = flip(place.seq, bits)
        cross[bits].wait_recv()
        mine = gmix.at[target, fsdp]
        goal = mine if bits else landed_mix.at[place.seq]
        add_rows(goal, mine, crossed.at[target], 0, share)
        if bits:
            plane[bits] = send(
                mine, landed_mix.at[place.seq], plane_boxes, bits, (target, fsdp)
            )
            plane[bits].start()
        if bits == SQUARE:
            scatter_n.relay()
    for number in range(2):
        spot = pl.ds(number * width, width)
        in_far[number].wait_recv()
        mine = gin.at[half, spot, fsdp]
        add_blocks(mine, mine, gin_z.at[spot], width)
    in_keep = pltpu.make_async_copy(gin.at[half, member, fsdp], in_o.at[member], in_local)
    in_keep.start()
    for bits in range(1, SQUARE):
        copy = send(
            gin.at[half, place.slot(bits), fsdp],
            in_o.at[member],
            square_boxes,
            bits,
            place.peer(bits),
        )
        copy.start()
        in_square.append(copy)
    down_cross[0].wait_recv()
    down_own = gdown.at[half, fsdp]
    add_rows(down_own, down_own, gdown_x.at[half], 0, units // 4)
    scatter_n.finish()
    gain_attn, grad_norm = norm_back(total[...], tok[...].astype(f32), gain[0:1, :D])
    gain_v[0:1, :D] = gain_attn
    tokens_o[...] = grad_mid[...] + grad_norm
    gain_boxes, sum_boxes = mail.take(FLEET), mail.take(FLEET)
    gain_copies = []
    for step in range(1, FLEET):
        rank, device = place.after(step)
        lane = pl.multiple_of(lax.div(rank * share, 128) * 128, 128)
        gain_copies.append(
            send(
                gain_v.at[:, pl.ds(lane, 256)], gain_w.at[place.rank], gain_boxes, step, device
            )
        )
        gain_copies[-1].start()
    lane = pl.multiple_of(lax.div(place.rank * share, 128) * 128, 128)
    gain_w[place.rank] = gain_v[:, pl.ds(lane, 256)]
    for bits in range(1, SEQ):
        plane[bits].wait_recv()
    wide, key_width = 2 * HEAD_DIM, KV_HEADS * HEAD_DIM
    sums_mix = [
        landed_mix[number].astype(f32) + landed_mix[number + SQUARE].astype(f32)
        for number in range(SQUARE)
    ]
    for number in range(SQUARE // 2):
        block = jnp.concatenate([v[:, :wide] for v in sums_mix[2 * number : 2 * number + 2]], 1)
        mix_o[:, number * 2 * wide : (number + 1) * 2 * wide] = block
    for kind in range(2):
        lanes = slice(wide + kind * HEAD_DIM, wide + (kind + 1) * HEAD_DIM)
        for number in range(SQUARE // 4):
            block = jnp.concatenate([v[:, lanes] for v in sums_mix[4 * number : 4 * number + 4]], 1)
            start = D + kind * key_width + number * 2 * wide
            mix_o[:, start : start + 2 * wide] = block
    for number in range(2):
        source = number * SQUARE + lax.div(place.seq, 2)
        arrival = pltpu.make_async_remote_copy(
            src_ref=gout.at[0, 0],
            dst_ref=out_got.at[number],
            send_sem=owner_boxes[0].at[number],
            recv_sem=owner_boxes[1].at[number],
            device_id=(source, fsdp),
            device_id_type=MESH,
        )
        pl.when(source != place.seq)(arrival.wait_recv)
        remote, local, own_block = out_copy(number)
        pl.when(own_block)(local.wait)
    add_rows(out_o, out_got.at[0], out_got.at[1], 0, share)
    down_far.wait_recv()
    add_rows(down_o, down_own, gdown_z, 0, units // 4)
    squares = square_sum(mix_o) + square_sum(out_o) + square_sum(down_o)
    in_keep.wait()
    for copy in in_square:
        copy.wait_recv()
    squares = squares + square_sum(in_o)
    for copy in gain_copies:
        copy.wait()
    window = gain_w[0]
    for rank in range(1, FLEET):
        window = window + gain_w[rank]
    gain_o[...] = window
    start = lax.rem(place.rank * share, 128)
    at = lax.broadcasted_iota(jnp.int32, window.shape, 1)
    window = jnp.where((at >= start) & (at < start + share), window, 0.0)
    squares = squares + jnp.sum(window * window)
    mine_s[...] = jnp.broadcast_to(squares, mine_s.shape)
    sums[place.rank] = mine_s[...]
    copies = []
    for step in range(1, FLEET):
        rank, device = place.after(step)
        copies.append(send(mine_s, sums.at[place.rank], sum_boxes, step, device))
        copies[-1].start()
    for copy in copies:
        copy.wait()
    result = sums[0]
    for rank in range(1, FLEET):
        result = result + sums[rank]
    total_o[...] = result
    for copy in list(in_cross.values()) + list(in_far.values()) + list(down_cross.values()):
        copy.wait_send()
    for copy in [down_far, out_cross] + in_square + list(cross.values()) + list(plane.values()):
        copy.wait_send()
    for number in range(2):
        remote, local, own_block = out_copy(number)
        pl.when(jnp.logical_not(own_block))(remote.wait_send)


class Refs:
    def __init__(self, **refs):
        self.__dict__.update(refs)


ARGUMENTS = [
    "lengths",
    "frequency",
    "tok",
    "gain_in",
    "mix_in",
    "out_in",
    "inn_in",
    "down_in",
    "cot",
]
RESULTS = [
    "hidden_o",
    "tokens_o",
    "mix_o",
    "out_o",
    "in_o",
    "down_o",
    "gain_o",
    "total_o",
    "normed",
]


def scratch_of():
    share, unit = D // FLEET, FF // FLEET
    blocks = KEYS // BLOCK
    low = lambda *size: pltpu.VMEM(size, LOW)
    full = lambda *size: pltpu.VMEM(size, jnp.float32)
    scratch = {
        "mix": low(FLEET, share, 4 * HEAD_DIM),
        "out": low(2, 2, share, D),
        "inn": low(2, SQUARE, 2, share, 8 * unit),
        "down": low(2, 2, unit, D),
        "gain": full(16, D + 128),
        "pair": low(2 * blocks, 2 * HEAD_DIM, BLOCK),
        "att": full(2 * HEAD_DIM, KEYS),
        "att_low": low(2 * HEAD_DIM, KEYS),
        "keys": low(2 * KEYS, 128),
        "values": low(2 * KEYS, HEAD_DIM),
        "cosine": full(HEAD_DIM // 2, KEYS),
        "sine": full(HEAD_DIM // 2, KEYS),
        "tok_all": low(SQUARE, ROWS, D),
        "two_all": low(SQUARE, ROWS, D),
        "cot_all": low(SQUARE, ROWS, D),
        "two": low(ROWS, D),
        "gains": low(FLEET, 16, 256),
        "query_c": low(blocks, 128, 2 * BLOCK),
        "query_r": low(blocks, 2 * BLOCK, 128),
        "grad_c": low(blocks, HEAD_DIM, 2 * BLOCK),
        "grad_r": low(blocks, 2 * BLOCK, HEAD_DIM),
        "level_s": full(blocks, 8, 2 * BLOCK),
        "shift_s": full(blocks, 8, 2 * BLOCK),
        "top_s": full(8, 2 * BLOCK),
        "sum_s": full(8, 2 * BLOCK),
        "dq_s": full(blocks, HEAD_DIM, 2 * BLOCK),
        "middle": full(ROWS, D),
        "total": full(ROWS, D),
        "grad_mid": full(ROWS, D),
        "part": low(SQUARE, ROWS, D),
        "hidden": low(KEYS, 4 * unit),
        "gate_grad": low(KEYS, 8 * unit),
        "gin": low(2, SQUARE, 2, share, 8 * unit),
        "gin_x": low(2, SQUARE, share, 8 * unit),
        "gin_z": low(SQUARE, share, 8 * unit),
        "gdown": low(2, 2, unit, D),
        "gdown_x": low(2, unit, D),
        "gdown_z": low(unit, D),
        "gout": low(2, 2, share, D),
        "gout_x": low(2, share, D),
        "out_got": low(2, share, D),
        "back": low(blocks, 2 * HEAD_DIM, BLOCK),
        "back_in": low(blocks, 2 * HEAD_DIM, BLOCK),
        "gproj_t": full(2 * HEAD_DIM, KEYS),
        "gproj_r": low(KEYS, 4 * HEAD_DIM),
        "gmix": low(SEQ, 2, share, 4 * HEAD_DIM),
        "crossed": low(SEQ, share, 4 * HEAD_DIM),
        "landed_mix": low(SEQ, share, 4 * HEAD_DIM),
        "gain_v": full(8, D + 128),
        "gain_w": full(FLEET, 8, 256),
        "sums": full(FLEET, 8, 128),
        "mine_s": full(8, 128),
        "sends": pltpu.SemaphoreType.DMA((360,)),
        "receives": pltpu.SemaphoreType.DMA((360,)),
        "locals": pltpu.SemaphoreType.DMA((24,)),
    }
    for set_name in "ab":
        for number, buffer in enumerate(SquareScatter.buffers(D)):
            scratch[set_name + str(number)] = buffer
    return scratch


def layer_kernel(names, *refs):
    r = Refs(**dict(zip(names, refs, strict=True)))
    r.buffers_a = (r.a0, r.a1, r.a2, r.a3)
    r.buffers_b = (r.b0, r.b1, r.b2, r.b3)
    place = Place()
    mail = Mailbox(r.sends, r.receives, r.locals)
    keep, drain = forward_part(place, mail, r)
    backward_part(place, mail, r, keep)
    drain()


def layer(*arrays):
    shape = jax.ShapeDtypeStruct
    f32 = jnp.float32
    share, unit = D // FLEET, FF // FLEET
    scratch = scratch_of()
    names = ARGUMENTS + RESULTS + list(scratch)
    return pl.pallas_call(
        functools.partial(layer_kernel, names),
        out_shape=(
            shape((ROWS, D), LOW),
            shape((ROWS, D), f32),
            shape((share, 8 * 4 * HEAD_DIM), f32),
            shape((share, D), f32),
            shape((SQUARE, share, 8 * unit), LOW),
            shape((unit, D), f32),
            shape((8, 256), f32),
            shape((8, 128), f32),
            shape((SQUARE, ROWS, D), LOW),
        ),
        in_specs=[pl.BlockSpec(memory_space=pltpu.SMEM)] + [VMEM] * 3 + [ANY] * 4 + [VMEM],
        out_specs=(VMEM,) * 8 + (ANY,),
        scratch_shapes=list(scratch.values()),
        compiler_params=pltpu.CompilerParams(
            collective_id=0, has_side_effects=True, vmem_limit_bytes=63 << 20
        ),
        name="layer",
    )(*arrays)


def adam_kernel(totals, *refs):
    scale = CLIP_NORM / jnp.maximum(jnp.sqrt(totals[0:1, 0:1]), CLIP_NORM)
    inputs, outputs = refs[:16], refs[16:]
    for kind, rate in enumerate((LEARN_RATE, OUT_RATE, LEARN_RATE, LEARN_RATE)):
        weight, first, second, grad = inputs[4 * kind : 4 * kind + 4]
        grad_o, new_o, first_o, second_o, copy_o = outputs[5 * kind : 5 * kind + 5]
        width = weight.shape[1] // SQUARE if grad.ndim == 3 else weight.shape[1]
        for number in range(weight.shape[1] // width):
            lanes = slice(number * width, (number + 1) * width)
            value = (grad[number] if grad.ndim == 3 else grad[...]).astype(jnp.float32)
            new, moment, square = adam_update(
                weight[:, lanes], first[:, lanes], second[:, lanes], value, scale, rate
            )
            grad_o[:, lanes] = value
            new_o[:, lanes] = new
            first_o[:, lanes] = moment
            second_o[:, lanes] = square
            copy_o[:, lanes] = new.astype(LOW)


def adam_all(totals, kinds):
    steps = 4
    shape = jax.ShapeDtypeStruct
    in_specs, out_specs, out_shapes = [pl.BlockSpec(totals.shape, lambda i: (0, 0))], [], []
    for weight, _, _, grad in kinds:
        spec = pl.BlockSpec((weight.shape[0], weight.shape[1] // steps), lambda i: (0, i))
        in_specs += [spec] * 3
        if grad.ndim == 3:
            block = (grad.shape[0], grad.shape[1], grad.shape[2] // steps)
            in_specs.append(pl.BlockSpec(block, lambda i: (0, 0, i)))
        else:
            in_specs.append(spec)
        out_specs += [spec] * 5
        out_shapes += [shape(weight.shape, jnp.float32)] * 4 + [shape(weight.shape, LOW)]
    return pl.pallas_call(
        adam_kernel,
        grid=(steps,),
        out_shape=out_shapes,
        in_specs=in_specs,
        out_specs=out_specs,
        compiler_params=pltpu.CompilerParams(vmem_limit_bytes=63 << 20),
        name="adam",
    )(totals, *[array for kind in kinds for array in kind])


def local_squares(
    tokens,
    cotangent,
    lengths,
    mix_weight,
    out_weight,
    in_weight,
    down_weight,
    norm_gains,
    mix_first,
    out_first,
    in_first,
    down_first,
    norm_first,
    mix_second,
    out_second,
    in_second,
    down_second,
    norm_second,
):
    f32 = jnp.float32
    fsdp = lax.axis_index("fsdp")
    seq = lax.axis_index("seq")
    frequency = ROPE_BASE ** (-jnp.arange(HEAD_DIM // 2, dtype=f32) * 2.0 / HEAD_DIM)

    wide = 2 * HEAD_DIM
    key_width = KV_HEADS * HEAD_DIM
    mix_low = mix_weight[0].astype(LOW)
    share = mix_low.shape[0]
    mix_blocks = jnp.concatenate(
        [
            mix_low[:, :D].reshape(share, SQUARE, wide),
            mix_low[:, D : D + key_width].reshape(share, SQUARE, HEAD_DIM),
            mix_low[:, D + key_width :].reshape(share, SQUARE, HEAD_DIM),
        ],
        axis=2,
    ).transpose(1, 0, 2)
    unit = FF // FLEET
    in_blocks = (
        in_weight[0]
        .astype(LOW)
        .reshape(share, 2, 2, SQUARE, 2 * unit)
        .transpose(3, 0, 1, 2, 4)
        .reshape(SQUARE, share, 8 * unit)
    )
    out_low = out_weight[0].astype(LOW)
    down_low = down_weight[0].astype(LOW)
    rank = seq * 2 + fsdp
    gain_block = lax.dynamic_update_slice(
        jnp.zeros((16, 256), LOW), norm_gains[0].astype(LOW), (0, rank * share % 128)
    )
    hidden_out, grad_tokens, mix_got, out_got, in_got, down_got, gain_got, totals, _ = layer(
        lengths,
        frequency[:, None],
        tokens,
        gain_block,
        mix_blocks,
        out_low,
        in_blocks,
        down_low,
        cotangent,
    )

    norm_grad = lax.dynamic_slice(gain_got[:2], (0, rank * share % 128), (2, share))[None]
    grad_norm = jnp.sqrt(totals[0, 0])
    clip_scale = CLIP_NORM / jnp.maximum(grad_norm, CLIP_NORM)
    updates = adam_all(
        totals,
        [
            (mix_weight[0], mix_first[0], mix_second[0], mix_got),
            (out_weight[0], out_first[0], out_second[0], out_got),
            (in_weight[0], in_first[0], in_second[0], in_got),
            (down_weight[0], down_first[0], down_second[0], down_got),
        ],
    )
    new, moment, square = adam_update(
        norm_gains, norm_first, norm_second, norm_grad, clip_scale, GAIN_RATE
    )
    results = [hidden_out, grad_tokens, grad_norm] + [array[None] for array in updates]
    return tuple(results + [norm_grad, new, moment, square, new.astype(LOW)])


def solution(mesh):
    squares = mesh.shape["seq"] == SEQ and mesh.shape["fsdp"] == 2
    return jax.shard_map(
        local_squares if squares else local,
        mesh=mesh,
        in_specs=(
            P(("seq", "fsdp"), None),
            P(("seq", "fsdp"), None),
            P(),
            P(None, ("seq", "fsdp"), None),
            P(None, ("seq", "fsdp"), None),
            P(None, ("seq", "fsdp"), None),
            P(None, ("seq", "fsdp"), None),
            P(None, None, ("seq", "fsdp")),
            P(None, ("seq", "fsdp"), None),
            P(None, ("seq", "fsdp"), None),
            P(None, ("seq", "fsdp"), None),
            P(None, ("seq", "fsdp"), None),
            P(None, None, ("seq", "fsdp")),
            P(None, ("seq", "fsdp"), None),
            P(None, ("seq", "fsdp"), None),
            P(None, ("seq", "fsdp"), None),
            P(None, ("seq", "fsdp"), None),
            P(None, None, ("seq", "fsdp")),
        ),
        out_specs=(
            P(("seq", "fsdp"), None),
            P(("seq", "fsdp"), None),
            P(),
            P(None, ("seq", "fsdp"), None),
            P(None, ("seq", "fsdp"), None),
            P(None, ("seq", "fsdp"), None),
            P(None, ("seq", "fsdp"), None),
            P(None, ("seq", "fsdp"), None),
            P(None, ("seq", "fsdp"), None),
            P(None, ("seq", "fsdp"), None),
            P(None, ("seq", "fsdp"), None),
            P(None, ("seq", "fsdp"), None),
            P(None, ("seq", "fsdp"), None),
            P(None, ("seq", "fsdp"), None),
            P(None, ("seq", "fsdp"), None),
            P(None, ("seq", "fsdp"), None),
            P(None, ("seq", "fsdp"), None),
            P(None, ("seq", "fsdp"), None),
            P(None, ("seq", "fsdp"), None),
            P(None, ("seq", "fsdp"), None),
            P(None, ("seq", "fsdp"), None),
            P(None, ("seq", "fsdp"), None),
            P(None, ("seq", "fsdp"), None),
            P(None, None, ("seq", "fsdp")),
            P(None, None, ("seq", "fsdp")),
            P(None, None, ("seq", "fsdp")),
            P(None, None, ("seq", "fsdp")),
            P(None, None, ("seq", "fsdp")),
        ),
        check_vma=False,
    )
```

```python
import functools

import jax
import jax.numpy as jnp
from jax import lax
from jax.experimental import pallas as pl
from jax.experimental.pallas import tpu as pltpu
from jax.sharding import PartitionSpec as P

D = 1536
HEADS = 16
KV_HEADS = 8
HEAD_DIM = 96
FF = 4096
LAYERS = 1
STEP_NUMBER = 10


EPS_NORM = 1e-05
ROPE_BASE = 100000.0
FLOOR_SCORE = -1e30
LEARN_RATE = 0.05
OUT_RATE = 0.2
GAIN_RATE = 2.0
BETA_ONE = 0.9
BETA_TWO = 0.99
EPS_ADAM = 1e-08
WEIGHT_DECAY = 0.1
CLIP_NORM = 1.0


def doc_layout(places, doc_lens):
    doc_ends = jnp.cumsum(doc_lens)
    passed = (places[:, None] >= doc_ends[None, :]).astype(jnp.int32)
    segment = jnp.sum(passed, axis=1)
    offset = jnp.sum(passed * doc_lens[None, :], axis=1)
    return (segment, places - offset)


def rotate(vectors, places, direction):
    half_dim = vectors.shape[-1] // 2
    inverse = ROPE_BASE ** (-jnp.arange(half_dim, dtype=jnp.float32) * 2.0 / vectors.shape[-1])
    angles = places.astype(jnp.float32)[:, None] * inverse[None, :]
    cosine = jnp.cos(angles)[:, None, :]
    sine_term = direction * jnp.sin(angles)[:, None, :]
    former = vectors[..., :half_dim]
    latter = vectors[..., half_dim:]
    return jnp.concatenate(
        [former * cosine - latter * sine_term, latter * cosine + former * sine_term], axis=-1
    )


def normalize(values, gain):
    scale_rows = lax.rsqrt(jnp.mean(values * values, axis=-1, keepdims=True) + EPS_NORM)
    unit_rows = values * scale_rows
    return (unit_rows * gain, unit_rows, scale_rows)


def norm_backward(grad_normed, unit_rows, scale_rows, gain):
    grad_gain = jnp.sum(grad_normed * unit_rows, axis=0)
    grad_unit = grad_normed * gain
    grad_values = scale_rows * (
        grad_unit - unit_rows * jnp.mean(grad_unit * unit_rows, axis=-1, keepdims=True)
    )
    return (grad_gain, grad_values)


def masked_scores(queries, key_block, first_key, query_places, query_segment, doc_lens):
    block_rows = key_block.shape[0]
    key_places = first_key + jnp.arange(block_rows, dtype=jnp.int32)
    key_segment, unused_places = doc_layout(key_places, doc_lens)
    allowed = (query_segment[:, None] == key_segment[None, :]) & (
        key_places[None, :] <= query_places[:, None]
    )
    key_heads = key_block.reshape(block_rows, KV_HEADS, HEAD_DIM)
    raw_scores = jnp.einsum(
        "qkgd,skd->qkgs", queries, key_heads, preferred_element_type=jnp.float32
    ) * HEAD_DIM ** (-0.5)
    return (jnp.where(allowed[:, None, None, :], raw_scores, FLOOR_SCORE), allowed)


def fold_block(carry, key_block, value_block, first_key, setting):
    queries, query_places, query_segment, doc_lens = setting
    running, totals, accumulated = carry
    block_rows = key_block.shape[0]
    scores, allowed = masked_scores(
        queries, key_block, first_key, query_places, query_segment, doc_lens
    )
    newest = jnp.maximum(running, jnp.max(scores, axis=-1))
    factor = jnp.exp(running - newest)
    weights = jnp.where(allowed[:, None, None, :], jnp.exp(scores - newest[..., None]), 0.0)
    totals = totals * factor + jnp.sum(weights, axis=-1)
    value_heads = value_block.reshape(block_rows, KV_HEADS, HEAD_DIM)
    accumulated = accumulated * factor[..., None] + jnp.einsum(
        "qkgs,skd->qkgd",
        weights.astype(jnp.bfloat16),
        value_heads,
        preferred_element_type=jnp.float32,
    )
    return (newest, totals, accumulated)


def fold_piece(carry, key_rows, value_rows, start, setting):
    total_rows = key_rows.shape[0]
    block_rows = 512

    def step(inner_state, number):
        first_key = start + number * block_rows
        key_block = lax.dynamic_slice_in_dim(key_rows, number * block_rows, block_rows, 0)
        value_block = lax.dynamic_slice_in_dim(value_rows, number * block_rows, block_rows, 0)
        state_out = fold_block(inner_state, key_block, value_block, first_key, setting)
        return (state_out, None)

    carry, unused_out = lax.scan(step, carry, jnp.arange(total_rows // block_rows, dtype=jnp.int32))
    return carry


def fetch_layer(mix_weight, out_weight, norm_gains, in_weight, down_weight, layer_index):
    mix_full, out_full, gain_full, in_full, down_full = (
        lax.all_gather(
            mix_weight[layer_index].astype(jnp.bfloat16), ("seq", "fsdp"), axis=0, tiled=True
        ),
        lax.all_gather(
            out_weight[layer_index].astype(jnp.bfloat16), ("seq", "fsdp"), axis=0, tiled=True
        ),
        lax.all_gather(
            norm_gains[layer_index].astype(jnp.bfloat16), ("seq", "fsdp"), axis=1, tiled=True
        ),
        lax.all_gather(
            in_weight[layer_index].astype(jnp.bfloat16), ("seq", "fsdp"), axis=0, tiled=True
        ),
        lax.all_gather(
            down_weight[layer_index].astype(jnp.bfloat16), ("seq", "fsdp"), axis=0, tiled=True
        ),
    )
    return ((mix_full, out_full, gain_full), (in_full, down_full))


def layer_forward(stream, attn_set, mlp_set, context):
    query_places, query_segment, positions, keep_rows, doc_lens = context
    mix_full, out_full, gain_full = attn_set
    in_full, down_full = mlp_set
    row_count = stream.shape[0]
    key_width = KV_HEADS * HEAD_DIM
    groups_per = HEADS // KV_HEADS
    gain_attn = gain_full[0].astype(jnp.float32)
    gain_mlp = gain_full[1].astype(jnp.float32)
    normed, unit_attn, scale_attn = normalize(stream, gain_attn)
    normed_low = normed.astype(jnp.bfloat16)
    projected = jnp.dot(normed_low, mix_full, preferred_element_type=jnp.float32)
    queries = (
        rotate(projected[:, :D].reshape(row_count, HEADS, HEAD_DIM), positions, 1.0)
        .astype(jnp.bfloat16)
        .reshape(row_count, KV_HEADS, groups_per, HEAD_DIM)
    )
    keys_low = (
        rotate(
            projected[:, D : D + key_width].reshape(row_count, KV_HEADS, HEAD_DIM), positions, 1.0
        )
        .astype(jnp.bfloat16)
        .reshape(row_count, key_width)
    )
    values_low = projected[:, D + key_width :].astype(jnp.bfloat16)
    setting = (queries, query_places, query_segment, doc_lens)
    key_all, value_all = (
        lax.all_gather(keys_low, "seq", axis=0, tiled=True),
        lax.all_gather(values_low, "seq", axis=0, tiled=True),
    )
    start_carry = (
        jnp.full((row_count, KV_HEADS, groups_per), FLOOR_SCORE, jnp.float32),
        jnp.zeros((row_count, KV_HEADS, groups_per), jnp.float32),
        jnp.zeros((row_count, KV_HEADS, groups_per, HEAD_DIM), jnp.float32),
    )
    running, totals, accumulated = fold_piece(start_carry, key_all, value_all, 0, setting)
    log_total = running + jnp.log(totals)
    attended = (accumulated / totals[..., None]).reshape(row_count, D) * keep_rows
    attended_low = attended.astype(jnp.bfloat16)
    middle = stream + jnp.dot(attended_low, out_full, preferred_element_type=jnp.float32)
    normed_two, unit_mlp, scale_mlp = normalize(middle, gain_mlp)
    normed_two_low = normed_two.astype(jnp.bfloat16)
    gate_up = jnp.dot(normed_two_low, in_full, preferred_element_type=jnp.float32)
    hidden_low = (jax.nn.silu(gate_up[:, :FF]) * gate_up[:, FF:]).astype(jnp.bfloat16)
    result = middle + jnp.dot(hidden_low, down_full, preferred_element_type=jnp.float32)
    kv_saved = (key_all, value_all)
    saved = (
        normed_low,
        unit_attn,
        scale_attn,
        queries,
        keys_low,
        values_low,
        log_total,
        attended,
        attended_low,
        unit_mlp,
        scale_mlp,
        normed_two_low,
        gate_up,
        hidden_low,
        kv_saved,
    )
    return (result, saved)


def layer_backward(grad_stream, saved, attn_set, mlp_set, context):
    query_places, query_segment, positions, keep_rows, doc_lens = context
    mix_full, out_full, gain_full = attn_set
    in_full, down_full = mlp_set
    (
        normed_low,
        unit_attn,
        scale_attn,
        queries,
        keys_low,
        values_low,
        log_total,
        attended,
        attended_low,
        unit_mlp,
        scale_mlp,
        normed_two_low,
        gate_up,
        hidden_low,
        kv_saved,
    ) = saved
    row_count = grad_stream.shape[0]
    key_width = KV_HEADS * HEAD_DIM
    groups_per = HEADS // KV_HEADS
    score_scale = HEAD_DIM ** (-0.5)
    gain_attn = gain_full[0].astype(jnp.float32)
    gain_mlp = gain_full[1].astype(jnp.float32)
    grad_branch = grad_stream.astype(jnp.bfloat16)
    grad_down = jnp.einsum("nf,nd->fd", hidden_low, grad_branch, preferred_element_type=jnp.float32)
    grad_hidden = jnp.einsum(
        "nd,fd->nf", grad_branch, down_full, preferred_element_type=jnp.float32
    )
    gate_part = gate_up[:, :FF]
    up_part = gate_up[:, FF:]
    sigmoid_gate = jax.nn.sigmoid(gate_part)
    grad_gate = grad_hidden * up_part * sigmoid_gate * (1.0 + gate_part * (1.0 - sigmoid_gate))
    grad_up = grad_hidden * gate_part * sigmoid_gate
    grad_gate_up = jnp.concatenate([grad_gate, grad_up], axis=1).astype(jnp.bfloat16)
    grad_in = jnp.einsum(
        "nd,nf->df", normed_two_low, grad_gate_up, preferred_element_type=jnp.float32
    )
    grad_normed_two = jnp.einsum(
        "nf,df->nd", grad_gate_up, in_full, preferred_element_type=jnp.float32
    )
    mlp_part = (
        lax.psum_scatter(grad_in, ("seq", "fsdp"), scatter_dimension=0, tiled=True),
        lax.psum_scatter(grad_down, ("seq", "fsdp"), scatter_dimension=0, tiled=True),
    )
    grad_gain_mlp, grad_middle_norm = norm_backward(grad_normed_two, unit_mlp, scale_mlp, gain_mlp)
    grad_middle = grad_stream + grad_middle_norm
    attn_branch = grad_middle.astype(jnp.bfloat16)
    grad_out = jnp.einsum(
        "nd,ne->de", attended_low, attn_branch, preferred_element_type=jnp.float32
    )
    grad_attended = (
        jnp.einsum("ne,de->nd", attn_branch, out_full, preferred_element_type=jnp.float32)
        * keep_rows
    )
    grad_heads = grad_attended.astype(jnp.bfloat16).reshape(
        row_count, KV_HEADS, groups_per, HEAD_DIM
    )
    row_delta = jnp.sum(
        grad_heads.astype(jnp.float32)
        * attended.reshape(row_count, KV_HEADS, groups_per, HEAD_DIM),
        axis=-1,
    )
    key_all, value_all = kv_saved
    total_keys = key_all.shape[0]
    block_rows = 512

    def back_step(grad_queries, number):
        first_key = number * block_rows
        key_block = lax.dynamic_slice_in_dim(key_all, first_key, block_rows, 0)
        value_block = lax.dynamic_slice_in_dim(value_all, first_key, block_rows, 0)
        scores, allowed = masked_scores(
            queries, key_block, first_key, query_places, query_segment, doc_lens
        )
        soft_weight = jnp.where(
            allowed[:, None, None, :], jnp.exp(scores - log_total[..., None]), 0.0
        )
        value_heads = value_block.reshape(block_rows, KV_HEADS, HEAD_DIM)
        key_heads = key_block.reshape(block_rows, KV_HEADS, HEAD_DIM)
        grad_weight = jnp.einsum(
            "qkgd,skd->qkgs", grad_heads, value_heads, preferred_element_type=jnp.float32
        )
        grad_score = (soft_weight * (grad_weight - row_delta[..., None])).astype(jnp.bfloat16)
        state_out = grad_queries + jnp.einsum(
            "qkgs,skd->qkgd", grad_score, key_heads, preferred_element_type=jnp.float32
        )
        grad_key = (
            jnp.einsum("qkgs,qkgd->skd", grad_score, queries, preferred_element_type=jnp.float32)
            * score_scale
        )
        grad_value = jnp.einsum(
            "qkgs,qkgd->skd",
            soft_weight.astype(jnp.bfloat16),
            grad_heads,
            preferred_element_type=jnp.float32,
        )
        return (
            state_out,
            jnp.concatenate(
                [
                    grad_key.reshape(block_rows, key_width),
                    grad_value.reshape(block_rows, key_width),
                ],
                axis=1,
            ),
        )

    start_grad = jnp.zeros((row_count, KV_HEADS, groups_per, HEAD_DIM), jnp.float32)
    grad_queries, pair_blocks = lax.scan(
        back_step, start_grad, jnp.arange(total_keys // block_rows, dtype=jnp.int32)
    )
    pair_terms = pair_blocks.reshape(total_keys, 2 * key_width)
    pair_sums = lax.psum_scatter(pair_terms, "seq", scatter_dimension=0, tiled=True)
    grad_rot_queries = rotate(
        (grad_queries * score_scale).reshape(row_count, HEADS, HEAD_DIM), positions, -1.0
    ).reshape(row_count, D)
    grad_rot_keys = rotate(
        pair_sums[:, :key_width].reshape(row_count, KV_HEADS, HEAD_DIM), positions, -1.0
    ).reshape(row_count, key_width)
    grad_projected = jnp.concatenate(
        [grad_rot_queries, grad_rot_keys, pair_sums[:, key_width:]], axis=1
    ).astype(jnp.bfloat16)
    grad_mix = jnp.einsum(
        "nd,nf->df", normed_low, grad_projected, preferred_element_type=jnp.float32
    )
    grad_normed = jnp.einsum(
        "nf,df->nd", grad_projected, mix_full, preferred_element_type=jnp.float32
    )
    grad_gain_attn, grad_input_norm = norm_backward(grad_normed, unit_attn, scale_attn, gain_attn)
    grad_gains = jnp.stack([grad_gain_attn, grad_gain_mlp])
    attn_part = (
        lax.psum_scatter(grad_mix, ("seq", "fsdp"), scatter_dimension=0, tiled=True),
        lax.psum_scatter(grad_out, ("seq", "fsdp"), scatter_dimension=0, tiled=True),
        lax.psum_scatter(grad_gains, ("seq", "fsdp"), scatter_dimension=1, tiled=True),
    )
    return (grad_middle + grad_input_norm, attn_part, mlp_part)


def adam_update(weight, first, second, grad, clip_scale, rate):
    clipped = grad * clip_scale
    first_new = BETA_ONE * first + (1.0 - BETA_ONE) * clipped
    second_new = BETA_TWO * second + (1.0 - BETA_TWO) * clipped * clipped
    first_hat = first_new / (1.0 - BETA_ONE**STEP_NUMBER)
    second_hat = second_new / (1.0 - BETA_TWO**STEP_NUMBER)
    updated = weight - rate * (
        first_hat / (jnp.sqrt(second_hat) + EPS_ADAM) + WEIGHT_DECAY * weight
    )
    return (updated, first_new, second_new)


def local(
    tokens,
    cotangent,
    lengths,
    mix_weight,
    out_weight,
    in_weight,
    down_weight,
    norm_gains,
    mix_first,
    out_first,
    in_first,
    down_first,
    norm_first,
    mix_second,
    out_second,
    in_second,
    down_second,
    norm_second,
):
    row_count = tokens.shape[0]
    group_index = lax.axis_index("fsdp")
    cycle_index = lax.axis_index("seq")
    doc_lens = lax.dynamic_index_in_dim(lengths, group_index, 0, keepdims=False)
    query_places = cycle_index * row_count + jnp.arange(row_count, dtype=jnp.int32)
    query_segment, positions = doc_layout(query_places, doc_lens)
    keep_rows = (query_segment < doc_lens.shape[0]).astype(jnp.float32)[:, None]
    context = (query_places, query_segment, positions, keep_rows, doc_lens)
    stream = tokens.astype(jnp.float32)
    layer_index = 0
    attn_set, mlp_set = fetch_layer(
        mix_weight, out_weight, norm_gains, in_weight, down_weight, layer_index
    )
    stream, saved = layer_forward(stream, attn_set, mlp_set, context)
    saved_list = [saved]
    weight_list = [(attn_set, mlp_set)]
    hidden_out = stream.astype(jnp.bfloat16)
    grad_stream = cotangent.astype(jnp.float32)
    attn_sums = [None] * LAYERS
    mlp_sums = [None] * LAYERS
    for layer_index in reversed(range(LAYERS)):
        attn_set, mlp_set = weight_list[layer_index]
        grad_stream, attn_part, mlp_part = layer_backward(
            grad_stream, saved_list[layer_index], attn_set, mlp_set, context
        )
        attn_sums[layer_index] = attn_part
        mlp_sums[layer_index] = mlp_part
    mix_grad = jnp.stack([attn_sums[0][0]])
    out_grad = jnp.stack([attn_sums[0][1]])
    norm_grad = jnp.stack([attn_sums[0][2]])
    in_grad = jnp.stack([mlp_sums[0][0]])
    down_grad = jnp.stack([mlp_sums[0][1]])
    squares = (
        jnp.sum(mix_grad * mix_grad)
        + jnp.sum(out_grad * out_grad)
        + jnp.sum(in_grad * in_grad)
        + jnp.sum(down_grad * down_grad)
        + jnp.sum(norm_grad * norm_grad)
    )
    total_squares = lax.psum(squares, ("seq", "fsdp"))
    grad_norm = jnp.sqrt(total_squares)
    clip_scale = CLIP_NORM / jnp.maximum(grad_norm, CLIP_NORM)
    mix_new, mix_moment, mix_square = adam_update(
        mix_weight, mix_first, mix_second, mix_grad, clip_scale, LEARN_RATE
    )
    out_new, out_moment, out_square = adam_update(
        out_weight, out_first, out_second, out_grad, clip_scale, OUT_RATE
    )
    in_new, in_moment, in_square = adam_update(
        in_weight, in_first, in_second, in_grad, clip_scale, LEARN_RATE
    )
    down_new, down_moment, down_square = adam_update(
        down_weight, down_first, down_second, down_grad, clip_scale, LEARN_RATE
    )
    norm_new, norm_moment, norm_square = adam_update(
        norm_gains, norm_first, norm_second, norm_grad, clip_scale, GAIN_RATE
    )
    return (
        hidden_out,
        grad_stream,
        grad_norm,
        mix_grad,
        mix_new,
        mix_moment,
        mix_square,
        mix_new.astype(jnp.bfloat16),
        out_grad,
        out_new,
        out_moment,
        out_square,
        out_new.astype(jnp.bfloat16),
        in_grad,
        in_new,
        in_moment,
        in_square,
        in_new.astype(jnp.bfloat16),
        down_grad,
        down_new,
        down_moment,
        down_square,
        down_new.astype(jnp.bfloat16),
        norm_grad,
        norm_new,
        norm_moment,
        norm_square,
        norm_new.astype(jnp.bfloat16),
    )


MESH = pl.DeviceIdType.MESH
ANY = pl.BlockSpec(memory_space=pl.ANY)
VMEM = pl.BlockSpec(memory_space=pltpu.VMEM)
LOW = jnp.bfloat16
SQUARE = 8
SEQ = 16
FLEET = 32
ROWS = 128
GATHER_TOP = 64
SCATTER_TOP = 64
DOC_KINDS = 6
KEYS = 1024
BLOCK = 256
CORE, NEAR_Y, NEAR_Z = 1, 2, 4
LOG2E = 1.4426950408889634
SCALE2 = HEAD_DIM ** (-0.5) * LOG2E
WALL = 2.0**100


def flip(value, bits):
    for bit in (1, 2, 4, 8):
        if bits & bit:
            value = value + bit - 2 * bit * (lax.rem(lax.div(value, bit), 2))
    return value


class Place:
    def __init__(self):
        self.seq = lax.axis_index("seq")
        self.fsdp = lax.axis_index("fsdp")
        self.member = lax.rem(self.seq, SQUARE)
        self.half = lax.div(self.seq, SQUARE)
        self.rank = self.seq * 2 + self.fsdp

    def peer(self, bits):
        return (flip(self.seq, bits), self.fsdp)

    def slot(self, bits):
        return flip(self.member, bits)

    def after(self, step):
        rank = lax.rem(self.rank + step, FLEET)
        return rank, (lax.div(rank, 2), lax.rem(rank, 2))

    def twin(self):
        return (self.seq, 1 - self.fsdp)


def send(src, dst, sems, index, device):
    return pltpu.make_async_remote_copy(
        src_ref=src,
        dst_ref=dst,
        send_sem=sems[0].at[index],
        recv_sem=sems[1].at[index],
        device_id=device,
        device_id_type=MESH,
    )


def greet(devices):
    barrier = pltpu.get_barrier_semaphore()
    for device in devices:
        pl.semaphore_signal(barrier, inc=1, device_id=device, device_id_type=MESH)
    pl.semaphore_wait(barrier, len(devices))


class SquareGather:
    COPIES = 10

    def __init__(self, place, src, out, sems, local_sem, top_rows):
        p, h = place, top_rows
        own, ys, zs = p.slot(0), p.slot(NEAR_Y), p.slot(NEAR_Z)
        ds = p.slot(NEAR_Y | NEAR_Z)
        to_y, to_z, to_c = p.peer(NEAR_Y), p.peer(NEAR_Z), p.peer(CORE)
        top, low = pl.ds(0, h), pl.ds(h, ROWS - h)
        self.local = pltpu.make_async_copy(src, out.at[own], local_sem)
        self.y0 = send(src.at[top], out.at[own, top], sems, 0, to_y)
        self.y1 = send(src.at[low], out.at[own, low], sems, 1, to_y)
        self.z1 = send(src.at[low], out.at[own, low], sems, 2, to_z)
        self.z0 = send(src.at[top], out.at[own, top], sems, 3, to_z)
        self.fz = send(out.at[ys, top], out.at[ys, top], sems, 4, to_z)
        self.fy = send(out.at[zs, low], out.at[zs, low], sems, 5, to_y)
        self.c = [
            send(src, out.at[own], sems, 6, to_c),
            send(out.at[ys], out.at[ys], sems, 7, to_c),
            send(out.at[zs], out.at[zs], sems, 8, to_c),
            send(out.at[ds], out.at[ds], sems, 9, to_c),
        ]

    def start(self):
        for copy in (self.y0, self.z1, self.y1, self.z0, self.c[0], self.local):
            copy.start()

    def relay(self):
        self.y0.wait_recv()
        self.fz.start()
        self.z1.wait_recv()
        self.fy.start()

    def share(self):
        self.y1.wait_recv()
        self.c[1].start()
        self.z0.wait_recv()
        self.c[2].start()

    def finish(self):
        self.fz.wait_recv()
        self.fy.wait_recv()
        self.c[3].start()
        for copy in self.c:
            copy.wait_recv()
        for copy in [self.y0, self.y1, self.z0, self.z1, self.fz, self.fy] + self.c:
            copy.wait_send()
        self.local.wait()


def mix_spread(place, mix, mix_o, plane_s, cross_s, local_sem):
    twin = (place.seq, 1 - place.fsdp)
    first = [
        send(
            mix.at[lax.rem(flip(place.seq, bits), SQUARE)],
            mix_o.at[place.rank],
            plane_s,
            bits,
            (flip(place.seq, bits), place.fsdp),
        )
        for bits in range(1, SEQ)
    ]
    second = []
    for bits in range(SEQ):
        spot = flip(place.seq, bits) * 2 + place.fsdp
        second.append(send(mix_o.at[spot], mix_o.at[spot], cross_s, bits, twin))
    local = pltpu.make_async_copy(mix.at[place.member], mix_o.at[place.rank], local_sem)
    return first, second, local


def add_rows(target, left, right, start, count):
    step = 16

    def body(number, _):
        rows = pl.ds(pl.multiple_of(start + number * step, step), step)
        target[rows] = (left[rows].astype(jnp.float32) + right[rows].astype(jnp.float32)).astype(
            target.dtype
        )
        return 0

    lax.fori_loop(0, count // step, body, 0)


class SquareScatter:
    def __init__(self, place, part, total, buffers, sems, top_rows):
        sib, away, passed, landed = buffers
        self.place, self.part, self.total = place, part, total
        self.sib, self.away, self.passed, self.landed = sib, away, passed, landed
        h = self.top_rows = top_rows
        top, low = pl.ds(0, h), pl.ds(h, ROWS - h)
        to_y, to_z, to_c = place.peer(NEAR_Y), place.peer(NEAR_Z), place.peer(CORE)
        self.order = (NEAR_Y | NEAR_Z, NEAR_Y, NEAR_Z, 0)
        self.cores = [
            send(part.at[place.slot(bits | CORE)], sib.at[number], sems, number, to_c)
            for number, bits in enumerate(self.order)
        ]
        self.d0 = send(away.at[0, top], passed.at[top], sems, 4, to_y)
        self.d1 = send(away.at[0, low], passed.at[low], sems, 5, to_z)
        self.y0 = send(away.at[1, top], landed.at[0, top], sems, 6, to_y)
        self.y1 = send(away.at[1, low], landed.at[0, low], sems, 7, to_y)
        self.z0 = send(away.at[2, top], landed.at[1, top], sems, 8, to_z)
        self.z1 = send(away.at[2, low], landed.at[1, low], sems, 9, to_z)

    @staticmethod
    def buffers(width):
        return [
            pltpu.VMEM((4, ROWS, width), LOW),
            pltpu.VMEM((3, ROWS, width), LOW),
            pltpu.VMEM((ROWS, width), LOW),
            pltpu.VMEM((2, ROWS, width), LOW),
        ]

    def start(self):
        for copy in self.cores:
            copy.start()

    def pair_one(self, number):
        self.cores[number].wait_recv()
        target = self.away.at[number] if number < 3 else self.total
        mine = self.part.at[self.place.slot(self.order[number])]
        add_rows(target, mine, self.sib.at[number], 0, ROWS)
        for copy in ((self.d0, self.d1), (self.y0,), (self.z1,), ())[number]:
            copy.start()

    def pair_up(self):
        for number in range(4):
            self.pair_one(number)

    def relay(self):
        h, rest = self.top_rows, ROWS - self.top_rows
        self.d0.wait_recv()
        add_rows(self.away.at[2], self.away.at[2], self.passed, 0, h)
        self.z0.start()
        self.d1.wait_recv()
        add_rows(self.away.at[1], self.away.at[1], self.passed, h, rest)
        self.y1.start()

    def finish(self):
        h, rest = self.top_rows, ROWS - self.top_rows
        total, landed = self.total, self.landed
        self.y0.wait_recv()
        add_rows(total, total, landed.at[0], 0, h)
        self.z1.wait_recv()
        add_rows(total, total, landed.at[1], h, rest)
        self.z0.wait_recv()
        add_rows(total, total, landed.at[1], 0, h)
        self.y1.wait_recv()
        add_rows(total, total, landed.at[0], h, rest)
        for copy in self.cores + [self.d0, self.d1, self.y0, self.y1, self.z0, self.z1]:
            copy.wait_send()


def dot32(left, right, dims=((1,), (0,))):
    return lax.dot_general(left, right, (dims, ((), ())), preferred_element_type=jnp.float32)


def block_of(number):
    return pl.ds(pl.multiple_of(number * BLOCK, BLOCK), BLOCK)


def later(number_of_columns):
    key_at = lax.broadcasted_iota(jnp.int32, (BLOCK, number_of_columns), 0)
    query_at = lax.rem(lax.broadcasted_iota(jnp.int32, (BLOCK, number_of_columns), 1), BLOCK)
    return key_at > query_at


class Mailbox:
    def __init__(self, sends, receives, locals_):
        self.sends, self.receives, self.locals_ = sends, receives, locals_
        self.taken, self.local_taken = 0, 0

    def take(self, count):
        start = self.taken
        self.taken += count
        spot = pl.ds(start, count)
        return (self.sends.at[spot], self.receives.at[spot])

    def local(self):
        self.local_taken += 1
        return self.locals_.at[self.local_taken - 1]


def token_layout(lengths, group, start, count):
    at = start + lax.broadcasted_iota(jnp.int32, (1, count), 1)
    segment = jnp.zeros((1, count), jnp.int32)
    offset = jnp.zeros((1, count), jnp.int32)
    end = jnp.int32(0)
    for number in range(lengths.shape[1]):
        length = lengths[group, number]
        end = end + length
        passed = (at >= end).astype(jnp.int32)
        segment = segment + passed
        offset = offset + passed * length
    return segment, at - offset


def wall_rows(segment):
    kind = lax.broadcasted_iota(jnp.int32, (32, segment.shape[1]), 0)
    return jnp.where((kind != segment) & (kind < DOC_KINDS), -WALL, 0.0)


def mark_rows(segment):
    kind = lax.broadcasted_iota(jnp.int32, (32, segment.shape[1]), 0)
    return jnp.where(kind == segment, 1.0, 0.0)


def turn_head(head, cosine, sine):
    former, latter = head[: HEAD_DIM // 2], head[HEAD_DIM // 2 :]
    return jnp.concatenate(
        [former * cosine - latter * sine, latter * cosine + former * sine], axis=0
    )


class WeightSpread:
    CHUNKS = 4

    def __init__(self, place, inn, down, in_o, down_o, mail):
        p = place
        twin, across = p.twin(), p.peer(SQUARE)
        self.square = [
            send(inn.at[p.slot(bits)], in_o.at[p.half, p.member, p.fsdp], box, 0, p.peer(bits))
            for bits in range(1, SQUARE)
            for box in (mail.take(1),)
        ]
        self.local = pltpu.make_async_copy(
            inn.at[p.member], in_o.at[p.half, p.member, p.fsdp], mail.local()
        )
        self.down_local = pltpu.make_async_copy(down, down_o.at[p.half, p.fsdp], mail.local())
        near = in_o.at[p.half, pl.ds(0, SQUARE), p.fsdp]
        self.near = send(near, near, mail.take(1), 0, twin)
        width = SQUARE // self.CHUNKS
        self.far, self.passed = [], []
        boxes, passed_boxes = mail.take(self.CHUNKS), mail.take(self.CHUNKS)
        for number in range(self.CHUNKS):
            rows = pl.ds(number * width, width)
            mine = in_o.at[p.half, rows, p.fsdp]
            other = in_o.at[1 - p.half, rows, p.fsdp]
            self.far.append(send(mine, mine, boxes, number, across))
            self.passed.append(send(other, other, passed_boxes, number, twin))
        boxes = mail.take(3)
        self.down_near = send(down, down_o.at[p.half, p.fsdp], boxes, 0, twin)
        self.down_far = send(down, down_o.at[p.half, p.fsdp], boxes, 1, across)
        other = down_o.at[1 - p.half, p.fsdp]
        self.down_passed = send(other, other, boxes, 2, twin)

    def start_square(self):
        for copy in self.square:
            copy.start()
        self.local.start()

    def square_done(self):
        for copy in self.square:
            copy.wait_recv()
        self.local.wait()

    def pass_on(self, number):
        self.far[number].wait_recv()
        self.passed[number].start()

    def arrived(self):
        for copy in self.passed + [self.near, self.down_near, self.down_passed]:
            copy.wait_recv()
        self.down_local.wait()

    def drain(self):
        for copy in self.square + self.far + self.passed:
            copy.wait_send()
        for copy in (self.near, self.down_far, self.down_near, self.down_passed):
            copy.wait_send()


def forward_part(place, mail, r):
    lengths, frequency, tok, gain, mix, out, inn, down, cot = (
        r.lengths, r.frequency, r.tok, r.gain_in, r.mix_in, r.out_in, r.inn_in, r.down_in, r.cot
    )
    mix_o, out_o, gain_o, pair_o, att_o = r.mix, r.out, r.gain, r.pair, r.att
    keys_o, values_o, cos_o, sin_o = r.keys, r.values, r.cosine, r.sine
    tok_all, gains, query_c, part, two = r.tok_all, r.gains, r.query_c, r.part, r.two
    top_s, sum_s, mixed_s, att_low, middle_o = r.top_s, r.sum_s, r.dq_s, r.att_low, r.middle
    f32 = jnp.float32
    twin = place.twin()
    blocks = KEYS // BLOCK
    greet([place.after(step)[1] for step in range(1, FLEET)])
    gather_tok = SquareGather(place, tok, tok_all, mail.take(10), mail.local(), GATHER_TOP)
    first, second, mix_local = mix_spread(
        place, mix, mix_o, mail.take(SEQ), mail.take(SEQ), mail.local()
    )
    mix_local.start()
    for bits in range(SEQ - 1, SQUARE - 1, -1):
        first[bits - 1].start()
    gather_tok.start()
    for bits in range(SQUARE - 1, 0, -1):
        first[bits - 1].start()
    gain_local = pltpu.make_async_copy(gain, gains.at[place.rank], mail.local())
    gain_local.start()
    gain_copies = []
    boxes = mail.take(FLEET)
    for step in range(1, FLEET):
        rank, device = place.after(step)
        gain_copies.append(send(gain, gains.at[place.rank], boxes, step, device))
        gain_copies[-1].start()

    keeper = lax.div(place.seq, 2)
    spot = lax.rem(place.seq, 2)
    out_boxes, out_local, twin_boxes = mail.take(2), mail.local(), mail.take(2)

    def out_copy(number):
        remote = pltpu.make_async_remote_copy(
            src_ref=out,
            dst_ref=out_o.at[spot, place.fsdp],
            send_sem=out_boxes[0].at[number],
            recv_sem=out_boxes[1].at[spot],
            device_id=(number * SQUARE + keeper, place.fsdp),
            device_id_type=MESH,
        )
        local = pltpu.make_async_copy(out, out_o.at[spot, place.fsdp], out_local)
        return remote, local, number * SQUARE + keeper == place.seq

    def out_arrival(number):
        source = place.member * 2 + number
        arrival = pltpu.make_async_remote_copy(
            src_ref=out,
            dst_ref=out_o.at[number, place.fsdp],
            send_sem=out_boxes[0].at[number],
            recv_sem=out_boxes[1].at[number],
            device_id=(source, place.fsdp),
            device_id_type=MESH,
        )
        return arrival, source == place.seq

    for number in range(2):
        remote, local, mine = out_copy(number)
        pl.when(mine)(local.start)
        pl.when(jnp.logical_not(mine))(remote.start)

    segment, position = token_layout(lengths, place.fsdp, place.half * KEYS, KEYS)
    angle = frequency[...] * position.astype(f32)
    cos_o[...] = jnp.cos(angle)
    sin_o[...] = jnp.sin(angle)
    keep = (segment < lengths.shape[1]).astype(f32)
    marks = mark_rows(segment).astype(LOW)
    for number in range(blocks):
        mark = marks[:, number * BLOCK : (number + 1) * BLOCK]
        query_c[number, HEAD_DIM:, :] = jnp.concatenate([mark, mark], axis=1)
    walls = wall_rows(segment)

    gather_tok.relay()
    mix_local.wait()
    second[0].start()
    for bits in range(SQUARE - 1, 0, -1):
        first[bits - 1].wait_recv()
        second[bits].start()
    gather_tok.share()
    for bits in range(SEQ - 1, SQUARE - 1, -1):
        first[bits - 1].wait_recv()
        second[bits].start()
    spread = WeightSpread(place, inn, down, r.inn, r.down, mail)
    spread.down_local.start()
    spread.start_square()
    gather_cot = SquareGather(place, cot, r.cot_all, mail.take(10), mail.local(), GATHER_TOP)
    gather_cot.start()
    gain_local.wait()
    for copy in gain_copies:
        copy.wait()
    gain_o[...] = jnp.zeros_like(gain_o)
    for rank in range(FLEET):
        lane = rank * (D // FLEET) // 128 * 128
        gain_o[:, lane : lane + 256] += gains[rank].astype(f32)
    gather_tok.finish()
    for copy in second:
        copy.wait_recv()

    up_boxes = mail.take(blocks)
    up = [
        send(pair_o.at[blocks + number], pair_o.at[number], up_boxes, number, place.peer(SQUARE))
        for number in range(blocks)
    ]
    for number in range(blocks):
        columns = pl.ds(number * BLOCK, BLOCK)
        halves = []
        for block in (2 * number, 2 * number + 1):
            x = tok_all[block].astype(f32)
            scale = lax.rsqrt(jnp.mean(x * x, axis=-1, keepdims=True) + EPS_NORM)
            low = (x * scale * gain_o[0:1, :D]).astype(LOW)
            tok_all[block] = low
            halves.append(dot32(low, mix_o[...].reshape(D, 4 * HEAD_DIM)).T)
        projected = jnp.concatenate(halves, axis=1)
        cosine, sine = cos_o[:, columns], sin_o[:, columns]
        for head in range(2):
            turned = turn_head(projected[head * HEAD_DIM : (head + 1) * HEAD_DIM], cosine, sine)
            side = pl.ds(head * BLOCK, BLOCK)
            query_c[number, :HEAD_DIM, side] = turned.astype(LOW)
        key = turn_head(projected[2 * HEAD_DIM : 3 * HEAD_DIM], cosine, sine).astype(LOW)
        value = projected[3 * HEAD_DIM :].astype(LOW)
        pair_o[blocks + number, :HEAD_DIM] = key
        pair_o[blocks + number, HEAD_DIM:] = value
        pl.when(place.half == 0)(up[number].start)
        rows = pl.ds(KEYS + number * BLOCK, BLOCK)
        wall = walls[:, number * BLOCK : (number + 1) * BLOCK]
        keys_o[rows, :] = jnp.concatenate([key.astype(f32), wall], axis=0).T.astype(LOW)
        values_o[rows, :] = value.astype(f32).T.astype(LOW)

    for number in range(2):
        remote, local, mine = out_copy(number)
        pl.when(mine)(local.wait)
        pl.when(jnp.logical_not(mine))(remote.wait_send)
    passing = []
    for number in range(2):
        arrival, mine = out_arrival(number)
        pl.when(jnp.logical_not(mine))(arrival.wait_recv)
        block = out_o.at[number, place.fsdp]
        passing.append(send(block, block, twin_boxes, number, twin))
        passing[-1].start()
    spread.square_done()
    spread.near.start()
    spread.down_near.start()
    for copy in spread.far:
        pl.when(place.half == 1)(copy.start)

    normed_out = pltpu.make_async_copy(tok_all, r.normed, mail.local())
    normed_out.start()
    gather_cot.relay()
    gather_cot.share()

    def fold(queries, spot, carry, diagonal=False):
        score = dot32(keys_o[block_of(spot), :], queries)
        if diagonal:
            score = jnp.where(later(2 * BLOCK), -WALL, score)
        top = jnp.max(score, axis=0, keepdims=True)
        if carry is not None:
            top = jnp.maximum(carry[0], top)
        weight = jnp.exp2((score - top) * SCALE2)
        total = jnp.sum(weight, axis=0, keepdims=True)
        mixed = dot32(pair_o[spot, HEAD_DIM:], weight.astype(LOW))
        if carry is not None:
            fade = jnp.exp2((carry[0] - top) * SCALE2)
            total = total + carry[1] * fade
            mixed = mixed + carry[2] * fade
        return (top, total, mixed)

    for number in range(blocks):
        queries = query_c[number]
        carry = fold(queries, blocks + number, None, diagonal=True)
        carry = lax.fori_loop(
            blocks, blocks + number, functools.partial(fold, queries), carry
        )
        top_s[number : number + 1, :], sum_s[number : number + 1, :] = carry[:2]
        mixed_s[number] = carry[2]

    spread.down_far.start()

    @pl.when(place.half == 1)
    def _():
        other_segment, _ = token_layout(lengths, place.fsdp, 0, KEYS)
        other_walls = wall_rows(other_segment)
        for number in range(blocks):
            up[number].wait_recv()
            rows = pl.ds(number * BLOCK, BLOCK)
            wall = other_walls[:, number * BLOCK : (number + 1) * BLOCK]
            keys_o[rows, :] = (
                jnp.concatenate([pair_o[number, :HEAD_DIM].astype(f32), wall], axis=0)
                .T.astype(LOW)
            )
            values_o[rows, :] = pair_o[number, HEAD_DIM:].astype(f32).T.astype(LOW)

    @pl.when(place.half == 0)
    def _():
        for number in range(blocks):
            up[number].wait_send()
            pair_o[number] = jnp.zeros_like(pair_o[number])
        keys_o[pl.ds(0, KEYS), :] = jnp.zeros((KEYS, 128), LOW)
        values_o[pl.ds(0, KEYS), :] = jnp.zeros((KEYS, HEAD_DIM), LOW)

    for copy in spread.far:
        pl.when(place.half == 0)(copy.start)
    for number in range(blocks):
        columns = pl.ds(number * BLOCK, BLOCK)
        carry = (top_s[number : number + 1, :], sum_s[number : number + 1, :], mixed_s[number])
        carry = lax.fori_loop(
            0,
            jnp.where(place.half == 1, blocks, 0),
            functools.partial(fold, query_c[number]),
            carry,
        )
        top, total, mixed = carry
        mixed = mixed * (1.0 / total)
        level = top * SCALE2 + jnp.log2(total)
        r.level_s[number] = jnp.broadcast_to(level, (8, 2 * BLOCK))
        for head in range(2):
            side = slice(head * BLOCK, (head + 1) * BLOCK)
            rows = pl.ds(head * HEAD_DIM, HEAD_DIM)
            kept = mixed[:, side] * keep[:, number * BLOCK : (number + 1) * BLOCK]
            att_o[rows, columns] = kept
            att_low[rows, columns] = kept.astype(LOW)

    for copy in passing:
        copy.wait_recv()
    normed_out.wait()
    scatter = SquareScatter(
        place, part, middle_o, r.buffers_a, mail.take(10), SCATTER_TOP
    )

    def out_block(slot):
        columns = pl.ds(pl.multiple_of(slot * ROWS, ROWS), ROWS)
        rows = att_low[:, columns].astype(f32).T.astype(LOW)
        part[slot] = dot32(rows, out_o[...].reshape(2 * HEAD_DIM, D)).astype(LOW)

    for number, bits in enumerate(scatter.order):
        out_block(place.slot(bits | CORE))
        scatter.cores[number].start()
    for bits in scatter.order:
        out_block(place.slot(bits))
    scatter.pair_up()
    spread.down_far.wait_recv()
    spread.down_passed.start()
    spread.pass_on(0)
    scatter.relay()
    scatter.finish()
    middle = middle_o[...] + tok[...].astype(f32)
    middle_o[...] = middle
    scale = lax.rsqrt(jnp.mean(middle * middle, axis=-1, keepdims=True) + EPS_NORM)
    two[...] = (middle * scale * gain_o[1:2, :D]).astype(LOW)
    gather_two = SquareGather(place, two, r.two_all, mail.take(10), mail.local(), GATHER_TOP)
    gather_two.start()
    spread.pass_on(1)
    gather_two.relay()
    gather_two.share()
    spread.pass_on(2)
    gather_two.finish()
    gather_cot.finish()
    spread.pass_on(3)
    spread.arrived()

    def drain():
        spread.drain()
        for copy in first + second + passing:
            copy.wait_send()

    return keep, drain


def norm_back(grad, values, gain):
    scale = lax.rsqrt(jnp.mean(values * values, axis=-1, keepdims=True) + EPS_NORM)
    unit = values * scale
    grad_gain = jnp.sum(grad * unit, axis=0, keepdims=True)
    grad_unit = grad * gain
    centre = jnp.mean(grad_unit * unit, axis=-1, keepdims=True)
    return grad_gain, scale * (grad_unit - unit * centre)


def add_blocks(target, left, right, count):
    for number in range(count):
        add_rows(target.at[number], left.at[number], right.at[number], 0, target.shape[1])


def square_sum(ref):
    value = ref[...].astype(jnp.float32)
    return jnp.sum(value * value)


def backward_part(place, mail, r, keep):
    tok, cot, middle, gain, mix, out = r.tok, r.cot, r.middle, r.gain, r.mix, r.out
    inn, down, keys, values, pair, att = r.inn, r.down, r.keys, r.values, r.pair, r.att
    cosine, sine, two_all, cot_all = r.cosine, r.sine, r.two_all, r.cot_all
    part, hidden, gate_grad, total, grad_mid = r.part, r.hidden, r.gate_grad, r.total, r.grad_mid
    gin, gin_x, gin_z, gdown, gdown_x, gdown_z = (
        r.gin, r.gin_x, r.gin_z, r.gdown, r.gdown_x, r.gdown_z
    )
    gout, gout_x, out_got, branch, branch_all = r.gout, r.gout_x, r.out_got, r.two, r.tok_all
    query_c, grad_c, query_r, grad_r = r.query_c, r.grad_c, r.query_r, r.grad_r
    level_s, shift_s, dq_s, back, back_in = r.level_s, r.shift_s, r.dq_s, r.back, r.back_in
    gproj_t, gproj_r, gmix, crossed = r.gproj_t, r.gproj_r, r.gmix, r.crossed
    landed_mix, gain_v, gain_w, sums, mine_s = r.landed_mix, r.gain_v, r.gain_w, r.sums, r.mine_s
    hidden_o, tokens_o, mix_o, out_o = r.hidden_o, r.tokens_o, r.mix_o, r.out_o
    in_o, down_o, gain_o, total_o = r.in_o, r.down_o, r.gain_o, r.total_o
    f32 = jnp.float32
    half, fsdp, member = place.half, place.fsdp, place.member
    twin, across = place.twin(), place.peer(SQUARE)
    blocks = KEYS // BLOCK
    rows_all = SQUARE * ROWS
    units = hidden.shape[1]
    buffers_a, buffers_b = r.buffers_a, r.buffers_b

    scatter = SquareScatter(place, part, total, buffers_a, mail.take(10), SCATTER_TOP)

    def feed_forward(chip):
        pair_of = pl.ds(chip * 2, 2)
        rows = pl.ds(pl.multiple_of(chip * 2 * ROWS, 2 * ROWS), 2 * ROWS)
        gate_up = dot32(two_all[pair_of].reshape(2 * ROWS, D), inn[...].reshape(D, 2 * units))
        gate, up = gate_up[:, :units], gate_up[:, units:]
        sigmoid = 1.0 / (1.0 + jnp.exp(-gate))
        silu = gate * sigmoid
        low = (silu * up).astype(LOW)
        hidden[rows, :] = low
        grad_hidden = dot32(cot_all[pair_of].reshape(2 * ROWS, D), down[...].reshape(units, D), ((1,), (1,)))
        grad_gate = grad_hidden * up * sigmoid * (1.0 + gate * (1.0 - sigmoid))
        grad_up = grad_hidden * silu
        low = jnp.concatenate([grad_gate, grad_up], axis=1).astype(LOW)
        gate_grad[rows, :] = low
        part[pair_of] = dot32(low, inn[...].reshape(D, 2 * units), ((1,), (1,))).astype(LOW).reshape(2, ROWS, D)

    for number, bits in enumerate(scatter.order):
        feed_forward(lax.div(place.slot(bits), 2))
        scatter.cores[number].start()
        if number:
            scatter.pair_one(number - 1)
    scatter.pair_one(3)

    in_boxes, far_boxes = mail.take(4), mail.take(2)
    in_cross, in_far = {}, {}
    down_boxes, down_far_box = mail.take(2), mail.take(1)
    down_cross = {}
    width = SQUARE // 2

    def in_grads(away, number):
        which = 1 - half if away else half
        spot = pl.ds(number * width, width)
        lanes = pl.ds(pl.multiple_of((which * 2 + number) * (D // 4), 128), D // 4)
        left = two_all[:, :, lanes].reshape(rows_all, D // 4)
        grad = dot32(left, gate_grad[...], ((0,), (0,)))
        gin[which, spot] = grad.astype(LOW).reshape(width, 2, D // FLEET, 2 * units)
        copy = send(
            gin.at[which, spot, 1 - fsdp], gin_x.at[which, spot], in_boxes, away * 2 + number, twin
        )
        copy.start()
        in_cross[away, number] = copy

    def down_grads(away):
        which = 1 - half if away else half
        lanes = pl.ds(pl.multiple_of(which * (units // 2), 128), units // 2)
        left = hidden[:, lanes]
        right = cot_all[...].reshape(rows_all, D)
        grad = dot32(left, right, ((0,), (0,)))
        gdown[which] = grad.astype(LOW).reshape(2, units // 4, D)
        copy = send(gdown.at[which, 1 - fsdp], gdown_x.at[which], down_boxes, away, twin)
        copy.start()
        down_cross[away] = copy

    in_grads(1, 0)
    in_grads(1, 1)
    scatter.relay()
    down_grads(1)
    in_grads(0, 0)
    in_grads(0, 1)
    down_grads(0)
    scatter.finish()
    gain_v[...] = jnp.zeros_like(gain_v)
    gain_mlp, grad_norm = norm_back(total[...], middle[...], gain[1:2, :D])
    gain_v[1:2, :D] = gain_mlp
    grad_middle = cot[...].astype(f32) + grad_norm
    grad_mid[...] = grad_middle
    branch[...] = grad_middle.astype(LOW)
    gather = SquareGather(place, branch, branch_all, mail.take(10), mail.local(), GATHER_TOP)
    gather.start()

    def in_onward(number):
        spot = pl.ds(number * width, width)
        in_cross[1, number].wait_recv()
        mine = gin.at[1 - half, spot, fsdp]
        add_blocks(mine, mine, gin_x.at[1 - half, spot], width)
        in_far[number] = send(mine, gin_z.at[spot], far_boxes, number, across)
        in_far[number].start()

    in_onward(0)
    gather.relay()
    for number in range(SQUARE // 2):
        rows = pl.ds(number * 2 * ROWS, 2 * ROWS)
        y_rows = dot32(hidden[rows, :], down[...].reshape(units, D)).astype(LOW)
        part[pl.ds(number * 2, 2)] = y_rows.reshape(2, ROWS, D)
    in_onward(1)
    gather.share()

    gather.finish()
    scatter_y = SquareScatter(place, part, total, buffers_a, mail.take(10), SCATTER_TOP)
    scatter_y.start()
    branch_rows = branch_all[...].reshape(rows_all, D)
    grad_att = dot32(out[...].reshape(2 * HEAD_DIM, D), branch_rows, ((1,), (1,))) * keep
    grad_low = grad_att.astype(LOW)
    delta = grad_low.astype(f32) * att[...]
    for head in range(2):
        rows = slice(head * HEAD_DIM, (head + 1) * HEAD_DIM)
        grad_head = grad_low[rows]
        shift = jnp.sum(delta[rows], axis=0, keepdims=True)
        for number in range(blocks):
            side = pl.ds(head * BLOCK, BLOCK)
            grad_block = grad_head[:, number * BLOCK : (number + 1) * BLOCK]
            grad_c[number, :, side] = grad_block
            query_r[number, side, :] = query_c[number, :, side].astype(f32).T.astype(LOW)
            grad_r[number, side, :] = grad_block.astype(f32).T.astype(LOW)
            shift_s[number, :, side] = jnp.broadcast_to(
                shift[:, number * BLOCK : (number + 1) * BLOCK], (8, BLOCK)
            )
    scatter_y.pair_up()

    dq_s[...] = jnp.zeros_like(dq_s)

    def fold(spot, number, carry, diagonal=False):
        grad_key, grad_value = carry
        rows = block_of(spot)
        score = dot32(keys[rows, :], query_c[number])
        if diagonal:
            score = jnp.where(later(2 * BLOCK), -WALL, score)
        weight = jnp.exp2(score * SCALE2 - level_s[number, 0:1, :])
        grad_weight = dot32(values[rows, :], grad_c[number])
        grad_score = (weight * (grad_weight - shift_s[number, 0:1, :])).astype(LOW)
        dq_s[number] += dot32(pair[spot, :HEAD_DIM], grad_score)
        grad_key = grad_key + dot32(grad_score, query_r[number])
        grad_value = grad_value + dot32(weight.astype(LOW), grad_r[number])
        return grad_key, grad_value

    none = (jnp.zeros((BLOCK, 128), f32), jnp.zeros((BLOCK, HEAD_DIM), f32))
    back_boxes = mail.take(blocks)
    returns = [
        send(back.at[number], back_in.at[number], back_boxes, number, across)
        for number in range(blocks)
    ]

    @pl.when(half == 1)
    def _():
        for number in range(blocks):
            grad_key, grad_value = lax.fori_loop(
                0, blocks, functools.partial(fold, number), none
            )
            back[number, :HEAD_DIM] = grad_key.T[:HEAD_DIM].astype(LOW)
            back[number, HEAD_DIM:] = grad_value.T.astype(LOW)
            returns[number].start()

    scatter_y.relay()
    down_cross[1].wait_recv()
    down_mine = gdown.at[1 - half, fsdp]
    add_rows(down_mine, down_mine, gdown_x.at[1 - half], 0, units // 4)
    down_far = send(down_mine, gdown_z, down_far_box, 0, across)
    down_far.start()

    out_boxes, owner_boxes = mail.take(1), mail.take(2)
    out_local = mail.local()
    grad_out = dot32(r.att_low[...], branch_all[...].reshape(rows_all, D))
    gout[...] = grad_out.astype(LOW).reshape(2, 2, D // FLEET, D)
    out_cross = send(gout.at[pl.ds(0, 2), 1 - fsdp], gout_x, out_boxes, 0, twin)
    out_cross.start()

    for number in range(blocks):
        carry = fold(blocks + number, number, none, diagonal=True)
        grad_key, grad_value = lax.fori_loop(
            number + 1, blocks, functools.partial(fold, blocks + number), carry
        )
        columns = pl.ds(number * BLOCK, BLOCK)
        gproj_t[pl.ds(0, HEAD_DIM), columns] = grad_key.T[:HEAD_DIM]
        gproj_t[pl.ds(HEAD_DIM, HEAD_DIM), columns] = grad_value.T
    scatter_y.finish()
    normed_load = pltpu.make_async_copy(r.normed, part, mail.local())
    normed_load.start()
    hidden_o[...] = (middle[...] + total[...]).astype(LOW)

    square_boxes = mail.take(SQUARE)
    in_local = mail.local()
    in_square = []
    for number in range(2):
        spot = pl.ds(number * width, width)
        in_cross[0, number].wait_recv()
        mine = gin.at[half, spot, fsdp]
        add_blocks(mine, mine, gin_x.at[half, spot], width)

    @pl.when(half == 0)
    def _():
        for number in range(blocks):
            returns[number].wait_recv()
            columns = pl.ds(number * BLOCK, BLOCK)
            gproj_t[:, columns] = gproj_t[:, columns] + back_in[number].astype(f32)

    @pl.when(half == 1)
    def _():
        for number in range(blocks):
            returns[number].wait_send()

    factor = HEAD_DIM ** (-0.5)
    for number in range(blocks):
        columns = pl.ds(number * BLOCK, BLOCK)
        cos_b, sin_b = cosine[:, columns], -sine[:, columns]
        pieces = []
        for head in range(2):
            dq = dq_s[number, :, head * BLOCK : (head + 1) * BLOCK]
            pieces.append(turn_head(dq * factor, cos_b, sin_b))
        dk = gproj_t[pl.ds(0, HEAD_DIM), columns]
        pieces.append(turn_head(dk * factor, cos_b, sin_b))
        pieces.append(gproj_t[pl.ds(HEAD_DIM, HEAD_DIM), columns])
        gproj_r[columns, :] = jnp.concatenate(pieces, axis=0).T.astype(LOW)

    cross_boxes, plane_boxes = mail.take(SEQ), mail.take(SEQ)
    share = D // FLEET
    normed_load.wait()
    for number in range(4):
        left = part[:, :, pl.ds(number * (D // 4), D // 4)].reshape(rows_all, D // 4)
        grad = dot32(left, gproj_r[...], ((0,), (0,)))
        gmix[pl.ds(number * 4, 4)] = grad.astype(LOW).reshape(4, 2, share, 4 * HEAD_DIM)
    order = list(range(SEQ - 1, -1, -1))
    cross = {}
    for bits in order:
        target = flip(place.seq, bits)
        cross[bits] = send(gmix.at[target, 1 - fsdp], crossed.at[target], cross_boxes, bits, twin)
        cross[bits].start()
    scatter_n = SquareScatter(place, part, total, buffers_b, mail.take(10), SCATTER_TOP)
    for number, bits in enumerate(scatter_n.order):
        chip = lax.div(place.slot(bits), 2)
        rows = pl.ds(pl.multiple_of(chip * 2 * ROWS, 2 * ROWS), 2 * ROWS)
        grad = dot32(gproj_r[rows, :], mix[...].reshape(D, 4 * HEAD_DIM), ((1,), (1,)))
        part[pl.ds(chip * 2, 2)] = grad.astype(LOW).reshape(2, ROWS, D)
        scatter_n.cores[number].start()
    scatter_n.pair_up()

    def out_copy(number):
        owner = member * 2 + number
        remote = pltpu.make_async_remote_copy(
            src_ref=gout.at[number, fsdp],
            dst_ref=out_got.at[half],
            send_sem=owner_boxes[0].at[number],
            recv_sem=owner_boxes[1].at[half],
            device_id=(owner, fsdp),
            device_id_type=MESH,
        )
        local = pltpu.make_async_copy(gout.at[number, fsdp], out_got.at[half], out_local)
        return remote, local, owner == place.seq

    out_cross.wait_recv()
    for number in range(2):
        mine = gout.at[number, fsdp]
        add_rows(mine, mine, gout_x.at[number], 0, share)
        remote, local, own_block = out_copy(number)
        pl.when(own_block)(local.start)
        pl.when(jnp.logical_not(own_block))(remote.start)
    plane = {}
    for bits in order:
        target = flip(place.seq, bits)
        cross[bits].wait_recv()
        mine = gmix.at[target, fsdp]
        goal = mine if bits else landed_mix.at[place.seq]
        add_rows(goal, mine, crossed.at[target], 0, share)
        if bits:
            plane[bits] = send(
                mine, landed_mix.at[place.seq], plane_boxes, bits, (target, fsdp)
            )
            plane[bits].start()
        if bits == SQUARE:
            scatter_n.relay()
    for number in range(2):
        spot = pl.ds(number * width, width)
        in_far[number].wait_recv()
        mine = gin.at[half, spot, fsdp]
        add_blocks(mine, mine, gin_z.at[spot], width)
    in_keep = pltpu.make_async_copy(gin.at[half, member, fsdp], in_o.at[member], in_local)
    in_keep.start()
    for bits in range(1, SQUARE):
        copy = send(
            gin.at[half, place.slot(bits), fsdp],
            in_o.at[member],
            square_boxes,
            bits,
            place.peer(bits),
        )
        copy.start()
        in_square.append(copy)
    down_cross[0].wait_recv()
    down_own = gdown.at[half, fsdp]
    add_rows(down_own, down_own, gdown_x.at[half], 0, units // 4)
    scatter_n.finish()
    gain_attn, grad_norm = norm_back(total[...], tok[...].astype(f32), gain[0:1, :D])
    gain_v[0:1, :D] = gain_attn
    tokens_o[...] = grad_mid[...] + grad_norm
    gain_boxes, sum_boxes = mail.take(FLEET), mail.take(FLEET)
    gain_copies = []
    for step in range(1, FLEET):
        rank, device = place.after(step)
        lane = pl.multiple_of(lax.div(rank * share, 128) * 128, 128)
        gain_copies.append(
            send(
                gain_v.at[:, pl.ds(lane, 256)], gain_w.at[place.rank], gain_boxes, step, device
            )
        )
        gain_copies[-1].start()
    lane = pl.multiple_of(lax.div(place.rank * share, 128) * 128, 128)
    gain_w[place.rank] = gain_v[:, pl.ds(lane, 256)]
    for bits in range(1, SEQ):
        plane[bits].wait_recv()
    wide, key_width = 2 * HEAD_DIM, KV_HEADS * HEAD_DIM
    sums_mix = [
        landed_mix[number].astype(f32) + landed_mix[number + SQUARE].astype(f32)
        for number in range(SQUARE)
    ]
    for number in range(SQUARE // 2):
        block = jnp.concatenate([v[:, :wide] for v in sums_mix[2 * number : 2 * number + 2]], 1)
        mix_o[:, number * 2 * wide : (number + 1) * 2 * wide] = block
    for kind in range(2):
        lanes = slice(wide + kind * HEAD_DIM, wide + (kind + 1) * HEAD_DIM)
        for number in range(SQUARE // 4):
            block = jnp.concatenate([v[:, lanes] for v in sums_mix[4 * number : 4 * number + 4]], 1)
            start = D + kind * key_width + number * 2 * wide
            mix_o[:, start : start + 2 * wide] = block
    for number in range(2):
        source = number * SQUARE + lax.div(place.seq, 2)
        arrival = pltpu.make_async_remote_copy(
            src_ref=gout.at[0, 0],
            dst_ref=out_got.at[number],
            send_sem=owner_boxes[0].at[number],
            recv_sem=owner_boxes[1].at[number],
            device_id=(source, fsdp),
            device_id_type=MESH,
        )
        pl.when(source != place.seq)(arrival.wait_recv)
        remote, local, own_block = out_copy(number)
        pl.when(own_block)(local.wait)
    add_rows(out_o, out_got.at[0], out_got.at[1], 0, share)
    down_far.wait_recv()
    add_rows(down_o, down_own, gdown_z, 0, units // 4)
    squares = square_sum(mix_o) + square_sum(out_o) + square_sum(down_o)
    in_keep.wait()
    for copy in in_square:
        copy.wait_recv()
    squares = squares + square_sum(in_o)
    for copy in gain_copies:
        copy.wait()
    window = gain_w[0]
    for rank in range(1, FLEET):
        window = window + gain_w[rank]
    start = lax.rem(place.rank * share, 128)
    own_gain = jnp.zeros((8, 128), f32)
    for lane in range(0, 128, 16):
        own_gain = jnp.where(start == lane, window[:, lane : lane + 128], own_gain)
    at = lax.broadcasted_iota(jnp.int32, own_gain.shape, 1)
    own_gain = jnp.where(at < share, own_gain, 0.0)
    gain_o[...] = own_gain
    squares = squares + jnp.sum(own_gain * own_gain)
    mine_s[...] = jnp.broadcast_to(squares, mine_s.shape)
    sums[place.rank] = mine_s[...]
    copies = []
    for step in range(1, FLEET):
        rank, device = place.after(step)
        copies.append(send(mine_s, sums.at[place.rank], sum_boxes, step, device))
        copies[-1].start()
    for copy in copies:
        copy.wait()
    result = sums[0]
    for rank in range(1, FLEET):
        result = result + sums[rank]
    total_o[...] = result
    for copy in list(in_cross.values()) + list(in_far.values()) + list(down_cross.values()):
        copy.wait_send()
    for copy in [down_far, out_cross] + in_square + list(cross.values()) + list(plane.values()):
        copy.wait_send()
    for number in range(2):
        remote, local, own_block = out_copy(number)
        pl.when(jnp.logical_not(own_block))(remote.wait_send)


class Refs:
    def __init__(self, **refs):
        self.__dict__.update(refs)


ARGUMENTS = [
    "lengths",
    "frequency",
    "tok",
    "gain_in",
    "mix_in",
    "out_in",
    "inn_in",
    "down_in",
    "cot",
]
RESULTS = [
    "hidden_o",
    "tokens_o",
    "mix_o",
    "out_o",
    "in_o",
    "down_o",
    "gain_o",
    "total_o",
    "normed",
]


def scratch_of():
    share, unit = D // FLEET, FF // FLEET
    blocks = KEYS // BLOCK
    low = lambda *size: pltpu.VMEM(size, LOW)
    full = lambda *size: pltpu.VMEM(size, jnp.float32)
    scratch = {
        "mix": low(FLEET, share, 4 * HEAD_DIM),
        "out": low(2, 2, share, D),
        "inn": low(2, SQUARE, 2, share, 8 * unit),
        "down": low(2, 2, unit, D),
        "gain": full(16, D + 128),
        "pair": low(2 * blocks, 2 * HEAD_DIM, BLOCK),
        "att": full(2 * HEAD_DIM, KEYS),
        "att_low": low(2 * HEAD_DIM, KEYS),
        "keys": low(2 * KEYS, 128),
        "values": low(2 * KEYS, HEAD_DIM),
        "cosine": full(HEAD_DIM // 2, KEYS),
        "sine": full(HEAD_DIM // 2, KEYS),
        "tok_all": low(SQUARE, ROWS, D),
        "two_all": low(SQUARE, ROWS, D),
        "cot_all": low(SQUARE, ROWS, D),
        "two": low(ROWS, D),
        "gains": low(FLEET, 16, 256),
        "query_c": low(blocks, 128, 2 * BLOCK),
        "query_r": low(blocks, 2 * BLOCK, 128),
        "grad_c": low(blocks, HEAD_DIM, 2 * BLOCK),
        "grad_r": low(blocks, 2 * BLOCK, HEAD_DIM),
        "level_s": full(blocks, 8, 2 * BLOCK),
        "shift_s": full(blocks, 8, 2 * BLOCK),
        "top_s": full(8, 2 * BLOCK),
        "sum_s": full(8, 2 * BLOCK),
        "dq_s": full(blocks, HEAD_DIM, 2 * BLOCK),
        "middle": full(ROWS, D),
        "total": full(ROWS, D),
        "grad_mid": full(ROWS, D),
        "part": low(SQUARE, ROWS, D),
        "hidden": low(KEYS, 4 * unit),
        "gate_grad": low(KEYS, 8 * unit),
        "gin": low(2, SQUARE, 2, share, 8 * unit),
        "gin_x": low(2, SQUARE, share, 8 * unit),
        "gin_z": low(SQUARE, share, 8 * unit),
        "gdown": low(2, 2, unit, D),
        "gdown_x": low(2, unit, D),
        "gdown_z": low(unit, D),
        "gout": low(2, 2, share, D),
        "gout_x": low(2, share, D),
        "out_got": low(2, share, D),
        "back": low(blocks, 2 * HEAD_DIM, BLOCK),
        "back_in": low(blocks, 2 * HEAD_DIM, BLOCK),
        "gproj_t": full(2 * HEAD_DIM, KEYS),
        "gproj_r": low(KEYS, 4 * HEAD_DIM),
        "gmix": low(SEQ, 2, share, 4 * HEAD_DIM),
        "crossed": low(SEQ, share, 4 * HEAD_DIM),
        "landed_mix": low(SEQ, share, 4 * HEAD_DIM),
        "gain_v": full(8, D + 128),
        "gain_w": full(FLEET, 8, 256),
        "sums": full(FLEET, 8, 128),
        "mine_s": full(8, 128),
        "sends": pltpu.SemaphoreType.DMA((360,)),
        "receives": pltpu.SemaphoreType.DMA((360,)),
        "locals": pltpu.SemaphoreType.DMA((24,)),
    }
    for set_name in "ab":
        for number, buffer in enumerate(SquareScatter.buffers(D)):
            scratch[set_name + str(number)] = buffer
    return scratch


def layer_kernel(names, *refs):
    r = Refs(**dict(zip(names, refs, strict=True)))
    r.buffers_a = (r.a0, r.a1, r.a2, r.a3)
    r.buffers_b = (r.b0, r.b1, r.b2, r.b3)
    place = Place()
    mail = Mailbox(r.sends, r.receives, r.locals)
    keep, drain = forward_part(place, mail, r)
    backward_part(place, mail, r, keep)
    drain()


def layer(*arrays):
    shape = jax.ShapeDtypeStruct
    f32 = jnp.float32
    share, unit = D // FLEET, FF // FLEET
    scratch = scratch_of()
    names = ARGUMENTS + RESULTS + list(scratch)
    return pl.pallas_call(
        functools.partial(layer_kernel, names),
        out_shape=(
            shape((ROWS, D), LOW),
            shape((ROWS, D), f32),
            shape((share, 8 * 4 * HEAD_DIM), f32),
            shape((share, D), f32),
            shape((SQUARE, share, 8 * unit), LOW),
            shape((unit, D), f32),
            shape((8, 128), f32),
            shape((8, 128), f32),
            shape((SQUARE, ROWS, D), LOW),
        ),
        in_specs=[pl.BlockSpec(memory_space=pltpu.SMEM)] + [VMEM] * 3 + [ANY] * 4 + [VMEM],
        out_specs=(VMEM,) * 8 + (ANY,),
        scratch_shapes=list(scratch.values()),
        compiler_params=pltpu.CompilerParams(
            collective_id=0, has_side_effects=True, vmem_limit_bytes=63 << 20
        ),
        name="layer",
    )(*arrays)


def adam_kernel(totals, *refs):
    scale = CLIP_NORM / jnp.maximum(jnp.sqrt(totals[0:1, 0:1]), CLIP_NORM)
    inputs, outputs = refs[2:18], refs[20:]
    for source, target in zip(refs[:2], refs[18:20], strict=True):
        target[...] = source[...]
    for kind, rate in enumerate((LEARN_RATE, OUT_RATE, LEARN_RATE, LEARN_RATE)):
        weight, first, second, grad = inputs[4 * kind : 4 * kind + 4]
        grad_o, new_o, first_o, second_o, copy_o = outputs[5 * kind : 5 * kind + 5]
        width = weight.shape[1] // SQUARE if grad.ndim == 3 else weight.shape[1]
        for number in range(weight.shape[1] // width):
            lanes = slice(number * width, (number + 1) * width)
            value = (grad[number] if grad.ndim == 3 else grad[...]).astype(jnp.float32)
            new, moment, square = adam_update(
                weight[:, lanes], first[:, lanes], second[:, lanes], value, scale, rate
            )
            grad_o[:, lanes] = value
            new_o[:, lanes] = new
            first_o[:, lanes] = moment
            second_o[:, lanes] = square
            copy_o[:, lanes] = new.astype(LOW)


def adam_all(totals, passing, kinds):
    steps = 4
    shape = jax.ShapeDtypeStruct
    in_specs, out_specs, out_shapes = [pl.BlockSpec(totals.shape, lambda i: (0, 0))], [], []
    for array in passing:
        spec = pl.BlockSpec((array.shape[0], array.shape[1] // steps), lambda i: (0, i))
        in_specs.append(spec)
        out_specs.append(spec)
        out_shapes.append(shape(array.shape, array.dtype))
    for weight, _, _, grad in kinds:
        spec = pl.BlockSpec((weight.shape[0], weight.shape[1] // steps), lambda i: (0, i))
        in_specs += [spec] * 3
        if grad.ndim == 3:
            block = (grad.shape[0], grad.shape[1], grad.shape[2] // steps)
            in_specs.append(pl.BlockSpec(block, lambda i: (0, 0, i)))
        else:
            in_specs.append(spec)
        out_specs += [spec] * 5
        out_shapes += [shape(weight.shape, jnp.float32)] * 4 + [shape(weight.shape, LOW)]
    return pl.pallas_call(
        adam_kernel,
        grid=(steps,),
        out_shape=out_shapes,
        in_specs=in_specs,
        out_specs=out_specs,
        compiler_params=pltpu.CompilerParams(vmem_limit_bytes=63 << 20),
        name="adam",
    )(totals, *passing, *[array for kind in kinds for array in kind])


def local_squares(
    tokens,
    cotangent,
    lengths,
    mix_weight,
    out_weight,
    in_weight,
    down_weight,
    norm_gains,
    mix_first,
    out_first,
    in_first,
    down_first,
    norm_first,
    mix_second,
    out_second,
    in_second,
    down_second,
    norm_second,
):
    f32 = jnp.float32
    fsdp = lax.axis_index("fsdp")
    seq = lax.axis_index("seq")
    frequency = ROPE_BASE ** (-jnp.arange(HEAD_DIM // 2, dtype=f32) * 2.0 / HEAD_DIM)

    wide = 2 * HEAD_DIM
    key_width = KV_HEADS * HEAD_DIM
    mix_low = mix_weight[0].astype(LOW)
    share = mix_low.shape[0]
    mix_blocks = jnp.concatenate(
        [
            mix_low[:, :D].reshape(share, SQUARE, wide),
            mix_low[:, D : D + key_width].reshape(share, SQUARE, HEAD_DIM),
            mix_low[:, D + key_width :].reshape(share, SQUARE, HEAD_DIM),
        ],
        axis=2,
    ).transpose(1, 0, 2)
    unit = FF // FLEET
    in_blocks = (
        in_weight[0]
        .astype(LOW)
        .reshape(share, 2, 2, SQUARE, 2 * unit)
        .transpose(3, 0, 1, 2, 4)
        .reshape(SQUARE, share, 8 * unit)
    )
    out_low = out_weight[0].astype(LOW)
    down_low = down_weight[0].astype(LOW)
    rank = seq * 2 + fsdp
    gain_block = lax.dynamic_update_slice(
        jnp.zeros((16, 256), LOW), norm_gains[0].astype(LOW), (0, rank * share % 128)
    )
    hidden_out, grad_tokens, mix_got, out_got, in_got, down_got, gain_got, totals, _ = layer(
        lengths,
        frequency[:, None],
        tokens,
        gain_block,
        mix_blocks,
        out_low,
        in_blocks,
        down_low,
        cotangent,
    )

    norm_grad = gain_got[None, :2, :share]
    grad_norm = jnp.sqrt(totals[0, 0])
    clip_scale = CLIP_NORM / jnp.maximum(grad_norm, CLIP_NORM)
    hidden_out, grad_tokens, *updates = adam_all(
        totals,
        (hidden_out, grad_tokens),
        [
            (mix_weight[0], mix_first[0], mix_second[0], mix_got),
            (out_weight[0], out_first[0], out_second[0], out_got),
            (in_weight[0], in_first[0], in_second[0], in_got),
            (down_weight[0], down_first[0], down_second[0], down_got),
        ],
    )
    new, moment, square = adam_update(
        norm_gains, norm_first, norm_second, norm_grad, clip_scale, GAIN_RATE
    )
    results = [hidden_out, grad_tokens, grad_norm] + [array[None] for array in updates]
    return tuple(results + [norm_grad, new, moment, square, new.astype(LOW)])


def solution(mesh):
    squares = mesh.shape["seq"] == SEQ and mesh.shape["fsdp"] == 2
    return jax.shard_map(
        local_squares if squares else local,
        mesh=mesh,
        in_specs=(
            P(("seq", "fsdp"), None),
            P(("seq", "fsdp"), None),
            P(),
            P(None, ("seq", "fsdp"), None),
            P(None, ("seq", "fsdp"), None),
            P(None, ("seq", "fsdp"), None),
            P(None, ("seq", "fsdp"), None),
            P(None, None, ("seq", "fsdp")),
            P(None, ("seq", "fsdp"), None),
            P(None, ("seq", "fsdp"), None),
            P(None, ("seq", "fsdp"), None),
            P(None, ("seq", "fsdp"), None),
            P(None, None, ("seq", "fsdp")),
            P(None, ("seq", "fsdp"), None),
            P(None, ("seq", "fsdp"), None),
            P(None, ("seq", "fsdp"), None),
            P(None, ("seq", "fsdp"), None),
            P(None, None, ("seq", "fsdp")),
        ),
        out_specs=(
            P(("seq", "fsdp"), None),
            P(("seq", "fsdp"), None),
            P(),
            P(None, ("seq", "fsdp"), None),
            P(None, ("seq", "fsdp"), None),
            P(None, ("seq", "fsdp"), None),
            P(None, ("seq", "fsdp"), None),
            P(None, ("seq", "fsdp"), None),
            P(None, ("seq", "fsdp"), None),
            P(None, ("seq", "fsdp"), None),
            P(None, ("seq", "fsdp"), None),
            P(None, ("seq", "fsdp"), None),
            P(None, ("seq", "fsdp"), None),
            P(None, ("seq", "fsdp"), None),
            P(None, ("seq", "fsdp"), None),
            P(None, ("seq", "fsdp"), None),
            P(None, ("seq", "fsdp"), None),
            P(None, ("seq", "fsdp"), None),
            P(None, ("seq", "fsdp"), None),
            P(None, ("seq", "fsdp"), None),
            P(None, ("seq", "fsdp"), None),
            P(None, ("seq", "fsdp"), None),
            P(None, ("seq", "fsdp"), None),
            P(None, None, ("seq", "fsdp")),
            P(None, None, ("seq", "fsdp")),
            P(None, None, ("seq", "fsdp")),
            P(None, None, ("seq", "fsdp")),
            P(None, None, ("seq", "fsdp")),
        ),
        check_vma=False,
    )
```

```python
import functools

import jax
import jax.numpy as jnp
from jax import lax
from jax.experimental import pallas as pl
from jax.experimental.pallas import tpu as pltpu
from jax.sharding import PartitionSpec as P

D = 1536
HEADS = 16
KV_HEADS = 8
HEAD_DIM = 96
FF = 4096
LAYERS = 1
STEP_NUMBER = 10


EPS_NORM = 1e-05
ROPE_BASE = 100000.0
FLOOR_SCORE = -1e30
LEARN_RATE = 0.05
OUT_RATE = 0.2
GAIN_RATE = 2.0
BETA_ONE = 0.9
BETA_TWO = 0.99
EPS_ADAM = 1e-08
WEIGHT_DECAY = 0.1
CLIP_NORM = 1.0


def doc_layout(places, doc_lens):
    doc_ends = jnp.cumsum(doc_lens)
    passed = (places[:, None] >= doc_ends[None, :]).astype(jnp.int32)
    segment = jnp.sum(passed, axis=1)
    offset = jnp.sum(passed * doc_lens[None, :], axis=1)
    return (segment, places - offset)


def rotate(vectors, places, direction):
    half_dim = vectors.shape[-1] // 2
    inverse = ROPE_BASE ** (-jnp.arange(half_dim, dtype=jnp.float32) * 2.0 / vectors.shape[-1])
    angles = places.astype(jnp.float32)[:, None] * inverse[None, :]
    cosine = jnp.cos(angles)[:, None, :]
    sine_term = direction * jnp.sin(angles)[:, None, :]
    former = vectors[..., :half_dim]
    latter = vectors[..., half_dim:]
    return jnp.concatenate(
        [former * cosine - latter * sine_term, latter * cosine + former * sine_term], axis=-1
    )


def normalize(values, gain):
    scale_rows = lax.rsqrt(jnp.mean(values * values, axis=-1, keepdims=True) + EPS_NORM)
    unit_rows = values * scale_rows
    return (unit_rows * gain, unit_rows, scale_rows)


def norm_backward(grad_normed, unit_rows, scale_rows, gain):
    grad_gain = jnp.sum(grad_normed * unit_rows, axis=0)
    grad_unit = grad_normed * gain
    grad_values = scale_rows * (
        grad_unit - unit_rows * jnp.mean(grad_unit * unit_rows, axis=-1, keepdims=True)
    )
    return (grad_gain, grad_values)


def masked_scores(queries, key_block, first_key, query_places, query_segment, doc_lens):
    block_rows = key_block.shape[0]
    key_places = first_key + jnp.arange(block_rows, dtype=jnp.int32)
    key_segment, unused_places = doc_layout(key_places, doc_lens)
    allowed = (query_segment[:, None] == key_segment[None, :]) & (
        key_places[None, :] <= query_places[:, None]
    )
    key_heads = key_block.reshape(block_rows, KV_HEADS, HEAD_DIM)
    raw_scores = jnp.einsum(
        "qkgd,skd->qkgs", queries, key_heads, preferred_element_type=jnp.float32
    ) * HEAD_DIM ** (-0.5)
    return (jnp.where(allowed[:, None, None, :], raw_scores, FLOOR_SCORE), allowed)


def fold_block(carry, key_block, value_block, first_key, setting):
    queries, query_places, query_segment, doc_lens = setting
    running, totals, accumulated = carry
    block_rows = key_block.shape[0]
    scores, allowed = masked_scores(
        queries, key_block, first_key, query_places, query_segment, doc_lens
    )
    newest = jnp.maximum(running, jnp.max(scores, axis=-1))
    factor = jnp.exp(running - newest)
    weights = jnp.where(allowed[:, None, None, :], jnp.exp(scores - newest[..., None]), 0.0)
    totals = totals * factor + jnp.sum(weights, axis=-1)
    value_heads = value_block.reshape(block_rows, KV_HEADS, HEAD_DIM)
    accumulated = accumulated * factor[..., None] + jnp.einsum(
        "qkgs,skd->qkgd",
        weights.astype(jnp.bfloat16),
        value_heads,
        preferred_element_type=jnp.float32,
    )
    return (newest, totals, accumulated)


def fold_piece(carry, key_rows, value_rows, start, setting):
    total_rows = key_rows.shape[0]
    block_rows = 512

    def step(inner_state, number):
        first_key = start + number * block_rows
        key_block = lax.dynamic_slice_in_dim(key_rows, number * block_rows, block_rows, 0)
        value_block = lax.dynamic_slice_in_dim(value_rows, number * block_rows, block_rows, 0)
        state_out = fold_block(inner_state, key_block, value_block, first_key, setting)
        return (state_out, None)

    carry, unused_out = lax.scan(step, carry, jnp.arange(total_rows // block_rows, dtype=jnp.int32))
    return carry


def fetch_layer(mix_weight, out_weight, norm_gains, in_weight, down_weight, layer_index):
    mix_full, out_full, gain_full, in_full, down_full = (
        lax.all_gather(
            mix_weight[layer_index].astype(jnp.bfloat16), ("seq", "fsdp"), axis=0, tiled=True
        ),
        lax.all_gather(
            out_weight[layer_index].astype(jnp.bfloat16), ("seq", "fsdp"), axis=0, tiled=True
        ),
        lax.all_gather(
            norm_gains[layer_index].astype(jnp.bfloat16), ("seq", "fsdp"), axis=1, tiled=True
        ),
        lax.all_gather(
            in_weight[layer_index].astype(jnp.bfloat16), ("seq", "fsdp"), axis=0, tiled=True
        ),
        lax.all_gather(
            down_weight[layer_index].astype(jnp.bfloat16), ("seq", "fsdp"), axis=0, tiled=True
        ),
    )
    return ((mix_full, out_full, gain_full), (in_full, down_full))


def layer_forward(stream, attn_set, mlp_set, context):
    query_places, query_segment, positions, keep_rows, doc_lens = context
    mix_full, out_full, gain_full = attn_set
    in_full, down_full = mlp_set
    row_count = stream.shape[0]
    key_width = KV_HEADS * HEAD_DIM
    groups_per = HEADS // KV_HEADS
    gain_attn = gain_full[0].astype(jnp.float32)
    gain_mlp = gain_full[1].astype(jnp.float32)
    normed, unit_attn, scale_attn = normalize(stream, gain_attn)
    normed_low = normed.astype(jnp.bfloat16)
    projected = jnp.dot(normed_low, mix_full, preferred_element_type=jnp.float32)
    queries = (
        rotate(projected[:, :D].reshape(row_count, HEADS, HEAD_DIM), positions, 1.0)
        .astype(jnp.bfloat16)
        .reshape(row_count, KV_HEADS, groups_per, HEAD_DIM)
    )
    keys_low = (
        rotate(
            projected[:, D : D + key_width].reshape(row_count, KV_HEADS, HEAD_DIM), positions, 1.0
        )
        .astype(jnp.bfloat16)
        .reshape(row_count, key_width)
    )
    values_low = projected[:, D + key_width :].astype(jnp.bfloat16)
    setting = (queries, query_places, query_segment, doc_lens)
    key_all, value_all = (
        lax.all_gather(keys_low, "seq", axis=0, tiled=True),
        lax.all_gather(values_low, "seq", axis=0, tiled=True),
    )
    start_carry = (
        jnp.full((row_count, KV_HEADS, groups_per), FLOOR_SCORE, jnp.float32),
        jnp.zeros((row_count, KV_HEADS, groups_per), jnp.float32),
        jnp.zeros((row_count, KV_HEADS, groups_per, HEAD_DIM), jnp.float32),
    )
    running, totals, accumulated = fold_piece(start_carry, key_all, value_all, 0, setting)
    log_total = running + jnp.log(totals)
    attended = (accumulated / totals[..., None]).reshape(row_count, D) * keep_rows
    attended_low = attended.astype(jnp.bfloat16)
    middle = stream + jnp.dot(attended_low, out_full, preferred_element_type=jnp.float32)
    normed_two, unit_mlp, scale_mlp = normalize(middle, gain_mlp)
    normed_two_low = normed_two.astype(jnp.bfloat16)
    gate_up = jnp.dot(normed_two_low, in_full, preferred_element_type=jnp.float32)
    hidden_low = (jax.nn.silu(gate_up[:, :FF]) * gate_up[:, FF:]).astype(jnp.bfloat16)
    result = middle + jnp.dot(hidden_low, down_full, preferred_element_type=jnp.float32)
    kv_saved = (key_all, value_all)
    saved = (
        normed_low,
        unit_attn,
        scale_attn,
        queries,
        keys_low,
        values_low,
        log_total,
        attended,
        attended_low,
        unit_mlp,
        scale_mlp,
        normed_two_low,
        gate_up,
        hidden_low,
        kv_saved,
    )
    return (result, saved)


def layer_backward(grad_stream, saved, attn_set, mlp_set, context):
    query_places, query_segment, positions, keep_rows, doc_lens = context
    mix_full, out_full, gain_full = attn_set
    in_full, down_full = mlp_set
    (
        normed_low,
        unit_attn,
        scale_attn,
        queries,
        keys_low,
        values_low,
        log_total,
        attended,
        attended_low,
        unit_mlp,
        scale_mlp,
        normed_two_low,
        gate_up,
        hidden_low,
        kv_saved,
    ) = saved
    row_count = grad_stream.shape[0]
    key_width = KV_HEADS * HEAD_DIM
    groups_per = HEADS // KV_HEADS
    score_scale = HEAD_DIM ** (-0.5)
    gain_attn = gain_full[0].astype(jnp.float32)
    gain_mlp = gain_full[1].astype(jnp.float32)
    grad_branch = grad_stream.astype(jnp.bfloat16)
    grad_down = jnp.einsum("nf,nd->fd", hidden_low, grad_branch, preferred_element_type=jnp.float32)
    grad_hidden = jnp.einsum(
        "nd,fd->nf", grad_branch, down_full, preferred_element_type=jnp.float32
    )
    gate_part = gate_up[:, :FF]
    up_part = gate_up[:, FF:]
    sigmoid_gate = jax.nn.sigmoid(gate_part)
    grad_gate = grad_hidden * up_part * sigmoid_gate * (1.0 + gate_part * (1.0 - sigmoid_gate))
    grad_up = grad_hidden * gate_part * sigmoid_gate
    grad_gate_up = jnp.concatenate([grad_gate, grad_up], axis=1).astype(jnp.bfloat16)
    grad_in = jnp.einsum(
        "nd,nf->df", normed_two_low, grad_gate_up, preferred_element_type=jnp.float32
    )
    grad_normed_two = jnp.einsum(
        "nf,df->nd", grad_gate_up, in_full, preferred_element_type=jnp.float32
    )
    mlp_part = (
        lax.psum_scatter(grad_in, ("seq", "fsdp"), scatter_dimension=0, tiled=True),
        lax.psum_scatter(grad_down, ("seq", "fsdp"), scatter_dimension=0, tiled=True),
    )
    grad_gain_mlp, grad_middle_norm = norm_backward(grad_normed_two, unit_mlp, scale_mlp, gain_mlp)
    grad_middle = grad_stream + grad_middle_norm
    attn_branch = grad_middle.astype(jnp.bfloat16)
    grad_out = jnp.einsum(
        "nd,ne->de", attended_low, attn_branch, preferred_element_type=jnp.float32
    )
    grad_attended = (
        jnp.einsum("ne,de->nd", attn_branch, out_full, preferred_element_type=jnp.float32)
        * keep_rows
    )
    grad_heads = grad_attended.astype(jnp.bfloat16).reshape(
        row_count, KV_HEADS, groups_per, HEAD_DIM
    )
    row_delta = jnp.sum(
        grad_heads.astype(jnp.float32)
        * attended.reshape(row_count, KV_HEADS, groups_per, HEAD_DIM),
        axis=-1,
    )
    key_all, value_all = kv_saved
    total_keys = key_all.shape[0]
    block_rows = 512

    def back_step(grad_queries, number):
        first_key = number * block_rows
        key_block = lax.dynamic_slice_in_dim(key_all, first_key, block_rows, 0)
        value_block = lax.dynamic_slice_in_dim(value_all, first_key, block_rows, 0)
        scores, allowed = masked_scores(
            queries, key_block, first_key, query_places, query_segment, doc_lens
        )
        soft_weight = jnp.where(
            allowed[:, None, None, :], jnp.exp(scores - log_total[..., None]), 0.0
        )
        value_heads = value_block.reshape(block_rows, KV_HEADS, HEAD_DIM)
        key_heads = key_block.reshape(block_rows, KV_HEADS, HEAD_DIM)
        grad_weight = jnp.einsum(
            "qkgd,skd->qkgs", grad_heads, value_heads, preferred_element_type=jnp.float32
        )
        grad_score = (soft_weight * (grad_weight - row_delta[..., None])).astype(jnp.bfloat16)
        state_out = grad_queries + jnp.einsum(
            "qkgs,skd->qkgd", grad_score, key_heads, preferred_element_type=jnp.float32
        )
        grad_key = (
            jnp.einsum("qkgs,qkgd->skd", grad_score, queries, preferred_element_type=jnp.float32)
            * score_scale
        )
        grad_value = jnp.einsum(
            "qkgs,qkgd->skd",
            soft_weight.astype(jnp.bfloat16),
            grad_heads,
            preferred_element_type=jnp.float32,
        )
        return (
            state_out,
            jnp.concatenate(
                [
                    grad_key.reshape(block_rows, key_width),
                    grad_value.reshape(block_rows, key_width),
                ],
                axis=1,
            ),
        )

    start_grad = jnp.zeros((row_count, KV_HEADS, groups_per, HEAD_DIM), jnp.float32)
    grad_queries, pair_blocks = lax.scan(
        back_step, start_grad, jnp.arange(total_keys // block_rows, dtype=jnp.int32)
    )
    pair_terms = pair_blocks.reshape(total_keys, 2 * key_width)
    pair_sums = lax.psum_scatter(pair_terms, "seq", scatter_dimension=0, tiled=True)
    grad_rot_queries = rotate(
        (grad_queries * score_scale).reshape(row_count, HEADS, HEAD_DIM), positions, -1.0
    ).reshape(row_count, D)
    grad_rot_keys = rotate(
        pair_sums[:, :key_width].reshape(row_count, KV_HEADS, HEAD_DIM), positions, -1.0
    ).reshape(row_count, key_width)
    grad_projected = jnp.concatenate(
        [grad_rot_queries, grad_rot_keys, pair_sums[:, key_width:]], axis=1
    ).astype(jnp.bfloat16)
    grad_mix = jnp.einsum(
        "nd,nf->df", normed_low, grad_projected, preferred_element_type=jnp.float32
    )
    grad_normed = jnp.einsum(
        "nf,df->nd", grad_projected, mix_full, preferred_element_type=jnp.float32
    )
    grad_gain_attn, grad_input_norm = norm_backward(grad_normed, unit_attn, scale_attn, gain_attn)
    grad_gains = jnp.stack([grad_gain_attn, grad_gain_mlp])
    attn_part = (
        lax.psum_scatter(grad_mix, ("seq", "fsdp"), scatter_dimension=0, tiled=True),
        lax.psum_scatter(grad_out, ("seq", "fsdp"), scatter_dimension=0, tiled=True),
        lax.psum_scatter(grad_gains, ("seq", "fsdp"), scatter_dimension=1, tiled=True),
    )
    return (grad_middle + grad_input_norm, attn_part, mlp_part)


def adam_update(weight, first, second, grad, clip_scale, rate):
    clipped = grad * clip_scale
    first_new = BETA_ONE * first + (1.0 - BETA_ONE) * clipped
    second_new = BETA_TWO * second + (1.0 - BETA_TWO) * clipped * clipped
    first_hat = first_new / (1.0 - BETA_ONE**STEP_NUMBER)
    second_hat = second_new / (1.0 - BETA_TWO**STEP_NUMBER)
    updated = weight - rate * (
        first_hat / (jnp.sqrt(second_hat) + EPS_ADAM) + WEIGHT_DECAY * weight
    )
    return (updated, first_new, second_new)


def local(
    tokens,
    cotangent,
    lengths,
    mix_weight,
    out_weight,
    in_weight,
    down_weight,
    norm_gains,
    mix_first,
    out_first,
    in_first,
    down_first,
    norm_first,
    mix_second,
    out_second,
    in_second,
    down_second,
    norm_second,
):
    row_count = tokens.shape[0]
    group_index = lax.axis_index("fsdp")
    cycle_index = lax.axis_index("seq")
    doc_lens = lax.dynamic_index_in_dim(lengths, group_index, 0, keepdims=False)
    query_places = cycle_index * row_count + jnp.arange(row_count, dtype=jnp.int32)
    query_segment, positions = doc_layout(query_places, doc_lens)
    keep_rows = (query_segment < doc_lens.shape[0]).astype(jnp.float32)[:, None]
    context = (query_places, query_segment, positions, keep_rows, doc_lens)
    stream = tokens.astype(jnp.float32)
    layer_index = 0
    attn_set, mlp_set = fetch_layer(
        mix_weight, out_weight, norm_gains, in_weight, down_weight, layer_index
    )
    stream, saved = layer_forward(stream, attn_set, mlp_set, context)
    saved_list = [saved]
    weight_list = [(attn_set, mlp_set)]
    hidden_out = stream.astype(jnp.bfloat16)
    grad_stream = cotangent.astype(jnp.float32)
    attn_sums = [None] * LAYERS
    mlp_sums = [None] * LAYERS
    for layer_index in reversed(range(LAYERS)):
        attn_set, mlp_set = weight_list[layer_index]
        grad_stream, attn_part, mlp_part = layer_backward(
            grad_stream, saved_list[layer_index], attn_set, mlp_set, context
        )
        attn_sums[layer_index] = attn_part
        mlp_sums[layer_index] = mlp_part
    mix_grad = jnp.stack([attn_sums[0][0]])
    out_grad = jnp.stack([attn_sums[0][1]])
    norm_grad = jnp.stack([attn_sums[0][2]])
    in_grad = jnp.stack([mlp_sums[0][0]])
    down_grad = jnp.stack([mlp_sums[0][1]])
    squares = (
        jnp.sum(mix_grad * mix_grad)
        + jnp.sum(out_grad * out_grad)
        + jnp.sum(in_grad * in_grad)
        + jnp.sum(down_grad * down_grad)
        + jnp.sum(norm_grad * norm_grad)
    )
    total_squares = lax.psum(squares, ("seq", "fsdp"))
    grad_norm = jnp.sqrt(total_squares)
    clip_scale = CLIP_NORM / jnp.maximum(grad_norm, CLIP_NORM)
    mix_new, mix_moment, mix_square = adam_update(
        mix_weight, mix_first, mix_second, mix_grad, clip_scale, LEARN_RATE
    )
    out_new, out_moment, out_square = adam_update(
        out_weight, out_first, out_second, out_grad, clip_scale, OUT_RATE
    )
    in_new, in_moment, in_square = adam_update(
        in_weight, in_first, in_second, in_grad, clip_scale, LEARN_RATE
    )
    down_new, down_moment, down_square = adam_update(
        down_weight, down_first, down_second, down_grad, clip_scale, LEARN_RATE
    )
    norm_new, norm_moment, norm_square = adam_update(
        norm_gains, norm_first, norm_second, norm_grad, clip_scale, GAIN_RATE
    )
    return (
        hidden_out,
        grad_stream,
        grad_norm,
        mix_grad,
        mix_new,
        mix_moment,
        mix_square,
        mix_new.astype(jnp.bfloat16),
        out_grad,
        out_new,
        out_moment,
        out_square,
        out_new.astype(jnp.bfloat16),
        in_grad,
        in_new,
        in_moment,
        in_square,
        in_new.astype(jnp.bfloat16),
        down_grad,
        down_new,
        down_moment,
        down_square,
        down_new.astype(jnp.bfloat16),
        norm_grad,
        norm_new,
        norm_moment,
        norm_square,
        norm_new.astype(jnp.bfloat16),
    )


MESH = pl.DeviceIdType.MESH
ANY = pl.BlockSpec(memory_space=pl.ANY)
VMEM = pl.BlockSpec(memory_space=pltpu.VMEM)
LOW = jnp.bfloat16
SQUARE = 8
SEQ = 16
FLEET = 32
ROWS = 128
GATHER_TOP = 64
SCATTER_TOP = 64
DOC_KINDS = 6
KEYS = 1024
BLOCK = 256
CORE, NEAR_Y, NEAR_Z = 1, 2, 4
LOG2E = 1.4426950408889634
SCALE2 = HEAD_DIM ** (-0.5) * LOG2E
WALL = 2.0**100


def flip(value, bits):
    for bit in (1, 2, 4, 8):
        if bits & bit:
            value = value + bit - 2 * bit * (lax.rem(lax.div(value, bit), 2))
    return value


class Place:
    def __init__(self):
        self.seq = lax.axis_index("seq")
        self.fsdp = lax.axis_index("fsdp")
        self.member = lax.rem(self.seq, SQUARE)
        self.half = lax.div(self.seq, SQUARE)
        self.rank = self.seq * 2 + self.fsdp

    def peer(self, bits):
        return (flip(self.seq, bits), self.fsdp)

    def slot(self, bits):
        return flip(self.member, bits)

    def after(self, step):
        rank = lax.rem(self.rank + step, FLEET)
        return rank, (lax.div(rank, 2), lax.rem(rank, 2))

    def twin(self):
        return (self.seq, 1 - self.fsdp)


def send(src, dst, sems, index, device):
    return pltpu.make_async_remote_copy(
        src_ref=src,
        dst_ref=dst,
        send_sem=sems[0].at[index],
        recv_sem=sems[1].at[index],
        device_id=device,
        device_id_type=MESH,
    )


def greet(devices):
    barrier = pltpu.get_barrier_semaphore()
    for device in devices:
        pl.semaphore_signal(barrier, inc=1, device_id=device, device_id_type=MESH)
    pl.semaphore_wait(barrier, len(devices))


class SquareGather:
    COPIES = 10

    def __init__(self, place, src, out, sems, local_sem, top_rows):
        p, h = place, top_rows
        own, ys, zs = p.slot(0), p.slot(NEAR_Y), p.slot(NEAR_Z)
        ds = p.slot(NEAR_Y | NEAR_Z)
        to_y, to_z, to_c = p.peer(NEAR_Y), p.peer(NEAR_Z), p.peer(CORE)
        top, low = pl.ds(0, h), pl.ds(h, ROWS - h)
        self.local = pltpu.make_async_copy(src, out.at[own], local_sem)
        self.y0 = send(src.at[top], out.at[own, top], sems, 0, to_y)
        self.y1 = send(src.at[low], out.at[own, low], sems, 1, to_y)
        self.z1 = send(src.at[low], out.at[own, low], sems, 2, to_z)
        self.z0 = send(src.at[top], out.at[own, top], sems, 3, to_z)
        self.fz = send(out.at[ys, top], out.at[ys, top], sems, 4, to_z)
        self.fy = send(out.at[zs, low], out.at[zs, low], sems, 5, to_y)
        self.c = [
            send(src, out.at[own], sems, 6, to_c),
            send(out.at[ys], out.at[ys], sems, 7, to_c),
            send(out.at[zs], out.at[zs], sems, 8, to_c),
            send(out.at[ds], out.at[ds], sems, 9, to_c),
        ]

    def start(self):
        for copy in (self.y0, self.z1, self.y1, self.z0, self.c[0], self.local):
            copy.start()

    def relay(self):
        self.y0.wait_recv()
        self.fz.start()
        self.z1.wait_recv()
        self.fy.start()

    def share(self):
        self.y1.wait_recv()
        self.c[1].start()
        self.z0.wait_recv()
        self.c[2].start()

    def finish(self):
        self.fz.wait_recv()
        self.fy.wait_recv()
        self.c[3].start()
        for copy in self.c:
            copy.wait_recv()
        for copy in [self.y0, self.y1, self.z0, self.z1, self.fz, self.fy] + self.c:
            copy.wait_send()
        self.local.wait()


def mix_spread(place, mix, mix_o, plane_s, cross_s, local_sem):
    twin = (place.seq, 1 - place.fsdp)
    first = [
        send(
            mix.at[lax.rem(flip(place.seq, bits), SQUARE)],
            mix_o.at[place.rank],
            plane_s,
            bits,
            (flip(place.seq, bits), place.fsdp),
        )
        for bits in range(1, SEQ)
    ]
    second = []
    for bits in range(SEQ):
        spot = flip(place.seq, bits) * 2 + place.fsdp
        second.append(send(mix_o.at[spot], mix_o.at[spot], cross_s, bits, twin))
    local = pltpu.make_async_copy(mix.at[place.member], mix_o.at[place.rank], local_sem)
    return first, second, local


def add_rows(target, left, right, start, count):
    step = 16

    def body(number, _):
        rows = pl.ds(pl.multiple_of(start + number * step, step), step)
        target[rows] = (left[rows].astype(jnp.float32) + right[rows].astype(jnp.float32)).astype(
            target.dtype
        )
        return 0

    lax.fori_loop(0, count // step, body, 0)


class SquareScatter:
    def __init__(self, place, part, total, buffers, sems, top_rows):
        sib, away, passed, landed = buffers
        self.place, self.part, self.total = place, part, total
        self.sib, self.away, self.passed, self.landed = sib, away, passed, landed
        h = self.top_rows = top_rows
        top, low = pl.ds(0, h), pl.ds(h, ROWS - h)
        to_y, to_z, to_c = place.peer(NEAR_Y), place.peer(NEAR_Z), place.peer(CORE)
        self.order = (NEAR_Y | NEAR_Z, NEAR_Y, NEAR_Z, 0)
        self.cores = [
            send(part.at[place.slot(bits | CORE)], sib.at[number], sems, number, to_c)
            for number, bits in enumerate(self.order)
        ]
        self.d0 = send(away.at[0, top], passed.at[top], sems, 4, to_y)
        self.d1 = send(away.at[0, low], passed.at[low], sems, 5, to_z)
        self.y0 = send(away.at[1, top], landed.at[0, top], sems, 6, to_y)
        self.y1 = send(away.at[1, low], landed.at[0, low], sems, 7, to_y)
        self.z0 = send(away.at[2, top], landed.at[1, top], sems, 8, to_z)
        self.z1 = send(away.at[2, low], landed.at[1, low], sems, 9, to_z)

    @staticmethod
    def buffers(width):
        return [
            pltpu.VMEM((4, ROWS, width), LOW),
            pltpu.VMEM((3, ROWS, width), LOW),
            pltpu.VMEM((ROWS, width), LOW),
            pltpu.VMEM((2, ROWS, width), LOW),
        ]

    def start(self):
        for copy in self.cores:
            copy.start()

    def pair_one(self, number):
        self.cores[number].wait_recv()
        target = self.away.at[number] if number < 3 else self.total
        mine = self.part.at[self.place.slot(self.order[number])]
        add_rows(target, mine, self.sib.at[number], 0, ROWS)
        for copy in ((self.d0, self.d1), (self.y0,), (self.z1,), ())[number]:
            copy.start()

    def pair_up(self):
        for number in range(4):
            self.pair_one(number)

    def relay(self):
        h, rest = self.top_rows, ROWS - self.top_rows
        self.d0.wait_recv()
        add_rows(self.away.at[2], self.away.at[2], self.passed, 0, h)
        self.z0.start()
        self.d1.wait_recv()
        add_rows(self.away.at[1], self.away.at[1], self.passed, h, rest)
        self.y1.start()

    def finish(self):
        h, rest = self.top_rows, ROWS - self.top_rows
        total, landed = self.total, self.landed
        self.y0.wait_recv()
        add_rows(total, total, landed.at[0], 0, h)
        self.z1.wait_recv()
        add_rows(total, total, landed.at[1], h, rest)
        self.z0.wait_recv()
        add_rows(total, total, landed.at[1], 0, h)
        self.y1.wait_recv()
        add_rows(total, total, landed.at[0], h, rest)
        for copy in self.cores + [self.d0, self.d1, self.y0, self.y1, self.z0, self.z1]:
            copy.wait_send()


def dot32(left, right, dims=((1,), (0,))):
    return lax.dot_general(left, right, (dims, ((), ())), preferred_element_type=jnp.float32)


def block_of(number):
    return pl.ds(pl.multiple_of(number * BLOCK, BLOCK), BLOCK)


def later(number_of_columns):
    key_at = lax.broadcasted_iota(jnp.int32, (BLOCK, number_of_columns), 0)
    query_at = lax.rem(lax.broadcasted_iota(jnp.int32, (BLOCK, number_of_columns), 1), BLOCK)
    return key_at > query_at


class Mailbox:
    def __init__(self, sends, receives, locals_):
        self.sends, self.receives, self.locals_ = sends, receives, locals_
        self.taken, self.local_taken = 0, 0

    def take(self, count):
        start = self.taken
        self.taken += count
        spot = pl.ds(start, count)
        return (self.sends.at[spot], self.receives.at[spot])

    def local(self):
        self.local_taken += 1
        return self.locals_.at[self.local_taken - 1]


def token_layout(lengths, group, start, count):
    at = start + lax.broadcasted_iota(jnp.int32, (1, count), 1)
    segment = jnp.zeros((1, count), jnp.int32)
    offset = jnp.zeros((1, count), jnp.int32)
    end = jnp.int32(0)
    for number in range(lengths.shape[1]):
        length = lengths[group, number]
        end = end + length
        passed = (at >= end).astype(jnp.int32)
        segment = segment + passed
        offset = offset + passed * length
    return segment, at - offset


def wall_rows(segment):
    kind = lax.broadcasted_iota(jnp.int32, (32, segment.shape[1]), 0)
    return jnp.where((kind != segment) & (kind < DOC_KINDS), -WALL, 0.0)


def mark_rows(segment):
    kind = lax.broadcasted_iota(jnp.int32, (32, segment.shape[1]), 0)
    return jnp.where(kind == segment, 1.0, 0.0)


def turn_head(head, cosine, sine):
    former, latter = head[: HEAD_DIM // 2], head[HEAD_DIM // 2 :]
    return jnp.concatenate(
        [former * cosine - latter * sine, latter * cosine + former * sine], axis=0
    )


class WeightSpread:
    CHUNKS = 4

    def __init__(self, place, inn, down, in_o, down_o, mail):
        p = place
        twin, across = p.twin(), p.peer(SQUARE)
        quarter = inn.shape[1] // 4
        piece = quarter // SQUARE

        def columns(member, number):
            return inn.at[:, pl.ds(pl.multiple_of(number * quarter + member * piece, piece), piece)]

        def landing(number):
            return in_o.at[p.half, p.member, p.fsdp, :, pl.ds(number * piece, piece)]

        self.square = [
            send(columns(p.slot(bits), number), landing(number), box, 0, p.peer(bits))
            for bits in range(1, SQUARE)
            for number in range(4)
            for box in (mail.take(1),)
        ]
        self.locals_ = [
            pltpu.make_async_copy(columns(p.member, number), landing(number), mail.local())
            for number in range(4)
        ]
        self.down_local = pltpu.make_async_copy(down, down_o.at[p.half, p.fsdp], mail.local())
        near = in_o.at[p.half, pl.ds(0, SQUARE), p.fsdp]
        self.near = send(near, near, mail.take(1), 0, twin)
        width = SQUARE // self.CHUNKS
        self.far, self.passed = [], []
        boxes, passed_boxes = mail.take(self.CHUNKS), mail.take(self.CHUNKS)
        for number in range(self.CHUNKS):
            rows = pl.ds(number * width, width)
            mine = in_o.at[p.half, rows, p.fsdp]
            other = in_o.at[1 - p.half, rows, p.fsdp]
            self.far.append(send(mine, mine, boxes, number, across))
            self.passed.append(send(other, other, passed_boxes, number, twin))
        boxes = mail.take(3)
        self.down_near = send(down, down_o.at[p.half, p.fsdp], boxes, 0, twin)
        self.down_far = send(down, down_o.at[p.half, p.fsdp], boxes, 1, across)
        other = down_o.at[1 - p.half, p.fsdp]
        self.down_passed = send(other, other, boxes, 2, twin)

    def start_square(self):
        for copy in self.square:
            copy.start()
        for copy in self.locals_:
            copy.start()

    def square_done(self):
        for copy in self.square:
            copy.wait_recv()
        for copy in self.locals_:
            copy.wait()

    def pass_on(self, number):
        self.far[number].wait_recv()
        self.passed[number].start()

    def arrived(self):
        for copy in self.passed + [self.near, self.down_near, self.down_passed]:
            copy.wait_recv()
        self.down_local.wait()

    def drain(self):
        for copy in self.square + self.far + self.passed:
            copy.wait_send()
        for copy in (self.near, self.down_far, self.down_near, self.down_passed):
            copy.wait_send()


def forward_part(place, mail, r):
    lengths, frequency, tok, gain, mix, out, inn, down, cot = (
        r.lengths, r.frequency, r.tok, r.gain_in, r.mix_in, r.out_in, r.inn_in, r.down_in, r.cot
    )
    mix_o, out_o, gain_o, pair_o, att_o = r.mix, r.out, r.gain, r.pair, r.att
    keys_o, values_o, cos_o, sin_o = r.keys, r.values, r.cosine, r.sine
    tok_all, gains, query_c, part, two = r.tok_all, r.gains, r.query_c, r.part, r.two
    top_s, sum_s, mixed_s, att_low, middle_o = r.top_s, r.sum_s, r.dq_s, r.att_low, r.middle
    f32 = jnp.float32
    twin = place.twin()
    blocks = KEYS // BLOCK
    greet([place.after(step)[1] for step in range(1, FLEET)])
    gather_tok = SquareGather(place, tok, tok_all, mail.take(10), mail.local(), GATHER_TOP)
    first, second, mix_local = mix_spread(
        place, mix, mix_o, mail.take(SEQ), mail.take(SEQ), mail.local()
    )
    mix_local.start()
    for bits in range(SEQ - 1, SQUARE - 1, -1):
        first[bits - 1].start()
    gather_tok.start()
    for bits in range(SQUARE - 1, 0, -1):
        first[bits - 1].start()
    gain_local = pltpu.make_async_copy(gain, gains.at[place.rank], mail.local())
    gain_local.start()
    gain_copies = []
    boxes = mail.take(FLEET)
    for step in range(1, FLEET):
        rank, device = place.after(step)
        gain_copies.append(send(gain, gains.at[place.rank], boxes, step, device))
        gain_copies[-1].start()

    keeper = lax.div(place.seq, 2)
    spot = lax.rem(place.seq, 2)
    out_boxes, out_local, twin_boxes = mail.take(2), mail.local(), mail.take(2)

    def out_copy(number):
        remote = pltpu.make_async_remote_copy(
            src_ref=out,
            dst_ref=out_o.at[spot, place.fsdp],
            send_sem=out_boxes[0].at[number],
            recv_sem=out_boxes[1].at[spot],
            device_id=(number * SQUARE + keeper, place.fsdp),
            device_id_type=MESH,
        )
        local = pltpu.make_async_copy(out, out_o.at[spot, place.fsdp], out_local)
        return remote, local, number * SQUARE + keeper == place.seq

    def out_arrival(number):
        source = place.member * 2 + number
        arrival = pltpu.make_async_remote_copy(
            src_ref=out,
            dst_ref=out_o.at[number, place.fsdp],
            send_sem=out_boxes[0].at[number],
            recv_sem=out_boxes[1].at[number],
            device_id=(source, place.fsdp),
            device_id_type=MESH,
        )
        return arrival, source == place.seq

    for number in range(2):
        remote, local, mine = out_copy(number)
        pl.when(mine)(local.start)
        pl.when(jnp.logical_not(mine))(remote.start)

    segment, position = token_layout(lengths, place.fsdp, place.half * KEYS, KEYS)
    angle = frequency[...] * position.astype(f32)
    cos_o[...] = jnp.cos(angle)
    sin_o[...] = jnp.sin(angle)
    keep = (segment < lengths.shape[1]).astype(f32)
    marks = mark_rows(segment).astype(LOW)
    for number in range(blocks):
        mark = marks[:, number * BLOCK : (number + 1) * BLOCK]
        query_c[number, HEAD_DIM:, :] = jnp.concatenate([mark, mark], axis=1)
    walls = wall_rows(segment)

    gather_tok.relay()
    mix_local.wait()
    second[0].start()
    for bits in range(SQUARE - 1, 0, -1):
        first[bits - 1].wait_recv()
        second[bits].start()
    gather_tok.share()
    for bits in range(SEQ - 1, SQUARE - 1, -1):
        first[bits - 1].wait_recv()
        second[bits].start()
    spread = WeightSpread(place, inn, down, r.inn, r.down, mail)
    spread.down_local.start()
    spread.start_square()
    gather_cot = SquareGather(place, cot, r.cot_all, mail.take(10), mail.local(), GATHER_TOP)
    gather_cot.start()
    gain_local.wait()
    for copy in gain_copies:
        copy.wait()
    gain_o[...] = jnp.zeros_like(gain_o)
    for rank in range(FLEET):
        lane = rank * (D // FLEET) // 128 * 128
        gain_o[:, lane : lane + 256] += gains[rank].astype(f32)
    gather_tok.finish()
    for copy in second:
        copy.wait_recv()

    up_boxes = mail.take(blocks)
    up = [
        send(pair_o.at[blocks + number], pair_o.at[number], up_boxes, number, place.peer(SQUARE))
        for number in range(blocks)
    ]
    for number in range(blocks):
        columns = pl.ds(number * BLOCK, BLOCK)
        halves = []
        for block in (2 * number, 2 * number + 1):
            x = tok_all[block].astype(f32)
            scale = lax.rsqrt(jnp.mean(x * x, axis=-1, keepdims=True) + EPS_NORM)
            low = (x * scale * gain_o[0:1, :D]).astype(LOW)
            tok_all[block] = low
            halves.append(dot32(low, mix_o[...].reshape(D, 4 * HEAD_DIM)).T)
        projected = jnp.concatenate(halves, axis=1)
        cosine, sine = cos_o[:, columns], sin_o[:, columns]
        for head in range(2):
            turned = turn_head(projected[head * HEAD_DIM : (head + 1) * HEAD_DIM], cosine, sine)
            side = pl.ds(head * BLOCK, BLOCK)
            query_c[number, :HEAD_DIM, side] = turned.astype(LOW)
        key = turn_head(projected[2 * HEAD_DIM : 3 * HEAD_DIM], cosine, sine).astype(LOW)
        value = projected[3 * HEAD_DIM :].astype(LOW)
        pair_o[blocks + number, :HEAD_DIM] = key
        pair_o[blocks + number, HEAD_DIM:] = value
        pl.when(place.half == 0)(up[number].start)
        rows = pl.ds(KEYS + number * BLOCK, BLOCK)
        wall = walls[:, number * BLOCK : (number + 1) * BLOCK]
        keys_o[rows, :] = jnp.concatenate([key.astype(f32), wall], axis=0).T.astype(LOW)
        values_o[rows, :] = value.astype(f32).T.astype(LOW)

    for number in range(2):
        remote, local, mine = out_copy(number)
        pl.when(mine)(local.wait)
        pl.when(jnp.logical_not(mine))(remote.wait_send)
    passing = []
    for number in range(2):
        arrival, mine = out_arrival(number)
        pl.when(jnp.logical_not(mine))(arrival.wait_recv)
        block = out_o.at[number, place.fsdp]
        passing.append(send(block, block, twin_boxes, number, twin))
        passing[-1].start()
    spread.square_done()
    spread.near.start()
    spread.down_near.start()
    for copy in spread.far:
        pl.when(place.half == 1)(copy.start)

    normed_out = pltpu.make_async_copy(tok_all, r.normed, mail.local())
    normed_out.start()
    gather_cot.relay()
    gather_cot.share()

    def fold(queries, spot, carry, diagonal=False):
        score = dot32(keys_o[block_of(spot), :], queries)
        if diagonal:
            score = jnp.where(later(2 * BLOCK), -WALL, score)
        top = jnp.max(score, axis=0, keepdims=True)
        if carry is not None:
            top = jnp.maximum(carry[0], top)
        weight = jnp.exp2((score - top) * SCALE2)
        total = jnp.sum(weight, axis=0, keepdims=True)
        mixed = dot32(pair_o[spot, HEAD_DIM:], weight.astype(LOW))
        if carry is not None:
            fade = jnp.exp2((carry[0] - top) * SCALE2)
            total = total + carry[1] * fade
            mixed = mixed + carry[2] * fade
        return (top, total, mixed)

    for number in range(blocks):
        queries = query_c[number]
        carry = fold(queries, blocks + number, None, diagonal=True)
        carry = lax.fori_loop(
            blocks, blocks + number, functools.partial(fold, queries), carry
        )
        top_s[number : number + 1, :], sum_s[number : number + 1, :] = carry[:2]
        mixed_s[number] = carry[2]

    spread.down_far.start()

    @pl.when(place.half == 1)
    def _():
        other_segment, _ = token_layout(lengths, place.fsdp, 0, KEYS)
        other_walls = wall_rows(other_segment)
        for number in range(blocks):
            up[number].wait_recv()
            rows = pl.ds(number * BLOCK, BLOCK)
            wall = other_walls[:, number * BLOCK : (number + 1) * BLOCK]
            keys_o[rows, :] = (
                jnp.concatenate([pair_o[number, :HEAD_DIM].astype(f32), wall], axis=0)
                .T.astype(LOW)
            )
            values_o[rows, :] = pair_o[number, HEAD_DIM:].astype(f32).T.astype(LOW)

    @pl.when(place.half == 0)
    def _():
        for number in range(blocks):
            up[number].wait_send()
            pair_o[number] = jnp.zeros_like(pair_o[number])
        keys_o[pl.ds(0, KEYS), :] = jnp.zeros((KEYS, 128), LOW)
        values_o[pl.ds(0, KEYS), :] = jnp.zeros((KEYS, HEAD_DIM), LOW)

    for copy in spread.far:
        pl.when(place.half == 0)(copy.start)
    for number in range(blocks):
        columns = pl.ds(number * BLOCK, BLOCK)
        carry = (top_s[number : number + 1, :], sum_s[number : number + 1, :], mixed_s[number])
        carry = lax.fori_loop(
            0,
            jnp.where(place.half == 1, blocks, 0),
            functools.partial(fold, query_c[number]),
            carry,
        )
        top, total, mixed = carry
        mixed = mixed * (1.0 / total)
        level = top * SCALE2 + jnp.log2(total)
        r.level_s[number] = jnp.broadcast_to(level, (8, 2 * BLOCK))
        for head in range(2):
            side = slice(head * BLOCK, (head + 1) * BLOCK)
            rows = pl.ds(head * HEAD_DIM, HEAD_DIM)
            kept = mixed[:, side] * keep[:, number * BLOCK : (number + 1) * BLOCK]
            att_o[rows, columns] = kept
            att_low[rows, columns] = kept.astype(LOW)

    for copy in passing:
        copy.wait_recv()
    normed_out.wait()
    scatter = SquareScatter(
        place, part, middle_o, r.buffers_a, mail.take(10), SCATTER_TOP
    )

    def out_block(slot):
        columns = pl.ds(pl.multiple_of(slot * ROWS, ROWS), ROWS)
        rows = att_low[:, columns].astype(f32).T.astype(LOW)
        part[slot] = dot32(rows, out_o[...].reshape(2 * HEAD_DIM, D)).astype(LOW)

    for number, bits in enumerate(scatter.order):
        out_block(place.slot(bits | CORE))
        scatter.cores[number].start()
    for bits in scatter.order:
        out_block(place.slot(bits))
    scatter.pair_up()
    spread.down_far.wait_recv()
    spread.down_passed.start()
    spread.pass_on(0)
    scatter.relay()
    scatter.finish()
    middle = middle_o[...] + tok[...].astype(f32)
    middle_o[...] = middle
    scale = lax.rsqrt(jnp.mean(middle * middle, axis=-1, keepdims=True) + EPS_NORM)
    two[...] = (middle * scale * gain_o[1:2, :D]).astype(LOW)
    gather_two = SquareGather(place, two, r.two_all, mail.take(10), mail.local(), GATHER_TOP)
    gather_two.start()
    spread.pass_on(1)
    gather_two.relay()
    gather_two.share()
    spread.pass_on(2)
    gather_two.finish()
    gather_cot.finish()
    spread.pass_on(3)
    spread.arrived()

    def drain():
        spread.drain()
        for copy in first + second + passing:
            copy.wait_send()

    return keep, drain


def norm_back(grad, values, gain):
    scale = lax.rsqrt(jnp.mean(values * values, axis=-1, keepdims=True) + EPS_NORM)
    unit = values * scale
    grad_gain = jnp.sum(grad * unit, axis=0, keepdims=True)
    grad_unit = grad * gain
    centre = jnp.mean(grad_unit * unit, axis=-1, keepdims=True)
    return grad_gain, scale * (grad_unit - unit * centre)


def add_blocks(target, left, right, count):
    for number in range(count):
        add_rows(target.at[number], left.at[number], right.at[number], 0, target.shape[1])


def square_sum(ref):
    value = ref[...].astype(jnp.float32)
    return jnp.sum(value * value)


def backward_part(place, mail, r, keep):
    tok, cot, middle, gain, mix, out = r.tok, r.cot, r.middle, r.gain, r.mix, r.out
    inn, down, keys, values, pair, att = r.inn, r.down, r.keys, r.values, r.pair, r.att
    cosine, sine, two_all, cot_all = r.cosine, r.sine, r.two_all, r.cot_all
    part, hidden, gate_grad, total, grad_mid = r.part, r.hidden, r.gate_grad, r.total, r.grad_mid
    gin, gin_x, gin_z, gdown, gdown_x, gdown_z = (
        r.gin, r.gin_x, r.gin_z, r.gdown, r.gdown_x, r.gdown_z
    )
    gout, gout_x, out_got, branch, branch_all = r.gout, r.gout_x, r.out_got, r.two, r.tok_all
    query_c, grad_c, query_r, grad_r = r.query_c, r.grad_c, r.query_r, r.grad_r
    level_s, shift_s, dq_s, back, back_in = r.level_s, r.shift_s, r.dq_s, r.back, r.back_in
    gproj_t, gproj_r, gmix, crossed = r.gproj_t, r.gproj_r, r.gmix, r.crossed
    landed_mix, gain_v, gain_w, sums, mine_s = r.landed_mix, r.gain_v, r.gain_w, r.sums, r.mine_s
    hidden_o, tokens_o, mix_o, out_o = r.hidden_o, r.tokens_o, r.mix_o, r.out_o
    in_o, down_o, gain_o, total_o = r.in_o, r.down_o, r.gain_o, r.total_o
    f32 = jnp.float32
    half, fsdp, member = place.half, place.fsdp, place.member
    twin, across = place.twin(), place.peer(SQUARE)
    blocks = KEYS // BLOCK
    rows_all = SQUARE * ROWS
    units = hidden.shape[1]
    buffers_a, buffers_b = r.buffers_a, r.buffers_b

    scatter = SquareScatter(place, part, total, buffers_a, mail.take(10), SCATTER_TOP)

    def feed_forward(chip):
        pair_of = pl.ds(chip * 2, 2)
        rows = pl.ds(pl.multiple_of(chip * 2 * ROWS, 2 * ROWS), 2 * ROWS)
        gate_up = dot32(two_all[pair_of].reshape(2 * ROWS, D), inn[...].reshape(D, 2 * units))
        gate, up = gate_up[:, :units], gate_up[:, units:]
        sigmoid = 1.0 / (1.0 + jnp.exp(-gate))
        silu = gate * sigmoid
        low = (silu * up).astype(LOW)
        hidden[rows, :] = low
        grad_hidden = dot32(cot_all[pair_of].reshape(2 * ROWS, D), down[...].reshape(units, D), ((1,), (1,)))
        grad_gate = grad_hidden * up * sigmoid * (1.0 + gate * (1.0 - sigmoid))
        grad_up = grad_hidden * silu
        low = jnp.concatenate([grad_gate, grad_up], axis=1).astype(LOW)
        gate_grad[rows, :] = low
        part[pair_of] = dot32(low, inn[...].reshape(D, 2 * units), ((1,), (1,))).astype(LOW).reshape(2, ROWS, D)

    for number, bits in enumerate(scatter.order):
        feed_forward(lax.div(place.slot(bits), 2))
        scatter.cores[number].start()
        if number:
            scatter.pair_one(number - 1)
    scatter.pair_one(3)

    in_boxes, far_boxes = mail.take(4), mail.take(2)
    in_cross, in_far = {}, {}
    down_boxes, down_far_box = mail.take(2), mail.take(1)
    down_cross = {}
    width = SQUARE // 2

    def in_grads(away, number):
        which = 1 - half if away else half
        spot = pl.ds(number * width, width)
        lanes = pl.ds(pl.multiple_of((which * 2 + number) * (D // 4), 128), D // 4)
        left = two_all[:, :, lanes].reshape(rows_all, D // 4)
        grad = dot32(left, gate_grad[...], ((0,), (0,)))
        gin[which, spot] = grad.astype(LOW).reshape(width, 2, D // FLEET, 2 * units)
        copy = send(
            gin.at[which, spot, 1 - fsdp], gin_x.at[which, spot], in_boxes, away * 2 + number, twin
        )
        copy.start()
        in_cross[away, number] = copy

    def down_grads(away):
        which = 1 - half if away else half
        lanes = pl.ds(pl.multiple_of(which * (units // 2), 128), units // 2)
        left = hidden[:, lanes]
        right = cot_all[...].reshape(rows_all, D)
        grad = dot32(left, right, ((0,), (0,)))
        gdown[which] = grad.astype(LOW).reshape(2, units // 4, D)
        copy = send(gdown.at[which, 1 - fsdp], gdown_x.at[which], down_boxes, away, twin)
        copy.start()
        down_cross[away] = copy

    in_grads(1, 0)
    in_grads(1, 1)
    scatter.relay()
    down_grads(1)
    in_grads(0, 0)
    in_grads(0, 1)
    down_grads(0)
    scatter.finish()
    gain_v[...] = jnp.zeros_like(gain_v)
    gain_mlp, grad_norm = norm_back(total[...], middle[...], gain[1:2, :D])
    gain_v[1:2, :D] = gain_mlp
    grad_middle = cot[...].astype(f32) + grad_norm
    grad_mid[...] = grad_middle
    branch[...] = grad_middle.astype(LOW)
    gather = SquareGather(place, branch, branch_all, mail.take(10), mail.local(), GATHER_TOP)
    gather.start()

    def in_onward(number):
        spot = pl.ds(number * width, width)
        in_cross[1, number].wait_recv()
        mine = gin.at[1 - half, spot, fsdp]
        add_blocks(mine, mine, gin_x.at[1 - half, spot], width)
        in_far[number] = send(mine, gin_z.at[spot], far_boxes, number, across)
        in_far[number].start()

    in_onward(0)
    gather.relay()
    for number in range(SQUARE // 2):
        rows = pl.ds(number * 2 * ROWS, 2 * ROWS)
        y_rows = dot32(hidden[rows, :], down[...].reshape(units, D)).astype(LOW)
        part[pl.ds(number * 2, 2)] = y_rows.reshape(2, ROWS, D)
    in_onward(1)
    gather.share()

    gather.finish()
    scatter_y = SquareScatter(place, part, total, buffers_a, mail.take(10), SCATTER_TOP)
    scatter_y.start()
    branch_rows = branch_all[...].reshape(rows_all, D)
    grad_att = dot32(out[...].reshape(2 * HEAD_DIM, D), branch_rows, ((1,), (1,))) * keep
    grad_low = grad_att.astype(LOW)
    delta = grad_low.astype(f32) * att[...]
    for head in range(2):
        rows = slice(head * HEAD_DIM, (head + 1) * HEAD_DIM)
        grad_head = grad_low[rows]
        shift = jnp.sum(delta[rows], axis=0, keepdims=True)
        for number in range(blocks):
            side = pl.ds(head * BLOCK, BLOCK)
            grad_block = grad_head[:, number * BLOCK : (number + 1) * BLOCK]
            grad_c[number, :, side] = grad_block
            query_r[number, side, :] = query_c[number, :, side].astype(f32).T.astype(LOW)
            grad_r[number, side, :] = grad_block.astype(f32).T.astype(LOW)
            shift_s[number, :, side] = jnp.broadcast_to(
                shift[:, number * BLOCK : (number + 1) * BLOCK], (8, BLOCK)
            )
    scatter_y.pair_up()

    dq_s[...] = jnp.zeros_like(dq_s)

    def fold(spot, number, carry, diagonal=False):
        grad_key, grad_value = carry
        rows = block_of(spot)
        score = dot32(keys[rows, :], query_c[number])
        if diagonal:
            score = jnp.where(later(2 * BLOCK), -WALL, score)
        weight = jnp.exp2(score * SCALE2 - level_s[number, 0:1, :])
        grad_weight = dot32(values[rows, :], grad_c[number])
        grad_score = (weight * (grad_weight - shift_s[number, 0:1, :])).astype(LOW)
        dq_s[number] += dot32(pair[spot, :HEAD_DIM], grad_score)
        grad_key = grad_key + dot32(grad_score, query_r[number])
        grad_value = grad_value + dot32(weight.astype(LOW), grad_r[number])
        return grad_key, grad_value

    none = (jnp.zeros((BLOCK, 128), f32), jnp.zeros((BLOCK, HEAD_DIM), f32))
    back_boxes = mail.take(blocks)
    returns = [
        send(back.at[number], back_in.at[number], back_boxes, number, across)
        for number in range(blocks)
    ]

    @pl.when(half == 1)
    def _():
        for number in range(blocks):
            grad_key, grad_value = lax.fori_loop(
                0, blocks, functools.partial(fold, number), none
            )
            back[number, :HEAD_DIM] = grad_key.T[:HEAD_DIM].astype(LOW)
            back[number, HEAD_DIM:] = grad_value.T.astype(LOW)
            returns[number].start()

    scatter_y.relay()
    down_cross[1].wait_recv()
    down_mine = gdown.at[1 - half, fsdp]
    add_rows(down_mine, down_mine, gdown_x.at[1 - half], 0, units // 4)
    down_far = send(down_mine, gdown_z, down_far_box, 0, across)
    down_far.start()

    out_boxes, owner_boxes = mail.take(1), mail.take(2)
    out_local = mail.local()
    grad_out = dot32(r.att_low[...], branch_all[...].reshape(rows_all, D))
    gout[...] = grad_out.astype(LOW).reshape(2, 2, D // FLEET, D)
    out_cross = send(gout.at[pl.ds(0, 2), 1 - fsdp], gout_x, out_boxes, 0, twin)
    out_cross.start()

    for number in range(blocks):
        carry = fold(blocks + number, number, none, diagonal=True)
        grad_key, grad_value = lax.fori_loop(
            number + 1, blocks, functools.partial(fold, blocks + number), carry
        )
        columns = pl.ds(number * BLOCK, BLOCK)
        gproj_t[pl.ds(0, HEAD_DIM), columns] = grad_key.T[:HEAD_DIM]
        gproj_t[pl.ds(HEAD_DIM, HEAD_DIM), columns] = grad_value.T
    scatter_y.finish()
    normed_load = pltpu.make_async_copy(r.normed, part, mail.local())
    normed_load.start()
    hidden_o[...] = (middle[...] + total[...]).astype(LOW)

    square_boxes = mail.take(SQUARE)
    in_local = mail.local()
    in_square = []
    for number in range(2):
        spot = pl.ds(number * width, width)
        in_cross[0, number].wait_recv()
        mine = gin.at[half, spot, fsdp]
        add_blocks(mine, mine, gin_x.at[half, spot], width)

    @pl.when(half == 0)
    def _():
        for number in range(blocks):
            returns[number].wait_recv()
            columns = pl.ds(number * BLOCK, BLOCK)
            gproj_t[:, columns] = gproj_t[:, columns] + back_in[number].astype(f32)

    @pl.when(half == 1)
    def _():
        for number in range(blocks):
            returns[number].wait_send()

    factor = HEAD_DIM ** (-0.5)
    for number in range(blocks):
        columns = pl.ds(number * BLOCK, BLOCK)
        cos_b, sin_b = cosine[:, columns], -sine[:, columns]
        pieces = []
        for head in range(2):
            dq = dq_s[number, :, head * BLOCK : (head + 1) * BLOCK]
            pieces.append(turn_head(dq * factor, cos_b, sin_b))
        dk = gproj_t[pl.ds(0, HEAD_DIM), columns]
        pieces.append(turn_head(dk * factor, cos_b, sin_b))
        pieces.append(gproj_t[pl.ds(HEAD_DIM, HEAD_DIM), columns])
        gproj_r[columns, :] = jnp.concatenate(pieces, axis=0).T.astype(LOW)

    cross_boxes, plane_boxes = mail.take(SEQ), mail.take(SEQ)
    share = D // FLEET
    normed_load.wait()
    for number in range(4):
        left = part[:, :, pl.ds(number * (D // 4), D // 4)].reshape(rows_all, D // 4)
        grad = dot32(left, gproj_r[...], ((0,), (0,)))
        gmix[pl.ds(number * 4, 4)] = grad.astype(LOW).reshape(4, 2, share, 4 * HEAD_DIM)
    order = list(range(SEQ - 1, -1, -1))
    cross = {}
    for bits in order:
        target = flip(place.seq, bits)
        cross[bits] = send(gmix.at[target, 1 - fsdp], crossed.at[target], cross_boxes, bits, twin)
        cross[bits].start()
    scatter_n = SquareScatter(place, part, total, buffers_b, mail.take(10), SCATTER_TOP)
    for number, bits in enumerate(scatter_n.order):
        chip = lax.div(place.slot(bits), 2)
        rows = pl.ds(pl.multiple_of(chip * 2 * ROWS, 2 * ROWS), 2 * ROWS)
        grad = dot32(gproj_r[rows, :], mix[...].reshape(D, 4 * HEAD_DIM), ((1,), (1,)))
        part[pl.ds(chip * 2, 2)] = grad.astype(LOW).reshape(2, ROWS, D)
        scatter_n.cores[number].start()
    scatter_n.pair_up()

    def out_copy(number):
        owner = member * 2 + number
        remote = pltpu.make_async_remote_copy(
            src_ref=gout.at[number, fsdp],
            dst_ref=out_got.at[half],
            send_sem=owner_boxes[0].at[number],
            recv_sem=owner_boxes[1].at[half],
            device_id=(owner, fsdp),
            device_id_type=MESH,
        )
        local = pltpu.make_async_copy(gout.at[number, fsdp], out_got.at[half], out_local)
        return remote, local, owner == place.seq

    out_cross.wait_recv()
    for number in range(2):
        mine = gout.at[number, fsdp]
        add_rows(mine, mine, gout_x.at[number], 0, share)
        remote, local, own_block = out_copy(number)
        pl.when(own_block)(local.start)
        pl.when(jnp.logical_not(own_block))(remote.start)
    plane = {}
    for bits in order:
        target = flip(place.seq, bits)
        cross[bits].wait_recv()
        mine = gmix.at[target, fsdp]
        goal = mine if bits else landed_mix.at[place.seq]
        add_rows(goal, mine, crossed.at[target], 0, share)
        if bits:
            plane[bits] = send(
                mine, landed_mix.at[place.seq], plane_boxes, bits, (target, fsdp)
            )
            plane[bits].start()
        if bits == SQUARE:
            scatter_n.relay()
    for number in range(2):
        spot = pl.ds(number * width, width)
        in_far[number].wait_recv()
        mine = gin.at[half, spot, fsdp]
        add_blocks(mine, mine, gin_z.at[spot], width)
    in_keep = pltpu.make_async_copy(gin.at[half, member, fsdp], in_o.at[member], in_local)
    in_keep.start()
    for bits in range(1, SQUARE):
        copy = send(
            gin.at[half, place.slot(bits), fsdp],
            in_o.at[member],
            square_boxes,
            bits,
            place.peer(bits),
        )
        copy.start()
        in_square.append(copy)
    down_cross[0].wait_recv()
    down_own = gdown.at[half, fsdp]
    add_rows(down_own, down_own, gdown_x.at[half], 0, units // 4)
    scatter_n.finish()
    gain_attn, grad_norm = norm_back(total[...], tok[...].astype(f32), gain[0:1, :D])
    gain_v[0:1, :D] = gain_attn
    tokens_o[...] = grad_mid[...] + grad_norm
    gain_boxes, sum_boxes = mail.take(FLEET), mail.take(FLEET)
    gain_copies = []
    for step in range(1, FLEET):
        rank, device = place.after(step)
        lane = pl.multiple_of(lax.div(rank * share, 128) * 128, 128)
        gain_copies.append(
            send(
                gain_v.at[:, pl.ds(lane, 256)], gain_w.at[place.rank], gain_boxes, step, device
            )
        )
        gain_copies[-1].start()
    lane = pl.multiple_of(lax.div(place.rank * share, 128) * 128, 128)
    gain_w[place.rank] = gain_v[:, pl.ds(lane, 256)]
    for bits in range(1, SEQ):
        plane[bits].wait_recv()
    wide, key_width = 2 * HEAD_DIM, KV_HEADS * HEAD_DIM
    sums_mix = [
        landed_mix[number].astype(f32) + landed_mix[number + SQUARE].astype(f32)
        for number in range(SQUARE)
    ]
    for number in range(SQUARE // 2):
        block = jnp.concatenate([v[:, :wide] for v in sums_mix[2 * number : 2 * number + 2]], 1)
        mix_o[:, number * 2 * wide : (number + 1) * 2 * wide] = block
    for kind in range(2):
        lanes = slice(wide + kind * HEAD_DIM, wide + (kind + 1) * HEAD_DIM)
        for number in range(SQUARE // 4):
            block = jnp.concatenate([v[:, lanes] for v in sums_mix[4 * number : 4 * number + 4]], 1)
            start = D + kind * key_width + number * 2 * wide
            mix_o[:, start : start + 2 * wide] = block
    for number in range(2):
        source = number * SQUARE + lax.div(place.seq, 2)
        arrival = pltpu.make_async_remote_copy(
            src_ref=gout.at[0, 0],
            dst_ref=out_got.at[number],
            send_sem=owner_boxes[0].at[number],
            recv_sem=owner_boxes[1].at[number],
            device_id=(source, fsdp),
            device_id_type=MESH,
        )
        pl.when(source != place.seq)(arrival.wait_recv)
        remote, local, own_block = out_copy(number)
        pl.when(own_block)(local.wait)
    add_rows(out_o, out_got.at[0], out_got.at[1], 0, share)
    down_far.wait_recv()
    add_rows(down_o, down_own, gdown_z, 0, units // 4)
    squares = square_sum(mix_o) + square_sum(out_o) + square_sum(down_o)
    in_keep.wait()
    for copy in in_square:
        copy.wait_recv()
    squares = squares + square_sum(in_o)
    for copy in gain_copies:
        copy.wait()
    window = gain_w[0]
    for rank in range(1, FLEET):
        window = window + gain_w[rank]
    start = lax.rem(place.rank * share, 128)
    own_gain = jnp.zeros((8, 128), f32)
    for lane in range(0, 128, 16):
        own_gain = jnp.where(start == lane, window[:, lane : lane + 128], own_gain)
    at = lax.broadcasted_iota(jnp.int32, own_gain.shape, 1)
    own_gain = jnp.where(at < share, own_gain, 0.0)
    gain_o[...] = own_gain
    squares = squares + jnp.sum(own_gain * own_gain)
    mine_s[...] = jnp.broadcast_to(squares, mine_s.shape)
    sums[place.rank] = mine_s[...]
    copies = []
    for step in range(1, FLEET):
        rank, device = place.after(step)
        copies.append(send(mine_s, sums.at[place.rank], sum_boxes, step, device))
        copies[-1].start()
    for copy in copies:
        copy.wait()
    result = sums[0]
    for rank in range(1, FLEET):
        result = result + sums[rank]
    total_o[...] = result
    for copy in list(in_cross.values()) + list(in_far.values()) + list(down_cross.values()):
        copy.wait_send()
    for copy in [down_far, out_cross] + in_square + list(cross.values()) + list(plane.values()):
        copy.wait_send()
    for number in range(2):
        remote, local, own_block = out_copy(number)
        pl.when(jnp.logical_not(own_block))(remote.wait_send)


class Refs:
    def __init__(self, **refs):
        self.__dict__.update(refs)


ARGUMENTS = [
    "lengths",
    "frequency",
    "tok",
    "gain_in",
    "mix_in",
    "out_in",
    "inn_in",
    "down_in",
    "cot",
]
RESULTS = [
    "hidden_o",
    "tokens_o",
    "mix_o",
    "out_o",
    "in_o",
    "down_o",
    "gain_o",
    "total_o",
    "normed",
]


def scratch_of():
    share, unit = D // FLEET, FF // FLEET
    blocks = KEYS // BLOCK
    low = lambda *size: pltpu.VMEM(size, LOW)
    full = lambda *size: pltpu.VMEM(size, jnp.float32)
    scratch = {
        "mix": low(FLEET, share, 4 * HEAD_DIM),
        "out": low(2, 2, share, D),
        "inn": low(2, SQUARE, 2, share, 8 * unit),
        "down": low(2, 2, unit, D),
        "gain": full(16, D + 128),
        "pair": low(2 * blocks, 2 * HEAD_DIM, BLOCK),
        "att": full(2 * HEAD_DIM, KEYS),
        "att_low": low(2 * HEAD_DIM, KEYS),
        "keys": low(2 * KEYS, 128),
        "values": low(2 * KEYS, HEAD_DIM),
        "cosine": full(HEAD_DIM // 2, KEYS),
        "sine": full(HEAD_DIM // 2, KEYS),
        "tok_all": low(SQUARE, ROWS, D),
        "two_all": low(SQUARE, ROWS, D),
        "cot_all": low(SQUARE, ROWS, D),
        "two": low(ROWS, D),
        "gains": low(FLEET, 16, 256),
        "query_c": low(blocks, 128, 2 * BLOCK),
        "query_r": low(blocks, 2 * BLOCK, 128),
        "grad_c": low(blocks, HEAD_DIM, 2 * BLOCK),
        "grad_r": low(blocks, 2 * BLOCK, HEAD_DIM),
        "level_s": full(blocks, 8, 2 * BLOCK),
        "shift_s": full(blocks, 8, 2 * BLOCK),
        "top_s": full(8, 2 * BLOCK),
        "sum_s": full(8, 2 * BLOCK),
        "dq_s": full(blocks, HEAD_DIM, 2 * BLOCK),
        "middle": full(ROWS, D),
        "total": full(ROWS, D),
        "grad_mid": full(ROWS, D),
        "part": low(SQUARE, ROWS, D),
        "hidden": low(KEYS, 4 * unit),
        "gate_grad": low(KEYS, 8 * unit),
        "gin": low(2, SQUARE, 2, share, 8 * unit),
        "gin_x": low(2, SQUARE, share, 8 * unit),
        "gin_z": low(SQUARE, share, 8 * unit),
        "gdown": low(2, 2, unit, D),
        "gdown_x": low(2, unit, D),
        "gdown_z": low(unit, D),
        "gout": low(2, 2, share, D),
        "gout_x": low(2, share, D),
        "out_got": low(2, share, D),
        "back": low(blocks, 2 * HEAD_DIM, BLOCK),
        "back_in": low(blocks, 2 * HEAD_DIM, BLOCK),
        "gproj_t": full(2 * HEAD_DIM, KEYS),
        "gproj_r": low(KEYS, 4 * HEAD_DIM),
        "gmix": low(SEQ, 2, share, 4 * HEAD_DIM),
        "crossed": low(SEQ, share, 4 * HEAD_DIM),
        "landed_mix": low(SEQ, share, 4 * HEAD_DIM),
        "gain_v": full(8, D + 128),
        "gain_w": full(FLEET, 8, 256),
        "sums": full(FLEET, 8, 128),
        "mine_s": full(8, 128),
        "sends": pltpu.SemaphoreType.DMA((360,)),
        "receives": pltpu.SemaphoreType.DMA((360,)),
        "locals": pltpu.SemaphoreType.DMA((24,)),
    }
    for set_name in "ab":
        for number, buffer in enumerate(SquareScatter.buffers(D)):
            scratch[set_name + str(number)] = buffer
    return scratch


def layer_kernel(names, *refs):
    r = Refs(**dict(zip(names, refs, strict=True)))
    r.buffers_a = (r.a0, r.a1, r.a2, r.a3)
    r.buffers_b = (r.b0, r.b1, r.b2, r.b3)
    place = Place()
    mail = Mailbox(r.sends, r.receives, r.locals)
    keep, drain = forward_part(place, mail, r)
    backward_part(place, mail, r, keep)
    drain()


def layer(*arrays):
    shape = jax.ShapeDtypeStruct
    f32 = jnp.float32
    share, unit = D // FLEET, FF // FLEET
    scratch = scratch_of()
    names = ARGUMENTS + RESULTS + list(scratch)
    return pl.pallas_call(
        functools.partial(layer_kernel, names),
        out_shape=(
            shape((ROWS, D), LOW),
            shape((ROWS, D), f32),
            shape((share, 8 * 4 * HEAD_DIM), f32),
            shape((share, D), f32),
            shape((SQUARE, share, 8 * unit), LOW),
            shape((unit, D), f32),
            shape((8, 128), f32),
            shape((8, 128), f32),
            shape((SQUARE, ROWS, D), LOW),
        ),
        in_specs=[pl.BlockSpec(memory_space=pltpu.SMEM)] + [VMEM] * 3 + [ANY] * 4 + [VMEM],
        out_specs=(VMEM,) * 8 + (ANY,),
        scratch_shapes=list(scratch.values()),
        compiler_params=pltpu.CompilerParams(
            collective_id=0, has_side_effects=True, vmem_limit_bytes=63 << 20
        ),
        name="layer",
    )(*arrays)


def adam_kernel(totals, *refs):
    scale = CLIP_NORM / jnp.maximum(jnp.sqrt(totals[0:1, 0:1]), CLIP_NORM)
    inputs, outputs = refs[2:18], refs[20:]
    for source, target in zip(refs[:2], refs[18:20], strict=True):
        target[...] = source[...]
    for kind, rate in enumerate((LEARN_RATE, OUT_RATE, LEARN_RATE, LEARN_RATE)):
        weight, first, second, grad = inputs[4 * kind : 4 * kind + 4]
        grad_o, new_o, first_o, second_o, copy_o = outputs[5 * kind : 5 * kind + 5]
        width = weight.shape[1] // SQUARE if grad.ndim == 3 else weight.shape[1]
        for number in range(weight.shape[1] // width):
            lanes = slice(number * width, (number + 1) * width)
            value = (grad[number] if grad.ndim == 3 else grad[...]).astype(jnp.float32)
            new, moment, square = adam_update(
                weight[:, lanes], first[:, lanes], second[:, lanes], value, scale, rate
            )
            grad_o[:, lanes] = value
            new_o[:, lanes] = new
            first_o[:, lanes] = moment
            second_o[:, lanes] = square
            copy_o[:, lanes] = new.astype(LOW)


def adam_all(totals, passing, kinds):
    steps = 4
    shape = jax.ShapeDtypeStruct
    in_specs, out_specs, out_shapes = [pl.BlockSpec(totals.shape, lambda i: (0, 0))], [], []
    for array in passing:
        spec = pl.BlockSpec((array.shape[0], array.shape[1] // steps), lambda i: (0, i))
        in_specs.append(spec)
        out_specs.append(spec)
        out_shapes.append(shape(array.shape, array.dtype))
    for weight, _, _, grad in kinds:
        spec = pl.BlockSpec((weight.shape[0], weight.shape[1] // steps), lambda i: (0, i))
        in_specs += [spec] * 3
        if grad.ndim == 3:
            block = (grad.shape[0], grad.shape[1], grad.shape[2] // steps)
            in_specs.append(pl.BlockSpec(block, lambda i: (0, 0, i)))
        else:
            in_specs.append(spec)
        out_specs += [spec] * 5
        out_shapes += [shape(weight.shape, jnp.float32)] * 4 + [shape(weight.shape, LOW)]
    return pl.pallas_call(
        adam_kernel,
        grid=(steps,),
        out_shape=out_shapes,
        in_specs=in_specs,
        out_specs=out_specs,
        compiler_params=pltpu.CompilerParams(vmem_limit_bytes=63 << 20),
        name="adam",
    )(totals, *passing, *[array for kind in kinds for array in kind])


def local_squares(
    tokens,
    cotangent,
    lengths,
    mix_weight,
    out_weight,
    in_weight,
    down_weight,
    norm_gains,
    mix_first,
    out_first,
    in_first,
    down_first,
    norm_first,
    mix_second,
    out_second,
    in_second,
    down_second,
    norm_second,
):
    f32 = jnp.float32
    fsdp = lax.axis_index("fsdp")
    seq = lax.axis_index("seq")
    frequency = ROPE_BASE ** (-jnp.arange(HEAD_DIM // 2, dtype=f32) * 2.0 / HEAD_DIM)

    wide = 2 * HEAD_DIM
    key_width = KV_HEADS * HEAD_DIM
    mix_low = mix_weight[0].astype(LOW)
    share = mix_low.shape[0]
    mix_blocks = jnp.concatenate(
        [
            mix_low[:, :D].reshape(share, SQUARE, wide),
            mix_low[:, D : D + key_width].reshape(share, SQUARE, HEAD_DIM),
            mix_low[:, D + key_width :].reshape(share, SQUARE, HEAD_DIM),
        ],
        axis=2,
    ).transpose(1, 0, 2)
    unit = FF // FLEET
    in_low = in_weight[0].astype(LOW)
    out_low = out_weight[0].astype(LOW)
    down_low = down_weight[0].astype(LOW)
    rank = seq * 2 + fsdp
    gain_block = lax.dynamic_update_slice(
        jnp.zeros((16, 256), LOW), norm_gains[0].astype(LOW), (0, rank * share % 128)
    )
    hidden_out, grad_tokens, mix_got, out_got, in_got, down_got, gain_got, totals, _ = layer(
        lengths,
        frequency[:, None],
        tokens,
        gain_block,
        mix_blocks,
        out_low,
        in_low,
        down_low,
        cotangent,
    )

    norm_grad = gain_got[None, :2, :share]
    grad_norm = jnp.sqrt(totals[0, 0])
    clip_scale = CLIP_NORM / jnp.maximum(grad_norm, CLIP_NORM)
    hidden_out, grad_tokens, *updates = adam_all(
        totals,
        (hidden_out, grad_tokens),
        [
            (mix_weight[0], mix_first[0], mix_second[0], mix_got),
            (out_weight[0], out_first[0], out_second[0], out_got),
            (in_weight[0], in_first[0], in_second[0], in_got),
            (down_weight[0], down_first[0], down_second[0], down_got),
        ],
    )
    new, moment, square = adam_update(
        norm_gains, norm_first, norm_second, norm_grad, clip_scale, GAIN_RATE
    )
    results = [hidden_out, grad_tokens, grad_norm] + [array[None] for array in updates]
    return tuple(results + [norm_grad, new, moment, square, new.astype(LOW)])


def solution(mesh):
    squares = mesh.shape["seq"] == SEQ and mesh.shape["fsdp"] == 2
    return jax.shard_map(
        local_squares if squares else local,
        mesh=mesh,
        in_specs=(
            P(("seq", "fsdp"), None),
            P(("seq", "fsdp"), None),
            P(),
            P(None, ("seq", "fsdp"), None),
            P(None, ("seq", "fsdp"), None),
            P(None, ("seq", "fsdp"), None),
            P(None, ("seq", "fsdp"), None),
            P(None, None, ("seq", "fsdp")),
            P(None, ("seq", "fsdp"), None),
            P(None, ("seq", "fsdp"), None),
            P(None, ("seq", "fsdp"), None),
            P(None, ("seq", "fsdp"), None),
            P(None, None, ("seq", "fsdp")),
            P(None, ("seq", "fsdp"), None),
            P(None, ("seq", "fsdp"), None),
            P(None, ("seq", "fsdp"), None),
            P(None, ("seq", "fsdp"), None),
            P(None, None, ("seq", "fsdp")),
        ),
        out_specs=(
            P(("seq", "fsdp"), None),
            P(("seq", "fsdp"), None),
            P(),
            P(None, ("seq", "fsdp"), None),
            P(None, ("seq", "fsdp"), None),
            P(None, ("seq", "fsdp"), None),
            P(None, ("seq", "fsdp"), None),
            P(None, ("seq", "fsdp"), None),
            P(None, ("seq", "fsdp"), None),
            P(None, ("seq", "fsdp"), None),
            P(None, ("seq", "fsdp"), None),
            P(None, ("seq", "fsdp"), None),
            P(None, ("seq", "fsdp"), None),
            P(None, ("seq", "fsdp"), None),
            P(None, ("seq", "fsdp"), None),
            P(None, ("seq", "fsdp"), None),
            P(None, ("seq", "fsdp"), None),
            P(None, ("seq", "fsdp"), None),
            P(None, ("seq", "fsdp"), None),
            P(None, ("seq", "fsdp"), None),
            P(None, ("seq", "fsdp"), None),
            P(None, ("seq", "fsdp"), None),
            P(None, ("seq", "fsdp"), None),
            P(None, None, ("seq", "fsdp")),
            P(None, None, ("seq", "fsdp")),
            P(None, None, ("seq", "fsdp")),
            P(None, None, ("seq", "fsdp")),
            P(None, None, ("seq", "fsdp")),
        ),
        check_vma=False,
    )
```
